32 devices in a mesh: wide: 8 (over z, x), narrow: 4 (over y, core).
Axes of the slice: x: 2, y: 2, z: 4, core: 2. Of those that a mesh axis runs over, the one named last changes fastest.
Arguments:
- images: bfloat16 [50176, 512], P(('wide', 'narrow')), may hold values from -6 to 6
- tag_ids: int32 [64, 512], P(('wide', 'narrow')), may hold values from 0 to 31
- tag_lengths: int32 [64], P(('wide', 'narrow')), may hold values from 20 to 512, as said below
- cell_mask: int32 [64, 128], P(('wide', 'narrow')), may hold values 0 or 1
- cell_index: int32 [64, 128], P(('wide', 'narrow')), may hold values from 0 to 511
- box_targets: float32 [64, 4, 128], P(('wide', 'narrow')), may hold values from 0.1 to 0.6
- encoder_params: float32 [2099200], P(('wide', 'narrow'))
- encoder_first: float32 [2099200], P(('wide', 'narrow')), may hold values from -6.1035156e-05 to 6.1035156e-05
- encoder_second: float32 [2099200], P(('wide', 'narrow')), may hold values from 9.015533e-12 to 1.4424853e-10
- encoder_average: float32 [2099200], P(('wide', 'narrow'))
- decoder_params: float32 [3446784], P(('wide', 'narrow'))
- decoder_first: float32 [3446784], P(('wide', 'narrow')), may hold values from -6.1035156e-05 to 6.1035156e-05
- decoder_second: float32 [3446784], P(('wide', 'narrow')), may hold values from 9.015533e-12 to 1.4424853e-10
- decoder_average: float32 [3446784], P(('wide', 'narrow'))
Outputs:
- loss_sum: float32 [], replicated
- cell_total: float32 [], replicated
- grad_norm: float32 [], replicated
- encoder_first_new: float32 [2099200], P(('wide', 'narrow'))
- encoder_second_new: float32 [2099200], P(('wide', 'narrow'))
- encoder_params_new: float32 [2099200], P(('wide', 'narrow'))
- encoder_average_new: float32 [2099200], P(('wide', 'narrow'))
- decoder_first_new: float32 [3446784], P(('wide', 'narrow'))
- decoder_second_new: float32 [3446784], P(('wide', 'narrow'))
- decoder_params_new: float32 [3446784], P(('wide', 'narrow'))
- decoder_average_new: float32 [3446784], P(('wide', 'narrow'))
The draws below stay inside these ranges and needn't reach their ends.
Inputs may be any that keep to these rules, and one draw needn't show every extreme that they name: `tag_lengths`: the number of tags in use of each table; the first table has 20 and the last table has 512.
All inputs are finite; a program needn't handle non-finite values. No bound on the sum of `cell_mask` on one device may be relied on, other than what follows from the above.
Results may differ from the reference program's by a relative error of at most 0.012.
The reference program's roundings to bfloat16 on the way count: a program that leaves them out, or rounds other values in their place, can miss the bound.
Values may be sent and summed in bfloat16 or wider, within the bound.
A program may use at most 256 MiB of HBM per device.

```python
import math
import jax
import jax.numpy as jnp
from jax import lax

D = 512
HEADS = 8
FF = 1024
V = 32
IMG = 784
TAGS = 512
STEP = 5
TAB_DEV = 2
CELLS = 128
TABLES = 64
P_ENC = 2099200
P_DEC = 3446784
N_WIDE = 8
N_NARROW = 4


def encoder_spreads():
    return [('qkv', D, 3 * D, D ** (-0.5), 2 * D), ('out', D, D, (max(IMG / 54.0, 1.0) / D) ** 0.5, 0), ('ffn_in', D, FF, D ** (-0.5), 0), ('ffn_out', FF, D, FF ** (-0.5), 0), ('norms', 4, D, 0.0, 0)]


def decoder_spreads():
    return [('qkv', D, 3 * D, D ** (-0.5), 2 * D), ('out', D, D, (max(TAGS / 100.0, 1.0) / D) ** 0.5, 0), ('cross_q', D, D, D ** (-0.5), D), ('cross_kv', D, 2 * D, D ** (-0.5), 0), ('cross_out', D, D, (max(IMG / 54.0, 1.0) / D) ** 0.5, 0), ('ffn_in', D, FF, D ** (-0.5), 0), ('ffn_out', FF, D, FF ** (-0.5), 0), ('embed', V, D, 1.0, 0), ('head', D, V, D ** (-0.5), 0), ('box_in', D, D, D ** (-0.5), 0), ('norms', 8, D, 0.0, 0), ('box_out', D, 4, 2.0 * D ** (-0.5), 0)]


def shape_params(noise, layout):
    segments = []
    offset = 0
    for piece_name, height, breadth, spread, sharp in layout:
        amount = height * breadth
        segment = noise[offset:offset + amount].reshape(height, breadth)
        offset = offset + amount
        if spread > 0.0:
            column_factor = jnp.where(jnp.arange(breadth) < sharp, 1.4142135, 1.0).astype(jnp.float32)
            segments.append((segment * spread * column_factor[None, :]).reshape(-1))
        else:
            rising = 0.5 + jnp.arange(breadth, dtype=jnp.float32) / breadth
            parity = (jnp.arange(height) % 2 == 0)[:, None]
            segments.append(jnp.where(parity, rising[None, :] * (1.0 + 0.1 * segment), 0.1 * segment).reshape(-1))
    return jnp.concatenate(segments)


def draw_tag_lengths(key, part):
    key = jax.random.fold_in(key, 5)
    device = jnp.arange(TABLES, dtype=jnp.int32) // TAB_DEV
    along_wide = device // N_NARROW
    along_narrow = device % N_NARROW
    scale_wide = N_WIDE - 1 + 2 * along_wide
    scale_narrow = N_NARROW - 1 + 2 * along_narrow
    ceiling = 20 + (TAGS - 20) * scale_wide * scale_narrow // (9 * (N_WIDE - 1) * (N_NARROW - 1))
    trimmed = ceiling - jax.random.randint(key, (TABLES,), 0, ceiling // 4 + 1)
    trimmed = jnp.maximum(trimmed, 20)
    trimmed = jnp.where(jnp.arange(TABLES) == 0, 20, trimmed)
    trimmed = jnp.where(jnp.arange(TABLES) == TABLES - 1, TAGS, trimmed)
    return trimmed.astype(jnp.int32)


def draw_encoder_params(key, part):
    key = jax.random.fold_in(key, 11)
    noise = jax.random.normal(key, (P_ENC,), jnp.float32)
    return shape_params(noise, encoder_spreads())


def draw_encoder_average(key, part):
    key = jax.random.fold_in(key, 13)
    noise = jax.random.normal(key, (P_ENC,), jnp.float32)
    return shape_params(noise, encoder_spreads())


def draw_decoder_params(key, part):
    key = jax.random.fold_in(key, 17)
    noise = jax.random.normal(key, (P_DEC,), jnp.float32)
    return shape_params(noise, decoder_spreads())


def draw_decoder_average(key, part):
    key = jax.random.fold_in(key, 19)
    noise = jax.random.normal(key, (P_DEC,), jnp.float32)
    return shape_params(noise, decoder_spreads())


def set_ends(values, rng, smallest, top_value):
    shape = values.shape
    spot = [jax.random.randint(jax.random.fold_in(rng, axis), (), 0, shape[axis]) for axis in range(len(shape))]
    values = values.at[tuple(spot)].set(smallest)
    longest = shape.index(max(shape))
    spot[longest] = (spot[longest] + 1) % shape[longest]
    return values.at[tuple(spot)].set(top_value)


def levels(own_key, dims, shards, least, high):
    factor_of, own = 1.0, jax.random.fold_in(own_key, 6)
    for dim, shards_of in shards:
        steps = jnp.exp(jax.random.uniform(jax.random.fold_in(own, dim), (shards_of,), jnp.float32, least / len(shards), high / len(shards)))
        factor_of = factor_of * jnp.repeat(steps, dims[dim] // shards_of).reshape([-1 if axis == dim else 1 for axis in range(len(dims))])
    return factor_of


def gaussian(own_key, shape, scale, reach, split=(), kind=jnp.bfloat16):
    loudness = levels(own_key, shape, split, -0.22, 0.18) if split else 1.0
    drawn = jax.random.normal(own_key, shape, jnp.float32) * scale * loudness
    return jnp.minimum(jnp.maximum(drawn, -reach), reach).astype(kind)


def setup_inputs(seed: int = 0) -> dict:
    key_list = jax.random.split(jax.random.key(seed), 15)
    return {
        "images": gaussian(key_list[0], (TABLES * IMG, D), 1.0, 6.0, ((0, 32),)),
        "tag_ids": set_ends(jax.random.randint(key_list[1], (TABLES, TAGS), 0, V), jax.random.fold_in(key_list[1], 1), 0, V - 1).astype(jnp.int32),
        "tag_lengths": draw_tag_lengths(jax.random.fold_in(key_list[14], 71), 0),
        "cell_mask": set_ends((jax.random.randint(key_list[3], (TABLES, CELLS), 0, 4) < 3).astype(jnp.int32), jax.random.fold_in(key_list[3], 1), 0, 1),
        "cell_index": set_ends(jax.random.randint(key_list[4], (TABLES, CELLS), 0, TAGS), jax.random.fold_in(key_list[4], 1), 0, TAGS - 1).astype(jnp.int32),
        "box_targets": jnp.clip(0.1 + 0.5 * jax.random.uniform(key_list[5], (TABLES, 4, CELLS), jnp.float32) ** levels(key_list[5], (TABLES, 4, CELLS), ((0, 32),), -0.2, 0.2), 0.1, 0.6),
        "encoder_params": draw_encoder_params(jax.random.fold_in(key_list[14], 71), 0),
        "encoder_first": gaussian(key_list[7], (P_ENC,), (0.01 * (P_ENC + P_DEC) ** -0.5), 6.103515625e-05, ((0, 32),), jnp.float32),
        "encoder_second": jnp.clip(jnp.exp(math.log(1.4424852978756064e-10) - 2.7725887 * jax.random.uniform(key_list[8], (P_ENC,), jnp.float32) ** levels(key_list[8], (P_ENC,), ((0, 32),), -0.2, 0.2)), 9.01553311172254e-12, 1.4424852978756064e-10),
        "encoder_average": draw_encoder_average(jax.random.fold_in(key_list[14], 71), 0),
        "decoder_params": draw_decoder_params(jax.random.fold_in(key_list[14], 71), 0),
        "decoder_first": gaussian(key_list[11], (P_DEC,), (0.01 * (P_ENC + P_DEC) ** -0.5), 6.103515625e-05, ((0, 32),), jnp.float32),
        "decoder_second": jnp.clip(jnp.exp(math.log(1.4424852978756064e-10) - 2.7725887 * jax.random.uniform(key_list[12], (P_DEC,), jnp.float32) ** levels(key_list[12], (P_DEC,), ((0, 32),), -0.2, 0.2)), 9.01553311172254e-12, 1.4424852978756064e-10),
        "decoder_average": draw_decoder_average(jax.random.fold_in(key_list[14], 71), 0),
    }


TOP_MATMUL_MODE = lax.Precision.HIGHEST
BETA_ONE = 0.5
BETA_TWO = 0.5
CLIP_NORM = 0.01
LEARN_RATE = 0.05
WEIGHT_DECAY = 0.01
EPSILON = 1e-08
SMOOTH = 0.9

@jax.custom_vjp
def low(v):
    return lax.optimization_barrier(v.astype(jnp.bfloat16)).astype(jnp.float32)

@jax.custom_vjp
def low_back(v):
    return v

def low_keep(v):
    return (low(v), None)

def low_pass(kept, grad):
    return (grad,)

def back_keep(v):
    return (v, None)

def back_low(kept, grad):
    return (low(grad),)
low.defvjp(low_keep, low_pass)
low_back.defvjp(back_keep, back_low)

def encoder_layout():
    return [('qkv', (D, 3 * D)), ('out', (D, D)), ('ffn_in', (D, FF)), ('ffn_out', (FF, D)), ('norms', (4, D))]

def decoder_layout():
    return [('qkv', (D, 3 * D)), ('out', (D, D)), ('cross_q', (D, D)), ('cross_kv', (D, 2 * D)), ('cross_out', (D, D)), ('ffn_in', (D, FF)), ('ffn_out', (FF, D)), ('embed', (V, D)), ('head', (D, V)), ('box_in', (D, D)), ('norms', (8, D)), ('box_out', (D, 4))]

def unflatten(flat_values, layout):
    pieces = {}
    offset = 0
    for piece_name, extent in layout:
        amount = extent[0] * extent[1]
        pieces[piece_name] = flat_values[offset:offset + amount].reshape(extent)
        offset = offset + amount
    return pieces

def matmul_high(left, right):
    return jnp.matmul(left, right, precision=TOP_MATMUL_MODE)

def layer_norm(inputs, gain, shift):
    centred = inputs - lax.optimization_barrier(jnp.mean(inputs, -1, keepdims=True))
    variance = lax.optimization_barrier(jnp.mean(centred * centred, -1, keepdims=True))
    return centred * lax.rsqrt(variance + 1e-05) * gain + shift

def soft_low(first_one, other_one):
    return 0.5 * (first_one + other_one - jnp.sqrt((first_one - other_one) ** 2 + 0.0001))

def soft_high(first_one, other_one):
    return 0.5 * (first_one + other_one + jnp.sqrt((first_one - other_one) ** 2 + 0.0001))

def table_loss(logits, raw_box, tag_row, length, alive_row, target):
    row_index = jnp.arange(TAGS)
    upcoming = jnp.concatenate([tag_row[1:], tag_row[:1]])
    counted = (row_index < length - 1).astype(jnp.float32)
    logprob = jax.nn.log_softmax(logits, -1)
    chosen = lax.optimization_barrier(jnp.sum(jnp.where(upcoming[:, None] == jnp.arange(V)[None, :], logprob, 0.0), -1))
    tag_part = -jnp.sum(counted * chosen)
    predicted = jnp.transpose(jax.nn.sigmoid(raw_box))
    deviation = predicted - target
    absolute = lax.optimization_barrier(jnp.sum(jnp.sqrt(deviation * deviation + 0.01), 0))
    left_pred = predicted[0] - 0.5 * predicted[2]
    right_pred = predicted[0] + 0.5 * predicted[2]
    bottom_pred = predicted[1] - 0.5 * predicted[3]
    top_pred = predicted[1] + 0.5 * predicted[3]
    left_true = target[0] - 0.5 * target[2]
    right_true = target[0] + 0.5 * target[2]
    bottom_true = target[1] - 0.5 * target[3]
    top_true = target[1] + 0.5 * target[3]
    intersection_across = jax.nn.softplus(20.0 * (soft_low(right_pred, right_true) - soft_high(left_pred, left_true))) / 20.0
    intersection_upward = jax.nn.softplus(20.0 * (soft_low(top_pred, top_true) - soft_high(bottom_pred, bottom_true))) / 20.0
    common = intersection_across * intersection_upward
    union_area = predicted[2] * predicted[3] + target[2] * target[3] - common
    hull_area = (soft_high(right_pred, right_true) - soft_low(left_pred, left_true)) * (soft_high(top_pred, top_true) - soft_low(bottom_pred, bottom_true))
    ratio_term = common / union_area - (hull_area - union_area) / hull_area
    cell_part = 5.0 * absolute + 2.0 * (1.0 - ratio_term)
    return tag_part + jnp.sum(alive_row * cell_part)

def attention(queries, keys, values, causal):
    height = queries.shape[0]
    breadth = keys.shape[0]
    head_width = D // HEADS
    split_queries = queries.reshape(height, HEADS, head_width)
    split_keys = keys.reshape(breadth, HEADS, head_width)
    split_values = values.reshape(breadth, HEADS, head_width)
    score_matrix = low_back(jnp.einsum('qye,iye->yqi', split_queries, split_keys, precision=TOP_MATMUL_MODE)) * head_width ** (-0.5)
    if causal:
        allowed = jnp.arange(breadth)[None, :] <= jnp.arange(height)[:, None]
        score_matrix = jnp.where(allowed[None], score_matrix, -1e+30)
    row_peak = lax.optimization_barrier(jnp.max(score_matrix, -1, keepdims=True))
    exponent = jnp.exp(score_matrix - row_peak)
    attention_weights = low(exponent / lax.optimization_barrier(jnp.sum(exponent, -1, keepdims=True)))
    merged_heads = low_back(jnp.einsum('yqz,zyx->qyx', attention_weights, split_values, precision=TOP_MATMUL_MODE))
    return low(merged_heads.reshape(height, D))

def feed_forward(inputs, gain, shift, w_in, w_out):
    hidden = low(layer_norm(inputs, gain, shift))
    pre_active = low_back(matmul_high(hidden, w_in))
    return low_back(matmul_high(low(jax.nn.gelu(pre_active)), w_out))

def encoder(inputs, weights):
    norm_rows = weights['norms']
    hidden = low(layer_norm(inputs, norm_rows[0], norm_rows[1]))
    project = low(low_back(matmul_high(hidden, weights['qkv'])))
    merged_heads = attention(project[:, :D], project[:, D:2 * D], project[:, 2 * D:], False)
    middle = inputs + low_back(matmul_high(merged_heads, weights['out']))
    return middle + feed_forward(middle, norm_rows[2], norm_rows[3], weights['ffn_in'], weights['ffn_out'])

def decoder(tag_row, memory, length, position, alive_row, target, weights):
    norm_rows = weights['norms']
    onehot = (tag_row[:, None] == jnp.arange(V)[None, :]).astype(jnp.float32)
    embedded = matmul_high(onehot, weights['embed'])
    hidden = low(layer_norm(embedded, norm_rows[0], norm_rows[1]))
    project = low(low_back(matmul_high(hidden, weights['qkv'])))
    merged_heads = attention(project[:, :D], project[:, D:2 * D], project[:, 2 * D:], True)
    after_self = embedded + low_back(matmul_high(merged_heads, weights['out']))
    hidden = low(layer_norm(after_self, norm_rows[2], norm_rows[3]))
    queries = low(low_back(matmul_high(hidden, weights['cross_q'])))
    source = low(low_back(matmul_high(low(memory), weights['cross_kv'])))
    merged_heads = attention(queries, source[:, :D], source[:, D:], False)
    second = after_self + low_back(matmul_high(merged_heads, weights['cross_out']))
    after_dense = second + feed_forward(second, norm_rows[4], norm_rows[5], weights['ffn_in'], weights['ffn_out'])
    final_rows = low(layer_norm(after_dense, norm_rows[6], norm_rows[7]))
    logits = low_back(matmul_high(final_rows, weights['head']))
    picked = final_rows[position]
    box_inner = low_back(matmul_high(picked, weights['box_in']))
    raw_box = low_back(matmul_high(low(jax.nn.gelu(box_inner)), weights['box_out']))
    return table_loss(logits, raw_box, tag_row, length, alive_row, target)

def adam_update(gradient, master, first_state, second_state, average):
    first_new = BETA_ONE * first_state + (1.0 - BETA_ONE) * gradient
    second_new = BETA_TWO * second_state + (1.0 - BETA_TWO) * gradient * gradient
    first_hat = first_new / (1.0 - BETA_ONE ** STEP)
    second_hat = second_new / (1.0 - BETA_TWO ** STEP)
    master_new = master - LEARN_RATE * (first_hat / (jnp.sqrt(second_hat) + EPSILON) + WEIGHT_DECAY * master)
    average_new = SMOOTH * average + (1.0 - SMOOTH) * master_new
    return (first_new, second_new, master_new, average_new)

def reference(images, tag_ids, tag_lengths, cell_mask, cell_index, box_targets, encoder_params, encoder_first, encoder_second, encoder_average, decoder_params, decoder_first, decoder_second, decoder_average):
    cell_slots = jnp.arange(CELLS)
    alive_cells = ((cell_mask > 0) & (cell_slots[None, :] < (tag_lengths // 4)[:, None])).astype(jnp.float32)
    cell_total = jnp.sum(alive_cells)
    position = (cell_index % tag_lengths[:, None]).astype(jnp.int32)
    pictures = images.astype(jnp.float32).reshape(TABLES, IMG, D)

    def objective(encoder_flat, decoder_flat):
        encoder_weights = unflatten(low(encoder_flat), encoder_layout())
        decoder_weights = unflatten(low(decoder_flat), decoder_layout())

        def one_table(members):
            picture, tag_row, length, place, alive_row, target = members
            memory = encoder(picture, encoder_weights)
            return decoder(tag_row, memory, length, place, alive_row, target, decoder_weights)
        losses = lax.map(jax.checkpoint(one_table), (pictures, tag_ids, tag_lengths, position, alive_cells, box_targets))
        return jnp.sum(losses)
    loss_sum, pullback = jax.vjp(objective, encoder_params, decoder_params)
    encoder_grad, decoder_grad = pullback(1.0 / cell_total)
    grad_norm = jnp.sqrt(jnp.sum(encoder_grad * encoder_grad) + jnp.sum(decoder_grad * decoder_grad))
    factor = CLIP_NORM / jnp.maximum(grad_norm, CLIP_NORM)
    encoder_new = adam_update(encoder_grad * factor, encoder_params, encoder_first, encoder_second, encoder_average)
    decoder_new = adam_update(decoder_grad * factor, decoder_params, decoder_first, decoder_second, decoder_average)
    return (loss_sum, cell_total, grad_norm, encoder_new[0], encoder_new[1], encoder_new[2], encoder_new[3], decoder_new[0], decoder_new[1], decoder_new[2], decoder_new[3])
```

```python
import functools

import jax
import jax.numpy as jnp
from jax import lax
from jax.experimental import pallas as pl
from jax.experimental.pallas import tpu as pltpu
from jax.sharding import PartitionSpec as P

D = 512
HEADS = 8
HEAD = D // HEADS
PAIRS = HEADS // 2
FF = 1024
V = 32
IMG = 784
TAGS = 512
STEP = 5
CELLS = 128
IMG_CHUNK = 112
TAG_CHUNK = 128

BETA_ONE = 0.5
BETA_TWO = 0.5
CLIP_NORM = 0.01
LEARN_RATE = 0.05
WEIGHT_DECAY = 0.01
EPSILON = 1e-08
SMOOTH = 0.9

VMEM_LIMIT = 60 * 2**20
bf16 = jnp.bfloat16
f32 = jnp.float32


def encoder_layout():
    return [
        ("qkv", (D, 3 * D)),
        ("out", (D, D)),
        ("ffn_in", (D, FF)),
        ("ffn_out", (FF, D)),
        ("norms", (4, D)),
    ]


def decoder_layout():
    return [
        ("qkv", (D, 3 * D)),
        ("out", (D, D)),
        ("cross_q", (D, D)),
        ("cross_kv", (D, 2 * D)),
        ("cross_out", (D, D)),
        ("ffn_in", (D, FF)),
        ("ffn_out", (FF, D)),
        ("embed", (V, D)),
        ("head", (D, V)),
        ("box_in", (D, D)),
        ("norms", (8, D)),
        ("box_out", (D, 4)),
    ]


def dot(left, right, over_left=1, over_right=0):
    return lax.dot_general(
        left, right, (((over_left,), (over_right,)), ((), ())), preferred_element_type=f32
    )


def each_rows(total, step, body):
    @pl.loop(0, total // step)
    def _(index):
        body(pl.ds(pl.multiple_of(index * step, step), step))


def norm_rows(value, gain, shift):
    centred = value - jnp.mean(value, -1, keepdims=True)
    variance = jnp.mean(centred * centred, -1, keepdims=True)
    return centred * lax.rsqrt(variance + 1e-05) * gain + shift


def norm_rows_back(value, gain, upstream):
    centred = value - jnp.mean(value, -1, keepdims=True)
    variance = jnp.mean(centred * centred, -1, keepdims=True)
    scale = lax.rsqrt(variance + 1e-05)
    unit = centred * scale
    inner = upstream * gain
    mean_inner = jnp.mean(inner, -1, keepdims=True)
    mean_both = jnp.mean(inner * unit, -1, keepdims=True)
    down = scale * (inner - mean_inner - unit * mean_both)
    return (
        down,
        jnp.sum(upstream * unit, 0, keepdims=True),
        jnp.sum(upstream, 0, keepdims=True),
    )


GELU_A = 0.7978845608028654
GELU_B = 0.044715


def gelu(value):
    inner = jnp.tanh(GELU_A * (value + GELU_B * value * value * value))
    return 0.5 * value * (1.0 + inner)


def gelu_slope(value):
    square = value * value
    inner = jnp.tanh(GELU_A * (value + GELU_B * square * value))
    slope = GELU_A * (1.0 + 3.0 * GELU_B * square)
    return 0.5 * (1.0 + inner) + 0.5 * value * (1.0 - inner * inner) * slope


def half_masks():
    lane = lax.broadcasted_iota(jnp.int32, (1, 2 * HEAD), 1)
    first = (lane < HEAD).astype(f32)
    return (first.astype(bf16), (1.0 - first).astype(bf16))


def query_blocks(query_rows, key_rows, causal):
    if not causal:
        return [(0, query_rows, key_rows)]
    return [(start, 256, start + 256) for start in range(0, query_rows, 256)]


def causal_keep(start, width, depth):
    key = lax.broadcasted_iota(jnp.int32, (depth, width), 0)
    query = lax.broadcasted_iota(jnp.int32, (depth, width), 1) + start
    return key <= query


def attend(tables, q_ref, k_ref, k_col, v_ref, v_col, o_ref, lse_ref, query_rows, key_rows, causal):
    masks = half_masks()

    @pl.loop(0, tables * PAIRS)
    def _(step):
        table = lax.div(step, PAIRS)
        pair = lax.rem(step, PAIRS)
        q_rows = pl.ds(pl.multiple_of(table * query_rows, 16), query_rows)
        k_rows = pl.ds(pl.multiple_of(table * key_rows, 16), key_rows)
        lanes = pl.multiple_of(pair * 128, 128)
        queries = q_ref[q_rows, pl.ds(lanes, 128)]
        keys = k_ref[k_rows, pl.ds(k_col + lanes, 128)]
        values = v_ref[k_rows, pl.ds(v_col + lanes, 128)].T
        outs = []
        for half in range(2):
            own = queries * masks[half]
            own_values = values[half * HEAD : (half + 1) * HEAD, :]
            parts, sums = [], []
            for start, width, depth in query_blocks(query_rows, key_rows, causal):
                scores = dot(keys[:depth], own[start : start + width], 1, 1)
                if causal:
                    scores = jnp.where(causal_keep(start, width, depth), scores, -1e30)
                peak = jnp.max(scores, 0, keepdims=True)
                weight = jnp.exp(scores - peak)
                total = jnp.sum(weight, 0, keepdims=True)
                mixed = dot(own_values[:, :depth], weight.astype(bf16))
                parts.append(mixed * (1.0 / total))
                sums.append(peak + jnp.log(total))
            outs.append(parts[0] if len(parts) == 1 else jnp.concatenate(parts, 1))
            lse_ref[pl.ds(table * HEADS + pair * 2 + half, 1), :] = (
                sums[0] if len(sums) == 1 else jnp.concatenate(sums, 1)
            )
        joined = jnp.concatenate(outs, 0).astype(bf16)
        o_ref[q_rows, pl.ds(lanes, 128)] = joined.T


def head_sums(tables, up_ref, o_ref, delta_ref, query_rows):
    row = lax.broadcasted_iota(jnp.int32, (16, D), 0)
    lane = lax.broadcasted_iota(jnp.int32, (16, D), 1)
    member = (lax.shift_right_logical(lane, 6) == row).astype(f32).astype(bf16)
    for table in range(tables):
        rows = slice(table * query_rows, (table + 1) * query_rows)
        both = up_ref[rows, :].astype(f32) * o_ref[rows, :].astype(f32)
        high = both.astype(bf16)
        rest = (both - high.astype(f32)).astype(bf16)
        sums = dot(member, high, 1, 1) + dot(member, rest, 1, 1)
        delta_ref[table * HEADS : (table + 1) * HEADS, :] = sums[:HEADS]


def attend_back(
    tables, q_ref, k_ref, k_col, v_ref, v_col, up_ref, lse_ref, delta_ref,
    dq_ref, dk_ref, dv_ref, query_rows, key_rows, causal,
):
    masks = half_masks()

    @pl.loop(0, tables * PAIRS)
    def _(step):
        table = lax.div(step, PAIRS)
        pair = lax.rem(step, PAIRS)
        q_rows = pl.ds(pl.multiple_of(table * query_rows, 16), query_rows)
        k_rows = pl.ds(pl.multiple_of(table * key_rows, 16), key_rows)
        lanes = pl.multiple_of(pair * 128, 128)
        queries = q_ref[q_rows, pl.ds(lanes, 128)]
        keys = k_ref[k_rows, pl.ds(k_col + lanes, 128)]
        values = v_ref[k_rows, pl.ds(v_col + lanes, 128)]
        upstream = up_ref[q_rows, pl.ds(lanes, 128)]
        keys_across = keys.T
        blocks = query_blocks(query_rows, key_rows, causal)
        grad_q = []
        grad_k = [None] * len(blocks)
        grad_v = [None] * len(blocks)
        for half in range(2):
            index = pl.ds(table * HEADS + pair * 2 + half, 1)
            own = queries * masks[half]
            own_up = upstream * masks[half]
            logsum = lse_ref[index, :]
            delta = delta_ref[index, :]
            across = keys_across[half * HEAD : (half + 1) * HEAD, :]
            parts = []
            for number, (start, width, depth) in enumerate(blocks):
                span = slice(start, start + width)
                weight = jnp.exp(dot(keys[:depth], own[span], 1, 1) - logsum[:, span])
                if causal:
                    weight = jnp.where(causal_keep(start, width, depth), weight, 0.0)
                pull = dot(values[:depth], own_up[span], 1, 1)
                change = (weight * (pull - delta[:, span])).astype(bf16)
                add_v = dot(weight.astype(bf16), own_up[span])
                add_k = dot(change, own[span])
                grad_v[number] = add_v if half == 0 else grad_v[number] + add_v
                grad_k[number] = add_k if half == 0 else grad_k[number] + add_k
                parts.append(dot(across[:, :depth], change) * 0.125)
            grad_q.append(parts[0] if len(parts) == 1 else jnp.concatenate(parts, 1))
        dq_ref[q_rows, pl.ds(lanes, 128)] = jnp.concatenate(grad_q, 0).astype(bf16).T
        for ref, column, grads in ((dk_ref, k_col, grad_k), (dv_ref, v_col, grad_v)):
            total = grads[-1]
            if len(grads) == 2:
                low = blocks[0][2]
                total = jnp.concatenate([total[:low] + grads[0], total[low:]], 0)
            ref[k_rows, pl.ds(column + lanes, 128)] = total.astype(bf16)


def project(a_ref, w_ref, out_ref, width, first_scale=None):
    for start in range(0, width, 512):
        value = dot(a_ref[...], w_ref[:, start : start + 512])
        if first_scale is not None and start == 0:
            value = value * first_scale
        out_ref[:, start : start + 512] = value.astype(bf16)


def add_project(base_ref, a_ref, w_ref, out_ref):
    for start in range(0, D, 256):
        lanes = slice(start, start + 256)
        out_ref[:, lanes] = base_ref[:, lanes].astype(f32) + dot(a_ref[...], w_ref[:, lanes])


def weight_grad(a_ref, b_ref, out_ref):
    rows, columns = out_ref.shape
    for start in range(0, columns, 512):
        lanes = slice(start, start + 512)
        out_ref[:, lanes] = dot(a_ref[...], b_ref[:, lanes], 0, 0).astype(out_ref.dtype)


def ffn_forward(h_ref, w_in, u_ref, g_ref):
    for start in range(0, FF, 256):
        lanes = slice(start, start + 256)
        inner = dot(h_ref[...], w_in[:, lanes])
        if u_ref is not None:
            u_ref[:, lanes] = inner
        g_ref[:, lanes] = gelu(inner).astype(bf16)


def ffn_backward(og_ref, h_ref, u_ref, g_ref, w_in, w_out, d_in, d_out, dh_ref):
    weight_grad(g_ref, og_ref, d_out)
    for start in range(0, FF, 256):
        lanes = slice(start, start + 256)
        back = dot(og_ref[...], w_out[lanes, :], 1, 1)
        g_ref[:, lanes] = (gelu_slope(u_ref[:, lanes]) * back).astype(bf16)
    weight_grad(h_ref, g_ref, d_in)
    project_back(g_ref, w_in, dh_ref)


def project_back(g_ref, w_ref, out_ref):
    for start in range(0, D, 256):
        lanes = slice(start, start + 256)
        out_ref[:, lanes] = dot(g_ref[...], w_ref[lanes, :], 1, 1).astype(out_ref.dtype)


def norm_all(x_ref, norms_ref, row, out_ref, total, step):
    gain, shift = norms_ref[row : row + 1, :], norms_ref[row + 1 : row + 2, :]

    def body(rows):
        out_ref[rows, :] = norm_rows(x_ref[rows, :].astype(f32), gain, shift).astype(bf16)

    each_rows(total, step, body)


def norm_all_back(x_ref, norms_ref, row, up_ref, dnorms_ref, total, step, keep):
    gain = norms_ref[row : row + 1, :]
    dnorms_ref[row : row + 2, :] = jnp.zeros((2, D), f32)

    def body(rows):
        down, d_gain, d_shift = norm_rows_back(x_ref[rows, :].astype(f32), gain, up_ref[rows, :])
        dnorms_ref[row : row + 1, :] += d_gain
        dnorms_ref[row + 1 : row + 2, :] += d_shift
        if keep is not None:
            keep(rows, down)

    each_rows(total, step, body)


def encoder_forward_kernel(
    x_ref, w_qkv, w_out, w_in, w_ffo, norms, qkv_ref, o_ref, lse_ref, x1_ref, mem_ref, h_ref, g_ref
):
    rows = x_ref.shape[0]
    tables = rows // IMG
    norm_all(x_ref, norms, 0, h_ref, rows, IMG_CHUNK)
    project(h_ref, w_qkv, qkv_ref, 3 * D, 0.125)
    attend(tables, qkv_ref, qkv_ref, D, qkv_ref, 2 * D, o_ref, lse_ref, IMG, IMG, False)
    add_project(x_ref, o_ref, w_out, x1_ref)
    norm_all(x1_ref, norms, 2, h_ref, rows, IMG_CHUNK)
    ffn_forward(h_ref, w_in, None, g_ref)
    for start in range(0, D, 256):
        lanes = slice(start, start + 256)
        mem_ref[:, lanes] = (x1_ref[:, lanes] + dot(g_ref[...], w_ffo[:, lanes])).astype(bf16)


def encoder_forward(images, weights):
    rows = images.shape[0]
    tables = rows // IMG
    return pl.pallas_call(
        encoder_forward_kernel,
        out_shape=(
            jax.ShapeDtypeStruct((rows, 3 * D), bf16),
            jax.ShapeDtypeStruct((rows, D), bf16),
            jax.ShapeDtypeStruct((tables * HEADS, IMG), f32),
            jax.ShapeDtypeStruct((rows, D), f32),
            jax.ShapeDtypeStruct((rows, D), bf16),
        ),
        scratch_shapes=[pltpu.VMEM((rows, D), bf16), pltpu.VMEM((rows, FF), bf16)],
        compiler_params=pltpu.CompilerParams(vmem_limit_bytes=VMEM_LIMIT),
        name="encoder_forward",
    )(images, weights["qkv"], weights["out"], weights["ffn_in"], weights["ffn_out"], weights["norms"])


def encoder_backward_kernel(
    x_ref, qkv_ref, o_ref, lse_ref, x1_ref, dmem_ref, w_qkv, w_out, w_in, w_ffo, norms,
    d_qkv, d_out, d_in, d_ffo, d_norms,
    h_ref, u_ref, g_ref, dh_ref, og_ref, up_ref, dqkv_ref, delta_ref,
):
    rows = x_ref.shape[0]
    tables = rows // IMG
    norm_all(x1_ref, norms, 2, h_ref, rows, IMG_CHUNK)
    ffn_forward(h_ref, w_in, u_ref, g_ref)
    og_ref[...] = dmem_ref[...].astype(bf16)
    ffn_backward(og_ref, h_ref, u_ref, g_ref, w_in, w_ffo, d_in, d_ffo, dh_ref)

    def keep(block, down):
        og_ref[block, :] = (down + dmem_ref[block, :]).astype(bf16)

    norm_all_back(x1_ref, norms, 2, dh_ref, d_norms, rows, IMG_CHUNK, keep)
    weight_grad(o_ref, og_ref, d_out)
    project_back(og_ref, w_out, up_ref)
    head_sums(tables, up_ref, o_ref, delta_ref, IMG)
    attend_back(
        tables, qkv_ref, qkv_ref, D, qkv_ref, 2 * D, up_ref, lse_ref, delta_ref,
        dqkv_ref, dqkv_ref, dqkv_ref, IMG, IMG, False,
    )
    norm_all(x_ref, norms, 0, h_ref, rows, IMG_CHUNK)
    weight_grad(h_ref, dqkv_ref, d_qkv)
    project_back(dqkv_ref, w_qkv, dh_ref)
    norm_all_back(x_ref, norms, 0, dh_ref, d_norms, rows, IMG_CHUNK, None)


def encoder_backward(images, stored, dmem, weights):
    rows = images.shape[0]
    tables = rows // IMG
    qkv, mixed, lse, middle = stored
    outs = pl.pallas_call(
        encoder_backward_kernel,
        out_shape=(
            jax.ShapeDtypeStruct((D, 3 * D), bf16),
            jax.ShapeDtypeStruct((D, D), bf16),
            jax.ShapeDtypeStruct((D, FF), bf16),
            jax.ShapeDtypeStruct((FF, D), bf16),
            jax.ShapeDtypeStruct((4, D), f32),
        ),
        scratch_shapes=[
            pltpu.VMEM((rows, D), bf16),
            pltpu.VMEM((rows, FF), f32),
            pltpu.VMEM((rows, FF), bf16),
            pltpu.VMEM((rows, D), f32),
            pltpu.VMEM((rows, D), bf16),
            pltpu.VMEM((rows, D), bf16),
            pltpu.VMEM((rows, 3 * D), bf16),
            pltpu.VMEM((tables * HEADS, IMG), f32),
        ],
        compiler_params=pltpu.CompilerParams(vmem_limit_bytes=VMEM_LIMIT),
        name="encoder_backward",
    )(
        images, qkv, mixed, lse, middle, dmem,
        weights["qkv"], weights["out"], weights["ffn_in"], weights["ffn_out"], weights["norms"],
    )
    return dict(zip(("qkv", "out", "ffn_in", "ffn_out", "norms"), outs))


def soft_low(first_one, other_one):
    return 0.5 * (first_one + other_one - jnp.sqrt((first_one - other_one) ** 2 + 0.0001))


def soft_high(first_one, other_one):
    return 0.5 * (first_one + other_one + jnp.sqrt((first_one - other_one) ** 2 + 0.0001))


def softplus(value):
    return jnp.maximum(value, 0.0) + jnp.log1p(jnp.exp(-jnp.abs(value)))


@jax.custom_vjp
def smooth_relu(value):
    return softplus(value)


def smooth_relu_keep(value):
    return softplus(value), value


def smooth_relu_back(value, upstream):
    return (upstream * (1.0 / (1.0 + jnp.exp(-value))),)


smooth_relu.defvjp(smooth_relu_keep, smooth_relu_back)


def cell_losses(px, py, pw, ph, gx, gy, gw, gh):
    absolute = (
        jnp.sqrt((px - gx) ** 2 + 0.01)
        + jnp.sqrt((py - gy) ** 2 + 0.01)
        + jnp.sqrt((pw - gw) ** 2 + 0.01)
        + jnp.sqrt((ph - gh) ** 2 + 0.01)
    )
    left_p, right_p = px - 0.5 * pw, px + 0.5 * pw
    low_p, top_p = py - 0.5 * ph, py + 0.5 * ph
    left_g, right_g = gx - 0.5 * gw, gx + 0.5 * gw
    low_g, top_g = gy - 0.5 * gh, gy + 0.5 * gh
    across = smooth_relu(20.0 * (soft_low(right_p, right_g) - soft_high(left_p, left_g))) / 20.0
    upward = smooth_relu(20.0 * (soft_low(top_p, top_g) - soft_high(low_p, low_g))) / 20.0
    common = across * upward
    union = pw * ph + gw * gh - common
    hull = (soft_high(right_p, right_g) - soft_low(left_p, left_g)) * (
        soft_high(top_p, top_g) - soft_low(low_p, low_g)
    )
    ratio = common / union - (hull - union) / hull
    return 5.0 * absolute + 2.0 * (1.0 - ratio)


def split_sum(left, value):
    high = value.astype(bf16)
    rest = (value - high.astype(f32)).astype(bf16)
    return dot(left, high) + dot(left, rest)


def decoder_kernel(
    tags_ref, next_ref, counted_ref, place_ref, alive_ref, target_ref, scale_ref, mem_ref,
    w_qkv, w_out, w_cq, w_ckv, w_co, w_in, w_ffo, w_embed, w_head, w_box, norms, w_box_out,
    loss_ref, dmem_ref, d_qkv, d_out, d_cq, d_ckv, d_co, d_in, d_ffo, d_embed, d_head, d_box, d_norms, d_box_out,
    e_ref, h1_ref, qkv_ref, o1_ref, lse1_ref, y1_ref, h2_ref, cq_ref, ckv_ref, o2_ref, lse2_ref, y2_ref,
    h3_ref, u_ref, g_ref, y3_ref, z_ref, dy_ref, dh_ref, og_ref, up_ref, delta_ref,
):
    tables = tags_ref.shape[0]
    rows = tables * TAGS

    def tag_members(table):
        member = lax.broadcasted_iota(jnp.int32, (V, TAGS), 0) == tags_ref[table]
        return member.astype(f32).astype(bf16)

    for table in range(tables):
        e_ref[table * TAGS : (table + 1) * TAGS, :] = dot(tag_members(table), w_embed[...], 0, 0)
    norm_all(e_ref, norms, 0, h1_ref, rows, TAG_CHUNK)
    project(h1_ref, w_qkv, qkv_ref, 3 * D, 0.125)
    attend(tables, qkv_ref, qkv_ref, D, qkv_ref, 2 * D, o1_ref, lse1_ref, TAGS, TAGS, True)
    add_project(e_ref, o1_ref, w_out, y1_ref)
    norm_all(y1_ref, norms, 2, h2_ref, rows, TAG_CHUNK)
    project(h2_ref, w_cq, cq_ref, D, 0.125)
    project(mem_ref, w_ckv, ckv_ref, 2 * D)
    attend(tables, cq_ref, ckv_ref, 0, ckv_ref, D, o2_ref, lse2_ref, TAGS, IMG, False)
    add_project(y1_ref, o2_ref, w_co, y2_ref)
    norm_all(y2_ref, norms, 4, h3_ref, rows, TAG_CHUNK)
    ffn_forward(h3_ref, w_in, u_ref, g_ref)
    add_project(y2_ref, g_ref, w_ffo, y3_ref)
    norm_all(y3_ref, norms, 6, z_ref, rows, TAG_CHUNK)

    scale = scale_ref[0, 0]
    loss = jnp.zeros((1, 1), f32)
    picked, inners, box_ups = [], [], []
    head_sum = jnp.zeros((V, D), f32)
    box_in_sum = jnp.zeros((D, D), f32)
    box_out_sum = jnp.zeros((16, D), f32)
    for table in range(tables):
        own = slice(table * TAGS, (table + 1) * TAGS)
        final = z_ref[own, :]
        logits = dot(w_head[...], final, 1, 1)
        peak = jnp.max(logits, 0, keepdims=True)
        weight = jnp.exp(logits - peak)
        total = jnp.sum(weight, 0, keepdims=True)
        counted = counted_ref[table]
        wanted = lax.broadcasted_iota(jnp.int32, (V, TAGS), 0) == next_ref[table]
        chosen = jnp.sum(jnp.where(wanted, logits - peak - jnp.log(total), 0.0), 0, keepdims=True)
        loss = loss - jnp.sum(counted * chosen, 1, keepdims=True)
        dlogits = (weight / total - wanted.astype(f32)) * counted * scale
        tag_up = dlogits.astype(bf16)
        head_sum = head_sum + dot(tag_up, final)
        dfinal = dot(tag_up, w_head[...], 0, 0)
        select = (
            (lax.broadcasted_iota(jnp.int32, (TAGS, CELLS), 0) == place_ref[table])
            .astype(f32)
            .astype(bf16)
        )
        cells = dot(select, final, 0, 0).astype(bf16)
        inner = dot(cells, w_box[...])
        active = gelu(inner).astype(bf16)
        raw = dot(w_box_out[...], active, 1, 1)
        soft = 1.0 / (1.0 + jnp.exp(-raw))
        ratios = tuple(soft[k : k + 1, :] for k in range(4))
        wished = tuple(target_ref[table, k : k + 1, :] for k in range(4))
        alive = alive_ref[table]
        cell, pull = jax.vjp(lambda *parts: cell_losses(*parts, *wished), *ratios)
        loss = loss + jnp.sum(alive * cell, 1, keepdims=True)
        downs = pull(alive * scale)
        fill = jnp.zeros((16, CELLS), f32)
        index = lax.broadcasted_iota(jnp.int32, (16, CELLS), 0)
        for k in range(4):
            value = downs[k] * ratios[k] * (1.0 - ratios[k])
            fill = jnp.where(index == k, value, fill)
        box_up = fill.astype(bf16)
        box_out_sum = box_out_sum + dot(box_up, active)
        dinner = (gelu_slope(inner) * dot(box_up, w_box_out[...], 0, 0)).astype(bf16)
        box_in_sum = box_in_sum + dot(cells, dinner, 0, 0)
        dh_ref[own, :] = dfinal + split_sum(select, dot(dinner, w_box[...], 1, 1))
    loss_ref[...] = jnp.broadcast_to(loss, loss_ref.shape)
    d_head[...] = head_sum.astype(bf16)
    d_box[...] = box_in_sum.astype(bf16)
    d_box_out[...] = box_out_sum.astype(bf16)

    def start_sum(block, down):
        dy_ref[block, :] = down
        og_ref[block, :] = down.astype(bf16)

    def add_sum(block, down):
        total = down + dy_ref[block, :]
        dy_ref[block, :] = total
        og_ref[block, :] = total.astype(bf16)

    norm_all_back(y3_ref, norms, 6, dh_ref, d_norms, rows, TAG_CHUNK, start_sum)
    ffn_backward(og_ref, h3_ref, u_ref, g_ref, w_in, w_ffo, d_in, d_ffo, dh_ref)
    norm_all_back(y2_ref, norms, 4, dh_ref, d_norms, rows, TAG_CHUNK, add_sum)

    weight_grad(o2_ref, og_ref, d_co)
    project_back(og_ref, w_co, up_ref)
    head_sums(tables, up_ref, o2_ref, delta_ref, TAGS)
    attend_back(
        tables, cq_ref, ckv_ref, 0, ckv_ref, D, up_ref, lse2_ref, delta_ref,
        cq_ref, ckv_ref, ckv_ref, TAGS, IMG, False,
    )
    weight_grad(h2_ref, cq_ref, d_cq)
    weight_grad(mem_ref, ckv_ref, d_ckv)
    project_back(ckv_ref, w_ckv, dmem_ref)
    project_back(cq_ref, w_cq, dh_ref)
    norm_all_back(y1_ref, norms, 2, dh_ref, d_norms, rows, TAG_CHUNK, add_sum)

    weight_grad(o1_ref, og_ref, d_out)
    project_back(og_ref, w_out, up_ref)
    head_sums(tables, up_ref, o1_ref, delta_ref, TAGS)
    attend_back(
        tables, qkv_ref, qkv_ref, D, qkv_ref, 2 * D, up_ref, lse1_ref, delta_ref,
        qkv_ref, qkv_ref, qkv_ref, TAGS, TAGS, True,
    )
    weight_grad(h1_ref, qkv_ref, d_qkv)
    project_back(qkv_ref, w_qkv, dh_ref)
    norm_all_back(e_ref, norms, 0, dh_ref, d_norms, rows, TAG_CHUNK, add_sum)
    embed_sum = jnp.zeros((V, D), f32)
    for table in range(tables):
        embed_sum = embed_sum + split_sum(
            tag_members(table), dy_ref[table * TAGS : (table + 1) * TAGS, :]
        )
    d_embed[...] = embed_sum.astype(bf16)


DECODER_NAMES = (
    "qkv", "out", "cross_q", "cross_kv", "cross_out", "ffn_in", "ffn_out", "embed", "head", "box_in", "norms", "box_out",
)


def decoder_step(prepared, scale, memory, weights):
    tables = prepared[0].shape[0]
    rows = tables * TAGS
    image_rows = memory.shape[0]
    grads = {
        name: jax.ShapeDtypeStruct(weights[name].shape, f32 if name == "norms" else bf16)
        for name in DECODER_NAMES
    }
    vmem = pl.BlockSpec(memory_space=pltpu.VMEM)
    low = lambda width, height=rows: pltpu.VMEM((height, width), bf16)
    full = lambda width, height=rows: pltpu.VMEM((height, width), f32)
    stats = pltpu.VMEM((tables * HEADS, TAGS), f32)
    outs = pl.pallas_call(
        decoder_kernel,
        out_shape=(
            jax.ShapeDtypeStruct((8, 128), f32),
            jax.ShapeDtypeStruct((image_rows, D), f32),
            *[grads[name] for name in DECODER_NAMES],
        ),
        in_specs=[vmem] * 6 + [pl.BlockSpec(memory_space=pltpu.SMEM)] + [vmem] * 13,
        scratch_shapes=[
            full(D), low(D), low(3 * D), low(D), stats, full(D), low(D), low(D), low(2 * D, image_rows), low(D), stats,
            full(D), low(D), full(FF), low(FF), full(D), low(D), full(D), full(D), low(D), low(D), stats,
        ],
        compiler_params=pltpu.CompilerParams(vmem_limit_bytes=VMEM_LIMIT),
        name="decoder_step",
    )(*prepared, scale, memory, *[weights[name] for name in DECODER_NAMES])
    return outs[0], outs[1], dict(zip(DECODER_NAMES, outs[2:]))


AXES = ("wide", "narrow")
MESH = pl.DeviceIdType.MESH
ORDERS = (("a", "y", "b"), ("b", "a", "y"))


class Place:
    def __init__(self, wide, narrow):
        inner = 2 if wide % 2 == 0 else 1
        self.sizes = {"a": wide // inner, "b": inner, "y": narrow // 2, "c": 2}
        self.narrow = narrow
        self.count = wide * narrow

    def locate(self):
        wide, narrow = lax.axis_index("wide"), lax.axis_index("narrow")
        inner = self.sizes["b"]
        self.here = {
            "a": lax.div(wide, inner),
            "b": lax.rem(wide, inner),
            "y": lax.div(narrow, 2),
            "c": lax.rem(narrow, 2),
        }
        return self

    def moved(self, steps):
        there = dict(self.here)
        for part, step in steps.items():
            there[part] = lax.rem(there[part] + step, self.sizes[part])
        return there

    def device(self, there):
        return (there["a"] * self.sizes["b"] + there["b"], there["y"] * 2 + there["c"])

    def index(self, there):
        wide, narrow = self.device(there)
        return wide * self.narrow + narrow

    def peers(self):
        return [(part, step) for part, size in self.sizes.items() for step in range(1, size)]

    def greet(self):
        barrier = pltpu.get_barrier_semaphore()
        peers = self.peers()
        for part, step in peers:
            pl.semaphore_signal(
                barrier, inc=1, device_id=self.device(self.moved({part: step})), device_id_type=MESH
            )
        pl.semaphore_wait(barrier, len(peers))


def spread_blocks(place, order, all_ref, send_sem, recv_sem):
    one, two, three = order
    s1, s2, s3 = (place.sizes[part] for part in order)
    base2 = s1 - 1
    base3 = base2 + s1 * (s2 - 1)
    base4 = base3 + s1 * s2 * (s3 - 1)

    def copy(p, q, r, core, part, step, number):
        block = place.index(place.moved({one: p, two: q, three: r, "c": core}))
        return pltpu.make_async_remote_copy(
            src_ref=all_ref.at[block],
            dst_ref=all_ref.at[block],
            send_sem=send_sem.at[number],
            recv_sem=recv_sem.at[block],
            device_id=place.device(place.moved({part: step})),
            device_id_type=MESH,
        )

    def arrived(p, q, r, core=0):
        copy(p, q, r, core, "c", 1, 0).wait_recv()

    def to_sibling(p, q, r):
        copy(p, q, r, 0, "c", 1, base4 + (p * s2 + q) * s3 + r).start()

    def to_third(p, q):
        for step in range(1, s3):
            copy(p, q, 0, 0, three, step, base3 + (p * s2 + q) * (s3 - 1) + step - 1).start()

    @pl.loop(1, s1)
    def _(step):
        copy(0, 0, 0, 0, one, step, step - 1).start()

    @pl.loop(0, s1)
    def _(p):
        @pl.when(p > 0)
        def _():
            arrived(p, 0, 0)

        for step in range(1, s2):
            copy(p, 0, 0, 0, two, step, base2 + p * (s2 - 1) + step - 1).start()
        to_third(p, 0)
        to_sibling(p, 0, 0)

    @pl.loop(0, s1 * (s2 - 1))
    def _(number):
        p, q = lax.rem(number, s1), lax.div(number, s1) + 1
        arrived(p, q, 0)
        to_third(p, q)
        to_sibling(p, q, 0)

    @pl.loop(0, s1 * s2 * (s3 - 1))
    def _(number):
        p, q = lax.rem(number, s1), lax.rem(lax.div(number, s1), s2)
        r = lax.div(number, s1 * s2) + 1
        arrived(p, q, r)
        to_sibling(p, q, r)

    @pl.loop(0, s1 * s2 * s3)
    def _(number):
        p, q = lax.rem(number, s1), lax.rem(lax.div(number, s1), s2)
        arrived(p, q, lax.div(number, s1 * s2), 1)

    @pl.loop(0, place.count - 1)
    def _(number):
        copy(0, 0, 0, 0, "c", 1, number).wait_send()


def gather_all(place, all_ref, send_sem, recv_sem):
    for core in range(2):

        @pl.when(place.here["c"] == core)
        def _():
            spread_blocks(place, ORDERS[core], all_ref, send_sem, recv_sem)


def block_rows(amount):
    return -(-(amount // 128 + 3) // 16) * 16


def flat_rows(amount, count):
    return -(-((count - 1) * amount // 128 + block_rows(amount)) // 8) * 8


def layout_bases(layout):
    offset = 0
    for name, (height, breadth) in layout:
        yield name, height, breadth, offset // 128
        offset += height * breadth


def place_blocks(all_ref, flat_ref, amount):
    count, rows, _ = all_ref.shape
    used = amount // 128 + 2
    flat_ref[0:8, :] = jnp.zeros((8, 128), f32)

    @pl.loop(0, count)
    def _(device):
        start = lax.div(device * amount, 128)
        before = flat_ref[pl.ds(start, 1), :]
        flat_ref[pl.ds(start, used), :] = all_ref[device, :used, :].astype(f32)
        flat_ref[pl.ds(start, 1), :] = before + all_ref[device, 0:16, :].astype(f32)[0:1]


def one_hot(shape, match):
    first = lax.broadcasted_iota(jnp.int32, shape, 0)
    second = lax.broadcasted_iota(jnp.int32, shape, 1)
    return match(first, second).astype(f32).astype(bf16)


def take_matrices(flat_ref, layout, out_refs):
    for name, height, breadth, base in layout_bases(layout):
        out_ref = out_refs[name]
        if name == "head":
            turned = flat_ref[base : base + 128, :].T.astype(bf16)
            total = jnp.zeros((V, D), f32)
            for part in range(4):
                spread = one_hot((128, D), lambda row, column: column == 4 * row + part)
                total = total + dot(turned[part * V : (part + 1) * V, :], spread)
            out_ref[...] = total.astype(bf16)
        elif name == "box_out":
            block = flat_ref[base : base + 16, :].astype(bf16)
            own = one_hot((16, D), lambda row, column: lax.div(column, 32) == row).astype(f32)
            index = lax.broadcasted_iota(jnp.int32, (16, D), 0)
            total = jnp.zeros((16, D), f32)
            for k in range(4):
                pick = one_hot((128, D), lambda lane, column: lane == 4 * lax.rem(column, 32) + k)
                line = jnp.sum(dot(block, pick) * own, 0, keepdims=True)
                total = jnp.where(index == k, line, total)
            out_ref[...] = total.astype(bf16)
        else:
            wide = breadth // 128
            for column in range(wide):
                out_ref[:, column * 128 : (column + 1) * 128] = flat_ref[
                    pl.ds(base + column, height, stride=wide), :
                ].astype(out_ref.dtype)


def put_matrices(flat_ref, layout, refs):
    for name, height, breadth, base in layout_bases(layout):
        ref = refs[name]
        if name == "head":
            total = jnp.zeros((128, 128), f32)
            for part in range(4):
                pick = one_hot((128, D), lambda row, column: column == 4 * row + part)
                shift = one_hot((V, 128), lambda row, lane: lane == V * part + row)
                total = total + dot(dot(pick, ref[...], 1, 1).astype(bf16), shift)
            flat_ref[base : base + 128, :] = total
        elif name == "box_out":
            own = one_hot((16, D), lambda row, column: lax.div(column, 32) == row).astype(f32)
            total = jnp.zeros((16, 128), f32)
            for k in range(4):
                line = ref[...].astype(f32)[k : k + 1, :]
                spread = one_hot((D, 128), lambda column, lane: lane == 4 * lax.rem(column, 32) + k)
                total = total + dot((own * line).astype(bf16), spread)
            flat_ref[base : base + 16, :] = total
        else:
            wide = breadth // 128
            for column in range(wide):
                flat_ref[pl.ds(base + column, height, stride=wide), :] = ref[
                    :, column * 128 : (column + 1) * 128
                ].astype(f32)


def cut_blocks(flat_ref, amount, block_ref):
    count, rows, _ = block_ref.shape

    @pl.loop(0, count)
    def _(device):
        start = lax.div(device * amount, 128)
        block_ref[device, :, :] = flat_ref[pl.ds(start, rows), :].astype(bf16)


def weight_shapes(layout):
    shapes = {name: extent for name, extent in layout}
    if "head" in shapes:
        shapes["head"], shapes["box_out"] = (V, D), (16, D)
    return {
        name: jax.ShapeDtypeStruct(extent, f32 if name == "norms" else bf16)
        for name, extent in shapes.items()
    }


def gather_encoder(place, shard_block, amount):
    layout = encoder_layout()
    shapes = weight_shapes(layout)
    rows = shard_block.shape[0]

    def kernel(block_ref, *refs):
        outs = dict(zip(shapes, refs))
        count_ref, all_ref, flat_ref, send_sem, recv_sem = refs[len(shapes) :]
        place.locate()
        all_ref[place.index(place.here)] = block_ref[...].astype(bf16)
        place.greet()
        gather_all(place, all_ref, send_sem, recv_sem)
        total = jnp.zeros((1, 128), f32)
        for device in range(place.count):
            total = total + all_ref[device, rows - 16 :, :].astype(f32)[15:16]
        count_ref[...] = jnp.broadcast_to(jnp.sum(total, 1, keepdims=True), count_ref.shape)
        place_blocks(all_ref, flat_ref, amount)
        take_matrices(flat_ref, layout, outs)

    outs = pl.pallas_call(
        kernel,
        out_shape=(*shapes.values(), jax.ShapeDtypeStruct((8, 128), f32)),
        scratch_shapes=[
            pltpu.VMEM((place.count, rows, 128), bf16),
            pltpu.VMEM((flat_rows(amount, place.count), 128), f32),
            pltpu.SemaphoreType.DMA((place.count - 1,)),
            pltpu.SemaphoreType.DMA((place.count,)),
        ],
        compiler_params=pltpu.CompilerParams(
            collective_id=1, has_side_effects=True, vmem_limit_bytes=VMEM_LIMIT
        ),
        name="gather_encoder",
    )(shard_block)
    return dict(zip(shapes, outs)), outs[-1][0, 0]


def unpack_decoder(blocks, amount):
    layout = decoder_layout()
    shapes = weight_shapes(layout)

    def kernel(all_ref, *refs):
        flat_ref = refs[-1]
        place_blocks(all_ref, flat_ref, amount)
        take_matrices(flat_ref, layout, dict(zip(shapes, refs)))

    outs = pl.pallas_call(
        kernel,
        out_shape=tuple(shapes.values()),
        scratch_shapes=[pltpu.VMEM((flat_rows(amount, blocks.shape[0]), 128), f32)],
        compiler_params=pltpu.CompilerParams(vmem_limit_bytes=VMEM_LIMIT),
        name="unpack_decoder",
    )(blocks)
    return dict(zip(shapes, outs))


def pack_grads(grads, layout, amount, count, name):
    names = [piece for piece, _ in layout]

    def kernel(*refs):
        block_ref, flat_ref = refs[-2:]
        tail = sum(extent[0] * extent[1] for _, extent in layout) // 128
        flat_ref[tail:, :] = jnp.zeros((flat_ref.shape[0] - tail, 128), f32)
        put_matrices(flat_ref, layout, dict(zip(names, refs)))
        cut_blocks(flat_ref, amount, block_ref)

    return pl.pallas_call(
        kernel,
        out_shape=jax.ShapeDtypeStruct((count, block_rows(amount), 128), bf16),
        scratch_shapes=[pltpu.VMEM((flat_rows(amount, count), 128), f32)],
        compiler_params=pltpu.CompilerParams(vmem_limit_bytes=VMEM_LIMIT),
        name=name,
    )(*[grads[piece] for piece in names])


class Reduction:
    def __init__(self, place, core, own_ref, got_ref, acc_ref, send_sem, recv_sem):
        self.place, self.own, self.got, self.acc = place, own_ref, got_ref, acc_ref
        self.send_sem, self.recv_sem = send_sem, recv_sem
        self.order, self.other = ORDERS[core], ORDERS[1 - core]
        self.s1, self.s2, self.s3 = (place.sizes[part] for part in self.order)
        self.half = place.count // 2
        self.base3 = self.half
        self.base2 = self.base3 + (self.s3 - 1) * self.s1 * self.s2
        self.base1 = self.base2 + (self.s2 - 1) * self.s1

    def slot(self, steps):
        sizes = self.place.sizes
        return (steps["a"] * sizes["b"] + steps["b"]) * sizes["y"] + steps["y"]

    def copy(self, source, slot, part, step):
        return pltpu.make_async_remote_copy(
            src_ref=source,
            dst_ref=self.got.at[slot],
            send_sem=self.send_sem.at[slot],
            recv_sem=self.recv_sem.at[slot],
            device_id=self.place.device(self.place.moved({part: step})),
            device_id_type=MESH,
        )

    def took(self, slot):
        self.copy(self.acc.at[0], slot, "c", 1).wait_recv()

    def value(self, slot):
        return self.got[slot].astype(f32)

    def levels(self, order):
        s1, s2, s3 = (self.place.sizes[part] for part in order)
        return (
            (s1 * s2 * (s3 - 1), lambda n: (lax.rem(n, s1), lax.rem(lax.div(n, s1), s2), lax.div(n, s1 * s2) + 1)),
            (s1 * (s2 - 1), lambda n: (lax.rem(n, s1), lax.div(n, s1) + 1, 0)),
            (s1, lambda n: (s1 - 1 - n, 0, 0)),
        )

    def to_sibling(self):
        for amount, where in self.levels(self.other):

            @pl.loop(0, amount)
            def _(number):
                steps = dict(zip(self.other, where(number)))
                block = self.place.index(self.place.moved({**steps, "c": 1}))
                self.copy(self.own.at[block], self.slot(steps), "c", 1).start()

    def partial(self, p, q, r):
        steps = dict(zip(self.order, (p, q, r)))
        slot = self.slot(steps)
        self.took(slot)
        return self.own[self.place.index(self.place.moved(steps))].astype(f32) + self.value(slot)

    def add_third(self, total, p, q):
        for step in range(1, self.s3):
            slot = self.base3 + ((step - 1) * self.s1 + p) * self.s2 + q
            self.took(slot)
            total = total + self.value(slot)
        return total

    def add_second(self, total, p):
        for step in range(1, self.s2):
            slot = self.base2 + (step - 1) * self.s1 + p
            self.took(slot)
            total = total + self.value(slot)
        return total

    def send(self, total, slot, part, step):
        source = self.acc.at[slot - self.half]
        self.acc[slot - self.half] = total.astype(bf16)
        self.copy(source, slot, part, step).start()

    def third(self):
        amount, where = self.levels(self.order)[0]

        @pl.loop(0, amount)
        def _(number):
            p, q, r = where(number)
            slot = self.base3 + ((r - 1) * self.s1 + p) * self.s2 + q
            self.send(self.partial(p, q, r), slot, self.order[2], r)

    def second(self):
        amount, where = self.levels(self.order)[1]

        @pl.loop(0, amount)
        def _(number):
            p, q, _ = where(number)
            total = self.add_third(self.partial(p, q, 0), p, q)
            self.send(total, self.base2 + (q - 1) * self.s1 + p, self.order[1], q)

    def first(self):
        @pl.loop(1, self.s1)
        def _(p):
            total = self.add_second(self.add_third(self.partial(p, 0, 0), p, 0), p)
            self.send(total, self.base1 + p - 1, self.order[0], p)

    def last(self, out_ref):
        out_ref[...] = self.add_second(self.add_third(self.partial(0, 0, 0), 0, 0), 0)

        @pl.loop(1, self.s1)
        def _(p):
            slot = self.base1 + p - 1
            self.took(slot)
            out_ref[...] += self.value(slot)

        @pl.loop(0, self.place.count - 1)
        def _(slot):
            self.copy(self.acc.at[0], slot, "c", 1).wait_send()


def sum_everywhere(place, value, box_ref, send_sem, recv_sem):
    base = 0
    for part in ("c", "b", "y", "a"):
        size = place.sizes[part]
        mine = place.here[part]
        box_ref[base + mine] = value

        def copy(step, base=base, mine=mine, part=part):
            return pltpu.make_async_remote_copy(
                src_ref=box_ref.at[base + mine],
                dst_ref=box_ref.at[base + mine],
                send_sem=send_sem.at[base + step],
                recv_sem=recv_sem.at[base + mine],
                device_id=place.device(place.moved({part: step})),
                device_id_type=MESH,
            )

        def coming(step, base=base, part=part):
            there = place.moved({part: step})[part]
            return pltpu.make_async_remote_copy(
                src_ref=box_ref.at[base + there],
                dst_ref=box_ref.at[base + there],
                send_sem=send_sem.at[base + step],
                recv_sem=recv_sem.at[base + there],
                device_id=place.device(place.moved({part: step})),
                device_id_type=MESH,
            )

        for step in range(1, size):
            copy(step).start()
        for step in range(1, size):
            coming(step).wait_recv()
        for step in range(1, size):
            copy(step).wait_send()
        value = box_ref[base]
        for other in range(1, size):
            value = value + box_ref[base + other]
        base += size
    return value


def own_squares(place, out_ref, amount):
    rows = out_ref.shape[0]
    offset = lax.rem(place.index(place.here) * amount, 128)
    position = (
        lax.broadcasted_iota(jnp.int32, (rows, 128), 0) * 128
        + lax.broadcasted_iota(jnp.int32, (rows, 128), 1)
        - offset
    )
    value = jnp.where((position >= 0) & (position < amount), out_ref[...], 0.0)
    return jnp.sum(jnp.sum(value * value, 0, keepdims=True), 1, keepdims=True)


def reduce_all(place, blocks, amounts, loss_block):
    parts = len(blocks)
    count = place.count
    steps = sum(place.sizes.values())

    def kernel(*refs):
        own, loss_ref = refs[:parts], refs[parts]
        outs, stat_ref = refs[parts + 1 : 2 * parts + 1], refs[2 * parts + 1]
        rest = refs[2 * parts + 2 :]
        got, acc = rest[:parts], rest[parts : 2 * parts]
        send, recv = rest[2 * parts : 3 * parts], rest[3 * parts : 4 * parts]
        box_ref, box_send, box_recv = rest[4 * parts :]
        place.locate()
        place.greet()
        for core in range(2):

            @pl.when(place.here["c"] == core)
            def _():
                work = [
                    Reduction(place, core, *members) for members in zip(own, got, acc, send, recv)
                ]
                for stage in ("to_sibling", "third", "second", "first"):
                    for one in work:
                        getattr(one, stage)()
                for one, out_ref in zip(work, outs):
                    one.last(out_ref)

        squares = sum(own_squares(place, *members) for members in zip(outs, amounts))
        index = lax.broadcasted_iota(jnp.int32, (8, 128), 0)
        value = jnp.where(index == 0, squares, jnp.where(index == 1, loss_ref[...], 0.0))
        stat_ref[...] = sum_everywhere(place, value, box_ref, box_send, box_recv)

    half = count // 2
    vmem = lambda shape, kind: pltpu.VMEM(shape, kind)
    outs = pl.pallas_call(
        kernel,
        out_shape=(
            *[jax.ShapeDtypeStruct(block.shape[1:], f32) for block in blocks],
            jax.ShapeDtypeStruct((8, 128), f32),
        ),
        scratch_shapes=[
            *[vmem((count - 1, *block.shape[1:]), bf16) for block in blocks],
            *[vmem((half - 1, *block.shape[1:]), bf16) for block in blocks],
            *[pltpu.SemaphoreType.DMA((count - 1,)) for _ in range(2 * parts)],
            vmem((steps, 8, 128), f32),
            pltpu.SemaphoreType.DMA((steps,)),
            pltpu.SemaphoreType.DMA((steps,)),
        ],
        compiler_params=pltpu.CompilerParams(
            collective_id=2, has_side_effects=True, vmem_limit_bytes=VMEM_LIMIT
        ),
        name="reduce_all",
    )(*blocks, loss_block)
    return outs[:-1], outs[-1]


def adam_update(gradient, master, first_state, second_state, average):
    first_new = BETA_ONE * first_state + (1.0 - BETA_ONE) * gradient
    second_new = BETA_TWO * second_state + (1.0 - BETA_TWO) * gradient * gradient
    first_hat = first_new / (1.0 - BETA_ONE**STEP)
    second_hat = second_new / (1.0 - BETA_TWO**STEP)
    master_new = master - LEARN_RATE * (
        first_hat / (jnp.sqrt(second_hat) + EPSILON) + WEIGHT_DECAY * master
    )
    average_new = SMOOTH * average + (1.0 - SMOOTH) * master_new
    return (first_new, second_new, master_new, average_new)


def shard_block(shard, offset, tail=None):
    rows = block_rows(shard.shape[0])
    values = lax.dynamic_update_slice(jnp.zeros((rows * 128,), shard.dtype), shard, (offset,))
    if tail is not None:
        values = lax.dynamic_update_slice(values, tail, ((rows - 1) * 128,))
    return values.reshape(rows, 128)


def on_device(place, *arguments):
    (
        images, tag_ids, tag_lengths, cell_mask, cell_index, box_targets,
        encoder_params, encoder_first, encoder_second, encoder_average,
        decoder_params, decoder_first, decoder_second, decoder_average,
    ) = arguments
    encoder_amount, decoder_amount = encoder_params.shape[0], decoder_params.shape[0]
    me = lax.axis_index("wide") * lax.axis_size("narrow") + lax.axis_index("narrow")
    encoder_offset = lax.rem(me * encoder_amount, 128)
    decoder_offset = lax.rem(me * decoder_amount, 128)
    cell_slots = jnp.arange(CELLS)
    alive = ((cell_mask > 0) & (cell_slots[None, :] < (tag_lengths // 4)[:, None])).astype(f32)
    cells = cell_index % tag_lengths[:, None]
    counted = (jnp.arange(TAGS)[None, :] < (tag_lengths - 1)[:, None]).astype(f32)
    upcoming = jnp.roll(tag_ids, -1, 1)
    prepared = (
        tag_ids[:, None, :], upcoming[:, None, :], counted[:, None, :], cells[:, None, :], alive[:, None, :], box_targets,
    )

    decoder_blocks = lax.all_gather(
        shard_block(decoder_params.astype(bf16), decoder_offset), AXES, axis=0, tiled=False
    )
    encoder_weights, cell_total = gather_encoder(
        place, shard_block(encoder_params, encoder_offset, jnp.sum(alive, 1)), encoder_amount
    )
    *stored, memory = encoder_forward(images, encoder_weights)
    decoder_weights = unpack_decoder(decoder_blocks, decoder_amount)
    scale = (1.0 / cell_total).reshape(1, 1)
    loss_block, dmemory, decoder_grads = decoder_step(prepared, scale, memory, decoder_weights)
    decoder_packed = pack_grads(
        decoder_grads, decoder_layout(), decoder_amount, place.count, "pack_decoder"
    )
    encoder_grads = encoder_backward(images, stored, dmemory, encoder_weights)
    encoder_packed = pack_grads(
        encoder_grads, encoder_layout(), encoder_amount, place.count, "pack_encoder"
    )
    (decoder_sum, encoder_sum), stats = reduce_all(
        place, (decoder_packed, encoder_packed), (decoder_amount, encoder_amount), loss_block
    )
    grad_norm = jnp.sqrt(stats[0, 0])
    factor = CLIP_NORM / jnp.maximum(grad_norm, CLIP_NORM)
    encoder_grad = lax.dynamic_slice(encoder_sum.reshape(-1), (encoder_offset,), (encoder_amount,))
    decoder_grad = lax.dynamic_slice(decoder_sum.reshape(-1), (decoder_offset,), (decoder_amount,))
    encoder_new = adam_update(
        encoder_grad * factor, encoder_params, encoder_first, encoder_second, encoder_average
    )
    decoder_new = adam_update(
        decoder_grad * factor, decoder_params, decoder_first, decoder_second, decoder_average
    )
    return (stats[1, 0], cell_total, grad_norm, *encoder_new, *decoder_new)


def solution(mesh):
    rows, flat = P(AXES, None), P(AXES)
    return jax.shard_map(
        functools.partial(on_device, Place(mesh.shape["wide"], mesh.shape["narrow"])),
        mesh=mesh,
        in_specs=(rows, rows, flat, rows, rows, P(AXES, None, None)) + (flat,) * 8,
        out_specs=(P(), P(), P()) + (flat,) * 8,
        check_vma=False,
    )
```

```python
import functools

import jax
import jax.numpy as jnp
from jax import lax
from jax.experimental import pallas as pl
from jax.experimental.pallas import tpu as pltpu
from jax.sharding import PartitionSpec as P

D = 512
HEADS = 8
HEAD = D // HEADS
PAIRS = HEADS // 2
FF = 1024
V = 32
IMG = 784
TAGS = 512
STEP = 5
CELLS = 128
IMG_CHUNK = 784
TAG_CHUNK = 512
SAFE_SCORE = 50.0

BETA_ONE = 0.5
BETA_TWO = 0.5
CLIP_NORM = 0.01
LEARN_RATE = 0.05
WEIGHT_DECAY = 0.01
EPSILON = 1e-08
SMOOTH = 0.9

VMEM_LIMIT = 60 * 2**20
bf16 = jnp.bfloat16
f32 = jnp.float32


def encoder_layout():
    return [
        ("qkv", (D, 3 * D)),
        ("out", (D, D)),
        ("ffn_in", (D, FF)),
        ("ffn_out", (FF, D)),
        ("norms", (4, D)),
    ]


def decoder_layout():
    return [
        ("qkv", (D, 3 * D)),
        ("out", (D, D)),
        ("cross_q", (D, D)),
        ("cross_kv", (D, 2 * D)),
        ("cross_out", (D, D)),
        ("ffn_in", (D, FF)),
        ("ffn_out", (FF, D)),
        ("embed", (V, D)),
        ("head", (D, V)),
        ("box_in", (D, D)),
        ("norms", (8, D)),
        ("box_out", (D, 4)),
    ]


def dot(left, right, over_left=1, over_right=0):
    return lax.dot_general(
        left, right, (((over_left,), (over_right,)), ((), ())), preferred_element_type=f32
    )


def each_rows(total, step, body):
    @pl.loop(0, total // step)
    def _(index):
        body(pl.ds(pl.multiple_of(index * step, step), step))


def norm_rows(value, gain, shift):
    centred = value - jnp.mean(value, -1, keepdims=True)
    variance = jnp.mean(centred * centred, -1, keepdims=True)
    return centred * lax.rsqrt(variance + 1e-05) * gain + shift


def norm_rows_back(value, gain, upstream):
    centred = value - jnp.mean(value, -1, keepdims=True)
    variance = jnp.mean(centred * centred, -1, keepdims=True)
    scale = lax.rsqrt(variance + 1e-05)
    unit = centred * scale
    inner = upstream * gain
    mean_inner = jnp.mean(inner, -1, keepdims=True)
    mean_both = jnp.mean(inner * unit, -1, keepdims=True)
    down = scale * (inner - mean_inner - unit * mean_both)
    return (
        down,
        jnp.sum(upstream * unit, 0, keepdims=True),
        jnp.sum(upstream, 0, keepdims=True),
    )


GELU_A = 0.7978845608028654
GELU_B = 0.044715


def gelu(value):
    inner = jnp.tanh(GELU_A * (value + GELU_B * value * value * value))
    return 0.5 * value * (1.0 + inner)


def gelu_slope(value):
    square = value * value
    inner = jnp.tanh(GELU_A * (value + GELU_B * square * value))
    slope = GELU_A * (1.0 + 3.0 * GELU_B * square)
    return 0.5 * (1.0 + inner) + 0.5 * value * (1.0 - inner * inner) * slope


def half_masks():
    lane = lax.broadcasted_iota(jnp.int32, (1, 2 * HEAD), 1)
    first = (lane < HEAD).astype(f32)
    return (first.astype(bf16), (1.0 - first).astype(bf16))


def query_blocks(query_rows, key_rows, causal):
    if not causal:
        return [(0, query_rows, key_rows)]
    return [(start, 256, start + 256) for start in range(0, query_rows, 256)]


def key_tiles(start, depth, causal):
    if not causal or start == 0:
        return [(0, depth)]
    return [(0, start), (start, depth)]


def causal_keep(depth, width):
    key = lax.broadcasted_iota(jnp.int32, (depth, width), 0)
    query = lax.broadcasted_iota(jnp.int32, (depth, width), 1)
    return key <= query


def head_members():
    row = lax.broadcasted_iota(jnp.int32, (16, D), 0)
    lane = lax.broadcasted_iota(jnp.int32, (16, D), 1)
    return (lax.shift_right_logical(lane, 6) == row).astype(f32).astype(bf16)


def largest_norm(ref, column, rows, start):
    value = ref[start : start + rows, column : column + D]
    return jnp.max(dot(head_members(), value * value, 1, 1), 1, keepdims=True)


def attend(tables, q_ref, k_ref, k_col, v_ref, v_col, o_ref, lse_ref, query_rows, key_rows, causal):
    bound = jnp.zeros((16, 1), f32)
    for table in range(tables):
        of_queries = largest_norm(q_ref, 0, query_rows, table * query_rows)
        of_keys = largest_norm(k_ref, k_col, key_rows, table * key_rows)
        bound = jnp.maximum(bound, of_queries * of_keys)
    small = jnp.max(bound) < (0.98 * SAFE_SCORE) ** 2
    for wanted in (True, False):

        @pl.when(small == wanted)
        def _():
            attend_with(
                tables, q_ref, k_ref, k_col, v_ref, v_col, o_ref, lse_ref,
                query_rows, key_rows, causal, not wanted,
            )


def attend_with(
    tables, q_ref, k_ref, k_col, v_ref, v_col, o_ref, lse_ref, query_rows, key_rows, causal, take_peak,
):
    masks = half_masks()
    blocks = query_blocks(query_rows, key_rows, causal)

    @pl.loop(0, tables * PAIRS)
    def _(step):
        table = lax.div(step, PAIRS)
        pair = lax.rem(step, PAIRS)
        q_rows = pl.ds(pl.multiple_of(table * query_rows, 16), query_rows)
        k_rows = pl.ds(pl.multiple_of(table * key_rows, 16), key_rows)
        lanes = pl.multiple_of(pair * 128, 128)
        queries = q_ref[q_rows, pl.ds(lanes, 128)]
        keys = k_ref[k_rows, pl.ds(k_col + lanes, 128)]
        values = v_ref[k_rows, pl.ds(v_col + lanes, 128)].T
        scores = {}
        for half in range(2):
            own = queries * masks[half]
            for start, width, depth in blocks:
                for low, high in key_tiles(start, depth, causal):
                    tile = dot(keys[low:high], own[start : start + width], 1, 1)
                    if causal and low == start:
                        tile = jnp.where(causal_keep(high - low, width), tile, -1e30)
                    scores[half, start, low] = tile
        outs = []
        for half in range(2):
            own_values = values[half * HEAD : (half + 1) * HEAD, :]
            parts, sums = [], []
            for start, width, depth in blocks:
                tiles = key_tiles(start, depth, causal)
                weights = [scores[half, start, low] for low, _ in tiles]
                peak = jnp.zeros((1, width), f32)
                if take_peak:
                    peak = functools.reduce(
                        jnp.maximum, [jnp.max(tile, 0, keepdims=True) for tile in weights]
                    )
                    weights = [tile - peak for tile in weights]
                weights = [jnp.exp(tile) for tile in weights]
                total = sum(jnp.sum(tile, 0, keepdims=True) for tile in weights)
                mixed = sum(
                    dot(own_values[:, low:high], tile.astype(bf16))
                    for tile, (low, high) in zip(weights, tiles)
                )
                parts.append(mixed * (1.0 / total))
                sums.append(peak + jnp.log(total))
            outs.append(parts[0] if len(parts) == 1 else jnp.concatenate(parts, 1))
            lse_ref[pl.ds(table * HEADS + pair * 2 + half, 1), :] = (
                sums[0] if len(sums) == 1 else jnp.concatenate(sums, 1)
            )
        joined = jnp.concatenate(outs, 0).astype(bf16)
        o_ref[q_rows, pl.ds(lanes, 128)] = joined.T


def head_sums(tables, up_ref, o_ref, delta_ref, query_rows):
    member = head_members()
    for table in range(tables):
        rows = slice(table * query_rows, (table + 1) * query_rows)
        both = up_ref[rows, :].astype(f32) * o_ref[rows, :].astype(f32)
        high = both.astype(bf16)
        rest = (both - high.astype(f32)).astype(bf16)
        sums = dot(member, high, 1, 1) + dot(member, rest, 1, 1)
        delta_ref[table * HEADS : (table + 1) * HEADS, :] = sums[:HEADS]


def attend_back(
    span_of_tables, q_ref, k_ref, k_col, v_ref, v_col, up_ref, lse_ref, delta_ref,
    dq_ref, dk_ref, dv_ref, query_rows, key_rows, causal,
):
    masks = half_masks()

    @pl.loop(span_of_tables[0] * PAIRS, span_of_tables[1] * PAIRS)
    def _(step):
        table = lax.div(step, PAIRS)
        pair = lax.rem(step, PAIRS)
        q_rows = pl.ds(pl.multiple_of(table * query_rows, 16), query_rows)
        k_rows = pl.ds(pl.multiple_of(table * key_rows, 16), key_rows)
        lanes = pl.multiple_of(pair * 128, 128)
        queries = q_ref[q_rows, pl.ds(lanes, 128)]
        keys = k_ref[k_rows, pl.ds(k_col + lanes, 128)]
        values = v_ref[k_rows, pl.ds(v_col + lanes, 128)]
        upstream = up_ref[q_rows, pl.ds(lanes, 128)]
        keys_across = keys.T
        blocks = query_blocks(query_rows, key_rows, causal)
        grad_q = []
        grad_k = [None] * len(blocks)
        grad_v = [None] * len(blocks)
        for half in range(2):
            index = pl.ds(table * HEADS + pair * 2 + half, 1)
            own = queries * masks[half]
            own_up = upstream * masks[half]
            logsum = lse_ref[index, :]
            delta = delta_ref[index, :]
            across = keys_across[half * HEAD : (half + 1) * HEAD, :]
            parts = []
            for number, (start, width, depth) in enumerate(blocks):
                span = slice(start, start + width)
                weight = jnp.exp(dot(keys[:depth], own[span], 1, 1) - logsum[:, span])
                if causal:
                    edge = jnp.where(causal_keep(width, width), weight[start:], 0.0)
                    weight = edge if start == 0 else jnp.concatenate([weight[:start], edge], 0)
                pull = dot(values[:depth], own_up[span], 1, 1)
                change = (weight * (pull - delta[:, span])).astype(bf16)
                add_v = dot(weight.astype(bf16), own_up[span])
                add_k = dot(change, own[span])
                grad_v[number] = add_v if half == 0 else grad_v[number] + add_v
                grad_k[number] = add_k if half == 0 else grad_k[number] + add_k
                parts.append(dot(across[:, :depth], change) * 0.125)
            grad_q.append(parts[0] if len(parts) == 1 else jnp.concatenate(parts, 1))
        dq_ref[q_rows, pl.ds(lanes, 128)] = jnp.concatenate(grad_q, 0).astype(bf16).T
        for ref, column, grads in ((dk_ref, k_col, grad_k), (dv_ref, v_col, grad_v)):
            total = grads[-1]
            if len(grads) == 2:
                low = blocks[0][2]
                total = jnp.concatenate([total[:low] + grads[0], total[low:]], 0)
            ref[k_rows, pl.ds(column + lanes, 128)] = total.astype(bf16)


def project(a_ref, w_ref, out_ref, width, first_scale=None):
    for start in range(0, width, 512):
        value = dot(a_ref[...], w_ref[:, start : start + 512])
        if first_scale is not None and start == 0:
            value = value * first_scale
        out_ref[:, start : start + 512] = value.astype(bf16)


def add_project(base_ref, a_ref, w_ref, out_ref):
    for start in range(0, D, 256):
        lanes = slice(start, start + 256)
        out_ref[:, lanes] = base_ref[:, lanes].astype(f32) + dot(a_ref[...], w_ref[:, lanes])


def weight_grad(a_ref, b_ref, out_ref):
    rows, columns = out_ref.shape
    for start in range(0, columns, 512):
        lanes = slice(start, start + 512)
        out_ref[:, lanes] = dot(a_ref[...], b_ref[:, lanes], 0, 0).astype(out_ref.dtype)


def ffn_forward(h_ref, w_in, u_ref, g_ref):
    for start in range(0, FF, 256):
        lanes = slice(start, start + 256)
        inner = dot(h_ref[...], w_in[:, lanes])
        if u_ref is not None:
            u_ref[:, lanes] = inner
        g_ref[:, lanes] = gelu(inner).astype(bf16)


def ffn_backward(og_ref, h_ref, u_ref, g_ref, w_in, w_out, d_in, d_out, dh_ref):
    weight_grad(g_ref, og_ref, d_out)
    for start in range(0, FF, 256):
        lanes = slice(start, start + 256)
        back = dot(og_ref[...], w_out[lanes, :], 1, 1)
        g_ref[:, lanes] = (gelu_slope(u_ref[:, lanes]) * back).astype(bf16)
    weight_grad(h_ref, g_ref, d_in)
    project_back(g_ref, w_in, dh_ref)


def project_back(g_ref, w_ref, out_ref):
    for start in range(0, D, 256):
        lanes = slice(start, start + 256)
        out_ref[:, lanes] = dot(g_ref[...], w_ref[lanes, :], 1, 1).astype(out_ref.dtype)


def norm_all(x_ref, norms_ref, row, out_ref, total, step):
    gain, shift = norms_ref[row : row + 1, :], norms_ref[row + 1 : row + 2, :]

    def body(rows):
        out_ref[rows, :] = norm_rows(x_ref[rows, :].astype(f32), gain, shift).astype(bf16)

    each_rows(total, step, body)


def norm_all_back(x_ref, norms_ref, row, up_ref, dnorms_ref, total, step, keep):
    gain = norms_ref[row : row + 1, :]
    dnorms_ref[row : row + 2, :] = jnp.zeros((2, D), f32)

    def body(rows):
        down, d_gain, d_shift = norm_rows_back(x_ref[rows, :].astype(f32), gain, up_ref[rows, :])
        dnorms_ref[row : row + 1, :] += d_gain
        dnorms_ref[row + 1 : row + 2, :] += d_shift
        if keep is not None:
            keep(rows, down)

    each_rows(total, step, body)


def encoder_forward_kernel(
    x_ref, w_qkv, w_out, w_in, w_ffo, norms, qkv_ref, o_ref, lse_ref, x1_ref, mem_ref, h_ref, g_ref
):
    rows = x_ref.shape[0]
    tables = rows // IMG
    norm_all(x_ref, norms, 0, h_ref, rows, IMG_CHUNK)
    project(h_ref, w_qkv, qkv_ref, 3 * D, 0.125)
    attend(tables, qkv_ref, qkv_ref, D, qkv_ref, 2 * D, o_ref, lse_ref, IMG, IMG, False)
    add_project(x_ref, o_ref, w_out, x1_ref)
    norm_all(x1_ref, norms, 2, h_ref, rows, IMG_CHUNK)
    ffn_forward(h_ref, w_in, None, g_ref)
    for start in range(0, D, 256):
        lanes = slice(start, start + 256)
        mem_ref[:, lanes] = (x1_ref[:, lanes] + dot(g_ref[...], w_ffo[:, lanes])).astype(bf16)


def encoder_forward(images, weights):
    rows = images.shape[0]
    tables = rows // IMG
    return pl.pallas_call(
        encoder_forward_kernel,
        out_shape=(
            jax.ShapeDtypeStruct((rows, 3 * D), bf16),
            jax.ShapeDtypeStruct((rows, D), bf16),
            jax.ShapeDtypeStruct((tables * HEADS, IMG), f32),
            jax.ShapeDtypeStruct((rows, D), f32),
            jax.ShapeDtypeStruct((rows, D), bf16),
        ),
        scratch_shapes=[pltpu.VMEM((rows, D), bf16), pltpu.VMEM((rows, FF), bf16)],
        compiler_params=pltpu.CompilerParams(vmem_limit_bytes=VMEM_LIMIT),
        name="encoder_forward",
    )(images, weights["qkv"], weights["out"], weights["ffn_in"], weights["ffn_out"], weights["norms"])


def soft_low(first_one, other_one):
    return 0.5 * (first_one + other_one - jnp.sqrt((first_one - other_one) ** 2 + 0.0001))


def soft_high(first_one, other_one):
    return 0.5 * (first_one + other_one + jnp.sqrt((first_one - other_one) ** 2 + 0.0001))


def softplus(value):
    return jnp.maximum(value, 0.0) + jnp.log1p(jnp.exp(-jnp.abs(value)))


@jax.custom_vjp
def smooth_relu(value):
    return softplus(value)


def smooth_relu_keep(value):
    return softplus(value), value


def smooth_relu_back(value, upstream):
    return (upstream * (1.0 / (1.0 + jnp.exp(-value))),)


smooth_relu.defvjp(smooth_relu_keep, smooth_relu_back)


def cell_losses(px, py, pw, ph, gx, gy, gw, gh):
    absolute = (
        jnp.sqrt((px - gx) ** 2 + 0.01)
        + jnp.sqrt((py - gy) ** 2 + 0.01)
        + jnp.sqrt((pw - gw) ** 2 + 0.01)
        + jnp.sqrt((ph - gh) ** 2 + 0.01)
    )
    left_p, right_p = px - 0.5 * pw, px + 0.5 * pw
    low_p, top_p = py - 0.5 * ph, py + 0.5 * ph
    left_g, right_g = gx - 0.5 * gw, gx + 0.5 * gw
    low_g, top_g = gy - 0.5 * gh, gy + 0.5 * gh
    across = smooth_relu(20.0 * (soft_low(right_p, right_g) - soft_high(left_p, left_g))) / 20.0
    upward = smooth_relu(20.0 * (soft_low(top_p, top_g) - soft_high(low_p, low_g))) / 20.0
    common = across * upward
    union = pw * ph + gw * gh - common
    hull = (soft_high(right_p, right_g) - soft_low(left_p, left_g)) * (
        soft_high(top_p, top_g) - soft_low(low_p, low_g)
    )
    ratio = common / union - (hull - union) / hull
    return 5.0 * absolute + 2.0 * (1.0 - ratio)


def split_sum(left, value):
    high = value.astype(bf16)
    rest = (value - high.astype(f32)).astype(bf16)
    return dot(left, high) + dot(left, rest)


def decoder_kernel(
    tags_ref, next_ref, counted_ref, place_ref, alive_ref, target_ref, scale_ref, mem_ref,
    w_qkv, w_out, w_cq, w_ckv, w_co, w_in, w_ffo, w_embed, w_head, w_box, norms, w_box_out,
    loss_ref, dmem_ref, d_qkv, d_out, d_cq, d_ckv, d_co, d_in, d_ffo, d_embed, d_head, d_box, d_norms, d_box_out,
    e_ref, h1_ref, qkv_ref, o1_ref, lse1_ref, y1_ref, h2_ref, cq_ref, ckv_ref, o2_ref, lse2_ref, y2_ref,
    h3_ref, u_ref, g_ref, y3_ref, z_ref, dy_ref, dh_ref, og_ref, up_ref, delta_ref,
):
    tables = tags_ref.shape[0]
    rows = tables * TAGS

    def tag_members(table):
        member = lax.broadcasted_iota(jnp.int32, (V, TAGS), 0) == tags_ref[table]
        return member.astype(f32).astype(bf16)

    for table in range(tables):
        e_ref[table * TAGS : (table + 1) * TAGS, :] = dot(tag_members(table), w_embed[...], 0, 0)
    norm_all(e_ref, norms, 0, h1_ref, rows, TAG_CHUNK)
    project(h1_ref, w_qkv, qkv_ref, 3 * D, 0.125)
    attend(tables, qkv_ref, qkv_ref, D, qkv_ref, 2 * D, o1_ref, lse1_ref, TAGS, TAGS, True)
    add_project(e_ref, o1_ref, w_out, y1_ref)
    norm_all(y1_ref, norms, 2, h2_ref, rows, TAG_CHUNK)
    project(h2_ref, w_cq, cq_ref, D, 0.125)
    project(mem_ref, w_ckv, ckv_ref, 2 * D)
    attend(tables, cq_ref, ckv_ref, 0, ckv_ref, D, o2_ref, lse2_ref, TAGS, IMG, False)
    add_project(y1_ref, o2_ref, w_co, y2_ref)
    norm_all(y2_ref, norms, 4, h3_ref, rows, TAG_CHUNK)
    ffn_forward(h3_ref, w_in, u_ref, g_ref)
    add_project(y2_ref, g_ref, w_ffo, y3_ref)
    norm_all(y3_ref, norms, 6, z_ref, rows, TAG_CHUNK)

    scale = scale_ref[0, 0]
    loss = jnp.zeros((1, 1), f32)
    picked, inners, box_ups = [], [], []
    head_sum = jnp.zeros((V, D), f32)
    box_in_sum = jnp.zeros((D, D), f32)
    box_out_sum = jnp.zeros((16, D), f32)
    for table in range(tables):
        own = slice(table * TAGS, (table + 1) * TAGS)
        final = z_ref[own, :]
        logits = dot(w_head[...], final, 1, 1)
        peak = jnp.max(logits, 0, keepdims=True)
        weight = jnp.exp(logits - peak)
        total = jnp.sum(weight, 0, keepdims=True)
        counted = counted_ref[table]
        wanted = lax.broadcasted_iota(jnp.int32, (V, TAGS), 0) == next_ref[table]
        chosen = jnp.sum(jnp.where(wanted, logits - peak - jnp.log(total), 0.0), 0, keepdims=True)
        loss = loss - jnp.sum(counted * chosen, 1, keepdims=True)
        dlogits = (weight / total - wanted.astype(f32)) * counted * scale
        tag_up = dlogits.astype(bf16)
        head_sum = head_sum + dot(tag_up, final)
        dfinal = dot(tag_up, w_head[...], 0, 0)
        select = (
            (lax.broadcasted_iota(jnp.int32, (TAGS, CELLS), 0) == place_ref[table])
            .astype(f32)
            .astype(bf16)
        )
        cells = dot(select, final, 0, 0).astype(bf16)
        inner = dot(cells, w_box[...])
        active = gelu(inner).astype(bf16)
        raw = dot(w_box_out[...], active, 1, 1)
        soft = 1.0 / (1.0 + jnp.exp(-raw))
        ratios = tuple(soft[k : k + 1, :] for k in range(4))
        wished = tuple(target_ref[table, k : k + 1, :] for k in range(4))
        alive = alive_ref[table]
        cell, pull = jax.vjp(lambda *parts: cell_losses(*parts, *wished), *ratios)
        loss = loss + jnp.sum(alive * cell, 1, keepdims=True)
        downs = pull(alive * scale)
        fill = jnp.zeros((16, CELLS), f32)
        index = lax.broadcasted_iota(jnp.int32, (16, CELLS), 0)
        for k in range(4):
            value = downs[k] * ratios[k] * (1.0 - ratios[k])
            fill = jnp.where(index == k, value, fill)
        box_up = fill.astype(bf16)
        box_out_sum = box_out_sum + dot(box_up, active)
        dinner = (gelu_slope(inner) * dot(box_up, w_box_out[...], 0, 0)).astype(bf16)
        box_in_sum = box_in_sum + dot(cells, dinner, 0, 0)
        dh_ref[own, :] = dfinal + split_sum(select, dot(dinner, w_box[...], 1, 1))
    loss_ref[...] = jnp.broadcast_to(loss, loss_ref.shape)
    d_head[...] = head_sum.astype(bf16)
    d_box[...] = box_in_sum.astype(bf16)
    d_box_out[...] = box_out_sum.astype(bf16)

    def start_sum(block, down):
        dy_ref[block, :] = down
        og_ref[block, :] = down.astype(bf16)

    def add_sum(block, down):
        total = down + dy_ref[block, :]
        dy_ref[block, :] = total
        og_ref[block, :] = total.astype(bf16)

    norm_all_back(y3_ref, norms, 6, dh_ref, d_norms, rows, TAG_CHUNK, start_sum)
    ffn_backward(og_ref, h3_ref, u_ref, g_ref, w_in, w_ffo, d_in, d_ffo, dh_ref)
    norm_all_back(y2_ref, norms, 4, dh_ref, d_norms, rows, TAG_CHUNK, add_sum)

    weight_grad(o2_ref, og_ref, d_co)
    project_back(og_ref, w_co, up_ref)
    head_sums(tables, up_ref, o2_ref, delta_ref, TAGS)
    attend_back(
        (0, tables), cq_ref, ckv_ref, 0, ckv_ref, D, up_ref, lse2_ref, delta_ref,
        cq_ref, ckv_ref, ckv_ref, TAGS, IMG, False,
    )
    weight_grad(h2_ref, cq_ref, d_cq)
    weight_grad(mem_ref, ckv_ref, d_ckv)
    project_back(ckv_ref, w_ckv, dmem_ref)
    project_back(cq_ref, w_cq, dh_ref)
    norm_all_back(y1_ref, norms, 2, dh_ref, d_norms, rows, TAG_CHUNK, add_sum)

    weight_grad(o1_ref, og_ref, d_out)
    project_back(og_ref, w_out, up_ref)
    head_sums(tables, up_ref, o1_ref, delta_ref, TAGS)
    attend_back(
        (0, tables), qkv_ref, qkv_ref, D, qkv_ref, 2 * D, up_ref, lse1_ref, delta_ref,
        qkv_ref, qkv_ref, qkv_ref, TAGS, TAGS, True,
    )
    weight_grad(h1_ref, qkv_ref, d_qkv)
    project_back(qkv_ref, w_qkv, dh_ref)
    norm_all_back(e_ref, norms, 0, dh_ref, d_norms, rows, TAG_CHUNK, add_sum)
    embed_sum = jnp.zeros((V, D), f32)
    for table in range(tables):
        embed_sum = embed_sum + split_sum(
            tag_members(table), dy_ref[table * TAGS : (table + 1) * TAGS, :]
        )
    d_embed[...] = embed_sum.astype(bf16)


DECODER_NAMES = (
    "qkv", "out", "cross_q", "cross_kv", "cross_out", "ffn_in", "ffn_out", "embed", "head", "box_in", "norms", "box_out",
)


def decoder_step(prepared, scale, memory, weights):
    tables = prepared[0].shape[0]
    rows = tables * TAGS
    image_rows = memory.shape[0]
    grads = {
        name: jax.ShapeDtypeStruct(weights[name].shape, f32 if name == "norms" else bf16)
        for name in DECODER_NAMES
    }
    vmem = pl.BlockSpec(memory_space=pltpu.VMEM)
    low = lambda width, height=rows: pltpu.VMEM((height, width), bf16)
    full = lambda width, height=rows: pltpu.VMEM((height, width), f32)
    stats = pltpu.VMEM((tables * HEADS, TAGS), f32)
    outs = pl.pallas_call(
        decoder_kernel,
        out_shape=(
            jax.ShapeDtypeStruct((8, 128), f32),
            jax.ShapeDtypeStruct((image_rows, D), f32),
            *[grads[name] for name in DECODER_NAMES],
        ),
        in_specs=[vmem] * 6 + [pl.BlockSpec(memory_space=pltpu.SMEM)] + [vmem] * 13,
        scratch_shapes=[
            full(D), low(D), low(3 * D), low(D), stats, full(D), low(D), low(D), low(2 * D, image_rows), low(D), stats,
            full(D), low(D), full(FF), low(FF), full(D), low(D), full(D), full(D), low(D), low(D), stats,
        ],
        compiler_params=pltpu.CompilerParams(vmem_limit_bytes=VMEM_LIMIT),
        name="decoder_step",
    )(*prepared, scale, memory, *[weights[name] for name in DECODER_NAMES])
    return outs[0], outs[1], dict(zip(DECODER_NAMES, outs[2:]))


AXES = ("wide", "narrow")
MESH = pl.DeviceIdType.MESH
ORDERS = (("a", "y", "b"), ("b", "a", "y"))


class Place:
    def __init__(self, wide, narrow):
        inner = 2 if wide % 2 == 0 else 1
        self.sizes = {"a": wide // inner, "b": inner, "y": narrow // 2, "c": 2}
        self.narrow = narrow
        self.count = wide * narrow

    def locate(self):
        wide, narrow = lax.axis_index("wide"), lax.axis_index("narrow")
        inner = self.sizes["b"]
        self.here = {
            "a": lax.div(wide, inner),
            "b": lax.rem(wide, inner),
            "y": lax.div(narrow, 2),
            "c": lax.rem(narrow, 2),
        }
        return self

    def moved(self, steps):
        there = dict(self.here)
        for part, step in steps.items():
            there[part] = lax.rem(there[part] + step, self.sizes[part])
        return there

    def device(self, there):
        return (there["a"] * self.sizes["b"] + there["b"], there["y"] * 2 + there["c"])

    def index(self, there):
        wide, narrow = self.device(there)
        return wide * self.narrow + narrow

    def peers(self):
        return [(part, step) for part, size in self.sizes.items() for step in range(1, size)]

    def greet(self):
        barrier = pltpu.get_barrier_semaphore()
        peers = self.peers()
        for part, step in peers:
            pl.semaphore_signal(
                barrier, inc=1, device_id=self.device(self.moved({part: step})), device_id_type=MESH
            )
        pl.semaphore_wait(barrier, len(peers))


def spread_blocks(place, order, all_ref, send_sem, recv_sem):
    one, two, three = order
    s1, s2, s3 = (place.sizes[part] for part in order)
    base2 = s1 - 1
    base3 = base2 + s1 * (s2 - 1)
    base4 = base3 + s1 * s2 * (s3 - 1)

    def copy(p, q, r, core, part, step, number):
        block = place.index(place.moved({one: p, two: q, three: r, "c": core}))
        return pltpu.make_async_remote_copy(
            src_ref=all_ref.at[block],
            dst_ref=all_ref.at[block],
            send_sem=send_sem.at[number],
            recv_sem=recv_sem.at[block],
            device_id=place.device(place.moved({part: step})),
            device_id_type=MESH,
        )

    def arrived(p, q, r, core=0):
        copy(p, q, r, core, "c", 1, 0).wait_recv()

    def to_sibling(p, q, r):
        copy(p, q, r, 0, "c", 1, base4 + (p * s2 + q) * s3 + r).start()

    def to_third(p, q):
        for step in range(1, s3):
            copy(p, q, 0, 0, three, step, base3 + (p * s2 + q) * (s3 - 1) + step - 1).start()

    @pl.loop(1, s1)
    def _(step):
        copy(0, 0, 0, 0, one, step, step - 1).start()

    @pl.loop(0, s1)
    def _(p):
        @pl.when(p > 0)
        def _():
            arrived(p, 0, 0)

        for step in range(1, s2):
            copy(p, 0, 0, 0, two, step, base2 + p * (s2 - 1) + step - 1).start()
        to_third(p, 0)
        to_sibling(p, 0, 0)

    @pl.loop(0, s1 * (s2 - 1))
    def _(number):
        p, q = lax.rem(number, s1), lax.div(number, s1) + 1
        arrived(p, q, 0)
        to_third(p, q)
        to_sibling(p, q, 0)

    @pl.loop(0, s1 * s2 * (s3 - 1))
    def _(number):
        p, q = lax.rem(number, s1), lax.rem(lax.div(number, s1), s2)
        r = lax.div(number, s1 * s2) + 1
        arrived(p, q, r)
        to_sibling(p, q, r)

    @pl.loop(0, s1 * s2 * s3)
    def _(number):
        p, q = lax.rem(number, s1), lax.rem(lax.div(number, s1), s2)
        arrived(p, q, lax.div(number, s1 * s2), 1)

    @pl.loop(0, place.count - 1)
    def _(number):
        copy(0, 0, 0, 0, "c", 1, number).wait_send()


def gather_all(place, all_ref, send_sem, recv_sem):
    for core in range(2):

        @pl.when(place.here["c"] == core)
        def _():
            spread_blocks(place, ORDERS[core], all_ref, send_sem, recv_sem)


def block_rows(amount):
    return -(-(amount // 128 + 3) // 16) * 16


def flat_rows(amount, count):
    return -(-((count - 1) * amount // 128 + block_rows(amount)) // 8) * 8


def layout_bases(layout):
    offset = 0
    for name, (height, breadth) in layout:
        yield name, height, breadth, offset // 128
        offset += height * breadth


def place_blocks(all_ref, flat_ref, amount):
    count, rows, _ = all_ref.shape
    used = amount // 128 + 2
    flat_ref[0:8, :] = jnp.zeros((8, 128), f32)

    @pl.loop(0, count)
    def _(device):
        start = lax.div(device * amount, 128)
        before = flat_ref[pl.ds(start, 1), :]
        flat_ref[pl.ds(start, used), :] = all_ref[device, :used, :].astype(f32)
        flat_ref[pl.ds(start, 1), :] = before + all_ref[device, 0:16, :].astype(f32)[0:1]


def one_hot(shape, match):
    first = lax.broadcasted_iota(jnp.int32, shape, 0)
    second = lax.broadcasted_iota(jnp.int32, shape, 1)
    return match(first, second).astype(f32).astype(bf16)


def take_matrices(flat_ref, layout, out_refs):
    for name, height, breadth, base in layout_bases(layout):
        out_ref = out_refs[name]
        if name == "head":
            turned = flat_ref[base : base + 128, :].T.astype(bf16)
            total = jnp.zeros((V, D), f32)
            for part in range(4):
                spread = one_hot((128, D), lambda row, column: column == 4 * row + part)
                total = total + dot(turned[part * V : (part + 1) * V, :], spread)
            out_ref[...] = total.astype(bf16)
        elif name == "box_out":
            block = flat_ref[base : base + 16, :].astype(bf16)
            own = one_hot((16, D), lambda row, column: lax.div(column, 32) == row).astype(f32)
            index = lax.broadcasted_iota(jnp.int32, (16, D), 0)
            total = jnp.zeros((16, D), f32)
            for k in range(4):
                pick = one_hot((128, D), lambda lane, column: lane == 4 * lax.rem(column, 32) + k)
                line = jnp.sum(dot(block, pick) * own, 0, keepdims=True)
                total = jnp.where(index == k, line, total)
            out_ref[...] = total.astype(bf16)
        else:
            wide = breadth // 128
            for column in range(wide):
                out_ref[:, column * 128 : (column + 1) * 128] = flat_ref[
                    pl.ds(base + column, height, stride=wide), :
                ].astype(out_ref.dtype)


def put_matrices(flat_ref, layout, refs):
    for name, height, breadth, base in layout_bases(layout):
        ref = refs[name]
        if name == "head":
            total = jnp.zeros((128, 128), f32)
            for part in range(4):
                pick = one_hot((128, D), lambda row, column: column == 4 * row + part)
                shift = one_hot((V, 128), lambda row, lane: lane == V * part + row)
                total = total + dot(dot(pick, ref[...], 1, 1).astype(bf16), shift)
            flat_ref[base : base + 128, :] = total
        elif name == "box_out":
            own = one_hot((16, D), lambda row, column: lax.div(column, 32) == row).astype(f32)
            total = jnp.zeros((16, 128), f32)
            for k in range(4):
                line = ref[...].astype(f32)[k : k + 1, :]
                spread = one_hot((D, 128), lambda column, lane: lane == 4 * lax.rem(column, 32) + k)
                total = total + dot((own * line).astype(bf16), spread)
            flat_ref[base : base + 16, :] = total
        else:
            wide = breadth // 128
            for column in range(wide):
                flat_ref[pl.ds(base + column, height, stride=wide), :] = ref[
                    :, column * 128 : (column + 1) * 128
                ].astype(f32)


def cut_blocks(flat_ref, amount, block_ref):
    count, rows, _ = block_ref.shape

    @pl.loop(0, count)
    def _(device):
        start = lax.div(device * amount, 128)
        block_ref[device, :, :] = flat_ref[pl.ds(start, rows), :].astype(bf16)


def weight_shapes(layout):
    shapes = {name: extent for name, extent in layout}
    if "head" in shapes:
        shapes["head"], shapes["box_out"] = (V, D), (16, D)
    return {
        name: jax.ShapeDtypeStruct(extent, f32 if name == "norms" else bf16)
        for name, extent in shapes.items()
    }


def gather_encoder(place, shard_block, amount):
    layout = encoder_layout()
    shapes = weight_shapes(layout)
    rows = shard_block.shape[0]

    def kernel(block_ref, *refs):
        outs = dict(zip(shapes, refs))
        count_ref, all_ref, flat_ref, send_sem, recv_sem = refs[len(shapes) :]
        place.locate()
        all_ref[place.index(place.here)] = block_ref[...].astype(bf16)
        place.greet()
        gather_all(place, all_ref, send_sem, recv_sem)
        total = jnp.zeros((1, 128), f32)
        for device in range(place.count):
            total = total + all_ref[device, rows - 16 :, :].astype(f32)[15:16]
        count_ref[...] = jnp.broadcast_to(jnp.sum(total, 1, keepdims=True), count_ref.shape)
        place_blocks(all_ref, flat_ref, amount)
        take_matrices(flat_ref, layout, outs)

    outs = pl.pallas_call(
        kernel,
        out_shape=(*shapes.values(), jax.ShapeDtypeStruct((8, 128), f32)),
        scratch_shapes=[
            pltpu.VMEM((place.count, rows, 128), bf16),
            pltpu.VMEM((flat_rows(amount, place.count), 128), f32),
            pltpu.SemaphoreType.DMA((place.count - 1,)),
            pltpu.SemaphoreType.DMA((place.count,)),
        ],
        compiler_params=pltpu.CompilerParams(
            collective_id=1, has_side_effects=True, vmem_limit_bytes=VMEM_LIMIT
        ),
        name="gather_encoder",
    )(shard_block)
    return dict(zip(shapes, outs)), outs[-1][0, 0]


def unpack_decoder(blocks, amount):
    layout = decoder_layout()
    shapes = weight_shapes(layout)

    def kernel(all_ref, *refs):
        flat_ref = refs[-1]
        place_blocks(all_ref, flat_ref, amount)
        take_matrices(flat_ref, layout, dict(zip(shapes, refs)))

    outs = pl.pallas_call(
        kernel,
        out_shape=tuple(shapes.values()),
        scratch_shapes=[pltpu.VMEM((flat_rows(amount, blocks.shape[0]), 128), f32)],
        compiler_params=pltpu.CompilerParams(vmem_limit_bytes=VMEM_LIMIT),
        name="unpack_decoder",
    )(blocks)
    return dict(zip(shapes, outs))


def pack_grads(grads, layout, amount, count, name):
    names = [piece for piece, _ in layout]

    def kernel(*refs):
        block_ref, flat_ref = refs[-2:]
        tail = sum(extent[0] * extent[1] for _, extent in layout) // 128
        flat_ref[tail:, :] = jnp.zeros((flat_ref.shape[0] - tail, 128), f32)
        put_matrices(flat_ref, layout, dict(zip(names, refs)))
        cut_blocks(flat_ref, amount, block_ref)

    return pl.pallas_call(
        kernel,
        out_shape=jax.ShapeDtypeStruct((count, block_rows(amount), 128), bf16),
        scratch_shapes=[pltpu.VMEM((flat_rows(amount, count), 128), f32)],
        compiler_params=pltpu.CompilerParams(vmem_limit_bytes=VMEM_LIMIT),
        name=name,
    )(*[grads[piece] for piece in names])


class Reduction:
    def __init__(self, place, core, own_ref, mine_ref, got_ref, load_sem, send_sem, recv_sem):
        self.place, self.own, self.mine, self.got = place, own_ref, mine_ref, got_ref
        self.load_sem, self.send_sem, self.recv_sem = load_sem, send_sem, recv_sem
        self.order, self.other = ORDERS[core], ORDERS[1 - core]
        self.s1, self.s2, self.s3 = (place.sizes[part] for part in self.order)
        self.half = place.count // 2
        self.base3 = self.half
        self.base2 = self.base3 + (self.s3 - 1) * self.s1 * self.s2
        self.base1 = self.base2 + (self.s2 - 1) * self.s1

    def slot(self, steps):
        sizes = self.place.sizes
        return (steps["a"] * sizes["b"] + steps["b"]) * sizes["y"] + steps["y"]

    def copy(self, source, slot, part, step):
        return pltpu.make_async_remote_copy(
            src_ref=source,
            dst_ref=self.got.at[slot],
            send_sem=self.send_sem.at[slot],
            recv_sem=self.recv_sem.at[slot],
            device_id=self.place.device(self.place.moved({part: step})),
            device_id_type=MESH,
        )

    def load(self, steps):
        slot = self.slot(steps)
        block = self.place.index(self.place.moved(steps))
        return pltpu.make_async_copy(self.own.at[block], self.mine.at[slot], self.load_sem.at[slot])

    def took(self, slot):
        self.copy(self.mine.at[0], slot, "c", 1).wait_recv()

    def value(self, slot):
        return self.got[slot].astype(f32)

    def levels(self, order):
        s1, s2, s3 = (self.place.sizes[part] for part in order)
        return (
            (s1 * s2 * (s3 - 1), lambda n: (s1 - 1 - lax.rem(n, s1), s2 - 1 - lax.rem(lax.div(n, s1), s2), lax.div(n, s1 * s2) + 1)),
            (s1 * (s2 - 1), lambda n: (s1 - 1 - lax.rem(n, s1), lax.div(n, s1) + 1, 0)),
            (s1, lambda n: (s1 - 1 - n, 0, 0)),
        )

    def to_sibling(self):
        for amount, where in self.levels(self.order):

            @pl.loop(0, amount)
            def _(number):
                self.load(dict(zip(self.order, where(number)))).start()

        for amount, where in self.levels(self.other):

            @pl.loop(0, amount)
            def _(number):
                steps = dict(zip(self.other, where(number)))
                block = self.place.index(self.place.moved({**steps, "c": 1}))
                self.copy(self.own.at[block], self.slot(steps), "c", 1).start()

    def partial(self, p, q, r):
        steps = dict(zip(self.order, (p, q, r)))
        slot = self.slot(steps)
        self.load(steps).wait()
        self.took(slot)
        return slot, self.mine[slot].astype(f32) + self.value(slot)

    def add_third(self, total, p, q):
        for step in range(1, self.s3):
            slot = self.base3 + ((step - 1) * self.s1 + p) * self.s2 + q
            self.took(slot)
            total = total + self.value(slot)
        return total

    def add_second(self, total, p):
        for step in range(1, self.s2):
            slot = self.base2 + (step - 1) * self.s1 + p
            self.took(slot)
            total = total + self.value(slot)
        return total

    def send(self, own_slot, total, slot, part, step):
        self.mine[own_slot] = total.astype(bf16)
        self.copy(self.mine.at[own_slot], slot, part, step).start()

    def third(self):
        amount, where = self.levels(self.order)[0]

        @pl.loop(0, amount)
        def _(number):
            p, q, r = where(number)
            own_slot, total = self.partial(p, q, r)
            slot = self.base3 + ((r - 1) * self.s1 + p) * self.s2 + q
            self.send(own_slot, total, slot, self.order[2], r)

    def second(self):
        amount, where = self.levels(self.order)[1]

        @pl.loop(0, amount)
        def _(number):
            p, q, _ = where(number)
            own_slot, total = self.partial(p, q, 0)
            total = self.add_third(total, p, q)
            self.send(own_slot, total, self.base2 + (q - 1) * self.s1 + p, self.order[1], q)

    def first(self):
        @pl.loop(1, self.s1)
        def _(p):
            own_slot, total = self.partial(p, 0, 0)
            total = self.add_second(self.add_third(total, p, 0), p)
            self.send(own_slot, total, self.base1 + p - 1, self.order[0], p)

    def last(self, out_ref):
        _, total = self.partial(0, 0, 0)
        out_ref[...] = self.add_second(self.add_third(total, 0, 0), 0)

        @pl.loop(1, self.s1)
        def _(p):
            slot = self.base1 + p - 1
            self.took(slot)
            out_ref[...] += self.value(slot)

        @pl.loop(0, self.place.count - 1)
        def _(slot):
            self.copy(self.mine.at[0], slot, "c", 1).wait_send()


def reduction_scratch(count, rows):
    half = count // 2
    return [
        pltpu.VMEM((half, rows, 128), bf16),
        pltpu.VMEM((count - 1, rows, 128), bf16),
        pltpu.SemaphoreType.DMA((half,)),
        pltpu.SemaphoreType.DMA((count - 1,)),
        pltpu.SemaphoreType.DMA((count - 1,)),
    ]


def reduce_stage(place, stage, *members):
    for core in range(2):

        @pl.when(place.here["c"] == core)
        def _():
            stage(Reduction(place, core, *members))


def sum_everywhere(place, value, box_ref, send_sem, recv_sem):
    base = 0
    for part in ("c", "b", "y", "a"):
        size = place.sizes[part]
        mine = place.here[part]
        box_ref[base + mine] = value

        def copy(step, base=base, mine=mine, part=part):
            return pltpu.make_async_remote_copy(
                src_ref=box_ref.at[base + mine],
                dst_ref=box_ref.at[base + mine],
                send_sem=send_sem.at[base + step],
                recv_sem=recv_sem.at[base + mine],
                device_id=place.device(place.moved({part: step})),
                device_id_type=MESH,
            )

        def coming(step, base=base, part=part):
            there = place.moved({part: step})[part]
            return pltpu.make_async_remote_copy(
                src_ref=box_ref.at[base + there],
                dst_ref=box_ref.at[base + there],
                send_sem=send_sem.at[base + step],
                recv_sem=recv_sem.at[base + there],
                device_id=place.device(place.moved({part: step})),
                device_id_type=MESH,
            )

        for step in range(1, size):
            copy(step).start()
        for step in range(1, size):
            coming(step).wait_recv()
        for step in range(1, size):
            copy(step).wait_send()
        value = box_ref[base]
        for other in range(1, size):
            value = value + box_ref[base + other]
        base += size
    return value


def own_squares(place, out_ref, amount):
    rows = out_ref.shape[0]
    offset = lax.rem(place.index(place.here) * amount, 128)
    position = (
        lax.broadcasted_iota(jnp.int32, (rows, 128), 0) * 128
        + lax.broadcasted_iota(jnp.int32, (rows, 128), 1)
        - offset
    )
    value = jnp.where((position >= 0) & (position < amount), out_ref[...], 0.0)
    return jnp.sum(jnp.sum(value * value, 0, keepdims=True), 1, keepdims=True)


def reduce_encoder(place, blocks, amounts, other_sum, loss_block):
    count = place.count
    steps = sum(place.sizes.values())
    rows = blocks.shape[1]

    def kernel(own_ref, other_ref, loss_ref, out_ref, stat_ref, *rest):
        members = (own_ref, *rest[:5])
        box_ref, box_send, box_recv = rest[5:]
        place.locate()
        place.greet()

        def whole(work):
            work.to_sibling()
            work.third()
            work.second()
            work.first()
            work.last(out_ref)

        reduce_stage(place, whole, *members)
        squares = own_squares(place, out_ref, amounts[0]) + own_squares(place, other_ref, amounts[1])
        index = lax.broadcasted_iota(jnp.int32, (8, 128), 0)
        value = jnp.where(index == 0, squares, jnp.where(index == 1, loss_ref[...], 0.0))
        stat_ref[...] = sum_everywhere(place, value, box_ref, box_send, box_recv)

    vmem = pl.BlockSpec(memory_space=pltpu.VMEM)
    return pl.pallas_call(
        kernel,
        out_shape=(jax.ShapeDtypeStruct((rows, 128), f32), jax.ShapeDtypeStruct((8, 128), f32)),
        in_specs=[pl.BlockSpec(memory_space=pl.ANY), vmem, vmem],
        scratch_shapes=[
            *reduction_scratch(count, rows),
            pltpu.VMEM((steps, 8, 128), f32),
            pltpu.SemaphoreType.DMA((steps,)),
            pltpu.SemaphoreType.DMA((steps,)),
        ],
        compiler_params=pltpu.CompilerParams(
            collective_id=3, has_side_effects=True, vmem_limit_bytes=VMEM_LIMIT
        ),
        name="reduce_encoder",
    )(blocks, other_sum, loss_block)


def encoder_backward(place, images, stored, dmem, weights, decoder_blocks):
    rows = images.shape[0]
    tables = rows // IMG
    qkv, mixed, lse, middle = stored
    layout = encoder_layout()
    shapes = weight_shapes(layout)
    block = decoder_blocks.shape[1]

    def kernel(
        x_ref, qkv_hbm, o_ref, lse_ref, x1_ref, dmem_ref, w_qkv, w_out, w_in, w_ffo, norms, own_ref,
        d_qkv, d_out, d_in, d_ffo, d_norms, sum_ref,
        h_ref, g_ref, dh_ref, og_ref, up_ref, qkv_ref, delta_ref, qkv_sem, *members,
    ):
        work = functools.partial(reduce_stage, place)
        members = (own_ref, *members)
        place.locate()
        place.greet()
        work(lambda one: one.to_sibling(), *members)
        fetch = pltpu.make_async_copy(qkv_hbm, qkv_ref, qkv_sem.at[0])
        fetch.start()
        norm_all(x1_ref, norms, 2, h_ref, rows, IMG_CHUNK)
        og_ref[...] = dmem_ref[...].astype(bf16)
        for start in range(0, FF, 256):
            lanes = slice(start, start + 256)
            inner = dot(h_ref[...], w_in[:, lanes])
            back = dot(og_ref[...], w_ffo[lanes, :], 1, 1)
            d_ffo[lanes, :] = dot(gelu(inner).astype(bf16), og_ref[...], 0, 0).astype(bf16)
            g_ref[:, lanes] = (gelu_slope(inner) * back).astype(bf16)
        work(lambda one: one.third(), *members)
        weight_grad(h_ref, g_ref, d_in)
        project_back(g_ref, w_in, dh_ref)

        def keep(part, down):
            og_ref[part, :] = (down + dmem_ref[part, :]).astype(bf16)

        norm_all_back(x1_ref, norms, 2, dh_ref, d_norms, rows, IMG_CHUNK, keep)
        weight_grad(o_ref, og_ref, d_out)
        project_back(og_ref, w_out, up_ref)
        head_sums(tables, up_ref, o_ref, delta_ref, IMG)
        fetch.wait()
        for table in range(tables):
            attend_back(
                (table, table + 1), qkv_ref, qkv_ref, D, qkv_ref, 2 * D, up_ref, lse_ref, delta_ref,
                qkv_ref, qkv_ref, qkv_ref, IMG, IMG, False,
            )
            if table == 0:
                work(lambda one: one.second(), *members)
        work(lambda one: one.first(), *members)
        norm_all(x_ref, norms, 0, h_ref, rows, IMG_CHUNK)
        weight_grad(h_ref, qkv_ref, d_qkv)
        project_back(qkv_ref, w_qkv, dh_ref)
        norm_all_back(x_ref, norms, 0, dh_ref, d_norms, rows, IMG_CHUNK, None)
        work(lambda one: one.last(sum_ref), *members)

    vmem, hbm = pl.BlockSpec(memory_space=pltpu.VMEM), pl.BlockSpec(memory_space=pl.ANY)
    outs = pl.pallas_call(
        kernel,
        out_shape=(*shapes.values(), jax.ShapeDtypeStruct((block, 128), f32)),
        in_specs=[vmem, hbm] + [vmem] * 9 + [hbm],
        scratch_shapes=[
            pltpu.VMEM((rows, D), bf16),
            pltpu.VMEM((rows, FF), bf16),
            pltpu.VMEM((rows, D), f32),
            pltpu.VMEM((rows, D), bf16),
            pltpu.VMEM((rows, D), bf16),
            pltpu.VMEM((rows, 3 * D), bf16),
            pltpu.VMEM((tables * HEADS, IMG), f32),
            pltpu.SemaphoreType.DMA((1,)),
            *reduction_scratch(place.count, block),
        ],
        compiler_params=pltpu.CompilerParams(
            collective_id=2, has_side_effects=True, vmem_limit_bytes=VMEM_LIMIT
        ),
        name="encoder_backward",
    )(
        images, qkv, mixed, lse, middle, dmem,
        weights["qkv"], weights["out"], weights["ffn_in"], weights["ffn_out"], weights["norms"], decoder_blocks,
    )
    return dict(zip(shapes, outs)), outs[-1]


def adam_update(gradient, master, first_state, second_state, average):
    first_new = BETA_ONE * first_state + (1.0 - BETA_ONE) * gradient
    second_new = BETA_TWO * second_state + (1.0 - BETA_TWO) * gradient * gradient
    first_hat = first_new / (1.0 - BETA_ONE**STEP)
    second_hat = second_new / (1.0 - BETA_TWO**STEP)
    master_new = master - LEARN_RATE * (
        first_hat / (jnp.sqrt(second_hat) + EPSILON) + WEIGHT_DECAY * master
    )
    average_new = SMOOTH * average + (1.0 - SMOOTH) * master_new
    return (first_new, second_new, master_new, average_new)


def shard_block(shard, offset, tail=None):
    rows = block_rows(shard.shape[0])
    values = lax.dynamic_update_slice(jnp.zeros((rows * 128,), shard.dtype), shard, (offset,))
    if tail is not None:
        values = lax.dynamic_update_slice(values, tail, ((rows - 1) * 128,))
    return values.reshape(rows, 128)


def on_device(place, *arguments):
    (
        images, tag_ids, tag_lengths, cell_mask, cell_index, box_targets,
        encoder_params, encoder_first, encoder_second, encoder_average,
        decoder_params, decoder_first, decoder_second, decoder_average,
    ) = arguments
    encoder_amount, decoder_amount = encoder_params.shape[0], decoder_params.shape[0]
    me = lax.axis_index("wide") * lax.axis_size("narrow") + lax.axis_index("narrow")
    encoder_offset = lax.rem(me * encoder_amount, 128)
    decoder_offset = lax.rem(me * decoder_amount, 128)
    cell_slots = jnp.arange(CELLS)
    alive = ((cell_mask > 0) & (cell_slots[None, :] < (tag_lengths // 4)[:, None])).astype(f32)
    cells = cell_index % tag_lengths[:, None]
    counted = (jnp.arange(TAGS)[None, :] < (tag_lengths - 1)[:, None]).astype(f32)
    upcoming = jnp.roll(tag_ids, -1, 1)
    prepared = (
        tag_ids[:, None, :], upcoming[:, None, :], counted[:, None, :], cells[:, None, :], alive[:, None, :], box_targets,
    )

    decoder_blocks = lax.all_gather(
        shard_block(decoder_params.astype(bf16), decoder_offset), AXES, axis=0, tiled=False
    )
    encoder_weights, cell_total = gather_encoder(
        place, shard_block(encoder_params, encoder_offset, jnp.sum(alive, 1)), encoder_amount
    )
    *stored, memory = encoder_forward(images, encoder_weights)
    decoder_weights = unpack_decoder(decoder_blocks, decoder_amount)
    scale = (1.0 / cell_total).reshape(1, 1)
    loss_block, dmemory, decoder_grads = decoder_step(prepared, scale, memory, decoder_weights)
    decoder_packed = pack_grads(
        decoder_grads, decoder_layout(), decoder_amount, place.count, "pack_decoder"
    )
    encoder_grads, decoder_sum = encoder_backward(
        place, images, stored, dmemory, encoder_weights, decoder_packed
    )
    encoder_packed = pack_grads(
        encoder_grads, encoder_layout(), encoder_amount, place.count, "pack_encoder"
    )
    encoder_sum, stats = reduce_encoder(
        place, encoder_packed, (encoder_amount, decoder_amount), decoder_sum, loss_block
    )
    grad_norm = jnp.sqrt(stats[0, 0])
    factor = CLIP_NORM / jnp.maximum(grad_norm, CLIP_NORM)
    encoder_grad = lax.dynamic_slice(encoder_sum.reshape(-1), (encoder_offset,), (encoder_amount,))
    decoder_grad = lax.dynamic_slice(decoder_sum.reshape(-1), (decoder_offset,), (decoder_amount,))
    encoder_new = adam_update(
        encoder_grad * factor, encoder_params, encoder_first, encoder_second, encoder_average
    )
    decoder_new = adam_update(
        decoder_grad * factor, decoder_params, decoder_first, decoder_second, decoder_average
    )
    return (stats[1, 0], cell_total, grad_norm, *encoder_new, *decoder_new)


def solution(mesh):
    rows, flat = P(AXES, None), P(AXES)
    return jax.shard_map(
        functools.partial(on_device, Place(mesh.shape["wide"], mesh.shape["narrow"])),
        mesh=mesh,
        in_specs=(rows, rows, flat, rows, rows, P(AXES, None, None)) + (flat,) * 8,
        out_specs=(P(), P(), P()) + (flat,) * 8,
        check_vma=False,
    )
```

```python
import functools

import jax
import jax.numpy as jnp
from jax import lax
from jax.experimental import pallas as pl
from jax.experimental.pallas import tpu as pltpu
from jax.sharding import PartitionSpec as P

D = 512
HEADS = 8
HEAD = D // HEADS
PAIRS = HEADS // 2
FF = 1024
V = 32
IMG = 784
TAGS = 512
STEP = 5
CELLS = 128
IMG_CHUNK = 784
TAG_CHUNK = 512
SAFE_SCORE = 50.0

BETA_ONE = 0.5
BETA_TWO = 0.5
CLIP_NORM = 0.01
LEARN_RATE = 0.05
WEIGHT_DECAY = 0.01
EPSILON = 1e-08
SMOOTH = 0.9

VMEM_LIMIT = 62 * 2**20
bf16 = jnp.bfloat16
f32 = jnp.float32


def encoder_layout():
    return [
        ("qkv", (D, 3 * D)),
        ("out", (D, D)),
        ("ffn_in", (D, FF)),
        ("ffn_out", (FF, D)),
        ("norms", (4, D)),
    ]


def decoder_layout():
    return [
        ("qkv", (D, 3 * D)),
        ("out", (D, D)),
        ("cross_q", (D, D)),
        ("cross_kv", (D, 2 * D)),
        ("cross_out", (D, D)),
        ("ffn_in", (D, FF)),
        ("ffn_out", (FF, D)),
        ("embed", (V, D)),
        ("head", (D, V)),
        ("box_in", (D, D)),
        ("norms", (8, D)),
        ("box_out", (D, 4)),
    ]


def dot(left, right, over_left=1, over_right=0):
    return lax.dot_general(
        left, right, (((over_left,), (over_right,)), ((), ())), preferred_element_type=f32
    )


def each_rows(total, step, body):
    @pl.loop(0, total // step)
    def _(index):
        body(pl.ds(pl.multiple_of(index * step, step), step))


def norm_rows(value, gain, shift):
    centred = value - jnp.mean(value, -1, keepdims=True)
    variance = jnp.mean(centred * centred, -1, keepdims=True)
    return centred * lax.rsqrt(variance + 1e-05) * gain + shift


def norm_rows_back(value, gain, upstream):
    centred = value - jnp.mean(value, -1, keepdims=True)
    variance = jnp.mean(centred * centred, -1, keepdims=True)
    scale = lax.rsqrt(variance + 1e-05)
    unit = centred * scale
    inner = upstream * gain
    mean_inner = jnp.mean(inner, -1, keepdims=True)
    mean_both = jnp.mean(inner * unit, -1, keepdims=True)
    down = scale * (inner - mean_inner - unit * mean_both)
    return (
        down,
        jnp.sum(upstream * unit, 0, keepdims=True),
        jnp.sum(upstream, 0, keepdims=True),
    )


GELU_A = 0.7978845608028654
GELU_B = 0.044715


def gelu(value):
    inner = jnp.tanh(GELU_A * (value + GELU_B * value * value * value))
    return 0.5 * value * (1.0 + inner)


def gelu_slope(value):
    square = value * value
    inner = jnp.tanh(GELU_A * (value + GELU_B * square * value))
    slope = GELU_A * (1.0 + 3.0 * GELU_B * square)
    return 0.5 * (1.0 + inner) + 0.5 * value * (1.0 - inner * inner) * slope


def half_masks():
    lane = lax.broadcasted_iota(jnp.int32, (1, 2 * HEAD), 1)
    first = (lane < HEAD).astype(f32)
    return (first.astype(bf16), (1.0 - first).astype(bf16))


def query_blocks(query_rows, key_rows, causal):
    if not causal:
        return [(0, query_rows, key_rows)]
    return [(start, 256, start + 256) for start in range(0, query_rows, 256)]


def key_tiles(start, depth, causal):
    if not causal or start == 0:
        return [(0, depth)]
    return [(0, start), (start, depth)]


def causal_keep(depth, width):
    key = lax.broadcasted_iota(jnp.int32, (depth, width), 0)
    query = lax.broadcasted_iota(jnp.int32, (depth, width), 1)
    return key <= query


def head_members():
    row = lax.broadcasted_iota(jnp.int32, (16, D), 0)
    lane = lax.broadcasted_iota(jnp.int32, (16, D), 1)
    return (lax.shift_right_logical(lane, 6) == row).astype(f32).astype(bf16)


def largest_norm(ref, column, rows, start):
    value = ref[start : start + rows, column : column + D]
    return jnp.max(dot(head_members(), value * value, 1, 1), 1, keepdims=True)


def attend(tables, q_ref, k_ref, k_col, v_ref, v_col, o_ref, lse_ref, query_rows, key_rows, causal):
    bound = jnp.zeros((16, 1), f32)
    for table in range(tables):
        of_queries = largest_norm(q_ref, 0, query_rows, table * query_rows)
        of_keys = largest_norm(k_ref, k_col, key_rows, table * key_rows)
        bound = jnp.maximum(bound, of_queries * of_keys)
    small = jnp.max(bound) < (0.98 * SAFE_SCORE) ** 2
    for wanted in (True, False):

        @pl.when(small == wanted)
        def _():
            attend_with(
                tables, q_ref, k_ref, k_col, v_ref, v_col, o_ref, lse_ref,
                query_rows, key_rows, causal, not wanted,
            )


def attend_with(
    tables, q_ref, k_ref, k_col, v_ref, v_col, o_ref, lse_ref, query_rows, key_rows, causal, take_peak,
):
    masks = half_masks()
    blocks = query_blocks(query_rows, key_rows, causal)

    @pl.loop(0, tables * PAIRS)
    def _(step):
        table = lax.div(step, PAIRS)
        pair = lax.rem(step, PAIRS)
        q_rows = pl.ds(pl.multiple_of(table * query_rows, 16), query_rows)
        k_rows = pl.ds(pl.multiple_of(table * key_rows, 16), key_rows)
        lanes = pl.multiple_of(pair * 128, 128)
        queries = q_ref[q_rows, pl.ds(lanes, 128)]
        keys = k_ref[k_rows, pl.ds(k_col + lanes, 128)]
        values = v_ref[k_rows, pl.ds(v_col + lanes, 128)].T
        scores = {}
        for half in range(2):
            own = queries * masks[half]
            for start, width, depth in blocks:
                for low, high in key_tiles(start, depth, causal):
                    tile = dot(keys[low:high], own[start : start + width], 1, 1)
                    if causal and low == start:
                        tile = jnp.where(causal_keep(high - low, width), tile, -1e30)
                    scores[half, start, low] = tile
        outs = []
        for half in range(2):
            own_values = values[half * HEAD : (half + 1) * HEAD, :]
            parts, sums = [], []
            for start, width, depth in blocks:
                tiles = key_tiles(start, depth, causal)
                weights = [scores[half, start, low] for low, _ in tiles]
                peak = jnp.zeros((1, width), f32)
                if take_peak:
                    peak = functools.reduce(
                        jnp.maximum, [jnp.max(tile, 0, keepdims=True) for tile in weights]
                    )
                    weights = [tile - peak for tile in weights]
                weights = [jnp.exp(tile) for tile in weights]
                total = sum(jnp.sum(tile, 0, keepdims=True) for tile in weights)
                mixed = sum(
                    dot(own_values[:, low:high], tile.astype(bf16))
                    for tile, (low, high) in zip(weights, tiles)
                )
                parts.append(mixed * (1.0 / total))
                sums.append(peak + jnp.log(total))
            outs.append(parts[0] if len(parts) == 1 else jnp.concatenate(parts, 1))
            lse_ref[pl.ds(table * HEADS + pair * 2 + half, 1), :] = (
                sums[0] if len(sums) == 1 else jnp.concatenate(sums, 1)
            )
        joined = jnp.concatenate(outs, 0).astype(bf16)
        o_ref[q_rows, pl.ds(lanes, 128)] = joined.T


def head_sums(tables, up_ref, o_ref, delta_ref, query_rows):
    member = head_members()
    for table in range(tables):
        rows = slice(table * query_rows, (table + 1) * query_rows)
        both = up_ref[rows, :].astype(f32) * o_ref[rows, :].astype(f32)
        high = both.astype(bf16)
        rest = (both - high.astype(f32)).astype(bf16)
        sums = dot(member, high, 1, 1) + dot(member, rest, 1, 1)
        delta_ref[table * HEADS : (table + 1) * HEADS, :] = sums[:HEADS]


def attend_back(
    span_of_tables, q_ref, k_ref, k_col, v_ref, v_col, up_ref, lse_ref, delta_ref,
    dq_ref, dk_ref, dv_ref, query_rows, key_rows, causal, between=None,
):
    masks = half_masks()

    @pl.loop(span_of_tables[0] * PAIRS, span_of_tables[1] * PAIRS)
    def _(step):
        table = lax.div(step, PAIRS)
        pair = lax.rem(step, PAIRS)
        q_rows = pl.ds(pl.multiple_of(table * query_rows, 16), query_rows)
        k_rows = pl.ds(pl.multiple_of(table * key_rows, 16), key_rows)
        lanes = pl.multiple_of(pair * 128, 128)
        queries = q_ref[q_rows, pl.ds(lanes, 128)]
        keys = k_ref[k_rows, pl.ds(k_col + lanes, 128)]
        values = v_ref[k_rows, pl.ds(v_col + lanes, 128)]
        upstream = up_ref[q_rows, pl.ds(lanes, 128)]
        keys_across = keys.T
        blocks = query_blocks(query_rows, key_rows, causal)
        grad_q = []
        grad_k = [None] * len(blocks)
        grad_v = [None] * len(blocks)
        for half in range(2):
            index = pl.ds(table * HEADS + pair * 2 + half, 1)
            own = queries * masks[half]
            own_up = upstream * masks[half]
            logsum = lse_ref[index, :]
            delta = delta_ref[index, :]
            across = keys_across[half * HEAD : (half + 1) * HEAD, :]
            parts = []
            for number, (start, width, depth) in enumerate(blocks):
                span = slice(start, start + width)
                weight = jnp.exp(dot(keys[:depth], own[span], 1, 1) - logsum[:, span])
                if causal:
                    edge = jnp.where(causal_keep(width, width), weight[start:], 0.0)
                    weight = edge if start == 0 else jnp.concatenate([weight[:start], edge], 0)
                pull = dot(values[:depth], own_up[span], 1, 1)
                change = (weight * (pull - delta[:, span])).astype(bf16)
                add_v = dot(weight.astype(bf16), own_up[span])
                add_k = dot(change, own[span])
                grad_v[number] = add_v if half == 0 else grad_v[number] + add_v
                grad_k[number] = add_k if half == 0 else grad_k[number] + add_k
                parts.append(dot(across[:, :depth], change) * 0.125)
            grad_q.append(parts[0] if len(parts) == 1 else jnp.concatenate(parts, 1))
        dq_ref[q_rows, pl.ds(lanes, 128)] = jnp.concatenate(grad_q, 0).astype(bf16).T
        for ref, column, grads in ((dk_ref, k_col, grad_k), (dv_ref, v_col, grad_v)):
            total = grads[-1]
            if len(grads) == 2:
                low = blocks[0][2]
                total = jnp.concatenate([total[:low] + grads[0], total[low:]], 0)
            ref[k_rows, pl.ds(column + lanes, 128)] = total.astype(bf16)
        if between is not None:
            between(step)


def project(a_ref, w_ref, out_ref, width, first_scale=None):
    for start in range(0, width, 512):
        value = dot(a_ref[...], w_ref[:, start : start + 512])
        if first_scale is not None and start == 0:
            value = value * first_scale
        out_ref[:, start : start + 512] = value.astype(bf16)


def add_project(base_ref, a_ref, w_ref, out_ref):
    for start in range(0, D, 256):
        lanes = slice(start, start + 256)
        out_ref[:, lanes] = base_ref[:, lanes].astype(f32) + dot(a_ref[...], w_ref[:, lanes])


def weight_grad(a_ref, b_ref, out_ref):
    rows, columns = out_ref.shape
    for start in range(0, columns, 512):
        lanes = slice(start, start + 512)
        out_ref[:, lanes] = dot(a_ref[...], b_ref[:, lanes], 0, 0).astype(out_ref.dtype)


def ffn_forward(h_ref, w_in, u_ref, g_ref):
    for start in range(0, FF, 256):
        lanes = slice(start, start + 256)
        inner = dot(h_ref[...], w_in[:, lanes])
        if u_ref is not None:
            u_ref[:, lanes] = inner
        g_ref[:, lanes] = gelu(inner).astype(bf16)


def ffn_backward(og_ref, h_ref, u_ref, g_ref, w_in, w_out, d_in, d_out, dh_ref):
    weight_grad(g_ref, og_ref, d_out)
    for start in range(0, FF, 256):
        lanes = slice(start, start + 256)
        back = dot(og_ref[...], w_out[lanes, :], 1, 1)
        g_ref[:, lanes] = (gelu_slope(u_ref[:, lanes]) * back).astype(bf16)
    weight_grad(h_ref, g_ref, d_in)
    project_back(g_ref, w_in, dh_ref)


def project_back(g_ref, w_ref, out_ref):
    for start in range(0, D, 256):
        lanes = slice(start, start + 256)
        out_ref[:, lanes] = dot(g_ref[...], w_ref[lanes, :], 1, 1).astype(out_ref.dtype)


def norm_all(x_ref, norms_ref, row, out_ref, total, step):
    gain, shift = norms_ref[row : row + 1, :], norms_ref[row + 1 : row + 2, :]

    def body(rows):
        out_ref[rows, :] = norm_rows(x_ref[rows, :].astype(f32), gain, shift).astype(bf16)

    each_rows(total, step, body)


def norm_all_back(x_ref, norms_ref, row, upstream, dnorms_ref, total, step, keep):
    gain = norms_ref[row : row + 1, :]
    dnorms_ref[row : row + 2, :] = jnp.zeros((2, D), f32)

    def body(rows):
        arriving = upstream(rows) if callable(upstream) else upstream[rows, :]
        down, d_gain, d_shift = norm_rows_back(x_ref[rows, :].astype(f32), gain, arriving)
        dnorms_ref[row : row + 1, :] += d_gain
        dnorms_ref[row + 1 : row + 2, :] += d_shift
        if keep is not None:
            keep(rows, down)

    each_rows(total, step, body)


def encoder_forward_kernel(
    x_ref, w_qkv, w_out, w_in, w_ffo, norms, qkv_ref, o_ref, lse_ref, x1_ref, mem_ref, h_ref, g_ref
):
    rows = x_ref.shape[0]
    tables = rows // IMG
    norm_all(x_ref, norms, 0, h_ref, rows, IMG_CHUNK)
    project(h_ref, w_qkv, qkv_ref, 3 * D, 0.125)
    attend(tables, qkv_ref, qkv_ref, D, qkv_ref, 2 * D, o_ref, lse_ref, IMG, IMG, False)
    add_project(x_ref, o_ref, w_out, x1_ref)
    norm_all(x1_ref, norms, 2, h_ref, rows, IMG_CHUNK)
    ffn_forward(h_ref, w_in, None, g_ref)
    for start in range(0, D, 256):
        lanes = slice(start, start + 256)
        mem_ref[:, lanes] = (x1_ref[:, lanes] + dot(g_ref[...], w_ffo[:, lanes])).astype(bf16)


def encoder_forward(images, weights):
    rows = images.shape[0]
    tables = rows // IMG
    return pl.pallas_call(
        encoder_forward_kernel,
        out_shape=(
            jax.ShapeDtypeStruct((rows, 3 * D), bf16),
            jax.ShapeDtypeStruct((rows, D), bf16),
            jax.ShapeDtypeStruct((tables * HEADS, IMG), f32),
            jax.ShapeDtypeStruct((rows, D), f32),
            jax.ShapeDtypeStruct((rows, D), bf16),
        ),
        scratch_shapes=[pltpu.VMEM((rows, D), bf16), pltpu.VMEM((rows, FF), bf16)],
        compiler_params=pltpu.CompilerParams(vmem_limit_bytes=VMEM_LIMIT),
        name="encoder_forward",
    )(images, weights["qkv"], weights["out"], weights["ffn_in"], weights["ffn_out"], weights["norms"])


def soft_low(first_one, other_one):
    return 0.5 * (first_one + other_one - jnp.sqrt((first_one - other_one) ** 2 + 0.0001))


def soft_high(first_one, other_one):
    return 0.5 * (first_one + other_one + jnp.sqrt((first_one - other_one) ** 2 + 0.0001))


def softplus(value):
    return jnp.maximum(value, 0.0) + jnp.log1p(jnp.exp(-jnp.abs(value)))


@jax.custom_vjp
def smooth_relu(value):
    return softplus(value)


def smooth_relu_keep(value):
    return softplus(value), value


def smooth_relu_back(value, upstream):
    return (upstream * (1.0 / (1.0 + jnp.exp(-value))),)


smooth_relu.defvjp(smooth_relu_keep, smooth_relu_back)


def cell_losses(px, py, pw, ph, gx, gy, gw, gh):
    absolute = (
        jnp.sqrt((px - gx) ** 2 + 0.01)
        + jnp.sqrt((py - gy) ** 2 + 0.01)
        + jnp.sqrt((pw - gw) ** 2 + 0.01)
        + jnp.sqrt((ph - gh) ** 2 + 0.01)
    )
    left_p, right_p = px - 0.5 * pw, px + 0.5 * pw
    low_p, top_p = py - 0.5 * ph, py + 0.5 * ph
    left_g, right_g = gx - 0.5 * gw, gx + 0.5 * gw
    low_g, top_g = gy - 0.5 * gh, gy + 0.5 * gh
    across = smooth_relu(20.0 * (soft_low(right_p, right_g) - soft_high(left_p, left_g))) / 20.0
    upward = smooth_relu(20.0 * (soft_low(top_p, top_g) - soft_high(low_p, low_g))) / 20.0
    common = across * upward
    union = pw * ph + gw * gh - common
    hull = (soft_high(right_p, right_g) - soft_low(left_p, left_g)) * (
        soft_high(top_p, top_g) - soft_low(low_p, low_g)
    )
    ratio = common / union - (hull - union) / hull
    return 5.0 * absolute + 2.0 * (1.0 - ratio)


def split_sum(left, value):
    high = value.astype(bf16)
    rest = (value - high.astype(f32)).astype(bf16)
    return dot(left, high) + dot(left, rest)


def decoder_kernel(
    tags_ref, next_ref, counted_ref, place_ref, alive_ref, target_ref, scale_ref, mem_ref,
    w_qkv, w_out, w_cq, w_ckv, w_co, w_in, w_ffo, w_embed, w_head, w_box, norms, w_box_out,
    loss_ref, dmem_ref, d_qkv, d_out, d_cq, d_ckv, d_co, d_in, d_ffo, d_embed, d_head, d_box, d_norms, d_box_out,
    e_ref, h1_ref, qkv_ref, o1_ref, lse1_ref, y1_ref, h2_ref, cq_ref, ckv_ref, o2_ref, lse2_ref, y2_ref,
    h3_ref, u_ref, g_ref, y3_ref, z_ref, dy_ref, dh_ref, og_ref, up_ref, delta_ref,
):
    tables = tags_ref.shape[0]
    rows = tables * TAGS

    def tag_members(table):
        member = lax.broadcasted_iota(jnp.int32, (V, TAGS), 0) == tags_ref[table]
        return member.astype(f32).astype(bf16)

    for table in range(tables):
        e_ref[table * TAGS : (table + 1) * TAGS, :] = dot(tag_members(table), w_embed[...], 0, 0)
    norm_all(e_ref, norms, 0, h1_ref, rows, TAG_CHUNK)
    project(h1_ref, w_qkv, qkv_ref, 3 * D, 0.125)
    attend(tables, qkv_ref, qkv_ref, D, qkv_ref, 2 * D, o1_ref, lse1_ref, TAGS, TAGS, True)
    add_project(e_ref, o1_ref, w_out, y1_ref)
    norm_all(y1_ref, norms, 2, h2_ref, rows, TAG_CHUNK)
    project(h2_ref, w_cq, cq_ref, D, 0.125)
    project(mem_ref, w_ckv, ckv_ref, 2 * D)
    attend(tables, cq_ref, ckv_ref, 0, ckv_ref, D, o2_ref, lse2_ref, TAGS, IMG, False)
    add_project(y1_ref, o2_ref, w_co, y2_ref)
    norm_all(y2_ref, norms, 4, h3_ref, rows, TAG_CHUNK)
    ffn_forward(h3_ref, w_in, u_ref, g_ref)
    add_project(y2_ref, g_ref, w_ffo, y3_ref)
    norm_all(y3_ref, norms, 6, z_ref, rows, TAG_CHUNK)

    scale = scale_ref[0, 0]
    loss = jnp.zeros((1, 1), f32)
    picked, inners, box_ups = [], [], []
    head_sum = jnp.zeros((V, D), f32)
    box_in_sum = jnp.zeros((D, D), f32)
    box_out_sum = jnp.zeros((16, D), f32)
    for table in range(tables):
        own = slice(table * TAGS, (table + 1) * TAGS)
        final = z_ref[own, :]
        logits = dot(w_head[...], final, 1, 1)
        peak = jnp.max(logits, 0, keepdims=True)
        weight = jnp.exp(logits - peak)
        total = jnp.sum(weight, 0, keepdims=True)
        counted = counted_ref[table]
        wanted = lax.broadcasted_iota(jnp.int32, (V, TAGS), 0) == next_ref[table]
        chosen = jnp.sum(jnp.where(wanted, logits - peak - jnp.log(total), 0.0), 0, keepdims=True)
        loss = loss - jnp.sum(counted * chosen, 1, keepdims=True)
        dlogits = (weight / total - wanted.astype(f32)) * counted * scale
        tag_up = dlogits.astype(bf16)
        head_sum = head_sum + dot(tag_up, final)
        dfinal = dot(tag_up, w_head[...], 0, 0)
        select = (
            (lax.broadcasted_iota(jnp.int32, (TAGS, CELLS), 0) == place_ref[table])
            .astype(f32)
            .astype(bf16)
        )
        cells = dot(select, final, 0, 0).astype(bf16)
        inner = dot(cells, w_box[...])
        active = gelu(inner).astype(bf16)
        raw = dot(w_box_out[...], active, 1, 1)
        soft = 1.0 / (1.0 + jnp.exp(-raw))
        ratios = tuple(soft[k : k + 1, :] for k in range(4))
        wished = tuple(target_ref[table, k : k + 1, :] for k in range(4))
        alive = alive_ref[table]
        cell, pull = jax.vjp(lambda *parts: cell_losses(*parts, *wished), *ratios)
        loss = loss + jnp.sum(alive * cell, 1, keepdims=True)
        downs = pull(alive * scale)
        fill = jnp.zeros((16, CELLS), f32)
        index = lax.broadcasted_iota(jnp.int32, (16, CELLS), 0)
        for k in range(4):
            value = downs[k] * ratios[k] * (1.0 - ratios[k])
            fill = jnp.where(index == k, value, fill)
        box_up = fill.astype(bf16)
        box_out_sum = box_out_sum + dot(box_up, active)
        dinner = (gelu_slope(inner) * dot(box_up, w_box_out[...], 0, 0)).astype(bf16)
        box_in_sum = box_in_sum + dot(cells, dinner, 0, 0)
        dh_ref[own, :] = dfinal + split_sum(select, dot(dinner, w_box[...], 1, 1))
    loss_ref[...] = jnp.broadcast_to(loss, loss_ref.shape)
    d_head[...] = head_sum.astype(bf16)
    d_box[...] = box_in_sum.astype(bf16)
    d_box_out[...] = box_out_sum.astype(bf16)

    def start_sum(block, down):
        dy_ref[block, :] = down
        og_ref[block, :] = down.astype(bf16)

    def add_sum(block, down):
        total = down + dy_ref[block, :]
        dy_ref[block, :] = total
        og_ref[block, :] = total.astype(bf16)

    norm_all_back(y3_ref, norms, 6, dh_ref, d_norms, rows, TAG_CHUNK, start_sum)
    ffn_backward(og_ref, h3_ref, u_ref, g_ref, w_in, w_ffo, d_in, d_ffo, dh_ref)
    norm_all_back(y2_ref, norms, 4, dh_ref, d_norms, rows, TAG_CHUNK, add_sum)

    weight_grad(o2_ref, og_ref, d_co)
    project_back(og_ref, w_co, up_ref)
    head_sums(tables, up_ref, o2_ref, delta_ref, TAGS)
    attend_back(
        (0, tables), cq_ref, ckv_ref, 0, ckv_ref, D, up_ref, lse2_ref, delta_ref,
        cq_ref, ckv_ref, ckv_ref, TAGS, IMG, False,
    )
    weight_grad(h2_ref, cq_ref, d_cq)
    weight_grad(mem_ref, ckv_ref, d_ckv)
    project_back(ckv_ref, w_ckv, dmem_ref)
    project_back(cq_ref, w_cq, dh_ref)
    norm_all_back(y1_ref, norms, 2, dh_ref, d_norms, rows, TAG_CHUNK, add_sum)

    weight_grad(o1_ref, og_ref, d_out)
    project_back(og_ref, w_out, up_ref)
    head_sums(tables, up_ref, o1_ref, delta_ref, TAGS)
    attend_back(
        (0, tables), qkv_ref, qkv_ref, D, qkv_ref, 2 * D, up_ref, lse1_ref, delta_ref,
        qkv_ref, qkv_ref, qkv_ref, TAGS, TAGS, True,
    )
    weight_grad(h1_ref, qkv_ref, d_qkv)
    project_back(qkv_ref, w_qkv, dh_ref)
    norm_all_back(e_ref, norms, 0, dh_ref, d_norms, rows, TAG_CHUNK, add_sum)
    embed_sum = jnp.zeros((V, D), f32)
    for table in range(tables):
        embed_sum = embed_sum + split_sum(
            tag_members(table), dy_ref[table * TAGS : (table + 1) * TAGS, :]
        )
    d_embed[...] = embed_sum.astype(bf16)


DECODER_NAMES = (
    "qkv", "out", "cross_q", "cross_kv", "cross_out", "ffn_in", "ffn_out", "embed", "head", "box_in", "norms", "box_out",
)


def decoder_step(prepared, scale, memory, weights):
    tables = prepared[0].shape[0]
    rows = tables * TAGS
    image_rows = memory.shape[0]
    grads = {
        name: jax.ShapeDtypeStruct(weights[name].shape, f32 if name == "norms" else bf16)
        for name in DECODER_NAMES
    }
    vmem = pl.BlockSpec(memory_space=pltpu.VMEM)
    low = lambda width, height=rows: pltpu.VMEM((height, width), bf16)
    full = lambda width, height=rows: pltpu.VMEM((height, width), f32)
    stats = pltpu.VMEM((tables * HEADS, TAGS), f32)
    outs = pl.pallas_call(
        decoder_kernel,
        out_shape=(
            jax.ShapeDtypeStruct((8, 128), f32),
            jax.ShapeDtypeStruct((image_rows, D), f32),
            *[grads[name] for name in DECODER_NAMES],
        ),
        in_specs=[vmem] * 6 + [pl.BlockSpec(memory_space=pltpu.SMEM)] + [vmem] * 13,
        scratch_shapes=[
            full(D), low(D), low(3 * D), low(D), stats, full(D), low(D), low(D), low(2 * D, image_rows), low(D), stats,
            full(D), low(D), full(FF), low(FF), full(D), low(D), full(D), full(D), low(D), low(D), stats,
        ],
        compiler_params=pltpu.CompilerParams(vmem_limit_bytes=VMEM_LIMIT),
        name="decoder_step",
    )(*prepared, scale, memory, *[weights[name] for name in DECODER_NAMES])
    return outs[0], outs[1], dict(zip(DECODER_NAMES, outs[2:]))


AXES = ("wide", "narrow")
MESH = pl.DeviceIdType.MESH
ORDERS = (("a", "y", "b"), ("b", "a", "y"))


class Place:
    def __init__(self, wide, narrow):
        inner = 2 if wide % 2 == 0 else 1
        self.sizes = {"a": wide // inner, "b": inner, "y": narrow // 2, "c": 2}
        self.narrow = narrow
        self.count = wide * narrow

    def locate(self):
        wide, narrow = lax.axis_index("wide"), lax.axis_index("narrow")
        inner = self.sizes["b"]
        self.here = {
            "a": lax.div(wide, inner),
            "b": lax.rem(wide, inner),
            "y": lax.div(narrow, 2),
            "c": lax.rem(narrow, 2),
        }
        return self

    def moved(self, steps):
        there = dict(self.here)
        for part, step in steps.items():
            there[part] = lax.rem(there[part] + step, self.sizes[part])
        return there

    def device(self, there):
        return (there["a"] * self.sizes["b"] + there["b"], there["y"] * 2 + there["c"])

    def index(self, there):
        wide, narrow = self.device(there)
        return wide * self.narrow + narrow

    def peers(self):
        return [(part, step) for part, size in self.sizes.items() for step in range(1, size)]

    def in_plane(self, step):
        size, wide = self.sizes["b"], self.sizes["y"]
        here = (self.here["b"] * wide + self.here["y"]) * 2 + self.here["c"]
        there = lax.rem(here + step, size * wide * 2)
        return there, {
            **self.here,
            "b": lax.div(there, wide * 2),
            "y": lax.rem(lax.div(there, 2), wide),
            "c": lax.rem(there, 2),
        }

    def plane(self):
        return self.sizes["b"] * self.sizes["y"] * 2

    def greet(self, whole_plane=False):
        barrier = pltpu.get_barrier_semaphore()
        peers = [self.moved({part: step}) for part, step in self.peers()]
        if whole_plane:
            peers = [self.in_plane(step)[1] for step in range(1, self.plane())] + [
                self.moved({"a": step}) for step in range(1, self.sizes["a"])
            ]
        for there in peers:
            pl.semaphore_signal(
                barrier, inc=1, device_id=self.device(there), device_id_type=MESH
            )
        pl.semaphore_wait(barrier, len(peers))


def spread_blocks(place, order, all_ref, send_sem, recv_sem):
    one, two, three = order
    s1, s2, s3 = (place.sizes[part] for part in order)
    base2 = s1 - 1
    base3 = base2 + s1 * (s2 - 1)
    base4 = base3 + s1 * s2 * (s3 - 1)

    def copy(p, q, r, core, part, step, number):
        block = place.index(place.moved({one: p, two: q, three: r, "c": core}))
        return pltpu.make_async_remote_copy(
            src_ref=all_ref.at[block],
            dst_ref=all_ref.at[block],
            send_sem=send_sem.at[number],
            recv_sem=recv_sem.at[block],
            device_id=place.device(place.moved({part: step})),
            device_id_type=MESH,
        )

    def arrived(p, q, r, core=0):
        copy(p, q, r, core, "c", 1, 0).wait_recv()

    def to_sibling(p, q, r):
        copy(p, q, r, 0, "c", 1, base4 + (p * s2 + q) * s3 + r).start()

    def to_third(p, q):
        for step in range(1, s3):
            copy(p, q, 0, 0, three, step, base3 + (p * s2 + q) * (s3 - 1) + step - 1).start()

    @pl.loop(1, s1)
    def _(step):
        copy(0, 0, 0, 0, one, step, step - 1).start()

    @pl.loop(0, s1)
    def _(p):
        @pl.when(p > 0)
        def _():
            arrived(p, 0, 0)

        for step in range(1, s2):
            copy(p, 0, 0, 0, two, step, base2 + p * (s2 - 1) + step - 1).start()
        to_third(p, 0)
        to_sibling(p, 0, 0)

    @pl.loop(0, s1 * (s2 - 1))
    def _(number):
        p, q = lax.rem(number, s1), lax.div(number, s1) + 1
        arrived(p, q, 0)
        to_third(p, q)
        to_sibling(p, q, 0)

    @pl.loop(0, s1 * s2 * (s3 - 1))
    def _(number):
        p, q = lax.rem(number, s1), lax.rem(lax.div(number, s1), s2)
        r = lax.div(number, s1 * s2) + 1
        arrived(p, q, r)
        to_sibling(p, q, r)

    @pl.loop(0, s1 * s2 * s3)
    def _(number):
        p, q = lax.rem(number, s1), lax.rem(lax.div(number, s1), s2)
        arrived(p, q, lax.div(number, s1 * s2), 1)

    @pl.loop(0, place.count - 1)
    def _(number):
        copy(0, 0, 0, 0, "c", 1, number).wait_send()


def gather_all(place, all_ref, send_sem, recv_sem):
    for core in range(2):

        @pl.when(place.here["c"] == core)
        def _():
            spread_blocks(place, ORDERS[core], all_ref, send_sem, recv_sem)


def block_rows(amount):
    return -(-(amount // 128 + 3) // 16) * 16


def flat_rows(amount, count):
    return -(-((count - 1) * amount // 128 + block_rows(amount)) // 8) * 8


def layout_bases(layout):
    offset = 0
    for name, (height, breadth) in layout:
        yield name, height, breadth, offset // 128
        offset += height * breadth


def place_blocks(all_ref, flat_ref, amount):
    count, rows, _ = all_ref.shape
    used = amount // 128 + 2
    flat_ref[0:8, :] = jnp.zeros((8, 128), f32)

    @pl.loop(0, count)
    def _(device):
        start = lax.div(device * amount, 128)
        before = flat_ref[pl.ds(start, 1), :]
        flat_ref[pl.ds(start, used), :] = all_ref[device, :used, :].astype(f32)
        flat_ref[pl.ds(start, 1), :] = before + all_ref[device, 0:16, :].astype(f32)[0:1]


def one_hot(shape, match):
    first = lax.broadcasted_iota(jnp.int32, shape, 0)
    second = lax.broadcasted_iota(jnp.int32, shape, 1)
    return match(first, second).astype(f32).astype(bf16)


def take_matrices(flat_ref, layout, out_refs):
    for name, height, breadth, base in layout_bases(layout):
        out_ref = out_refs[name]
        if name == "head":
            turned = flat_ref[base : base + 128, :].T.astype(bf16)
            total = jnp.zeros((V, D), f32)
            for part in range(4):
                spread = one_hot((128, D), lambda row, column: column == 4 * row + part)
                total = total + dot(turned[part * V : (part + 1) * V, :], spread)
            out_ref[...] = total.astype(bf16)
        elif name == "box_out":
            block = flat_ref[base : base + 16, :].astype(bf16)
            own = one_hot((16, D), lambda row, column: lax.div(column, 32) == row).astype(f32)
            index = lax.broadcasted_iota(jnp.int32, (16, D), 0)
            total = jnp.zeros((16, D), f32)
            for k in range(4):
                pick = one_hot((128, D), lambda lane, column: lane == 4 * lax.rem(column, 32) + k)
                line = jnp.sum(dot(block, pick) * own, 0, keepdims=True)
                total = jnp.where(index == k, line, total)
            out_ref[...] = total.astype(bf16)
        else:
            wide = breadth // 128
            for column in range(wide):
                out_ref[:, column * 128 : (column + 1) * 128] = flat_ref[
                    pl.ds(base + column, height, stride=wide), :
                ].astype(out_ref.dtype)


def put_matrices(flat_ref, layout, refs):
    for name, height, breadth, base in layout_bases(layout):
        ref = refs[name]
        if name == "head":
            total = jnp.zeros((128, 128), f32)
            for part in range(4):
                pick = one_hot((128, D), lambda row, column: column == 4 * row + part)
                shift = one_hot((V, 128), lambda row, lane: lane == V * part + row)
                total = total + dot(dot(pick, ref[...], 1, 1).astype(bf16), shift)
            flat_ref[base : base + 128, :] = total
        elif name == "box_out":
            own = one_hot((16, D), lambda row, column: lax.div(column, 32) == row).astype(f32)
            total = jnp.zeros((16, 128), f32)
            for k in range(4):
                line = ref[...].astype(f32)[k : k + 1, :]
                spread = one_hot((D, 128), lambda column, lane: lane == 4 * lax.rem(column, 32) + k)
                total = total + dot((own * line).astype(bf16), spread)
            flat_ref[base : base + 16, :] = total
        else:
            wide = breadth // 128
            for column in range(wide):
                flat_ref[pl.ds(base + column, height, stride=wide), :] = ref[
                    :, column * 128 : (column + 1) * 128
                ].astype(f32)


def cut_blocks(flat_ref, amount, block_ref):
    count, rows, _ = block_ref.shape

    @pl.loop(0, count)
    def _(device):
        start = lax.div(device * amount, 128)
        block_ref[device, :, :] = flat_ref[pl.ds(start, rows), :].astype(bf16)


def weight_shapes(layout):
    shapes = {name: extent for name, extent in layout}
    if "head" in shapes:
        shapes["head"], shapes["box_out"] = (V, D), (16, D)
    return {
        name: jax.ShapeDtypeStruct(extent, f32 if name == "norms" else bf16)
        for name, extent in shapes.items()
    }


def gather_encoder(place, shard_block, amount):
    layout = encoder_layout()
    shapes = weight_shapes(layout)
    rows = shard_block.shape[0]

    def kernel(block_ref, *refs):
        outs = dict(zip(shapes, refs))
        count_ref, all_ref, flat_ref, send_sem, recv_sem = refs[len(shapes) :]
        place.locate()
        all_ref[place.index(place.here)] = block_ref[...].astype(bf16)
        place.greet()
        gather_all(place, all_ref, send_sem, recv_sem)
        total = jnp.zeros((1, 128), f32)
        for device in range(place.count):
            total = total + all_ref[device, rows - 16 :, :].astype(f32)[15:16]
        count_ref[...] = jnp.broadcast_to(jnp.sum(total, 1, keepdims=True), count_ref.shape)
        place_blocks(all_ref, flat_ref, amount)
        take_matrices(flat_ref, layout, outs)

    outs = pl.pallas_call(
        kernel,
        out_shape=(*shapes.values(), jax.ShapeDtypeStruct((8, 128), f32)),
        scratch_shapes=[
            pltpu.VMEM((place.count, rows, 128), bf16),
            pltpu.VMEM((flat_rows(amount, place.count), 128), f32),
            pltpu.SemaphoreType.DMA((place.count - 1,)),
            pltpu.SemaphoreType.DMA((place.count,)),
        ],
        compiler_params=pltpu.CompilerParams(
            collective_id=1, has_side_effects=True, vmem_limit_bytes=VMEM_LIMIT
        ),
        name="gather_encoder",
    )(shard_block)
    return dict(zip(shapes, outs)), outs[-1][0, 0]


def unpack_decoder(blocks, amount):
    layout = decoder_layout()
    shapes = weight_shapes(layout)

    def kernel(all_ref, *refs):
        flat_ref = refs[-1]
        place_blocks(all_ref, flat_ref, amount)
        take_matrices(flat_ref, layout, dict(zip(shapes, refs)))

    outs = pl.pallas_call(
        kernel,
        out_shape=tuple(shapes.values()),
        scratch_shapes=[pltpu.VMEM((flat_rows(amount, blocks.shape[0]), 128), f32)],
        compiler_params=pltpu.CompilerParams(vmem_limit_bytes=VMEM_LIMIT),
        name="unpack_decoder",
    )(blocks)
    return dict(zip(shapes, outs))


def pack_grads(grads, layout, amount, count, name):
    names = [piece for piece, _ in layout]

    def kernel(*refs):
        block_ref, flat_ref = refs[-2:]
        tail = sum(extent[0] * extent[1] for _, extent in layout) // 128
        flat_ref[tail:, :] = jnp.zeros((flat_ref.shape[0] - tail, 128), f32)
        put_matrices(flat_ref, layout, dict(zip(names, refs)))
        cut_blocks(flat_ref, amount, block_ref)

    return pl.pallas_call(
        kernel,
        out_shape=jax.ShapeDtypeStruct((count, block_rows(amount), 128), bf16),
        scratch_shapes=[pltpu.VMEM((flat_rows(amount, count), 128), f32)],
        compiler_params=pltpu.CompilerParams(vmem_limit_bytes=VMEM_LIMIT),
        name=name,
    )(*[grads[piece] for piece in names])


class Reduction:
    def __init__(self, place, core, pick, own_ref, mine_ref, got_ref, load_sem, send_sem, recv_sem):
        self.place, self.pick = place, pick
        self.own, self.mine, self.got = own_ref, mine_ref, got_ref
        self.load_sem, self.send_sem, self.recv_sem = load_sem, send_sem, recv_sem
        self.order, self.other = ORDERS[core], ORDERS[1 - core]
        self.s1, self.s2, self.s3 = (place.sizes[part] for part in self.order)
        self.half = place.count // 2
        self.base3 = self.half
        self.base2 = self.base3 + (self.s3 - 1) * self.s1 * self.s2
        self.base1 = self.base2 + (self.s2 - 1) * self.s1

    def slot(self, steps):
        sizes = self.place.sizes
        return (steps["a"] * sizes["b"] + steps["b"]) * sizes["y"] + steps["y"]

    def owner(self, steps):
        return self.place.index(self.place.moved(steps))

    def only(self, steps, body):
        if self.pick is None:
            body()
        else:
            pl.when(self.pick(self.owner(steps)))(body)

    def copy(self, source, slot, part, step):
        return pltpu.make_async_remote_copy(
            src_ref=source,
            dst_ref=self.got.at[slot],
            send_sem=self.send_sem.at[slot],
            recv_sem=self.recv_sem.at[slot],
            device_id=self.place.device(self.place.moved({part: step})),
            device_id_type=MESH,
        )

    def load(self, steps):
        slot = self.slot(steps)
        return pltpu.make_async_copy(
            self.own.at[self.owner(steps)], self.mine.at[slot], self.load_sem.at[slot]
        )

    def took(self, slot):
        self.copy(self.mine.at[0], slot, "c", 1).wait_recv()

    def value(self, slot):
        return self.got[slot].astype(f32)

    def levels(self, order):
        s1, s2, s3 = (self.place.sizes[part] for part in order)
        return (
            (s1 * s2 * (s3 - 1), lambda n: (s1 - 1 - lax.rem(n, s1), s2 - 1 - lax.rem(lax.div(n, s1), s2), lax.div(n, s1 * s2) + 1)),
            (s1 * (s2 - 1), lambda n: (s1 - 1 - lax.rem(n, s1), lax.div(n, s1) + 1, 0)),
            (s1, lambda n: (s1 - 1 - n, 0, 0)),
        )

    def to_sibling(self):
        if self.load_sem is not None:
            for amount, where in self.levels(self.order):

                @pl.loop(0, amount)
                def _(number):
                    self.load(dict(zip(self.order, where(number)))).start()

        for amount, where in self.levels(self.other):

            @pl.loop(0, amount)
            def _(number):
                steps = dict(zip(self.other, where(number)))
                slot = self.slot(steps)

                def send():
                    block = slot if self.load_sem is None else self.owner({**steps, "c": 1})
                    self.copy(self.own.at[block], slot, "c", 1).start()

                self.only({**steps, "c": 1}, send)

    def partial(self, p, q, r):
        steps = dict(zip(self.order, (p, q, r)))
        slot = self.slot(steps)
        if self.load_sem is not None:
            self.load(steps).wait()
        self.took(slot)
        return slot, self.mine[slot].astype(f32) + self.value(slot)

    def add_third(self, total, p, q):
        for step in range(1, self.s3):
            slot = self.base3 + ((step - 1) * self.s1 + p) * self.s2 + q
            self.took(slot)
            total = total + self.value(slot)
        return total

    def add_second(self, total, p):
        for step in range(1, self.s2):
            slot = self.base2 + (step - 1) * self.s1 + p
            self.took(slot)
            total = total + self.value(slot)
        return total

    def send(self, own_slot, total, slot, part, step):
        self.mine[own_slot] = total.astype(bf16)
        self.copy(self.mine.at[own_slot], slot, part, step).start()

    def third(self):
        amount, where = self.levels(self.order)[0]

        @pl.loop(0, amount)
        def _(number):
            p, q, r = where(number)

            def body():
                own_slot, total = self.partial(p, q, r)
                slot = self.base3 + ((r - 1) * self.s1 + p) * self.s2 + q
                self.send(own_slot, total, slot, self.order[2], r)

            self.only(dict(zip(self.order, (p, q, r))), body)

    def second(self):
        amount, where = self.levels(self.order)[1]

        @pl.loop(0, amount)
        def _(number):
            p, q, _ = where(number)

            def body():
                own_slot, total = self.partial(p, q, 0)
                total = self.add_third(total, p, q)
                self.send(own_slot, total, self.base2 + (q - 1) * self.s1 + p, self.order[1], q)

            self.only(dict(zip(self.order, (p, q, 0))), body)

    def first(self):
        @pl.loop(1, self.s1)
        def _(p):
            def body():
                own_slot, total = self.partial(p, 0, 0)
                total = self.add_second(self.add_third(total, p, 0), p)
                self.send(own_slot, total, self.base1 + p - 1, self.order[0], p)

            self.only({self.order[0]: p}, body)

    def last(self, out_ref):
        def body():
            _, total = self.partial(0, 0, 0)
            out_ref[...] = self.add_second(self.add_third(total, 0, 0), 0)

            @pl.loop(1, self.s1)
            def _(p):
                slot = self.base1 + p - 1
                self.took(slot)
                out_ref[...] += self.value(slot)

        self.only({}, body)

    def close(self):
        @pl.loop(0, self.place.count - 1)
        def _(slot):
            self.copy(self.mine.at[0], slot, "c", 1).wait_send()


def reduction_memory(count, rows):
    half = count // 2
    return [pltpu.VMEM((half, rows, 128), bf16), pltpu.VMEM((count - 1, rows, 128), bf16)]


def reduction_signals(count, loads):
    return [pltpu.SemaphoreType.DMA((n,)) for n in ([count // 2] if loads else []) + [count - 1] * 2]


def reduce_stage(place, stage, pick, *members):
    for core in range(2):

        @pl.when(place.here["c"] == core)
        def _():
            stage(Reduction(place, core, pick, *members))


def cut_for_reduction(place, pick, flat_ref, amount, mine_ref, other_ref):
    rows = mine_ref.shape[1]
    sizes = place.sizes

    @pl.loop(0, place.count // 2)
    def _(slot):
        steps = {
            "a": lax.div(slot, sizes["b"] * sizes["y"]),
            "b": lax.rem(lax.div(slot, sizes["y"]), sizes["b"]),
            "y": lax.rem(slot, sizes["y"]),
        }
        for core, ref in ((0, mine_ref), (1, other_ref)):
            owner = place.index(place.moved({**steps, "c": core}))

            @pl.when(pick(owner))
            def _():
                ref[slot] = flat_ref[pl.ds(lax.div(owner * amount, 128), rows), :].astype(bf16)


def sum_everywhere(place, value, box_ref, send_sem, recv_sem):
    base = 0
    plane = [place.in_plane(step) for step in range(place.plane())]
    line = [place.moved({"a": step}) for step in range(place.sizes["a"])]
    for members in (plane, [(there["a"], there) for there in line]):

        def copy(step, number, base=base, members=members):
            return pltpu.make_async_remote_copy(
                src_ref=box_ref.at[base + number],
                dst_ref=box_ref.at[base + number],
                send_sem=send_sem.at[base + step],
                recv_sem=recv_sem.at[base + number],
                device_id=place.device(members[step][1]),
                device_id_type=MESH,
            )

        size = len(members)
        mine = members[0][0]
        box_ref[base + mine] = value
        for step in range(1, size):
            copy(step, mine).start()
        for step in range(1, size):
            copy(step, members[step][0]).wait_recv()
        for step in range(1, size):
            copy(step, mine).wait_send()
        value = box_ref[base]
        for other in range(1, size):
            value = value + box_ref[base + other]
        base += size
    return value


def own_squares(place, out_ref, amount):
    rows = out_ref.shape[0]
    offset = lax.rem(place.index(place.here) * amount, 128)
    position = (
        lax.broadcasted_iota(jnp.int32, (rows, 128), 0) * 128
        + lax.broadcasted_iota(jnp.int32, (rows, 128), 1)
        - offset
    )
    value = jnp.where((position >= 0) & (position < amount), out_ref[...], 0.0)
    return jnp.sum(jnp.sum(value * value, 0, keepdims=True), 1, keepdims=True)


def weight_grad_flat(a_ref, b_ref, flat_ref, base, breadth):
    wide = breadth // 128
    for start in range(0, breadth, 512):
        value = dot(a_ref[...], b_ref[:, start : start + 512], 0, 0)
        store_flat(value, flat_ref, base + start // 128, wide)


def store_flat(value, flat_ref, base, wide):
    rows, columns = value.shape
    for part in range(columns // 128):
        flat_ref[pl.ds(base + part, rows, stride=wide), :] = value[:, part * 128 : (part + 1) * 128]


def encoder_backward(place, images, stored, dmem, weights, decoder_blocks, amounts, loss_block):
    rows = images.shape[0]
    tables = rows // IMG
    qkv, mixed, lse, middle = stored
    bases = {name: base for name, _, _, base in layout_bases(encoder_layout())}
    block, small = decoder_blocks.shape[1], block_rows(amounts[0])
    flat_count = flat_rows(amounts[0], place.count)
    first_early = -(-bases["out"] * 128 // amounts[0])
    end_early = max((bases["norms"] - amounts[0] // 128 - 2) * 128 // amounts[0], first_early)
    steps = place.plane() + place.sizes["a"]
    early = lambda owner: (owner >= first_early) & (owner < end_early)
    late = lambda owner: (owner < first_early) | (owner >= end_early)

    def kernel(
        x_hbm, qkv_hbm, o_ref, lse_ref, x1_ref, dmem_ref, w_qkv_hbm, w_out, w_in, w_ffo, norms, own_ref, loss_ref,
        encoder_ref, decoder_ref, stat_ref,
        w_qkv, h_ref, g_ref, og_ref, qkv_ref, delta_ref, d_norms, flat_ref, fetch_sem,
        theirs_ref, mine_ref, got_ref, far_mine_ref, far_got_ref, *signals,
    ):
        far = (None, own_ref, far_mine_ref, far_got_ref, *signals[:3])
        near = (theirs_ref, mine_ref, got_ref, None, *signals[3:5])
        box_ref, box_send, box_recv = signals[5:]
        work = functools.partial(reduce_stage, place)
        place.locate()
        place.greet(True)
        work(lambda one: one.to_sibling(), *far)
        fetches = [
            pltpu.make_async_copy(source, target, fetch_sem.at[k])
            for k, (source, target) in enumerate(
                ((qkv_hbm, qkv_ref), (w_qkv_hbm, w_qkv), (x_hbm, g_ref.at[:, :D]))
            )
        ]
        x_ref = g_ref.at[:, :D]
        fetches[0].start()
        fetches[1].start()
        tail = bases["norms"] + 4 * D // 128
        flat_ref[tail:, :] = jnp.zeros((flat_count - tail, 128), f32)
        norm_all(x1_ref, norms, 2, h_ref, rows, IMG_CHUNK)
        og_ref[...] = dmem_ref[...].astype(bf16)
        for start in range(0, FF, 256):
            lanes = slice(start, start + 256)
            inner = dot(h_ref[...], w_in[:, lanes])
            back = dot(og_ref[...], w_ffo[lanes, :], 1, 1)
            part = dot(gelu(inner).astype(bf16), og_ref[...], 0, 0)
            store_flat(part, flat_ref, bases["ffn_out"] + start * 4, 4)
            g_ref[:, lanes] = (gelu_slope(inner) * back).astype(bf16)
        work(lambda one: one.third(), *far)
        weight_grad_flat(h_ref, g_ref, flat_ref, bases["ffn_in"], FF)

        def keep(part, down):
            og_ref[part, :] = (down + dmem_ref[part, :]).astype(bf16)

        norm_all_back(
            x1_ref, norms, 2, lambda part: dot(g_ref[part, :], w_in[...], 1, 1), d_norms, rows, IMG_CHUNK, keep
        )
        fetches[2].start()
        weight_grad_flat(o_ref, og_ref, flat_ref, bases["out"], D)
        cut_for_reduction(place, early, flat_ref, amounts[0], mine_ref, theirs_ref)
        work(lambda one: one.to_sibling(), early, *near)

        def project_rows(part):
            og_ref[part, :] = dot(og_ref[part, :], w_out[...], 1, 1).astype(bf16)

        each_rows(rows, IMG_CHUNK, project_rows)
        head_sums(tables, og_ref, o_ref, delta_ref, IMG)
        work(lambda one: one.second(), *far)
        fetches[0].wait()

        def between(step):
            @pl.when(step == 1)
            def _():
                work(lambda one: one.third(), early, *near)

            @pl.when(step == 2)
            def _():
                work(lambda one: one.first(), *far)

            @pl.when(step == 4)
            def _():
                work(lambda one: one.second(), early, *near)

            @pl.when(step == 5)
            def _():
                work(lambda one: one.last(decoder_ref), *far)

            @pl.when(step == 6)
            def _():
                work(lambda one: one.first(), early, *near)

        attend_back(
            (0, tables), qkv_ref, qkv_ref, D, qkv_ref, 2 * D, og_ref, lse_ref, delta_ref,
            qkv_ref, qkv_ref, qkv_ref, IMG, IMG, False, between,
        )
        work(lambda one: one.last(encoder_ref), early, *near)
        fetches[1].wait()
        fetches[2].wait()
        norm_all(x_ref, norms, 0, h_ref, rows, IMG_CHUNK)
        weight_grad_flat(h_ref, qkv_ref, flat_ref, bases["qkv"], 3 * D)
        norm_all_back(
            x_ref, norms, 0, lambda part: dot(qkv_ref[part, :], w_qkv[...], 1, 1), d_norms, rows, IMG_CHUNK, None
        )
        store_flat(d_norms[...], flat_ref, bases["norms"], 4)
        cut_for_reduction(place, late, flat_ref, amounts[0], mine_ref, theirs_ref)
        work(lambda one: one.to_sibling(), late, *near)
        work(lambda one: one.third(), late, *near)
        work(lambda one: one.second(), late, *near)
        work(lambda one: one.first(), late, *near)
        work(lambda one: one.last(encoder_ref), late, *near)
        squares = own_squares(place, encoder_ref, amounts[0]) + own_squares(
            place, decoder_ref, amounts[1]
        )
        index = lax.broadcasted_iota(jnp.int32, (8, 128), 0)
        value = jnp.where(index == 0, squares, jnp.where(index == 1, loss_ref[...], 0.0))
        stat_ref[...] = sum_everywhere(place, value, box_ref, box_send, box_recv)
        work(lambda one: one.close(), *far)
        work(lambda one: one.close(), early, *near)

    vmem, hbm = pl.BlockSpec(memory_space=pltpu.VMEM), pl.BlockSpec(memory_space=pl.ANY)
    count = place.count
    return pl.pallas_call(
        kernel,
        out_shape=(
            jax.ShapeDtypeStruct((small, 128), f32),
            jax.ShapeDtypeStruct((block, 128), f32),
            jax.ShapeDtypeStruct((8, 128), f32),
        ),
        in_specs=[hbm, hbm, vmem, vmem, vmem, vmem, hbm, vmem, vmem, vmem, vmem, hbm, vmem],
        scratch_shapes=[
            pltpu.VMEM((D, 3 * D), bf16),
            pltpu.VMEM((rows, D), bf16),
            pltpu.VMEM((rows, FF), bf16),
            pltpu.VMEM((rows, D), bf16),
            pltpu.VMEM((rows, 3 * D), bf16),
            pltpu.VMEM((tables * HEADS, IMG), f32),
            pltpu.VMEM((4, D), f32),
            pltpu.VMEM((flat_count, 128), f32),
            pltpu.SemaphoreType.DMA((3,)),
            pltpu.VMEM((count // 2, small, 128), bf16),
            *reduction_memory(count, small),
            *reduction_memory(count, block),
            *reduction_signals(count, True),
            *reduction_signals(count, False),
            pltpu.VMEM((steps, 8, 128), f32),
            pltpu.SemaphoreType.DMA((steps,)),
            pltpu.SemaphoreType.DMA((steps,)),
        ],
        compiler_params=pltpu.CompilerParams(
            collective_id=2, has_side_effects=True, vmem_limit_bytes=VMEM_LIMIT
        ),
        name="encoder_backward",
    )(
        images, qkv, mixed, lse, middle, dmem, weights["qkv"], weights["out"], weights["ffn_in"], weights["ffn_out"],
        weights["norms"], decoder_blocks, loss_block,
    )


def adam_update(gradient, master, first_state, second_state, average):
    first_new = BETA_ONE * first_state + (1.0 - BETA_ONE) * gradient
    second_new = BETA_TWO * second_state + (1.0 - BETA_TWO) * gradient * gradient
    first_hat = first_new / (1.0 - BETA_ONE**STEP)
    second_hat = second_new / (1.0 - BETA_TWO**STEP)
    master_new = master - LEARN_RATE * (
        first_hat / (jnp.sqrt(second_hat) + EPSILON) + WEIGHT_DECAY * master
    )
    average_new = SMOOTH * average + (1.0 - SMOOTH) * master_new
    return (first_new, second_new, master_new, average_new)


def shard_block(shard, offset, tail=None):
    rows = block_rows(shard.shape[0])
    values = lax.dynamic_update_slice(jnp.zeros((rows * 128,), shard.dtype), shard, (offset,))
    if tail is not None:
        values = lax.dynamic_update_slice(values, tail, ((rows - 1) * 128,))
    return values.reshape(rows, 128)


def on_device(place, *arguments):
    (
        images, tag_ids, tag_lengths, cell_mask, cell_index, box_targets,
        encoder_params, encoder_first, encoder_second, encoder_average,
        decoder_params, decoder_first, decoder_second, decoder_average,
    ) = arguments
    encoder_amount, decoder_amount = encoder_params.shape[0], decoder_params.shape[0]
    me = lax.axis_index("wide") * lax.axis_size("narrow") + lax.axis_index("narrow")
    encoder_offset = lax.rem(me * encoder_amount, 128)
    decoder_offset = lax.rem(me * decoder_amount, 128)
    cell_slots = jnp.arange(CELLS)
    alive = ((cell_mask > 0) & (cell_slots[None, :] < (tag_lengths // 4)[:, None])).astype(f32)
    cells = cell_index % tag_lengths[:, None]
    counted = (jnp.arange(TAGS)[None, :] < (tag_lengths - 1)[:, None]).astype(f32)
    upcoming = jnp.roll(tag_ids, -1, 1)
    prepared = (
        tag_ids[:, None, :], upcoming[:, None, :], counted[:, None, :], cells[:, None, :], alive[:, None, :], box_targets,
    )

    decoder_blocks = lax.all_gather(
        shard_block(decoder_params.astype(bf16), decoder_offset), AXES, axis=0, tiled=False
    )
    encoder_weights, cell_total = gather_encoder(
        place, shard_block(encoder_params, encoder_offset, jnp.sum(alive, 1)), encoder_amount
    )
    *stored, memory = encoder_forward(images, encoder_weights)
    decoder_weights = unpack_decoder(decoder_blocks, decoder_amount)
    scale = (1.0 / cell_total).reshape(1, 1)
    loss_block, dmemory, decoder_grads = decoder_step(prepared, scale, memory, decoder_weights)
    decoder_packed = pack_grads(
        decoder_grads, decoder_layout(), decoder_amount, place.count, "pack_decoder"
    )
    encoder_sum, decoder_sum, stats = encoder_backward(
        place, images, stored, dmemory, encoder_weights, decoder_packed, (encoder_amount, decoder_amount), loss_block
    )
    grad_norm = jnp.sqrt(stats[0, 0])
    factor = CLIP_NORM / jnp.maximum(grad_norm, CLIP_NORM)
    encoder_grad = lax.dynamic_slice(encoder_sum.reshape(-1), (encoder_offset,), (encoder_amount,))
    decoder_grad = lax.dynamic_slice(decoder_sum.reshape(-1), (decoder_offset,), (decoder_amount,))
    encoder_new = adam_update(
        encoder_grad * factor, encoder_params, encoder_first, encoder_second, encoder_average
    )
    decoder_new = adam_update(
        decoder_grad * factor, decoder_params, decoder_first, decoder_second, decoder_average
    )
    return (stats[1, 0], cell_total, grad_norm, *encoder_new, *decoder_new)


def solution(mesh):
    rows, flat = P(AXES, None), P(AXES)
    return jax.shard_map(
        functools.partial(on_device, Place(mesh.shape["wide"], mesh.shape["narrow"])),
        mesh=mesh,
        in_specs=(rows, rows, flat, rows, rows, P(AXES, None, None)) + (flat,) * 8,
        out_specs=(P(), P(), P()) + (flat,) * 8,
        check_vma=False,
    )
```

```python
import functools

import jax
import jax.numpy as jnp
from jax import lax
from jax.experimental import pallas as pl
from jax.experimental.pallas import tpu as pltpu
from jax.sharding import PartitionSpec as P

D = 512
HEADS = 8
HEAD = D // HEADS
PAIRS = HEADS // 2
FF = 1024
V = 32
IMG = 784
TAGS = 512
STEP = 5
CELLS = 128
IMG_CHUNK = 784
TAG_CHUNK = 512
SAFE_SCORE = 50.0

BETA_ONE = 0.5
BETA_TWO = 0.5
CLIP_NORM = 0.01
LEARN_RATE = 0.05
WEIGHT_DECAY = 0.01
EPSILON = 1e-08
SMOOTH = 0.9

VMEM_LIMIT = 62 * 2**20
bf16 = jnp.bfloat16
f32 = jnp.float32


def encoder_layout():
    return [
        ("qkv", (D, 3 * D)),
        ("out", (D, D)),
        ("ffn_in", (D, FF)),
        ("ffn_out", (FF, D)),
        ("norms", (4, D)),
    ]


def decoder_layout():
    return [
        ("qkv", (D, 3 * D)),
        ("out", (D, D)),
        ("cross_q", (D, D)),
        ("cross_kv", (D, 2 * D)),
        ("cross_out", (D, D)),
        ("ffn_in", (D, FF)),
        ("ffn_out", (FF, D)),
        ("embed", (V, D)),
        ("head", (D, V)),
        ("box_in", (D, D)),
        ("norms", (8, D)),
        ("box_out", (D, 4)),
    ]


def dot(left, right, over_left=1, over_right=0):
    return lax.dot_general(
        left, right, (((over_left,), (over_right,)), ((), ())), preferred_element_type=f32
    )


def each_rows(total, step, body):
    @pl.loop(0, total // step)
    def _(index):
        body(pl.ds(pl.multiple_of(index * step, step), step))


def norm_rows(value, gain, shift):
    centred = value - jnp.mean(value, -1, keepdims=True)
    variance = jnp.mean(centred * centred, -1, keepdims=True)
    return centred * lax.rsqrt(variance + 1e-05) * gain + shift


def norm_rows_back(value, gain, upstream):
    centred = value - jnp.mean(value, -1, keepdims=True)
    variance = jnp.mean(centred * centred, -1, keepdims=True)
    scale = lax.rsqrt(variance + 1e-05)
    unit = centred * scale
    inner = upstream * gain
    mean_inner = jnp.mean(inner, -1, keepdims=True)
    mean_both = jnp.mean(inner * unit, -1, keepdims=True)
    down = scale * (inner - mean_inner - unit * mean_both)
    return (
        down,
        jnp.sum(upstream * unit, 0, keepdims=True),
        jnp.sum(upstream, 0, keepdims=True),
    )


GELU_A = 0.7978845608028654
GELU_B = 0.044715


def gelu(value):
    inner = jnp.tanh(GELU_A * (value + GELU_B * value * value * value))
    return 0.5 * value * (1.0 + inner)


def gelu_slope(value):
    square = value * value
    inner = jnp.tanh(GELU_A * (value + GELU_B * square * value))
    slope = GELU_A * (1.0 + 3.0 * GELU_B * square)
    return 0.5 * (1.0 + inner) + 0.5 * value * (1.0 - inner * inner) * slope


def half_masks():
    lane = lax.broadcasted_iota(jnp.int32, (1, 2 * HEAD), 1)
    first = (lane < HEAD).astype(f32)
    return (first.astype(bf16), (1.0 - first).astype(bf16))


def query_blocks(query_rows, key_rows, causal):
    if not causal:
        return [(0, query_rows, key_rows)]
    return [(start, 256, start + 256) for start in range(0, query_rows, 256)]


def key_tiles(start, depth, causal):
    if not causal or start == 0:
        return [(0, depth)]
    return [(0, start), (start, depth)]


def causal_keep(depth, width):
    key = lax.broadcasted_iota(jnp.int32, (depth, width), 0)
    query = lax.broadcasted_iota(jnp.int32, (depth, width), 1)
    return key <= query


def head_members():
    row = lax.broadcasted_iota(jnp.int32, (16, D), 0)
    lane = lax.broadcasted_iota(jnp.int32, (16, D), 1)
    return (lax.shift_right_logical(lane, 6) == row).astype(f32).astype(bf16)


def largest_norm(ref, column, rows, start):
    value = ref[start : start + rows, column : column + D]
    return jnp.max(dot(head_members(), value * value, 1, 1), 1, keepdims=True)


def attend(tables, q_ref, k_ref, k_col, v_ref, v_col, o_ref, lse_ref, query_rows, key_rows, causal):
    bound = jnp.zeros((16, 1), f32)
    for table in range(tables):
        of_queries = largest_norm(q_ref, 0, query_rows, table * query_rows)
        of_keys = largest_norm(k_ref, k_col, key_rows, table * key_rows)
        bound = jnp.maximum(bound, of_queries * of_keys)
    small = jnp.max(bound) < (0.98 * SAFE_SCORE) ** 2
    for wanted in (True, False):

        @pl.when(small == wanted)
        def _():
            attend_with(
                tables, q_ref, k_ref, k_col, v_ref, v_col, o_ref, lse_ref,
                query_rows, key_rows, causal, not wanted,
            )


def attend_with(
    tables, q_ref, k_ref, k_col, v_ref, v_col, o_ref, lse_ref, query_rows, key_rows, causal, take_peak, between=None,
):
    masks = half_masks()
    blocks = query_blocks(query_rows, key_rows, causal)

    @pl.loop(0, tables * PAIRS)
    def _(step):
        table = lax.div(step, PAIRS)
        pair = lax.rem(step, PAIRS)
        q_rows = pl.ds(pl.multiple_of(table * query_rows, 16), query_rows)
        k_rows = pl.ds(pl.multiple_of(table * key_rows, 16), key_rows)
        lanes = pl.multiple_of(pair * 128, 128)
        queries = q_ref[q_rows, pl.ds(lanes, 128)]
        keys = k_ref[k_rows, pl.ds(k_col + lanes, 128)]
        values = v_ref[k_rows, pl.ds(v_col + lanes, 128)].T
        scores = {}
        for half in range(2):
            own = queries * masks[half]
            for start, width, depth in blocks:
                for low, high in key_tiles(start, depth, causal):
                    tile = dot(keys[low:high], own[start : start + width], 1, 1)
                    if causal and low == start:
                        tile = jnp.where(causal_keep(high - low, width), tile, -1e30)
                    scores[half, start, low] = tile
        outs = []
        for half in range(2):
            own_values = values[half * HEAD : (half + 1) * HEAD, :]
            parts, sums = [], []
            for start, width, depth in blocks:
                tiles = key_tiles(start, depth, causal)
                weights = [scores[half, start, low] for low, _ in tiles]
                peak = jnp.zeros((1, width), f32)
                if take_peak:
                    peak = functools.reduce(
                        jnp.maximum, [jnp.max(tile, 0, keepdims=True) for tile in weights]
                    )
                    weights = [tile - peak for tile in weights]
                weights = [jnp.exp(tile) for tile in weights]
                total = sum(jnp.sum(tile, 0, keepdims=True) for tile in weights)
                mixed = sum(
                    dot(own_values[:, low:high], tile.astype(bf16))
                    for tile, (low, high) in zip(weights, tiles)
                )
                parts.append(mixed * (1.0 / total))
                sums.append(peak + jnp.log(total))
            outs.append(parts[0] if len(parts) == 1 else jnp.concatenate(parts, 1))
            lse_ref[pl.ds(table * HEADS + pair * 2 + half, 1), :] = (
                sums[0] if len(sums) == 1 else jnp.concatenate(sums, 1)
            )
        joined = jnp.concatenate(outs, 0).astype(bf16)
        o_ref[q_rows, pl.ds(lanes, 128)] = joined.T
        if between is not None:
            between(step)


def head_sums(tables, up_ref, o_ref, delta_ref, query_rows):
    member = head_members()
    for table in range(tables):
        rows = slice(table * query_rows, (table + 1) * query_rows)
        both = up_ref[rows, :].astype(f32) * o_ref[rows, :].astype(f32)
        high = both.astype(bf16)
        rest = (both - high.astype(f32)).astype(bf16)
        sums = dot(member, high, 1, 1) + dot(member, rest, 1, 1)
        delta_ref[table * HEADS : (table + 1) * HEADS, :] = sums[:HEADS]


def attend_back(
    span_of_tables, q_ref, k_ref, k_col, v_ref, v_col, up_ref, lse_ref, delta_ref,
    dq_ref, dk_ref, dv_ref, query_rows, key_rows, causal, between=None,
):
    masks = half_masks()

    @pl.loop(span_of_tables[0] * PAIRS, span_of_tables[1] * PAIRS)
    def _(step):
        table = lax.div(step, PAIRS)
        pair = lax.rem(step, PAIRS)
        q_rows = pl.ds(pl.multiple_of(table * query_rows, 16), query_rows)
        k_rows = pl.ds(pl.multiple_of(table * key_rows, 16), key_rows)
        lanes = pl.multiple_of(pair * 128, 128)
        queries = q_ref[q_rows, pl.ds(lanes, 128)]
        keys = k_ref[k_rows, pl.ds(k_col + lanes, 128)]
        values = v_ref[k_rows, pl.ds(v_col + lanes, 128)]
        upstream = up_ref[q_rows, pl.ds(lanes, 128)]
        keys_across = keys.T
        blocks = query_blocks(query_rows, key_rows, causal)
        grad_q = []
        grad_k = [None] * len(blocks)
        grad_v = [None] * len(blocks)
        ahead = {}
        if causal:
            for half in range(2):
                own, own_up = queries * masks[half], upstream * masks[half]
                for number, (start, width, depth) in enumerate(blocks):
                    span = slice(start, start + width)
                    ahead[half, number] = (
                        dot(keys[:depth], own[span], 1, 1),
                        dot(values[:depth], own_up[span], 1, 1),
                    )
        for half in range(2):
            index = pl.ds(table * HEADS + pair * 2 + half, 1)
            own = queries * masks[half]
            own_up = upstream * masks[half]
            logsum = lse_ref[index, :]
            delta = delta_ref[index, :]
            across = keys_across[half * HEAD : (half + 1) * HEAD, :]
            parts = []
            for number, (start, width, depth) in enumerate(blocks):
                span = slice(start, start + width)
                if causal:
                    scores, pull = ahead[half, number]
                else:
                    scores = dot(keys[:depth], own[span], 1, 1)
                    pull = dot(values[:depth], own_up[span], 1, 1)
                weight = jnp.exp(scores - logsum[:, span])
                if causal:
                    edge = jnp.where(causal_keep(width, width), weight[start:], 0.0)
                    weight = edge if start == 0 else jnp.concatenate([weight[:start], edge], 0)
                change = (weight * (pull - delta[:, span])).astype(bf16)
                add_v = dot(weight.astype(bf16), own_up[span])
                add_k = dot(change, own[span])
                grad_v[number] = add_v if half == 0 else grad_v[number] + add_v
                grad_k[number] = add_k if half == 0 else grad_k[number] + add_k
                parts.append(dot(across[:, :depth], change) * 0.125)
            grad_q.append(parts[0] if len(parts) == 1 else jnp.concatenate(parts, 1))
        dq_ref[q_rows, pl.ds(lanes, 128)] = jnp.concatenate(grad_q, 0).astype(bf16).T
        for ref, column, grads in ((dk_ref, k_col, grad_k), (dv_ref, v_col, grad_v)):
            total = grads[-1]
            if len(grads) == 2:
                low = blocks[0][2]
                total = jnp.concatenate([total[:low] + grads[0], total[low:]], 0)
            ref[k_rows, pl.ds(column + lanes, 128)] = total.astype(bf16)
        if between is not None:
            between(step)


def project(a_ref, w_ref, out_ref, width, first_scale=None):
    for start in range(0, width, 512):
        value = dot(a_ref[...], w_ref[:, start : start + 512])
        if first_scale is not None and start == 0:
            value = value * first_scale
        out_ref[:, start : start + 512] = value.astype(bf16)


def add_project(base_ref, a_ref, w_ref, out_ref):
    for start in range(0, D, 256):
        lanes = slice(start, start + 256)
        out_ref[:, lanes] = base_ref[:, lanes].astype(f32) + dot(a_ref[...], w_ref[:, lanes])


def weight_grad(a_ref, b_ref, out_ref):
    rows, columns = out_ref.shape
    for start in range(0, columns, 512):
        lanes = slice(start, start + 512)
        out_ref[:, lanes] = dot(a_ref[...], b_ref[:, lanes], 0, 0).astype(out_ref.dtype)


def ffn_forward(h_ref, w_in, u_ref, g_ref):
    for start in range(0, FF, 256):
        lanes = slice(start, start + 256)
        inner = dot(h_ref[...], w_in[:, lanes])
        if u_ref is not None:
            u_ref[:, lanes] = inner
        g_ref[:, lanes] = gelu(inner).astype(bf16)


def ffn_backward(og_ref, h_ref, u_ref, g_ref, w_in, w_out, d_in, d_out, dh_ref):
    weight_grad(g_ref, og_ref, d_out)
    for start in range(0, FF, 256):
        lanes = slice(start, start + 256)
        back = dot(og_ref[...], w_out[lanes, :], 1, 1)
        g_ref[:, lanes] = (gelu_slope(u_ref[:, lanes]) * back).astype(bf16)
    weight_grad(h_ref, g_ref, d_in)
    project_back(g_ref, w_in, dh_ref)


def project_back(g_ref, w_ref, out_ref):
    for start in range(0, D, 256):
        lanes = slice(start, start + 256)
        out_ref[:, lanes] = dot(g_ref[...], w_ref[lanes, :], 1, 1).astype(out_ref.dtype)


def norm_all(x_ref, norms_ref, row, out_ref, total, step):
    gain, shift = norms_ref[row : row + 1, :], norms_ref[row + 1 : row + 2, :]

    def body(rows):
        out_ref[rows, :] = norm_rows(x_ref[rows, :].astype(f32), gain, shift).astype(bf16)

    each_rows(total, step, body)


def norm_all_back(x_ref, norms_ref, row, upstream, dnorms_ref, total, step, keep):
    gain = norms_ref[row : row + 1, :]
    dnorms_ref[row : row + 2, :] = jnp.zeros((2, D), f32)

    def body(rows):
        arriving = upstream(rows) if callable(upstream) else upstream[rows, :]
        down, d_gain, d_shift = norm_rows_back(x_ref[rows, :].astype(f32), gain, arriving)
        dnorms_ref[row : row + 1, :] += d_gain
        dnorms_ref[row + 1 : row + 2, :] += d_shift
        if keep is not None:
            keep(rows, down)

    each_rows(total, step, body)


def soft_low(first_one, other_one):
    return 0.5 * (first_one + other_one - jnp.sqrt((first_one - other_one) ** 2 + 0.0001))


def soft_high(first_one, other_one):
    return 0.5 * (first_one + other_one + jnp.sqrt((first_one - other_one) ** 2 + 0.0001))


def softplus(value):
    return jnp.maximum(value, 0.0) + jnp.log1p(jnp.exp(-jnp.abs(value)))


@jax.custom_vjp
def smooth_relu(value):
    return softplus(value)


def smooth_relu_keep(value):
    return softplus(value), value


def smooth_relu_back(value, upstream):
    return (upstream * (1.0 / (1.0 + jnp.exp(-value))),)


smooth_relu.defvjp(smooth_relu_keep, smooth_relu_back)


def cell_losses(px, py, pw, ph, gx, gy, gw, gh):
    absolute = (
        jnp.sqrt((px - gx) ** 2 + 0.01)
        + jnp.sqrt((py - gy) ** 2 + 0.01)
        + jnp.sqrt((pw - gw) ** 2 + 0.01)
        + jnp.sqrt((ph - gh) ** 2 + 0.01)
    )
    left_p, right_p = px - 0.5 * pw, px + 0.5 * pw
    low_p, top_p = py - 0.5 * ph, py + 0.5 * ph
    left_g, right_g = gx - 0.5 * gw, gx + 0.5 * gw
    low_g, top_g = gy - 0.5 * gh, gy + 0.5 * gh
    across = smooth_relu(20.0 * (soft_low(right_p, right_g) - soft_high(left_p, left_g))) / 20.0
    upward = smooth_relu(20.0 * (soft_low(top_p, top_g) - soft_high(low_p, low_g))) / 20.0
    common = across * upward
    union = pw * ph + gw * gh - common
    hull = (soft_high(right_p, right_g) - soft_low(left_p, left_g)) * (
        soft_high(top_p, top_g) - soft_low(low_p, low_g)
    )
    ratio = common / union - (hull - union) / hull
    return 5.0 * absolute + 2.0 * (1.0 - ratio)


def split_sum(left, value):
    high = value.astype(bf16)
    rest = (value - high.astype(f32)).astype(bf16)
    return dot(left, high) + dot(left, rest)


def decoder_kernel(
    tags_ref, next_ref, counted_ref, place_ref, alive_ref, target_ref, scale_ref, mem_ref,
    w_qkv, w_out, w_cq, w_ckv, w_co, w_in, w_ffo, w_embed, w_head, w_box, norms, w_box_out,
    loss_ref, dmem_ref, d_qkv, d_out, d_cq, d_ckv, d_co, d_in, d_ffo, d_embed, d_head, d_box, d_norms, d_box_out,
    e_ref, h1_ref, qkv_ref, o1_ref, lse1_ref, y1_ref, h2_ref, cq_ref, ckv_ref, o2_ref, lse2_ref, y2_ref,
    h3_ref, u_ref, g_ref, y3_ref, z_ref, dy_ref, dh_ref, og_ref, up_ref, delta_ref,
):
    tables = tags_ref.shape[0]
    rows = tables * TAGS

    def tag_members(table):
        member = lax.broadcasted_iota(jnp.int32, (V, TAGS), 0) == tags_ref[table]
        return member.astype(f32).astype(bf16)

    for table in range(tables):
        e_ref[table * TAGS : (table + 1) * TAGS, :] = dot(tag_members(table), w_embed[...], 0, 0)
    norm_all(e_ref, norms, 0, h1_ref, rows, TAG_CHUNK)
    project(h1_ref, w_qkv, qkv_ref, 3 * D, 0.125)
    attend(tables, qkv_ref, qkv_ref, D, qkv_ref, 2 * D, o1_ref, lse1_ref, TAGS, TAGS, True)
    add_project(e_ref, o1_ref, w_out, y1_ref)
    norm_all(y1_ref, norms, 2, h2_ref, rows, TAG_CHUNK)
    project(h2_ref, w_cq, cq_ref, D, 0.125)
    project(mem_ref, w_ckv, ckv_ref, 2 * D)
    attend(tables, cq_ref, ckv_ref, 0, ckv_ref, D, o2_ref, lse2_ref, TAGS, IMG, False)
    add_project(y1_ref, o2_ref, w_co, y2_ref)
    norm_all(y2_ref, norms, 4, h3_ref, rows, TAG_CHUNK)
    ffn_forward(h3_ref, w_in, u_ref, g_ref)
    add_project(y2_ref, g_ref, w_ffo, y3_ref)
    norm_all(y3_ref, norms, 6, z_ref, rows, TAG_CHUNK)

    scale = scale_ref[0, 0]
    loss = jnp.zeros((1, 1), f32)
    picked, inners, box_ups = [], [], []
    head_sum = jnp.zeros((V, D), f32)
    box_in_sum = jnp.zeros((D, D), f32)
    box_out_sum = jnp.zeros((16, D), f32)
    for table in range(tables):
        own = slice(table * TAGS, (table + 1) * TAGS)
        final = z_ref[own, :]
        logits = dot(w_head[...], final, 1, 1)
        peak = jnp.max(logits, 0, keepdims=True)
        weight = jnp.exp(logits - peak)
        total = jnp.sum(weight, 0, keepdims=True)
        counted = counted_ref[table]
        wanted = lax.broadcasted_iota(jnp.int32, (V, TAGS), 0) == next_ref[table]
        chosen = jnp.sum(jnp.where(wanted, logits - peak - jnp.log(total), 0.0), 0, keepdims=True)
        loss = loss - jnp.sum(counted * chosen, 1, keepdims=True)
        dlogits = (weight / total - wanted.astype(f32)) * counted * scale
        tag_up = dlogits.astype(bf16)
        head_sum = head_sum + dot(tag_up, final)
        dfinal = dot(tag_up, w_head[...], 0, 0)
        select = (
            (lax.broadcasted_iota(jnp.int32, (TAGS, CELLS), 0) == place_ref[table])
            .astype(f32)
            .astype(bf16)
        )
        cells = dot(select, final, 0, 0).astype(bf16)
        inner = dot(cells, w_box[...])
        active = gelu(inner).astype(bf16)
        raw = dot(w_box_out[...], active, 1, 1)
        soft = 1.0 / (1.0 + jnp.exp(-raw))
        ratios = tuple(soft[k : k + 1, :] for k in range(4))
        wished = tuple(target_ref[table, k : k + 1, :] for k in range(4))
        alive = alive_ref[table]
        cell, pull = jax.vjp(lambda *parts: cell_losses(*parts, *wished), *ratios)
        loss = loss + jnp.sum(alive * cell, 1, keepdims=True)
        downs = pull(alive * scale)
        fill = jnp.zeros((16, CELLS), f32)
        index = lax.broadcasted_iota(jnp.int32, (16, CELLS), 0)
        for k in range(4):
            value = downs[k] * ratios[k] * (1.0 - ratios[k])
            fill = jnp.where(index == k, value, fill)
        box_up = fill.astype(bf16)
        box_out_sum = box_out_sum + dot(box_up, active)
        dinner = (gelu_slope(inner) * dot(box_up, w_box_out[...], 0, 0)).astype(bf16)
        box_in_sum = box_in_sum + dot(cells, dinner, 0, 0)
        dh_ref[own, :] = dfinal + split_sum(select, dot(dinner, w_box[...], 1, 1))
    loss_ref[...] = jnp.broadcast_to(loss, loss_ref.shape)
    d_head[...] = head_sum.astype(bf16)
    d_box[...] = box_in_sum.astype(bf16)
    d_box_out[...] = box_out_sum.astype(bf16)

    def start_sum(block, down):
        dy_ref[block, :] = down
        og_ref[block, :] = down.astype(bf16)

    def add_sum(block, down):
        total = down + dy_ref[block, :]
        dy_ref[block, :] = total
        og_ref[block, :] = total.astype(bf16)

    norm_all_back(y3_ref, norms, 6, dh_ref, d_norms, rows, TAG_CHUNK, start_sum)
    ffn_backward(og_ref, h3_ref, u_ref, g_ref, w_in, w_ffo, d_in, d_ffo, dh_ref)
    norm_all_back(y2_ref, norms, 4, dh_ref, d_norms, rows, TAG_CHUNK, add_sum)

    weight_grad(o2_ref, og_ref, d_co)
    project_back(og_ref, w_co, up_ref)
    head_sums(tables, up_ref, o2_ref, delta_ref, TAGS)
    attend_back(
        (0, tables), cq_ref, ckv_ref, 0, ckv_ref, D, up_ref, lse2_ref, delta_ref,
        cq_ref, ckv_ref, ckv_ref, TAGS, IMG, False,
    )
    weight_grad(h2_ref, cq_ref, d_cq)
    weight_grad(mem_ref, ckv_ref, d_ckv)
    project_back(ckv_ref, w_ckv, dmem_ref)
    project_back(cq_ref, w_cq, dh_ref)
    norm_all_back(y1_ref, norms, 2, dh_ref, d_norms, rows, TAG_CHUNK, add_sum)

    weight_grad(o1_ref, og_ref, d_out)
    project_back(og_ref, w_out, up_ref)
    head_sums(tables, up_ref, o1_ref, delta_ref, TAGS)
    attend_back(
        (0, tables), qkv_ref, qkv_ref, D, qkv_ref, 2 * D, up_ref, lse1_ref, delta_ref,
        qkv_ref, qkv_ref, qkv_ref, TAGS, TAGS, True,
    )
    weight_grad(h1_ref, qkv_ref, d_qkv)
    project_back(qkv_ref, w_qkv, dh_ref)
    norm_all_back(e_ref, norms, 0, dh_ref, d_norms, rows, TAG_CHUNK, add_sum)
    embed_sum = jnp.zeros((V, D), f32)
    for table in range(tables):
        embed_sum = embed_sum + split_sum(
            tag_members(table), dy_ref[table * TAGS : (table + 1) * TAGS, :]
        )
    d_embed[...] = embed_sum.astype(bf16)


DECODER_NAMES = (
    "qkv", "out", "cross_q", "cross_kv", "cross_out", "ffn_in", "ffn_out", "embed", "head", "box_in", "norms", "box_out",
)


def decoder_step(prepared, scale, memory, weights):
    tables = prepared[0].shape[0]
    rows = tables * TAGS
    image_rows = memory.shape[0]
    grads = {
        name: jax.ShapeDtypeStruct(weights[name].shape, f32 if name == "norms" else bf16)
        for name in DECODER_NAMES
    }
    vmem = pl.BlockSpec(memory_space=pltpu.VMEM)
    low = lambda width, height=rows: pltpu.VMEM((height, width), bf16)
    full = lambda width, height=rows: pltpu.VMEM((height, width), f32)
    stats = pltpu.VMEM((tables * HEADS, TAGS), f32)
    outs = pl.pallas_call(
        decoder_kernel,
        out_shape=(
            jax.ShapeDtypeStruct((8, 128), f32),
            jax.ShapeDtypeStruct((image_rows, D), f32),
            *[grads[name] for name in DECODER_NAMES],
        ),
        in_specs=[vmem] * 6 + [pl.BlockSpec(memory_space=pltpu.SMEM)] + [vmem] * 13,
        scratch_shapes=[
            full(D), low(D), low(3 * D), low(D), stats, full(D), low(D), low(D), low(2 * D, image_rows), low(D), stats,
            full(D), low(D), full(FF), low(FF), full(D), low(D), full(D), full(D), low(D), low(D), stats,
        ],
        compiler_params=pltpu.CompilerParams(vmem_limit_bytes=VMEM_LIMIT),
        name="decoder_step",
    )(*prepared, scale, memory, *[weights[name] for name in DECODER_NAMES])
    return outs[0], outs[1], dict(zip(DECODER_NAMES, outs[2:]))


AXES = ("wide", "narrow")
MESH = pl.DeviceIdType.MESH
ORDERS = (("a", "y", "b"), ("a", "b", "y"))


class Place:
    def __init__(self, wide, narrow):
        inner = 2 if wide % 2 == 0 else 1
        self.sizes = {"a": wide // inner, "b": inner, "y": narrow // 2, "c": 2}
        self.narrow = narrow
        self.count = wide * narrow

    def locate(self):
        wide, narrow = lax.axis_index("wide"), lax.axis_index("narrow")
        inner = self.sizes["b"]
        self.here = {
            "a": lax.div(wide, inner),
            "b": lax.rem(wide, inner),
            "y": lax.div(narrow, 2),
            "c": lax.rem(narrow, 2),
        }
        return self

    def moved(self, steps):
        there = dict(self.here)
        for part, step in steps.items():
            there[part] = lax.rem(there[part] + step, self.sizes[part])
        return there

    def device(self, there):
        return (there["a"] * self.sizes["b"] + there["b"], there["y"] * 2 + there["c"])

    def index(self, there):
        wide, narrow = self.device(there)
        return wide * self.narrow + narrow

    def peers(self):
        return [(part, step) for part, size in self.sizes.items() for step in range(1, size)]

    def in_plane(self, step):
        size, wide = self.sizes["b"], self.sizes["y"]
        here = (self.here["b"] * wide + self.here["y"]) * 2 + self.here["c"]
        there = lax.rem(here + step, size * wide * 2)
        return there, {
            **self.here,
            "b": lax.div(there, wide * 2),
            "y": lax.rem(lax.div(there, 2), wide),
            "c": lax.rem(there, 2),
        }

    def plane(self):
        return self.sizes["b"] * self.sizes["y"] * 2

    def greet(self, whole_plane=False):
        barrier = pltpu.get_barrier_semaphore()
        peers = [self.moved({part: step}) for part, step in self.peers()]
        if whole_plane:
            peers = [self.in_plane(step)[1] for step in range(1, self.plane())] + [
                self.moved({"a": step}) for step in range(1, self.sizes["a"])
            ]
        for there in peers:
            pl.semaphore_signal(
                barrier, inc=1, device_id=self.device(there), device_id_type=MESH
            )
        pl.semaphore_wait(barrier, len(peers))


def block_rows(amount):
    return -(-(amount // 128 + 3) // 16) * 16


def flat_rows(amount, count):
    return -(-((count - 1) * amount // 128 + block_rows(amount)) // 8) * 8


def layout_bases(layout):
    offset = 0
    for name, (height, breadth) in layout:
        yield name, height, breadth, offset // 128
        offset += height * breadth


def place_blocks(all_ref, flat_ref, amount):
    count, rows, _ = all_ref.shape
    used = amount // 128 + 2
    flat_ref[0:8, :] = jnp.zeros((8, 128), f32)

    @pl.loop(0, count)
    def _(device):
        start = lax.div(device * amount, 128)
        before = flat_ref[pl.ds(start, 1), :]
        flat_ref[pl.ds(start, used), :] = all_ref[device, :used, :].astype(f32)
        flat_ref[pl.ds(start, 1), :] = before + all_ref[device, 0:16, :].astype(f32)[0:1]


def one_hot(shape, match):
    first = lax.broadcasted_iota(jnp.int32, shape, 0)
    second = lax.broadcasted_iota(jnp.int32, shape, 1)
    return match(first, second).astype(f32).astype(bf16)


def take_matrices(flat_ref, layout, out_refs):
    for name, height, breadth, base in layout_bases(layout):
        out_ref = out_refs[name]
        if name == "head":
            turned = flat_ref[base : base + 128, :].T.astype(bf16)
            total = jnp.zeros((V, D), f32)
            for part in range(4):
                spread = one_hot((128, D), lambda row, column: column == 4 * row + part)
                total = total + dot(turned[part * V : (part + 1) * V, :], spread)
            out_ref[...] = total.astype(bf16)
        elif name == "box_out":
            block = flat_ref[base : base + 16, :].astype(bf16)
            own = one_hot((16, D), lambda row, column: lax.div(column, 32) == row).astype(f32)
            index = lax.broadcasted_iota(jnp.int32, (16, D), 0)
            total = jnp.zeros((16, D), f32)
            for k in range(4):
                pick = one_hot((128, D), lambda lane, column: lane == 4 * lax.rem(column, 32) + k)
                line = jnp.sum(dot(block, pick) * own, 0, keepdims=True)
                total = jnp.where(index == k, line, total)
            out_ref[...] = total.astype(bf16)
        else:
            wide = breadth // 128
            for column in range(wide):
                out_ref[:, column * 128 : (column + 1) * 128] = flat_ref[
                    pl.ds(base + column, height, stride=wide), :
                ].astype(out_ref.dtype)


def put_matrices(flat_ref, layout, refs):
    for name, height, breadth, base in layout_bases(layout):
        ref = refs[name]
        if name == "head":
            total = jnp.zeros((128, 128), f32)
            for part in range(4):
                pick = one_hot((128, D), lambda row, column: column == 4 * row + part)
                shift = one_hot((V, 128), lambda row, lane: lane == V * part + row)
                total = total + dot(dot(pick, ref[...], 1, 1).astype(bf16), shift)
            flat_ref[base : base + 128, :] = total
        elif name == "box_out":
            own = one_hot((16, D), lambda row, column: lax.div(column, 32) == row).astype(f32)
            total = jnp.zeros((16, 128), f32)
            for k in range(4):
                line = ref[...].astype(f32)[k : k + 1, :]
                spread = one_hot((D, 128), lambda column, lane: lane == 4 * lax.rem(column, 32) + k)
                total = total + dot((own * line).astype(bf16), spread)
            flat_ref[base : base + 16, :] = total
        else:
            wide = breadth // 128
            for column in range(wide):
                flat_ref[pl.ds(base + column, height, stride=wide), :] = ref[
                    :, column * 128 : (column + 1) * 128
                ].astype(f32)


def cut_blocks(flat_ref, amount, block_ref):
    count, rows, _ = block_ref.shape

    @pl.loop(0, count)
    def _(device):
        start = lax.div(device * amount, 128)
        block_ref[device, :, :] = flat_ref[pl.ds(start, rows), :].astype(bf16)


def weight_shapes(layout):
    shapes = {name: extent for name, extent in layout}
    if "head" in shapes:
        shapes["head"], shapes["box_out"] = (V, D), (16, D)
    return {
        name: jax.ShapeDtypeStruct(extent, f32 if name == "norms" else bf16)
        for name, extent in shapes.items()
    }


def pack_grads(grads, layout, amount, count, name):
    names = [piece for piece, _ in layout]

    def kernel(*refs):
        block_ref, flat_ref = refs[-2:]
        tail = sum(extent[0] * extent[1] for _, extent in layout) // 128
        flat_ref[tail:, :] = jnp.zeros((flat_ref.shape[0] - tail, 128), f32)
        put_matrices(flat_ref, layout, dict(zip(names, refs)))
        cut_blocks(flat_ref, amount, block_ref)

    return pl.pallas_call(
        kernel,
        out_shape=jax.ShapeDtypeStruct((count, block_rows(amount), 128), bf16),
        scratch_shapes=[pltpu.VMEM((flat_rows(amount, count), 128), f32)],
        compiler_params=pltpu.CompilerParams(vmem_limit_bytes=VMEM_LIMIT),
        name=name,
    )(*[grads[piece] for piece in names])


class Reduction:
    def __init__(self, place, core, pick, own_ref, mine_ref, got_ref, load_sem, send_sem, recv_sem):
        self.place, self.pick = place, pick
        self.own, self.mine, self.got = own_ref, mine_ref, got_ref
        self.load_sem, self.send_sem, self.recv_sem = load_sem, send_sem, recv_sem
        self.order, self.other = ORDERS[core], ORDERS[1 - core]
        self.s1, self.s2, self.s3 = (place.sizes[part] for part in self.order)
        self.half = place.count // 2
        self.base3 = self.half
        self.base2 = self.base3 + (self.s3 - 1) * self.s1 * self.s2
        self.base1 = self.base2 + (self.s2 - 1) * self.s1

    def slot(self, steps):
        sizes = self.place.sizes
        return (steps["a"] * sizes["b"] + steps["b"]) * sizes["y"] + steps["y"]

    def owner(self, steps):
        return self.place.index(self.place.moved(steps))

    def only(self, steps, body):
        if self.pick is None:
            body()
        else:
            pl.when(self.pick(self.owner(steps)))(body)

    def copy(self, source, slot, part, step):
        return pltpu.make_async_remote_copy(
            src_ref=source,
            dst_ref=self.got.at[slot],
            send_sem=self.send_sem.at[slot],
            recv_sem=self.recv_sem.at[slot],
            device_id=self.place.device(self.place.moved({part: step})),
            device_id_type=MESH,
        )

    def load(self, steps):
        slot = self.slot(steps)
        return pltpu.make_async_copy(
            self.own.at[self.owner(steps)], self.mine.at[slot], self.load_sem.at[slot]
        )

    def took(self, slot):
        self.copy(self.mine.at[0], slot, "c", 1).wait_recv()

    def value(self, slot):
        return self.got[slot].astype(f32)

    def levels(self, order):
        s1, s2, s3 = (self.place.sizes[part] for part in order)
        return (
            (s1 * s2 * (s3 - 1), lambda n: (s1 - 1 - lax.rem(n, s1), s2 - 1 - lax.rem(lax.div(n, s1), s2), lax.div(n, s1 * s2) + 1)),
            (s1 * (s2 - 1), lambda n: (s1 - 1 - lax.rem(n, s1), lax.div(n, s1) + 1, 0)),
            (s1, lambda n: (s1 - 1 - n, 0, 0)),
        )

    def to_sibling(self):
        if self.load_sem is not None:
            for amount, where in self.levels(self.order):

                @pl.loop(0, amount)
                def _(number):
                    self.load(dict(zip(self.order, where(number)))).start()

        for amount, where in self.levels(self.other):

            @pl.loop(0, amount)
            def _(number):
                steps = dict(zip(self.other, where(number)))
                slot = self.slot(steps)

                def send():
                    block = slot if self.load_sem is None else self.owner({**steps, "c": 1})
                    self.copy(self.own.at[block], slot, "c", 1).start()

                self.only({**steps, "c": 1}, send)

    def partial(self, p, q, r):
        steps = dict(zip(self.order, (p, q, r)))
        slot = self.slot(steps)
        if self.load_sem is not None:
            self.load(steps).wait()
        self.took(slot)
        return slot, self.mine[slot].astype(f32) + self.value(slot)

    def add_third(self, total, p, q):
        for step in range(1, self.s3):
            slot = self.base3 + ((step - 1) * self.s1 + p) * self.s2 + q
            self.took(slot)
            total = total + self.value(slot)
        return total

    def add_second(self, total, p):
        for step in range(1, self.s2):
            slot = self.base2 + (step - 1) * self.s1 + p
            self.took(slot)
            total = total + self.value(slot)
        return total

    def send(self, own_slot, total, slot, part, step):
        self.mine[own_slot] = total.astype(bf16)
        self.copy(self.mine.at[own_slot], slot, part, step).start()

    def third(self):
        amount, where = self.levels(self.order)[0]

        @pl.loop(0, amount)
        def _(number):
            p, q, r = where(number)

            def body():
                own_slot, total = self.partial(p, q, r)
                slot = self.base3 + ((r - 1) * self.s1 + p) * self.s2 + q
                self.send(own_slot, total, slot, self.order[2], r)

            self.only(dict(zip(self.order, (p, q, r))), body)

    def second(self):
        amount, where = self.levels(self.order)[1]

        @pl.loop(0, amount)
        def _(number):
            p, q, _ = where(number)

            def body():
                own_slot, total = self.partial(p, q, 0)
                total = self.add_third(total, p, q)
                self.send(own_slot, total, self.base2 + (q - 1) * self.s1 + p, self.order[1], q)

            self.only(dict(zip(self.order, (p, q, 0))), body)

    def first(self):
        @pl.loop(1, self.s1)
        def _(p):
            def body():
                own_slot, total = self.partial(p, 0, 0)
                total = self.add_second(self.add_third(total, p, 0), p)
                self.send(own_slot, total, self.base1 + p - 1, self.order[0], p)

            self.only({self.order[0]: p}, body)

    def last(self, out_ref):
        def body():
            _, total = self.partial(0, 0, 0)
            out_ref[...] = self.add_second(self.add_third(total, 0, 0), 0)

            @pl.loop(1, self.s1)
            def _(p):
                slot = self.base1 + p - 1
                self.took(slot)
                out_ref[...] += self.value(slot)

        self.only({}, body)

    def close(self):
        @pl.loop(0, self.place.count - 1)
        def _(slot):
            self.copy(self.mine.at[0], slot, "c", 1).wait_send()


def reduction_memory(count, rows):
    half = count // 2
    return [pltpu.VMEM((half, rows, 128), bf16), pltpu.VMEM((count - 1, rows, 128), bf16)]


def reduction_signals(count, loads):
    return [pltpu.SemaphoreType.DMA((n,)) for n in ([count // 2] if loads else []) + [count - 1] * 2]


def reduce_stage(place, stage, pick, *members):
    for core in range(2):

        @pl.when(place.here["c"] == core)
        def _():
            stage(Reduction(place, core, pick, *members))


def cut_for_reduction(place, pick, flat_ref, amount, mine_ref, other_ref):
    rows = mine_ref.shape[1]
    sizes = place.sizes

    @pl.loop(0, place.count // 2)
    def _(slot):
        steps = {
            "a": lax.div(slot, sizes["b"] * sizes["y"]),
            "b": lax.rem(lax.div(slot, sizes["y"]), sizes["b"]),
            "y": lax.rem(slot, sizes["y"]),
        }
        for core, ref in ((0, mine_ref), (1, other_ref)):
            owner = place.index(place.moved({**steps, "c": core}))

            @pl.when(pick(owner))
            def _():
                ref[slot] = flat_ref[pl.ds(lax.div(owner * amount, 128), rows), :].astype(bf16)


def sum_everywhere(place, value, box_ref, send_sem, recv_sem):
    base = 0
    plane = [place.in_plane(step) for step in range(place.plane())]
    line = [place.moved({"a": step}) for step in range(place.sizes["a"])]
    for members in (plane, [(there["a"], there) for there in line]):

        def copy(step, number, base=base, members=members):
            return pltpu.make_async_remote_copy(
                src_ref=box_ref.at[base + number],
                dst_ref=box_ref.at[base + number],
                send_sem=send_sem.at[base + step],
                recv_sem=recv_sem.at[base + number],
                device_id=place.device(members[step][1]),
                device_id_type=MESH,
            )

        size = len(members)
        mine = members[0][0]
        box_ref[base + mine] = value
        for step in range(1, size):
            copy(step, mine).start()
        for step in range(1, size):
            copy(step, members[step][0]).wait_recv()
        for step in range(1, size):
            copy(step, mine).wait_send()
        value = box_ref[base]
        for other in range(1, size):
            value = value + box_ref[base + other]
        base += size
    return value


def own_squares(place, out_ref, amount):
    rows = out_ref.shape[0]
    offset = lax.rem(place.index(place.here) * amount, 128)
    position = (
        lax.broadcasted_iota(jnp.int32, (rows, 128), 0) * 128
        + lax.broadcasted_iota(jnp.int32, (rows, 128), 1)
        - offset
    )
    value = jnp.where((position >= 0) & (position < amount), out_ref[...], 0.0)
    return jnp.sum(jnp.sum(value * value, 0, keepdims=True), 1, keepdims=True)


def weight_grad_flat(a_ref, b_ref, flat_ref, base, breadth):
    wide = breadth // 128
    for start in range(0, breadth, 512):
        value = dot(a_ref[...], b_ref[:, start : start + 512], 0, 0)
        store_flat(value, flat_ref, base + start // 128, wide)


def store_flat(value, flat_ref, base, wide):
    rows, columns = value.shape
    for part in range(columns // 128):
        flat_ref[pl.ds(base + part, rows, stride=wide), :] = value[:, part * 128 : (part + 1) * 128]


def encoder_backward(place, images, stored, dmem, weights, decoder_blocks, amounts, loss_block):
    rows = images.shape[0]
    tables = rows // IMG
    qkv, mixed, lse, middle = stored
    bases = {name: base for name, _, _, base in layout_bases(encoder_layout())}
    block, small = decoder_blocks.shape[1], block_rows(amounts[0])
    flat_count = flat_rows(amounts[0], place.count)
    first_early = -(-bases["out"] * 128 // amounts[0])
    end_early = max((bases["norms"] - amounts[0] // 128 - 2) * 128 // amounts[0], first_early)
    steps = place.plane() + place.sizes["a"]
    early = lambda owner: (owner >= first_early) & (owner < end_early)
    late = lambda owner: (owner < first_early) | (owner >= end_early)

    def kernel(
        x_hbm, qkv_hbm, o_ref, lse_ref, x1_ref, dmem_ref, w_qkv_hbm, w_out, w_in, w_ffo, norms, own_ref, loss_ref,
        encoder_ref, decoder_ref, stat_ref,
        w_qkv, h_ref, g_ref, og_ref, qkv_ref, delta_ref, d_norms, flat_ref, fetch_sem,
        theirs_ref, mine_ref, got_ref, far_mine_ref, far_got_ref, *signals,
    ):
        far = (None, own_ref, far_mine_ref, far_got_ref, *signals[:3])
        near = (theirs_ref, mine_ref, got_ref, None, *signals[3:5])
        box_ref, box_send, box_recv = signals[5:]
        work = functools.partial(reduce_stage, place)
        place.locate()
        place.greet(True)
        work(lambda one: one.to_sibling(), *far)
        fetches = [
            pltpu.make_async_copy(source, target, fetch_sem.at[k])
            for k, (source, target) in enumerate(
                ((qkv_hbm, qkv_ref), (w_qkv_hbm, w_qkv), (x_hbm, g_ref.at[:, :D]))
            )
        ]
        x_ref = g_ref.at[:, :D]
        fetches[0].start()
        fetches[1].start()
        tail = bases["norms"] + 4 * D // 128
        flat_ref[tail:, :] = jnp.zeros((flat_count - tail, 128), f32)
        norm_all(x1_ref, norms, 2, h_ref, rows, IMG_CHUNK)
        og_ref[...] = dmem_ref[...].astype(bf16)
        for start in range(0, FF, 256):
            lanes = slice(start, start + 256)
            inner = dot(h_ref[...], w_in[:, lanes])
            back = dot(og_ref[...], w_ffo[lanes, :], 1, 1)
            part = dot(gelu(inner).astype(bf16), og_ref[...], 0, 0)
            store_flat(part, flat_ref, bases["ffn_out"] + start * 4, 4)
            g_ref[:, lanes] = (gelu_slope(inner) * back).astype(bf16)
        work(lambda one: one.third(), *far)
        weight_grad_flat(h_ref, g_ref, flat_ref, bases["ffn_in"], FF)

        def keep(part, down):
            og_ref[part, :] = (down + dmem_ref[part, :]).astype(bf16)

        norm_all_back(
            x1_ref, norms, 2, lambda part: dot(g_ref[part, :], w_in[...], 1, 1), d_norms, rows, IMG_CHUNK, keep
        )
        fetches[2].start()
        weight_grad_flat(o_ref, og_ref, flat_ref, bases["out"], D)
        cut_for_reduction(place, early, flat_ref, amounts[0], mine_ref, theirs_ref)
        work(lambda one: one.to_sibling(), early, *near)

        def project_rows(part):
            og_ref[part, :] = dot(og_ref[part, :], w_out[...], 1, 1).astype(bf16)

        each_rows(rows, IMG_CHUNK, project_rows)
        head_sums(tables, og_ref, o_ref, delta_ref, IMG)
        work(lambda one: one.second(), *far)
        fetches[0].wait()

        def between(step):
            @pl.when(step == 1)
            def _():
                work(lambda one: one.third(), early, *near)

            @pl.when(step == 2)
            def _():
                work(lambda one: one.first(), *far)

            @pl.when(step == 4)
            def _():
                work(lambda one: one.second(), early, *near)

            @pl.when(step == 5)
            def _():
                work(lambda one: one.last(decoder_ref), *far)

            @pl.when(step == 6)
            def _():
                work(lambda one: one.first(), early, *near)

        attend_back(
            (0, tables), qkv_ref, qkv_ref, D, qkv_ref, 2 * D, og_ref, lse_ref, delta_ref,
            qkv_ref, qkv_ref, qkv_ref, IMG, IMG, False, between,
        )
        work(lambda one: one.last(encoder_ref), early, *near)
        fetches[1].wait()
        fetches[2].wait()
        norm_all(x_ref, norms, 0, h_ref, rows, IMG_CHUNK)
        weight_grad_flat(h_ref, qkv_ref, flat_ref, bases["qkv"], 3 * D)
        norm_all_back(
            x_ref, norms, 0, lambda part: dot(qkv_ref[part, :], w_qkv[...], 1, 1), d_norms, rows, IMG_CHUNK, None
        )
        store_flat(d_norms[...], flat_ref, bases["norms"], 4)
        cut_for_reduction(place, late, flat_ref, amounts[0], mine_ref, theirs_ref)
        work(lambda one: one.to_sibling(), late, *near)
        work(lambda one: one.third(), late, *near)
        work(lambda one: one.second(), late, *near)
        work(lambda one: one.first(), late, *near)
        work(lambda one: one.last(encoder_ref), late, *near)
        squares = own_squares(place, encoder_ref, amounts[0]) + own_squares(
            place, decoder_ref, amounts[1]
        )
        me = place.index(place.here)
        for ref, amount in ((encoder_ref, amounts[0]), (decoder_ref, amounts[1])):
            ref[...] = shifted_back(ref[...], lax.rem(me * amount, 128))
        index = lax.broadcasted_iota(jnp.int32, (8, 128), 0)
        value = jnp.where(index == 0, squares, jnp.where(index == 1, loss_ref[...], 0.0))
        stat_ref[...] = sum_everywhere(place, value, box_ref, box_send, box_recv)
        work(lambda one: one.close(), *far)
        work(lambda one: one.close(), early, *near)

    vmem, hbm = pl.BlockSpec(memory_space=pltpu.VMEM), pl.BlockSpec(memory_space=pl.ANY)
    count = place.count
    return pl.pallas_call(
        kernel,
        out_shape=(
            jax.ShapeDtypeStruct((small, 128), f32),
            jax.ShapeDtypeStruct((block, 128), f32),
            jax.ShapeDtypeStruct((8, 128), f32),
        ),
        in_specs=[hbm, hbm, vmem, vmem, vmem, vmem, hbm, vmem, vmem, vmem, vmem, hbm, vmem],
        scratch_shapes=[
            pltpu.VMEM((D, 3 * D), bf16),
            pltpu.VMEM((rows, D), bf16),
            pltpu.VMEM((rows, FF), bf16),
            pltpu.VMEM((rows, D), bf16),
            pltpu.VMEM((rows, 3 * D), bf16),
            pltpu.VMEM((tables * HEADS, IMG), f32),
            pltpu.VMEM((4, D), f32),
            pltpu.VMEM((flat_count, 128), f32),
            pltpu.SemaphoreType.DMA((3,)),
            pltpu.VMEM((count // 2, small, 128), bf16),
            *reduction_memory(count, small),
            *reduction_memory(count, block),
            *reduction_signals(count, True),
            *reduction_signals(count, False),
            pltpu.VMEM((steps, 8, 128), f32),
            pltpu.SemaphoreType.DMA((steps,)),
            pltpu.SemaphoreType.DMA((steps,)),
        ],
        compiler_params=pltpu.CompilerParams(
            collective_id=2, has_side_effects=True, vmem_limit_bytes=VMEM_LIMIT
        ),
        name="encoder_backward",
    )(
        images, qkv, mixed, lse, middle, dmem, weights["qkv"], weights["out"], weights["ffn_in"], weights["ffn_out"],
        weights["norms"], decoder_blocks, loss_block,
    )


class Spread:
    def __init__(self, place, core, view, send_sem, recv_sem):
        self.place, self.view, self.send_sem, self.recv_sem = place, view, send_sem, recv_sem
        self.order = ORDERS[core]
        self.s1, self.s2, self.s3 = (place.sizes[part] for part in self.order)
        self.base2 = self.s1 - 1
        self.base3 = self.base2 + self.s1 * (self.s2 - 1)
        self.base4 = self.base3 + self.s1 * self.s2 * (self.s3 - 1)

    def copy(self, p, q, r, core, part, step, number):
        one, two, three = self.order
        block = self.place.index(self.place.moved({one: p, two: q, three: r, "c": core}))
        return pltpu.make_async_remote_copy(
            src_ref=self.view(block),
            dst_ref=self.view(block),
            send_sem=self.send_sem.at[number],
            recv_sem=self.recv_sem.at[block],
            device_id=self.place.device(self.place.moved({part: step})),
            device_id_type=MESH,
        )

    def arrived(self, p, q, r, core=0):
        self.copy(p, q, r, core, "c", 1, 0).wait_recv()

    def to_sibling(self, p, q, r):
        number = self.base4 + (p * self.s2 + q) * self.s3 + r
        self.copy(p, q, r, 0, "c", 1, number).start()

    def to_third(self, p, q):
        for step in range(1, self.s3):
            number = self.base3 + (p * self.s2 + q) * (self.s3 - 1) + step - 1
            self.copy(p, q, 0, 0, self.order[2], step, number).start()

    def to_second(self, p):
        for step in range(1, self.s2):
            number = self.base2 + p * (self.s2 - 1) + step - 1
            self.copy(p, 0, 0, 0, self.order[1], step, number).start()

    def one(self):
        @pl.loop(1, self.s1)
        def _(step):
            self.copy(0, 0, 0, 0, self.order[0], step, step - 1).start()

        self.to_second(0)
        self.to_third(0, 0)
        self.to_sibling(0, 0, 0)

    def two(self):
        @pl.loop(1, self.s1)
        def _(p):
            self.arrived(p, 0, 0)
            self.to_second(p)
            self.to_third(p, 0)
            self.to_sibling(p, 0, 0)

    def three(self):
        @pl.loop(0, self.s1 * (self.s2 - 1))
        def _(number):
            p, q = lax.rem(number, self.s1), lax.div(number, self.s1) + 1
            self.arrived(p, q, 0)
            self.to_third(p, q)
            self.to_sibling(p, q, 0)

    def four(self):
        @pl.loop(0, self.s1 * self.s2 * (self.s3 - 1))
        def _(number):
            p, q = lax.rem(number, self.s1), lax.rem(lax.div(number, self.s1), self.s2)
            r = lax.div(number, self.s1 * self.s2) + 1
            self.arrived(p, q, r)
            self.to_sibling(p, q, r)

    def five(self):
        @pl.loop(0, self.s1 * self.s2 * self.s3)
        def _(number):
            p, q = lax.rem(number, self.s1), lax.rem(lax.div(number, self.s1), self.s2)
            self.arrived(p, q, lax.div(number, self.s1 * self.s2), 1)

    def close(self):
        @pl.loop(0, self.place.count - 1)
        def _(number):
            self.copy(0, 0, 0, 0, "c", 1, number).wait_send()


def shifted(value, offset):
    lane = lax.broadcasted_iota(jnp.int32, value.shape, 1)
    turned = pltpu.roll(value, offset, 1)
    return jnp.where(lane < offset, pltpu.roll(turned, 1, 0), turned)


def shifted_back(value, offset):
    lane = lax.broadcasted_iota(jnp.int32, value.shape, 1)
    turned = pltpu.roll(value, lax.rem(128 - offset, 128), 1)
    return jnp.where(lane < 128 - offset, turned, pltpu.roll(turned, value.shape[0] - 1, 0))


def gather_and_encode(place, images, encoder_block, decoder_block, counts, amounts):
    rows = images.shape[0]
    tables = rows // IMG
    count = place.count
    layouts = (encoder_layout(), decoder_layout())
    shapes = [weight_shapes(layout) for layout in layouts]
    small, large = encoder_block.shape[0], decoder_block.shape[0]
    near, cut = small // 32 * 16, large // 32 * 16
    flat_counts = [flat_rows(amount, count) for amount in amounts]
    first, second = len(shapes[0]), len(shapes[1])
    matrices = [name for name in shapes[0] if name != "norms"]

    def kernel(x_ref, encoder_ref, decoder_ref, counts_ref, *refs):
        encoder_out = dict(zip(shapes[0], refs[:first]))
        decoder_out = dict(zip(shapes[1], refs[first : first + second]))
        count_ref, qkv_out, o_ref, lse_ref, x1_ref, mem_ref = refs[first + second : first + second + 6]
        rest = refs[first + second + 6 :]
        encoder_all, decoder_all, flat_ref, qkv_ref, h_ref, g_ref = rest[:6]
        local = dict(zip(matrices, rest[6 : 6 + len(matrices)]))
        local["norms"] = encoder_out["norms"]
        out_sem = rest[6 + len(matrices)]
        signals = rest[7 + len(matrices) :]
        views = (
            lambda block: encoder_all.at[block, :near],
            lambda block: encoder_all.at[block, near:],
            lambda block: decoder_all.at[block, :cut],
            lambda block: decoder_all.at[block, cut:],
        )
        place.locate()
        me = place.index(place.here)

        def go(*tasks):
            for core in range(2):

                @pl.when(place.here["c"] == core)
                def _():
                    for group, stage in tasks:
                        work = Spread(place, core, views[group], *signals[2 * group : 2 * group + 2])
                        getattr(work, stage)()

        own = shifted(encoder_ref[...], lax.rem(me * amounts[0], 128))
        row = lax.broadcasted_iota(jnp.int32, own.shape, 0)
        encoder_all[me] = jnp.where(row == small - 1, counts_ref[...], own).astype(bf16)
        place.greet()
        go((0, "one"), (1, "one"))
        decoder_all[me] = shifted(decoder_ref[...], lax.rem(me * amounts[1], 128)).astype(bf16)
        go(
            (0, "two"), (1, "two"), (0, "three"), (2, "one"), (1, "three"), (3, "one"), (0, "four"), (1, "four"), (0, "five"), (1, "five"),
        )
        total = jnp.zeros((1, 128), f32)
        for device in range(count):
            total = total + encoder_all[device, small - 16 :, :].astype(f32)[15:16]
        count_ref[...] = jnp.broadcast_to(jnp.sum(total, 1, keepdims=True), count_ref.shape)
        place_blocks(encoder_all, flat_ref, amounts[0])
        take_matrices(flat_ref, layouts[0], local)
        outs = [
            pltpu.make_async_copy(local[name], encoder_out[name], out_sem.at[k])
            for k, name in enumerate(matrices)
        ]
        outs.append(pltpu.make_async_copy(qkv_ref, qkv_out, out_sem.at[len(matrices)]))
        for out in outs[:-1]:
            out.start()
        go((2, "two"), (3, "two"))
        norms = local["norms"]
        norm_all(x_ref, norms, 0, h_ref, rows, IMG_CHUNK)
        project(h_ref, local["qkv"], qkv_ref, 3 * D, 0.125)
        outs[-1].start()

        def between(step):
            for number, task in ((0, (2, "three")), (1, (3, "three")), (4, (2, "four")), (7, (3, "four"))):

                @pl.when(step == number)
                def _():
                    go(task)

        attend_with(
            tables, qkv_ref, qkv_ref, D, qkv_ref, 2 * D, o_ref, lse_ref, IMG, IMG, False, True, between
        )
        add_project(x_ref, o_ref, local["out"], x1_ref)
        norm_all(x1_ref, norms, 2, h_ref, rows, IMG_CHUNK)

        @pl.loop(0, tables)
        def _(table):
            part = pl.ds(pl.multiple_of(table * IMG, 16), IMG)
            for start in range(0, FF, 256):
                lanes = slice(start, start + 256)
                g_ref[:, lanes] = gelu(dot(h_ref[part, :], local["ffn_in"][:, lanes])).astype(bf16)
            for start in range(0, D, 256):
                lanes = slice(start, start + 256)
                value = x1_ref[part, lanes] + dot(g_ref[...], local["ffn_out"][:, lanes])
                mem_ref[part, lanes] = value.astype(bf16)

        go((2, "five"), (3, "five"))
        place_blocks(decoder_all, flat_ref, amounts[1])
        take_matrices(flat_ref, layouts[1], decoder_out)
        go((0, "close"), (1, "close"), (2, "close"), (3, "close"))
        for out in outs:
            out.wait()

    vmem, hbm = pl.BlockSpec(memory_space=pltpu.VMEM), pl.BlockSpec(memory_space=pl.ANY)
    outs = pl.pallas_call(
        kernel,
        out_shape=(
            *shapes[0].values(),
            *shapes[1].values(),
            jax.ShapeDtypeStruct((8, 128), f32),
            jax.ShapeDtypeStruct((rows, 3 * D), bf16),
            jax.ShapeDtypeStruct((rows, D), bf16),
            jax.ShapeDtypeStruct((tables * HEADS, IMG), f32),
            jax.ShapeDtypeStruct((rows, D), f32),
            jax.ShapeDtypeStruct((rows, D), bf16),
        ),
        in_specs=[vmem] * 4,
        out_specs=(
            *[vmem if name == "norms" else hbm for name in shapes[0]],
            *[vmem] * second,
            vmem, hbm, vmem, vmem, vmem, vmem,
        ),
        scratch_shapes=[
            pltpu.VMEM((count, small, 128), bf16),
            pltpu.VMEM((count, large, 128), bf16),
            pltpu.VMEM((max(flat_counts), 128), f32),
            pltpu.VMEM((rows, 3 * D), bf16),
            pltpu.VMEM((rows, D), bf16),
            pltpu.VMEM((IMG, FF), bf16),
            *[pltpu.VMEM(shapes[0][name].shape, bf16) for name in matrices],
            pltpu.SemaphoreType.DMA((len(matrices) + 1,)),
            *[pltpu.SemaphoreType.DMA((n,)) for n in (count - 1, count) * 4],
        ],
        compiler_params=pltpu.CompilerParams(
            collective_id=1, has_side_effects=True, vmem_limit_bytes=VMEM_LIMIT
        ),
        name="gather_and_encode",
    )(images, encoder_block, decoder_block, counts)
    encoder_weights = dict(zip(shapes[0], outs[:first]))
    decoder_weights = dict(zip(shapes[1], outs[first : first + second]))
    number, *stored, memory = outs[first + second :]
    return encoder_weights, decoder_weights, number[0, 0], stored, memory


def adam_update(gradient, master, first_state, second_state, average):
    first_new = BETA_ONE * first_state + (1.0 - BETA_ONE) * gradient
    second_new = BETA_TWO * second_state + (1.0 - BETA_TWO) * gradient * gradient
    first_hat = first_new / (1.0 - BETA_ONE**STEP)
    second_hat = second_new / (1.0 - BETA_TWO**STEP)
    master_new = master - LEARN_RATE * (
        first_hat / (jnp.sqrt(second_hat) + EPSILON) + WEIGHT_DECAY * master
    )
    average_new = SMOOTH * average + (1.0 - SMOOTH) * master_new
    return (first_new, second_new, master_new, average_new)


def shard_block(shard):
    rows = block_rows(shard.shape[0])
    return jnp.pad(shard, (0, rows * 128 - shard.shape[0])).reshape(rows, 128)


def on_device(place, *arguments):
    (
        images, tag_ids, tag_lengths, cell_mask, cell_index, box_targets,
        encoder_params, encoder_first, encoder_second, encoder_average,
        decoder_params, decoder_first, decoder_second, decoder_average,
    ) = arguments
    encoder_amount, decoder_amount = encoder_params.shape[0], decoder_params.shape[0]
    cell_slots = jnp.arange(CELLS)
    alive = ((cell_mask > 0) & (cell_slots[None, :] < (tag_lengths // 4)[:, None])).astype(f32)
    cells = cell_index % tag_lengths[:, None]
    counted = (jnp.arange(TAGS)[None, :] < (tag_lengths - 1)[:, None]).astype(f32)
    upcoming = jnp.roll(tag_ids, -1, 1)
    prepared = (
        tag_ids[:, None, :], upcoming[:, None, :], counted[:, None, :], cells[:, None, :], alive[:, None, :], box_targets,
    )

    counts = jnp.sum(alive, 1)
    counts = jnp.pad(counts, (0, 128 - counts.shape[0])).reshape(1, 128)
    amounts = (encoder_amount, decoder_amount)
    encoder_weights, decoder_weights, cell_total, stored, memory = gather_and_encode(
        place, images, shard_block(encoder_params), shard_block(decoder_params), counts, amounts
    )
    scale = (1.0 / cell_total).reshape(1, 1)
    loss_block, dmemory, decoder_grads = decoder_step(prepared, scale, memory, decoder_weights)
    decoder_packed = pack_grads(
        decoder_grads, decoder_layout(), decoder_amount, place.count, "pack_decoder"
    )
    encoder_sum, decoder_sum, stats = encoder_backward(
        place, images, stored, dmemory, encoder_weights, decoder_packed, amounts, loss_block
    )
    grad_norm = jnp.sqrt(stats[0, 0])
    factor = CLIP_NORM / jnp.maximum(grad_norm, CLIP_NORM)
    encoder_grad = encoder_sum.reshape(-1)[:encoder_amount]
    decoder_grad = decoder_sum.reshape(-1)[:decoder_amount]
    encoder_new = adam_update(
        encoder_grad * factor, encoder_params, encoder_first, encoder_second, encoder_average
    )
    decoder_new = adam_update(
        decoder_grad * factor, decoder_params, decoder_first, decoder_second, decoder_average
    )
    return (stats[1, 0], cell_total, grad_norm, *encoder_new, *decoder_new)


def solution(mesh):
    rows, flat = P(AXES, None), P(AXES)
    return jax.shard_map(
        functools.partial(on_device, Place(mesh.shape["wide"], mesh.shape["narrow"])),
        mesh=mesh,
        in_specs=(rows, rows, flat, rows, rows, P(AXES, None, None)) + (flat,) * 8,
        out_specs=(P(), P(), P()) + (flat,) * 8,
        check_vma=False,
    )
```

```python
import functools

import jax
import jax.numpy as jnp
from jax import lax
from jax.experimental import pallas as pl
from jax.experimental.pallas import tpu as pltpu
from jax.sharding import PartitionSpec as P

D = 512
HEADS = 8
HEAD = D // HEADS
PAIRS = HEADS // 2
FF = 1024
V = 32
IMG = 784
TAGS = 512
STEP = 5
CELLS = 128
IMG_CHUNK = 784
TAG_CHUNK = 512
SAFE_SCORE = 50.0

BETA_ONE = 0.5
BETA_TWO = 0.5
CLIP_NORM = 0.01
LEARN_RATE = 0.05
WEIGHT_DECAY = 0.01
EPSILON = 1e-08
SMOOTH = 0.9

VMEM_LIMIT = 62 * 2**20
bf16 = jnp.bfloat16
f32 = jnp.float32


def encoder_layout():
    return [
        ("qkv", (D, 3 * D)),
        ("out", (D, D)),
        ("ffn_in", (D, FF)),
        ("ffn_out", (FF, D)),
        ("norms", (4, D)),
    ]


def decoder_layout():
    return [
        ("qkv", (D, 3 * D)),
        ("out", (D, D)),
        ("cross_q", (D, D)),
        ("cross_kv", (D, 2 * D)),
        ("cross_out", (D, D)),
        ("ffn_in", (D, FF)),
        ("ffn_out", (FF, D)),
        ("embed", (V, D)),
        ("head", (D, V)),
        ("box_in", (D, D)),
        ("norms", (8, D)),
        ("box_out", (D, 4)),
    ]


def dot(left, right, over_left=1, over_right=0):
    return lax.dot_general(
        left, right, (((over_left,), (over_right,)), ((), ())), preferred_element_type=f32
    )


def each_rows(total, step, body, first=0):
    @pl.loop(first // step, total // step)
    def _(index):
        body(pl.ds(pl.multiple_of(index * step, step), step))


def norm_rows(value, gain, shift):
    centred = value - jnp.mean(value, -1, keepdims=True)
    variance = jnp.mean(centred * centred, -1, keepdims=True)
    return centred * lax.rsqrt(variance + 1e-05) * gain + shift


def norm_rows_back(value, gain, upstream):
    centred = value - jnp.mean(value, -1, keepdims=True)
    variance = jnp.mean(centred * centred, -1, keepdims=True)
    scale = lax.rsqrt(variance + 1e-05)
    unit = centred * scale
    inner = upstream * gain
    mean_inner = jnp.mean(inner, -1, keepdims=True)
    mean_both = jnp.mean(inner * unit, -1, keepdims=True)
    down = scale * (inner - mean_inner - unit * mean_both)
    return (
        down,
        jnp.sum(upstream * unit, 0, keepdims=True),
        jnp.sum(upstream, 0, keepdims=True),
    )


GELU_A = 0.7978845608028654
GELU_B = 0.044715


def gelu(value):
    inner = jnp.tanh(GELU_A * (value + GELU_B * value * value * value))
    return 0.5 * value * (1.0 + inner)


def gelu_slope(value):
    square = value * value
    inner = jnp.tanh(GELU_A * (value + GELU_B * square * value))
    slope = GELU_A * (1.0 + 3.0 * GELU_B * square)
    return 0.5 * (1.0 + inner) + 0.5 * value * (1.0 - inner * inner) * slope


def half_masks():
    lane = lax.broadcasted_iota(jnp.int32, (1, 2 * HEAD), 1)
    first = (lane < HEAD).astype(f32)
    return (first.astype(bf16), (1.0 - first).astype(bf16))


def query_blocks(query_rows, key_rows, causal):
    if not causal:
        return [(0, query_rows, key_rows)]
    return [(start, 256, start + 256) for start in range(0, query_rows, 256)]


def key_tiles(start, depth, causal):
    if not causal or start == 0:
        return [(0, depth)]
    return [(0, start), (start, depth)]


def causal_keep(depth, width):
    key = lax.broadcasted_iota(jnp.int32, (depth, width), 0)
    query = lax.broadcasted_iota(jnp.int32, (depth, width), 1)
    return key <= query


def head_members():
    row = lax.broadcasted_iota(jnp.int32, (16, D), 0)
    lane = lax.broadcasted_iota(jnp.int32, (16, D), 1)
    return (lax.shift_right_logical(lane, 6) == row).astype(f32).astype(bf16)


def largest_norm(ref, column, rows, start):
    value = ref[start : start + rows, column : column + D]
    return jnp.max(dot(head_members(), value * value, 1, 1), 1, keepdims=True)


def attend(tables, q_ref, k_ref, k_col, v_ref, v_col, o_ref, lse_ref, query_rows, key_rows, causal):
    bound = jnp.zeros((16, 1), f32)
    for table in range(tables):
        of_queries = largest_norm(q_ref, 0, query_rows, table * query_rows)
        of_keys = largest_norm(k_ref, k_col, key_rows, table * key_rows)
        bound = jnp.maximum(bound, of_queries * of_keys)
    small = jnp.max(bound) < (0.98 * SAFE_SCORE) ** 2
    for wanted in (True, False):

        @pl.when(small == wanted)
        def _():
            attend_with(
                tables, q_ref, k_ref, k_col, v_ref, v_col, o_ref, lse_ref,
                query_rows, key_rows, causal, not wanted,
            )


def attend_with(
    tables, q_ref, k_ref, k_col, v_ref, v_col, o_ref, lse_ref, query_rows, key_rows, causal, take_peak, between=None,
):
    masks = half_masks()
    blocks = query_blocks(query_rows, key_rows, causal)

    @pl.loop(0, tables * PAIRS)
    def _(step):
        table = lax.div(step, PAIRS)
        pair = lax.rem(step, PAIRS)
        q_rows = pl.ds(pl.multiple_of(table * query_rows, 16), query_rows)
        k_rows = pl.ds(pl.multiple_of(table * key_rows, 16), key_rows)
        lanes = pl.multiple_of(pair * 128, 128)
        queries = q_ref[q_rows, pl.ds(lanes, 128)]
        keys = k_ref[k_rows, pl.ds(k_col + lanes, 128)]
        values = v_ref[k_rows, pl.ds(v_col + lanes, 128)].T
        scores = {}
        for half in range(2):
            own = queries * masks[half]
            for start, width, depth in blocks:
                for low, high in key_tiles(start, depth, causal):
                    tile = dot(keys[low:high], own[start : start + width], 1, 1)
                    if causal and low == start:
                        tile = jnp.where(causal_keep(high - low, width), tile, -1e30)
                    scores[half, start, low] = tile
        outs = []
        for half in range(2):
            own_values = values[half * HEAD : (half + 1) * HEAD, :]
            parts, sums = [], []
            for start, width, depth in blocks:
                tiles = key_tiles(start, depth, causal)
                weights = [scores[half, start, low] for low, _ in tiles]
                peak = jnp.zeros((1, width), f32)
                if take_peak:
                    peak = functools.reduce(
                        jnp.maximum, [jnp.max(tile, 0, keepdims=True) for tile in weights]
                    )
                    weights = [tile - peak for tile in weights]
                weights = [jnp.exp(tile) for tile in weights]
                total = sum(jnp.sum(tile, 0, keepdims=True) for tile in weights)
                mixed = sum(
                    dot(own_values[:, low:high], tile.astype(bf16))
                    for tile, (low, high) in zip(weights, tiles)
                )
                parts.append(mixed * (1.0 / total))
                sums.append(peak + jnp.log(total))
            outs.append(parts[0] if len(parts) == 1 else jnp.concatenate(parts, 1))
            lse_ref[pl.ds(table * HEADS + pair * 2 + half, 1), :] = (
                sums[0] if len(sums) == 1 else jnp.concatenate(sums, 1)
            )
        joined = jnp.concatenate(outs, 0).astype(bf16)
        o_ref[q_rows, pl.ds(lanes, 128)] = joined.T
        if between is not None:
            between(step)


def head_sums(tables, up_ref, o_ref, delta_ref, query_rows):
    member = head_members()
    for table in range(tables):
        rows = slice(table * query_rows, (table + 1) * query_rows)
        both = up_ref[rows, :].astype(f32) * o_ref[rows, :].astype(f32)
        high = both.astype(bf16)
        rest = (both - high.astype(f32)).astype(bf16)
        sums = dot(member, high, 1, 1) + dot(member, rest, 1, 1)
        delta_ref[table * HEADS : (table + 1) * HEADS, :] = sums[:HEADS]


def attend_back(
    span_of_tables, q_ref, k_ref, k_col, v_ref, v_col, up_ref, lse_ref, delta_ref,
    dq_ref, dk_ref, dv_ref, query_rows, key_rows, causal, between=None,
):
    masks = half_masks()

    @pl.loop(span_of_tables[0] * PAIRS, span_of_tables[1] * PAIRS)
    def _(step):
        table = lax.div(step, PAIRS)
        pair = lax.rem(step, PAIRS)
        q_rows = pl.ds(pl.multiple_of(table * query_rows, 16), query_rows)
        k_rows = pl.ds(pl.multiple_of(table * key_rows, 16), key_rows)
        lanes = pl.multiple_of(pair * 128, 128)
        queries = q_ref[q_rows, pl.ds(lanes, 128)]
        keys = k_ref[k_rows, pl.ds(k_col + lanes, 128)]
        values = v_ref[k_rows, pl.ds(v_col + lanes, 128)]
        upstream = up_ref[q_rows, pl.ds(lanes, 128)]
        keys_across = keys.T
        blocks = query_blocks(query_rows, key_rows, causal)
        grad_q = []
        grad_k = [None] * len(blocks)
        grad_v = [None] * len(blocks)
        ahead = {}
        if causal:
            for half in range(2):
                own, own_up = queries * masks[half], upstream * masks[half]
                for number, (start, width, depth) in enumerate(blocks):
                    span = slice(start, start + width)
                    ahead[half, number] = (
                        dot(keys[:depth], own[span], 1, 1),
                        dot(values[:depth], own_up[span], 1, 1),
                    )
        for half in range(2):
            index = pl.ds(table * HEADS + pair * 2 + half, 1)
            own = queries * masks[half]
            own_up = upstream * masks[half]
            logsum = lse_ref[index, :]
            delta = delta_ref[index, :]
            across = keys_across[half * HEAD : (half + 1) * HEAD, :]
            parts = []
            for number, (start, width, depth) in enumerate(blocks):
                span = slice(start, start + width)
                if causal:
                    scores, pull = ahead[half, number]
                else:
                    scores = dot(keys[:depth], own[span], 1, 1)
                    pull = dot(values[:depth], own_up[span], 1, 1)
                weight = jnp.exp(scores - logsum[:, span])
                if causal:
                    edge = jnp.where(causal_keep(width, width), weight[start:], 0.0)
                    weight = edge if start == 0 else jnp.concatenate([weight[:start], edge], 0)
                change = (weight * (pull - delta[:, span])).astype(bf16)
                add_v = dot(weight.astype(bf16), own_up[span])
                add_k = dot(change, own[span])
                grad_v[number] = add_v if half == 0 else grad_v[number] + add_v
                grad_k[number] = add_k if half == 0 else grad_k[number] + add_k
                parts.append(dot(across[:, :depth], change) * 0.125)
            grad_q.append(parts[0] if len(parts) == 1 else jnp.concatenate(parts, 1))
        dq_ref[q_rows, pl.ds(lanes, 128)] = jnp.concatenate(grad_q, 0).astype(bf16).T
        for ref, column, grads in ((dk_ref, k_col, grad_k), (dv_ref, v_col, grad_v)):
            total = grads[-1]
            if len(grads) == 2:
                low = blocks[0][2]
                total = jnp.concatenate([total[:low] + grads[0], total[low:]], 0)
            ref[k_rows, pl.ds(column + lanes, 128)] = total.astype(bf16)
        if between is not None:
            between(step)


def project(a_ref, w_ref, out_ref, width, first_scale=None):
    for start in range(0, width, 512):
        value = dot(a_ref[...], w_ref[:, start : start + 512])
        if first_scale is not None and start == 0:
            value = value * first_scale
        out_ref[:, start : start + 512] = value.astype(bf16)


def add_project(base_ref, a_ref, w_ref, out_ref):
    for start in range(0, D, 256):
        lanes = slice(start, start + 256)
        out_ref[:, lanes] = base_ref[:, lanes].astype(f32) + dot(a_ref[...], w_ref[:, lanes])


def weight_grad(a_ref, b_ref, out_ref):
    rows, columns = out_ref.shape
    for start in range(0, columns, 512):
        lanes = slice(start, start + 512)
        out_ref[:, lanes] = dot(a_ref[...], b_ref[:, lanes], 0, 0).astype(out_ref.dtype)


def ffn_forward(h_ref, w_in, u_ref, g_ref):
    for start in range(0, FF, 256):
        lanes = slice(start, start + 256)
        inner = dot(h_ref[...], w_in[:, lanes])
        if u_ref is not None:
            u_ref[:, lanes] = inner
        g_ref[:, lanes] = gelu(inner).astype(bf16)


def ffn_backward(og_ref, h_ref, u_ref, g_ref, w_in, w_out, d_in, d_out, dh_ref):
    weight_grad(g_ref, og_ref, d_out)
    for start in range(0, FF, 256):
        lanes = slice(start, start + 256)
        back = dot(og_ref[...], w_out[lanes, :], 1, 1)
        g_ref[:, lanes] = (gelu_slope(u_ref[:, lanes]) * back).astype(bf16)
    weight_grad(h_ref, g_ref, d_in)
    project_back(g_ref, w_in, dh_ref)


def project_back(g_ref, w_ref, out_ref):
    for start in range(0, D, 256):
        lanes = slice(start, start + 256)
        out_ref[:, lanes] = dot(g_ref[...], w_ref[lanes, :], 1, 1).astype(out_ref.dtype)


def norm_all(x_ref, norms_ref, row, out_ref, total, step):
    gain, shift = norms_ref[row : row + 1, :], norms_ref[row + 1 : row + 2, :]

    def body(rows):
        out_ref[rows, :] = norm_rows(x_ref[rows, :].astype(f32), gain, shift).astype(bf16)

    each_rows(total, step, body)


def norm_all_back(x_ref, norms_ref, row, upstream, dnorms_ref, total, step, keep, first=0):
    gain = norms_ref[row : row + 1, :]
    if first == 0:
        dnorms_ref[row : row + 2, :] = jnp.zeros((2, D), f32)

    def body(rows):
        arriving = upstream(rows) if callable(upstream) else upstream[rows, :]
        down, d_gain, d_shift = norm_rows_back(x_ref[rows, :].astype(f32), gain, arriving)
        dnorms_ref[row : row + 1, :] += d_gain
        dnorms_ref[row + 1 : row + 2, :] += d_shift
        if keep is not None:
            keep(rows, down)

    each_rows(total, step, body, first)


def soft_low(first_one, other_one):
    return 0.5 * (first_one + other_one - jnp.sqrt((first_one - other_one) ** 2 + 0.0001))


def soft_high(first_one, other_one):
    return 0.5 * (first_one + other_one + jnp.sqrt((first_one - other_one) ** 2 + 0.0001))


def softplus(value):
    return jnp.maximum(value, 0.0) + jnp.log1p(jnp.exp(-jnp.abs(value)))


@jax.custom_vjp
def smooth_relu(value):
    return softplus(value)


def smooth_relu_keep(value):
    return softplus(value), value


def smooth_relu_back(value, upstream):
    return (upstream * (1.0 / (1.0 + jnp.exp(-value))),)


smooth_relu.defvjp(smooth_relu_keep, smooth_relu_back)


def cell_losses(px, py, pw, ph, gx, gy, gw, gh):
    absolute = (
        jnp.sqrt((px - gx) ** 2 + 0.01)
        + jnp.sqrt((py - gy) ** 2 + 0.01)
        + jnp.sqrt((pw - gw) ** 2 + 0.01)
        + jnp.sqrt((ph - gh) ** 2 + 0.01)
    )
    left_p, right_p = px - 0.5 * pw, px + 0.5 * pw
    low_p, top_p = py - 0.5 * ph, py + 0.5 * ph
    left_g, right_g = gx - 0.5 * gw, gx + 0.5 * gw
    low_g, top_g = gy - 0.5 * gh, gy + 0.5 * gh
    across = smooth_relu(20.0 * (soft_low(right_p, right_g) - soft_high(left_p, left_g))) / 20.0
    upward = smooth_relu(20.0 * (soft_low(top_p, top_g) - soft_high(low_p, low_g))) / 20.0
    common = across * upward
    union = pw * ph + gw * gh - common
    hull = (soft_high(right_p, right_g) - soft_low(left_p, left_g)) * (
        soft_high(top_p, top_g) - soft_low(low_p, low_g)
    )
    ratio = common / union - (hull - union) / hull
    return 5.0 * absolute + 2.0 * (1.0 - ratio)


def split_sum(left, value):
    high = value.astype(bf16)
    rest = (value - high.astype(f32)).astype(bf16)
    return dot(left, high) + dot(left, rest)


def decoder_kernel(
    tags_ref, next_ref, counted_ref, place_ref, alive_ref, target_ref, scale_ref, mem_ref,
    w_qkv, w_out, w_cq, w_ckv, w_co, w_in, w_ffo, w_embed, w_head, w_box, norms, w_box_out,
    loss_ref, dmem_ref, d_qkv, d_out, d_cq, d_ckv, d_co, d_in, d_ffo, d_embed, d_head, d_box, d_norms, d_box_out,
    e_ref, h1_ref, qkv_ref, o1_ref, lse1_ref, y1_ref, h2_ref, cq_ref, ckv_ref, o2_ref, lse2_ref, y2_ref,
    h3_ref, u_ref, g_ref, y3_ref, z_ref, dy_ref, dh_ref, og_ref, up_ref, delta_ref, need, done,
):
    tables = tags_ref.shape[0]
    rows = tables * TAGS

    def tag_members(table):
        member = lax.broadcasted_iota(jnp.int32, (V, TAGS), 0) == tags_ref[table]
        return member.astype(f32).astype(bf16)

    for table in range(tables):
        e_ref[table * TAGS : (table + 1) * TAGS, :] = dot(tag_members(table), w_embed[...], 0, 0)
    norm_all(e_ref, norms, 0, h1_ref, rows, TAG_CHUNK)
    need("qkv")
    project(h1_ref, w_qkv, qkv_ref, 3 * D, 0.125)
    attend(tables, qkv_ref, qkv_ref, D, qkv_ref, 2 * D, o1_ref, lse1_ref, TAGS, TAGS, True)
    need("out")
    add_project(e_ref, o1_ref, w_out, y1_ref)
    norm_all(y1_ref, norms, 2, h2_ref, rows, TAG_CHUNK)
    need("cross_q")
    project(h2_ref, w_cq, cq_ref, D, 0.125)
    need("mem")
    need("cross_kv")
    project(mem_ref, w_ckv, ckv_ref, 2 * D)
    attend(tables, cq_ref, ckv_ref, 0, ckv_ref, D, o2_ref, lse2_ref, TAGS, IMG, False)
    need("cross_out")
    add_project(y1_ref, o2_ref, w_co, y2_ref)
    norm_all(y2_ref, norms, 4, h3_ref, rows, TAG_CHUNK)
    need("ffn_in")
    ffn_forward(h3_ref, w_in, u_ref, g_ref)
    need("ffn_out")
    add_project(y2_ref, g_ref, w_ffo, y3_ref)
    norm_all(y3_ref, norms, 6, z_ref, rows, TAG_CHUNK)

    need("box_in")
    scale = scale_ref[0, 0]
    loss = jnp.zeros((1, 1), f32)
    picked, inners, box_ups = [], [], []
    head_sum = jnp.zeros((V, D), f32)
    box_in_sum = jnp.zeros((D, D), f32)
    box_out_sum = jnp.zeros((16, D), f32)
    for table in range(tables):
        own = slice(table * TAGS, (table + 1) * TAGS)
        final = z_ref[own, :]
        logits = dot(w_head[...], final, 1, 1)
        peak = jnp.max(logits, 0, keepdims=True)
        weight = jnp.exp(logits - peak)
        total = jnp.sum(weight, 0, keepdims=True)
        counted = counted_ref[table]
        wanted = lax.broadcasted_iota(jnp.int32, (V, TAGS), 0) == next_ref[table]
        chosen = jnp.sum(jnp.where(wanted, logits - peak - jnp.log(total), 0.0), 0, keepdims=True)
        loss = loss - jnp.sum(counted * chosen, 1, keepdims=True)
        dlogits = (weight / total - wanted.astype(f32)) * counted * scale
        tag_up = dlogits.astype(bf16)
        head_sum = head_sum + dot(tag_up, final)
        dfinal = dot(tag_up, w_head[...], 0, 0)
        select = (
            (lax.broadcasted_iota(jnp.int32, (TAGS, CELLS), 0) == place_ref[table])
            .astype(f32)
            .astype(bf16)
        )
        cells = dot(select, final, 0, 0).astype(bf16)
        inner = dot(cells, w_box[...])
        active = gelu(inner).astype(bf16)
        raw = dot(w_box_out[...], active, 1, 1)
        soft = 1.0 / (1.0 + jnp.exp(-raw))
        ratios = tuple(soft[k : k + 1, :] for k in range(4))
        wished = tuple(target_ref[table, k : k + 1, :] for k in range(4))
        alive = alive_ref[table]
        cell, pull = jax.vjp(lambda *parts: cell_losses(*parts, *wished), *ratios)
        loss = loss + jnp.sum(alive * cell, 1, keepdims=True)
        downs = pull(alive * scale)
        fill = jnp.zeros((16, CELLS), f32)
        index = lax.broadcasted_iota(jnp.int32, (16, CELLS), 0)
        for k in range(4):
            value = downs[k] * ratios[k] * (1.0 - ratios[k])
            fill = jnp.where(index == k, value, fill)
        box_up = fill.astype(bf16)
        box_out_sum = box_out_sum + dot(box_up, active)
        dinner = (gelu_slope(inner) * dot(box_up, w_box_out[...], 0, 0)).astype(bf16)
        box_in_sum = box_in_sum + dot(cells, dinner, 0, 0)
        dh_ref[own, :] = dfinal + split_sum(select, dot(dinner, w_box[...], 1, 1))
    loss_ref[...] = jnp.broadcast_to(loss, loss_ref.shape)
    d_head[...] = head_sum.astype(bf16)
    d_box[...] = box_in_sum.astype(bf16)
    done("box_in")
    d_box_out[...] = box_out_sum.astype(bf16)

    def start_sum(block, down):
        dy_ref[block, :] = down
        og_ref[block, :] = down.astype(bf16)

    def add_sum(block, down):
        total = down + dy_ref[block, :]
        dy_ref[block, :] = total
        og_ref[block, :] = total.astype(bf16)

    norm_all_back(y3_ref, norms, 6, dh_ref, d_norms, rows, TAG_CHUNK, start_sum)
    ffn_backward(og_ref, h3_ref, u_ref, g_ref, w_in, w_ffo, d_in, d_ffo, dh_ref)
    done("ffn_in")
    done("ffn_out")
    norm_all_back(y2_ref, norms, 4, dh_ref, d_norms, rows, TAG_CHUNK, add_sum)

    weight_grad(o2_ref, og_ref, d_co)
    done("cross_out")
    project_back(og_ref, w_co, up_ref)
    head_sums(tables, up_ref, o2_ref, delta_ref, TAGS)
    attend_back(
        (0, tables), cq_ref, ckv_ref, 0, ckv_ref, D, up_ref, lse2_ref, delta_ref,
        cq_ref, ckv_ref, ckv_ref, TAGS, IMG, False,
    )
    weight_grad(h2_ref, cq_ref, d_cq)
    done("cross_q")
    weight_grad(mem_ref, ckv_ref, d_ckv)
    done("cross_kv")
    project_back(ckv_ref, w_ckv, dmem_ref)
    done("mem")
    project_back(cq_ref, w_cq, dh_ref)
    norm_all_back(y1_ref, norms, 2, dh_ref, d_norms, rows, TAG_CHUNK, add_sum)

    weight_grad(o1_ref, og_ref, d_out)
    done("out")
    project_back(og_ref, w_out, up_ref)
    head_sums(tables, up_ref, o1_ref, delta_ref, TAGS)
    attend_back(
        (0, tables), qkv_ref, qkv_ref, D, qkv_ref, 2 * D, up_ref, lse1_ref, delta_ref,
        qkv_ref, qkv_ref, qkv_ref, TAGS, TAGS, True,
    )
    weight_grad(h1_ref, qkv_ref, d_qkv)
    done("qkv")
    project_back(qkv_ref, w_qkv, dh_ref)
    norm_all_back(e_ref, norms, 0, dh_ref, d_norms, rows, TAG_CHUNK, add_sum)
    embed_sum = jnp.zeros((V, D), f32)
    for table in range(tables):
        embed_sum = embed_sum + split_sum(
            tag_members(table), dy_ref[table * TAGS : (table + 1) * TAGS, :]
        )
    d_embed[...] = embed_sum.astype(bf16)


DECODER_NAMES = (
    "qkv", "out", "cross_q", "cross_kv", "cross_out", "ffn_in", "ffn_out", "embed", "head", "box_in", "norms", "box_out",
)


DECODER_MOVED = ("qkv", "out", "cross_q", "mem", "cross_kv", "cross_out", "ffn_in", "ffn_out", "box_in")


def decoder_step(prepared, scale, memory, weights):
    tables = prepared[0].shape[0]
    rows = tables * TAGS
    image_rows = memory.shape[0]
    arrays = {"mem": memory, **{name: weights[name] for name in DECODER_NAMES}}
    grads = {
        name: jax.ShapeDtypeStruct(array.shape, f32 if name in ("norms", "mem") else bf16)
        for name, array in arrays.items()
    }
    vmem, hbm = pl.BlockSpec(memory_space=pltpu.VMEM), pl.BlockSpec(memory_space=pl.ANY)
    low = lambda width, height=rows: pltpu.VMEM((height, width), bf16)
    full = lambda width, height=rows: pltpu.VMEM((height, width), f32)
    stats = pltpu.VMEM((tables * HEADS, TAGS), f32)
    places = [hbm if name in DECODER_MOVED else vmem for name in arrays]
    moved, total = len(DECODER_MOVED), len(arrays)

    def kernel(*refs):
        ready, refs = refs[:7], refs[7:]
        sources, refs = dict(zip(arrays, refs[:total])), refs[total:]
        loss_ref, targets, refs = refs[0], dict(zip(arrays, refs[1 : total + 1])), refs[total + 1 :]
        inside = dict(zip(DECODER_MOVED, refs[:moved]))
        outside = dict(zip(DECODER_MOVED, refs[moved : 2 * moved]))
        in_sem, out_sem = refs[2 * moved : 2 * moved + 2]
        fetch = {
            name: pltpu.make_async_copy(sources[name], inside[name], in_sem.at[k])
            for k, name in enumerate(DECODER_MOVED)
        }
        give = {
            name: pltpu.make_async_copy(outside[name], targets[name], out_sem.at[k])
            for k, name in enumerate(DECODER_MOVED)
        }
        for name in DECODER_MOVED:
            fetch[name].start()
        given = {**sources, **inside}
        taken = {**targets, **outside}
        decoder_kernel(
            *ready, given["mem"], *[given[name] for name in DECODER_NAMES],
            loss_ref, taken["mem"], *[taken[name] for name in DECODER_NAMES],
            *refs[2 * moved + 2 :], lambda name: fetch[name].wait(), lambda name: give[name].start(),
        )
        for name in DECODER_MOVED:
            give[name].wait()

    outs = pl.pallas_call(
        kernel,
        out_shape=(jax.ShapeDtypeStruct((8, 128), f32), *grads.values()),
        in_specs=[vmem] * 6 + [pl.BlockSpec(memory_space=pltpu.SMEM)] + places,
        out_specs=(vmem, *places),
        scratch_shapes=[
            *[pltpu.VMEM(arrays[name].shape, arrays[name].dtype) for name in DECODER_MOVED],
            *[pltpu.VMEM(grads[name].shape, grads[name].dtype) for name in DECODER_MOVED],
            pltpu.SemaphoreType.DMA((moved,)), pltpu.SemaphoreType.DMA((moved,)),
            full(D), low(D), low(3 * D), low(D), stats, full(D), low(D), low(D), low(2 * D, image_rows), low(D), stats,
            full(D), low(D), full(FF), low(FF), full(D), low(D), full(D), full(D), low(D), low(D), stats,
        ],
        compiler_params=pltpu.CompilerParams(vmem_limit_bytes=VMEM_LIMIT),
        name="decoder_step",
    )(*prepared, scale, *arrays.values())
    return outs[0], outs[1], dict(zip(DECODER_NAMES, outs[2:]))


AXES = ("wide", "narrow")
MESH = pl.DeviceIdType.MESH
ORDERS = (("a", "y", "b"), ("a", "b", "y"))


class Place:
    def __init__(self, wide, narrow):
        inner = 2 if wide % 2 == 0 else 1
        self.sizes = {"a": wide // inner, "b": inner, "y": narrow // 2, "c": 2}
        self.narrow = narrow
        self.count = wide * narrow

    def locate(self):
        wide, narrow = lax.axis_index("wide"), lax.axis_index("narrow")
        inner = self.sizes["b"]
        self.here = {
            "a": lax.div(wide, inner),
            "b": lax.rem(wide, inner),
            "y": lax.div(narrow, 2),
            "c": lax.rem(narrow, 2),
        }
        return self

    def moved(self, steps):
        there = dict(self.here)
        for part, step in steps.items():
            there[part] = lax.rem(there[part] + step, self.sizes[part])
        return there

    def device(self, there):
        return (there["a"] * self.sizes["b"] + there["b"], there["y"] * 2 + there["c"])

    def index(self, there):
        wide, narrow = self.device(there)
        return wide * self.narrow + narrow

    def peers(self):
        return [(part, step) for part, size in self.sizes.items() for step in range(1, size)]

    def in_plane(self, step):
        size, wide = self.sizes["b"], self.sizes["y"]
        here = (self.here["b"] * wide + self.here["y"]) * 2 + self.here["c"]
        there = lax.rem(here + step, size * wide * 2)
        return there, {
            **self.here,
            "b": lax.div(there, wide * 2),
            "y": lax.rem(lax.div(there, 2), wide),
            "c": lax.rem(there, 2),
        }

    def plane(self):
        return self.sizes["b"] * self.sizes["y"] * 2

    def greet(self, whole_plane=False):
        barrier = pltpu.get_barrier_semaphore()
        peers = [self.moved({part: step}) for part, step in self.peers()]
        if whole_plane:
            peers = [self.in_plane(step)[1] for step in range(1, self.plane())] + [
                self.moved({"a": step}) for step in range(1, self.sizes["a"])
            ]
        for there in peers:
            pl.semaphore_signal(
                barrier, inc=1, device_id=self.device(there), device_id_type=MESH
            )
        pl.semaphore_wait(barrier, len(peers))


def block_rows(amount):
    return -(-(amount // 128 + 3) // 16) * 16


def flat_rows(amount, count):
    return -(-((count - 1) * amount // 128 + block_rows(amount)) // 8) * 8


def layout_bases(layout):
    offset = 0
    for name, (height, breadth) in layout:
        yield name, height, breadth, offset // 128
        offset += height * breadth


def place_blocks(all_ref, flat_ref, amount):
    count, rows, _ = all_ref.shape
    used = amount // 128 + 2
    flat_ref[0:8, :] = jnp.zeros((8, 128), f32)

    @pl.loop(0, count)
    def _(device):
        start = lax.div(device * amount, 128)
        before = flat_ref[pl.ds(start, 1), :]
        flat_ref[pl.ds(start, used), :] = all_ref[device, :used, :].astype(f32)
        flat_ref[pl.ds(start, 1), :] = before + all_ref[device, 0:16, :].astype(f32)[0:1]


def one_hot(shape, match):
    first = lax.broadcasted_iota(jnp.int32, shape, 0)
    second = lax.broadcasted_iota(jnp.int32, shape, 1)
    return match(first, second).astype(f32).astype(bf16)


def take_matrices(flat_ref, layout, out_refs):
    for name, height, breadth, base in layout_bases(layout):
        out_ref = out_refs[name]
        if name == "head":
            turned = flat_ref[base : base + 128, :].T.astype(bf16)
            total = jnp.zeros((V, D), f32)
            for part in range(4):
                spread = one_hot((128, D), lambda row, column: column == 4 * row + part)
                total = total + dot(turned[part * V : (part + 1) * V, :], spread)
            out_ref[...] = total.astype(bf16)
        elif name == "box_out":
            block = flat_ref[base : base + 16, :].astype(bf16)
            own = one_hot((16, D), lambda row, column: lax.div(column, 32) == row).astype(f32)
            index = lax.broadcasted_iota(jnp.int32, (16, D), 0)
            total = jnp.zeros((16, D), f32)
            for k in range(4):
                pick = one_hot((128, D), lambda lane, column: lane == 4 * lax.rem(column, 32) + k)
                line = jnp.sum(dot(block, pick) * own, 0, keepdims=True)
                total = jnp.where(index == k, line, total)
            out_ref[...] = total.astype(bf16)
        else:
            wide = breadth // 128
            for column in range(wide):
                out_ref[:, column * 128 : (column + 1) * 128] = flat_ref[
                    pl.ds(base + column, height, stride=wide), :
                ].astype(out_ref.dtype)


def put_matrices(flat_ref, layout, refs):
    for name, height, breadth, base in layout_bases(layout):
        ref = refs[name]
        if name == "head":
            total = jnp.zeros((128, 128), f32)
            for part in range(4):
                pick = one_hot((128, D), lambda row, column: column == 4 * row + part)
                shift = one_hot((V, 128), lambda row, lane: lane == V * part + row)
                total = total + dot(dot(pick, ref[...], 1, 1).astype(bf16), shift)
            flat_ref[base : base + 128, :] = total
        elif name == "box_out":
            own = one_hot((16, D), lambda row, column: lax.div(column, 32) == row).astype(f32)
            total = jnp.zeros((16, 128), f32)
            for k in range(4):
                line = ref[...].astype(f32)[k : k + 1, :]
                spread = one_hot((D, 128), lambda column, lane: lane == 4 * lax.rem(column, 32) + k)
                total = total + dot((own * line).astype(bf16), spread)
            flat_ref[base : base + 16, :] = total
        else:
            wide = breadth // 128
            for column in range(wide):
                flat_ref[pl.ds(base + column, height, stride=wide), :] = ref[
                    :, column * 128 : (column + 1) * 128
                ].astype(f32)


def cut_blocks(flat_ref, amount, block_ref):
    count, rows, _ = block_ref.shape

    @pl.loop(0, count)
    def _(device):
        start = lax.div(device * amount, 128)
        block_ref[device, :, :] = flat_ref[pl.ds(start, rows), :].astype(bf16)


def weight_shapes(layout):
    shapes = {name: extent for name, extent in layout}
    if "head" in shapes:
        shapes["head"], shapes["box_out"] = (V, D), (16, D)
    return {
        name: jax.ShapeDtypeStruct(extent, f32 if name == "norms" else bf16)
        for name, extent in shapes.items()
    }


def pack_grads(grads, layout, amount, count, name):
    names = [piece for piece, _ in layout]

    def kernel(*refs):
        block_ref, flat_ref = refs[-2:]
        tail = sum(extent[0] * extent[1] for _, extent in layout) // 128
        flat_ref[tail:, :] = jnp.zeros((flat_ref.shape[0] - tail, 128), f32)
        put_matrices(flat_ref, layout, dict(zip(names, refs)))
        cut_blocks(flat_ref, amount, block_ref)

    return pl.pallas_call(
        kernel,
        out_shape=jax.ShapeDtypeStruct((count, block_rows(amount), 128), bf16),
        scratch_shapes=[pltpu.VMEM((flat_rows(amount, count), 128), f32)],
        compiler_params=pltpu.CompilerParams(vmem_limit_bytes=VMEM_LIMIT),
        name=name,
    )(*[grads[piece] for piece in names])


class Reduction:
    def __init__(self, place, core, pick, own_ref, mine_ref, got_ref, load_sem, send_sem, recv_sem):
        self.place, self.pick = place, pick
        self.own, self.mine, self.got = own_ref, mine_ref, got_ref
        self.load_sem, self.send_sem, self.recv_sem = load_sem, send_sem, recv_sem
        self.order, self.other = ORDERS[core], ORDERS[1 - core]
        self.s1, self.s2, self.s3 = (place.sizes[part] for part in self.order)
        self.half = place.count // 2
        self.base3 = self.half
        self.base2 = self.base3 + (self.s3 - 1) * self.s1 * self.s2
        self.base1 = self.base2 + (self.s2 - 1) * self.s1

    def slot(self, steps):
        sizes = self.place.sizes
        return (steps["a"] * sizes["b"] + steps["b"]) * sizes["y"] + steps["y"]

    def owner(self, steps):
        return self.place.index(self.place.moved(steps))

    def only(self, steps, body):
        if self.pick is None:
            body()
        else:
            pl.when(self.pick(self.owner(steps)))(body)

    def copy(self, source, slot, part, step):
        return pltpu.make_async_remote_copy(
            src_ref=source,
            dst_ref=self.got.at[slot],
            send_sem=self.send_sem.at[slot],
            recv_sem=self.recv_sem.at[slot],
            device_id=self.place.device(self.place.moved({part: step})),
            device_id_type=MESH,
        )

    def load(self, steps):
        slot = self.slot(steps)
        return pltpu.make_async_copy(
            self.own.at[self.owner(steps)], self.mine.at[slot], self.load_sem.at[slot]
        )

    def took(self, slot):
        self.copy(self.mine.at[0], slot, "c", 1).wait_recv()

    def value(self, slot):
        return self.got[slot].astype(f32)

    def levels(self, order):
        s1, s2, s3 = (self.place.sizes[part] for part in order)
        return (
            (s1 * s2 * (s3 - 1), lambda n: (s1 - 1 - lax.rem(n, s1), s2 - 1 - lax.rem(lax.div(n, s1), s2), lax.div(n, s1 * s2) + 1)),
            (s1 * (s2 - 1), lambda n: (s1 - 1 - lax.rem(n, s1), lax.div(n, s1) + 1, 0)),
            (s1, lambda n: (s1 - 1 - n, 0, 0)),
        )

    def to_sibling(self):
        if self.load_sem is not None:
            for amount, where in self.levels(self.order):

                @pl.loop(0, amount)
                def _(number):
                    self.load(dict(zip(self.order, where(number)))).start()

        for amount, where in self.levels(self.other):

            @pl.loop(0, amount)
            def _(number):
                steps = dict(zip(self.other, where(number)))
                slot = self.slot(steps)

                def send():
                    block = slot if self.load_sem is None else self.owner({**steps, "c": 1})
                    self.copy(self.own.at[block], slot, "c", 1).start()

                self.only({**steps, "c": 1}, send)

    def partial(self, p, q, r):
        steps = dict(zip(self.order, (p, q, r)))
        slot = self.slot(steps)
        if self.load_sem is not None:
            self.load(steps).wait()
        self.took(slot)
        return slot, self.mine[slot].astype(f32) + self.value(slot)

    def add_third(self, total, p, q):
        for step in range(1, self.s3):
            slot = self.base3 + ((step - 1) * self.s1 + p) * self.s2 + q
            self.took(slot)
            total = total + self.value(slot)
        return total

    def add_second(self, total, p):
        for step in range(1, self.s2):
            slot = self.base2 + (step - 1) * self.s1 + p
            self.took(slot)
            total = total + self.value(slot)
        return total

    def send(self, own_slot, total, slot, part, step):
        self.mine[own_slot] = total.astype(bf16)
        self.copy(self.mine.at[own_slot], slot, part, step).start()

    def third(self):
        amount, where = self.levels(self.order)[0]

        @pl.loop(0, amount)
        def _(number):
            p, q, r = where(number)

            def body():
                own_slot, total = self.partial(p, q, r)
                slot = self.base3 + ((r - 1) * self.s1 + p) * self.s2 + q
                self.send(own_slot, total, slot, self.order[2], r)

            self.only(dict(zip(self.order, (p, q, r))), body)

    def second(self):
        amount, where = self.levels(self.order)[1]

        @pl.loop(0, amount)
        def _(number):
            p, q, _ = where(number)

            def body():
                own_slot, total = self.partial(p, q, 0)
                total = self.add_third(total, p, q)
                self.send(own_slot, total, self.base2 + (q - 1) * self.s1 + p, self.order[1], q)

            self.only(dict(zip(self.order, (p, q, 0))), body)

    def first(self):
        @pl.loop(1, self.s1)
        def _(p):
            def body():
                own_slot, total = self.partial(p, 0, 0)
                total = self.add_second(self.add_third(total, p, 0), p)
                self.send(own_slot, total, self.base1 + p - 1, self.order[0], p)

            self.only({self.order[0]: p}, body)

    def last(self, out_ref):
        def body():
            _, total = self.partial(0, 0, 0)
            out_ref[...] = self.add_second(self.add_third(total, 0, 0), 0)

            @pl.loop(1, self.s1)
            def _(p):
                slot = self.base1 + p - 1
                self.took(slot)
                out_ref[...] += self.value(slot)

        self.only({}, body)

    def close(self):
        @pl.loop(0, self.place.count - 1)
        def _(slot):
            self.copy(self.mine.at[0], slot, "c", 1).wait_send()


def reduction_memory(count, rows):
    half = count // 2
    return [pltpu.VMEM((half, rows, 128), bf16), pltpu.VMEM((count - 1, rows, 128), bf16)]


def reduction_signals(count, loads):
    return [pltpu.SemaphoreType.DMA((n,)) for n in ([count // 2] if loads else []) + [count - 1] * 2]


def reduce_stage(place, stage, pick, *members):
    for core in range(2):

        @pl.when(place.here["c"] == core)
        def _():
            stage(Reduction(place, core, pick, *members))


def cut_for_reduction(place, pick, flat_ref, amount, mine_ref, other_ref):
    rows = mine_ref.shape[1]
    sizes = place.sizes

    @pl.loop(0, place.count // 2)
    def _(slot):
        steps = {
            "a": lax.div(slot, sizes["b"] * sizes["y"]),
            "b": lax.rem(lax.div(slot, sizes["y"]), sizes["b"]),
            "y": lax.rem(slot, sizes["y"]),
        }
        for core, ref in ((0, mine_ref), (1, other_ref)):
            owner = place.index(place.moved({**steps, "c": core}))

            @pl.when(pick(owner))
            def _():
                ref[slot] = flat_ref[pl.ds(lax.div(owner * amount, 128), rows), :].astype(bf16)


def sum_everywhere(place, value, box_ref, send_sem, recv_sem):
    base = 0
    plane = [place.in_plane(step) for step in range(place.plane())]
    line = [place.moved({"a": step}) for step in range(place.sizes["a"])]
    for members in (plane, [(there["a"], there) for there in line]):

        def copy(step, number, base=base, members=members):
            return pltpu.make_async_remote_copy(
                src_ref=box_ref.at[base + number],
                dst_ref=box_ref.at[base + number],
                send_sem=send_sem.at[base + step],
                recv_sem=recv_sem.at[base + number],
                device_id=place.device(members[step][1]),
                device_id_type=MESH,
            )

        size = len(members)
        mine = members[0][0]
        box_ref[base + mine] = value
        for step in range(1, size):
            copy(step, mine).start()
        for step in range(1, size):
            copy(step, members[step][0]).wait_recv()
        for step in range(1, size):
            copy(step, mine).wait_send()
        value = box_ref[base]
        for other in range(1, size):
            value = value + box_ref[base + other]
        base += size
    return value


def own_squares(place, out_ref, amount):
    rows = out_ref.shape[0]
    offset = lax.rem(place.index(place.here) * amount, 128)
    position = (
        lax.broadcasted_iota(jnp.int32, (rows, 128), 0) * 128
        + lax.broadcasted_iota(jnp.int32, (rows, 128), 1)
        - offset
    )
    value = jnp.where((position >= 0) & (position < amount), out_ref[...], 0.0)
    return jnp.sum(jnp.sum(value * value, 0, keepdims=True), 1, keepdims=True)


def weight_grad_flat(a_ref, b_ref, flat_ref, base, breadth):
    wide = breadth // 128
    for start in range(0, breadth, 512):
        value = dot(a_ref[...], b_ref[:, start : start + 512], 0, 0)
        store_flat(value, flat_ref, base + start // 128, wide)


def store_flat(value, flat_ref, base, wide):
    rows, columns = value.shape
    for part in range(columns // 128):
        flat_ref[pl.ds(base + part, rows, stride=wide), :] = value[:, part * 128 : (part + 1) * 128]


def encoder_backward(place, images, stored, dmem, weights, decoder_blocks, amounts, loss_block):
    rows = images.shape[0]
    tables = rows // IMG
    qkv, mixed, lse, middle = stored
    bases = {name: base for name, _, _, base in layout_bases(encoder_layout())}
    block, small = decoder_blocks.shape[1], block_rows(amounts[0])
    flat_count = flat_rows(amounts[0], place.count)
    first_early = -(-bases["out"] * 128 // amounts[0])
    end_early = max((bases["norms"] - amounts[0] // 128 - 2) * 128 // amounts[0], first_early)
    steps = place.plane() + place.sizes["a"]
    early = lambda owner: (owner >= first_early) & (owner < end_early)
    late = lambda owner: owner < first_early
    latest = lambda owner: owner >= end_early

    def kernel(
        x_hbm, qkv_hbm, o_hbm, lse_ref, x1_hbm, dmem_hbm, w_qkv_hbm, w_out_hbm, w_in_hbm, w_ffo_hbm, norms, own_ref, loss_ref,
        encoder_ref, decoder_ref, stat_ref,
        w_qkv, h_ref, g_ref, og_ref, qkv_ref, delta_ref, d_norms, flat_ref, fetch_sem, o_ref, x1_ref, dmem_ref, w_out, w_in, w_ffo,
        theirs_ref, mine_ref, got_ref, far_mine_ref, far_got_ref, *signals,
    ):
        far = (None, own_ref, far_mine_ref, far_got_ref, *signals[:3])
        near = (theirs_ref, mine_ref, got_ref, None, *signals[3:5])
        box_ref, box_send, box_recv = signals[5:]
        work = functools.partial(reduce_stage, place)
        place.locate()
        fetches = [
            pltpu.make_async_copy(source, target, fetch_sem.at[k])
            for k, (source, target) in enumerate(
                (
                    (qkv_hbm, qkv_ref), (w_qkv_hbm, w_qkv), (x_hbm, g_ref.at[:, :D]), (x1_hbm, x1_ref), (dmem_hbm, dmem_ref),
                    (w_in_hbm, w_in), (w_ffo_hbm, w_ffo), (o_hbm, o_ref), (w_out_hbm, w_out),
                )
            )
        ]
        x_ref = g_ref.at[:, :D]
        for number in (3, 4, 5, 6, 7, 8, 0, 1):
            fetches[number].start()
        place.greet(True)
        work(lambda one: one.to_sibling(), *far)
        tail = bases["norms"] + 4 * D // 128
        flat_ref[tail:, :] = jnp.zeros((flat_count - tail, 128), f32)
        fetches[3].wait()
        norm_all(x1_ref, norms, 2, h_ref, rows, IMG_CHUNK)
        for number in (4, 5, 6, 7, 8):
            fetches[number].wait()
        og_ref[...] = dmem_ref[...].astype(bf16)
        for start in range(0, FF, 256):
            lanes = slice(start, start + 256)
            inner = dot(h_ref[...], w_in[:, lanes])
            back = dot(og_ref[...], w_ffo[lanes, :], 1, 1)
            part = dot(gelu(inner).astype(bf16), og_ref[...], 0, 0)
            store_flat(part, flat_ref, bases["ffn_out"] + start * 4, 4)
            g_ref[:, lanes] = (gelu_slope(inner) * back).astype(bf16)
        work(lambda one: one.third(), *far)
        weight_grad_flat(h_ref, g_ref, flat_ref, bases["ffn_in"], FF)

        def keep(part, down):
            og_ref[part, :] = (down + dmem_ref[part, :]).astype(bf16)

        norm_all_back(
            x1_ref, norms, 2, lambda part: dot(g_ref[part, :], w_in[...], 1, 1), d_norms, rows, IMG_CHUNK, keep
        )
        fetches[2].start()
        weight_grad_flat(o_ref, og_ref, flat_ref, bases["out"], D)
        cut_for_reduction(place, early, flat_ref, amounts[0], mine_ref, theirs_ref)
        work(lambda one: one.to_sibling(), early, *near)

        def project_rows(part):
            og_ref[part, :] = dot(og_ref[part, :], w_out[...], 1, 1).astype(bf16)

        each_rows(rows, IMG_CHUNK, project_rows)
        head_sums(tables, og_ref, o_ref, delta_ref, IMG)
        work(lambda one: one.second(), *far)
        fetches[0].wait()

        def between(step):
            @pl.when(step == 1)
            def _():
                work(lambda one: one.third(), early, *near)

            @pl.when(step == 2)
            def _():
                work(lambda one: one.first(), *far)

            @pl.when(step == 4)
            def _():
                work(lambda one: one.second(), early, *near)

            @pl.when(step == 5)
            def _():
                work(lambda one: one.last(decoder_ref), *far)

            @pl.when(step == 6)
            def _():
                work(lambda one: one.first(), early, *near)

        attend_back(
            (0, tables), qkv_ref, qkv_ref, D, qkv_ref, 2 * D, og_ref, lse_ref, delta_ref,
            qkv_ref, qkv_ref, qkv_ref, IMG, IMG, False, between,
        )
        work(lambda one: one.last(encoder_ref), early, *near)
        fetches[1].wait()
        fetches[2].wait()
        norm_all(x_ref, norms, 0, h_ref, rows, IMG_CHUNK)
        weight_grad_flat(h_ref, qkv_ref, flat_ref, bases["qkv"], 3 * D)
        cut_for_reduction(place, late, flat_ref, amounts[0], mine_ref, theirs_ref)
        work(lambda one: one.to_sibling(), late, *near)
        for table in range(tables):
            norm_all_back(
                x_ref, norms, 0, lambda part: dot(qkv_ref[part, :], w_qkv[...], 1, 1), d_norms,
                (table + 1) * IMG, IMG, None, table * IMG,
            )
            if table == 0:
                work(lambda one: one.third(), late, *near)
        store_flat(d_norms[...], flat_ref, bases["norms"], 4)
        cut_for_reduction(place, latest, flat_ref, amounts[0], mine_ref, theirs_ref)
        work(lambda one: one.to_sibling(), latest, *near)
        work(lambda one: one.second(), late, *near)
        work(lambda one: one.third(), latest, *near)
        work(lambda one: one.first(), late, *near)
        work(lambda one: one.second(), latest, *near)
        work(lambda one: one.first(), latest, *near)
        work(lambda one: one.last(encoder_ref), late, *near)
        work(lambda one: one.last(encoder_ref), latest, *near)
        squares = own_squares(place, encoder_ref, amounts[0]) + own_squares(
            place, decoder_ref, amounts[1]
        )
        me = place.index(place.here)
        for ref, amount in ((encoder_ref, amounts[0]), (decoder_ref, amounts[1])):
            ref[...] = shifted_back(ref[...], lax.rem(me * amount, 128))
        index = lax.broadcasted_iota(jnp.int32, (8, 128), 0)
        value = jnp.where(index == 0, squares, jnp.where(index == 1, loss_ref[...], 0.0))
        stat_ref[...] = sum_everywhere(place, value, box_ref, box_send, box_recv)
        work(lambda one: one.close(), *far)
        work(lambda one: one.close(), early, *near)

    vmem, hbm = pl.BlockSpec(memory_space=pltpu.VMEM), pl.BlockSpec(memory_space=pl.ANY)
    count = place.count
    return pl.pallas_call(
        kernel,
        out_shape=(
            jax.ShapeDtypeStruct((small, 128), f32),
            jax.ShapeDtypeStruct((block, 128), f32),
            jax.ShapeDtypeStruct((8, 128), f32),
        ),
        in_specs=[hbm, hbm, hbm, vmem, hbm, hbm, hbm, hbm, hbm, hbm, vmem, hbm, vmem],
        scratch_shapes=[
            pltpu.VMEM((D, 3 * D), bf16),
            pltpu.VMEM((rows, D), bf16),
            pltpu.VMEM((rows, FF), bf16),
            pltpu.VMEM((rows, D), bf16),
            pltpu.VMEM((rows, 3 * D), bf16),
            pltpu.VMEM((tables * HEADS, IMG), f32),
            pltpu.VMEM((4, D), f32),
            pltpu.VMEM((flat_count, 128), f32),
            pltpu.SemaphoreType.DMA((9,)),
            pltpu.VMEM((rows, D), bf16),
            pltpu.VMEM((rows, D), f32),
            pltpu.VMEM((rows, D), f32),
            pltpu.VMEM((D, D), bf16),
            pltpu.VMEM((D, FF), bf16),
            pltpu.VMEM((FF, D), bf16),
            pltpu.VMEM((count // 2, small, 128), bf16),
            *reduction_memory(count, small),
            *reduction_memory(count, block),
            *reduction_signals(count, True),
            *reduction_signals(count, False),
            pltpu.VMEM((steps, 8, 128), f32),
            pltpu.SemaphoreType.DMA((steps,)),
            pltpu.SemaphoreType.DMA((steps,)),
        ],
        compiler_params=pltpu.CompilerParams(
            collective_id=2, has_side_effects=True, vmem_limit_bytes=VMEM_LIMIT
        ),
        name="encoder_backward",
    )(
        images, qkv, mixed, lse, middle, dmem, weights["qkv"], weights["out"], weights["ffn_in"], weights["ffn_out"],
        weights["norms"], decoder_blocks, loss_block,
    )


class Spread:
    def __init__(self, place, core, view, send_sem, recv_sem):
        self.place, self.view, self.send_sem, self.recv_sem = place, view, send_sem, recv_sem
        self.order = ORDERS[core]
        self.s1, self.s2, self.s3 = (place.sizes[part] for part in self.order)
        self.base2 = self.s1 - 1
        self.base3 = self.base2 + self.s1 * (self.s2 - 1)
        self.base4 = self.base3 + self.s1 * self.s2 * (self.s3 - 1)

    def copy(self, p, q, r, core, part, step, number):
        one, two, three = self.order
        block = self.place.index(self.place.moved({one: p, two: q, three: r, "c": core}))
        return pltpu.make_async_remote_copy(
            src_ref=self.view(block),
            dst_ref=self.view(block),
            send_sem=self.send_sem.at[number],
            recv_sem=self.recv_sem.at[block],
            device_id=self.place.device(self.place.moved({part: step})),
            device_id_type=MESH,
        )

    def arrived(self, p, q, r, core=0):
        self.copy(p, q, r, core, "c", 1, 0).wait_recv()

    def to_sibling(self, p, q, r):
        number = self.base4 + (p * self.s2 + q) * self.s3 + r
        self.copy(p, q, r, 0, "c", 1, number).start()

    def to_third(self, p, q):
        for step in range(1, self.s3):
            number = self.base3 + (p * self.s2 + q) * (self.s3 - 1) + step - 1
            self.copy(p, q, 0, 0, self.order[2], step, number).start()

    def to_second(self, p):
        for step in range(1, self.s2):
            number = self.base2 + p * (self.s2 - 1) + step - 1
            self.copy(p, 0, 0, 0, self.order[1], step, number).start()

    def one(self):
        @pl.loop(1, self.s1)
        def _(step):
            self.copy(0, 0, 0, 0, self.order[0], step, step - 1).start()

        self.to_second(0)
        self.to_third(0, 0)
        self.to_sibling(0, 0, 0)

    def two(self):
        @pl.loop(1, self.s1)
        def _(p):
            self.arrived(p, 0, 0)
            self.to_second(p)
            self.to_third(p, 0)
            self.to_sibling(p, 0, 0)

    def three(self):
        @pl.loop(0, self.s1 * (self.s2 - 1))
        def _(number):
            p, q = lax.rem(number, self.s1), lax.div(number, self.s1) + 1
            self.arrived(p, q, 0)
            self.to_third(p, q)
            self.to_sibling(p, q, 0)

    def four(self):
        @pl.loop(0, self.s1 * self.s2 * (self.s3 - 1))
        def _(number):
            p, q = lax.rem(number, self.s1), lax.rem(lax.div(number, self.s1), self.s2)
            r = lax.div(number, self.s1 * self.s2) + 1
            self.arrived(p, q, r)
            self.to_sibling(p, q, r)

    def five(self):
        @pl.loop(0, self.s1 * self.s2 * self.s3)
        def _(number):
            p, q = lax.rem(number, self.s1), lax.rem(lax.div(number, self.s1), self.s2)
            self.arrived(p, q, lax.div(number, self.s1 * self.s2), 1)

    def close(self):
        @pl.loop(0, self.place.count - 1)
        def _(number):
            self.copy(0, 0, 0, 0, "c", 1, number).wait_send()


def shifted(value, offset):
    lane = lax.broadcasted_iota(jnp.int32, value.shape, 1)
    turned = pltpu.roll(value, offset, 1)
    return jnp.where(lane < offset, pltpu.roll(turned, 1, 0), turned)


def shifted_back(value, offset):
    lane = lax.broadcasted_iota(jnp.int32, value.shape, 1)
    turned = pltpu.roll(value, lax.rem(128 - offset, 128), 1)
    return jnp.where(lane < 128 - offset, turned, pltpu.roll(turned, value.shape[0] - 1, 0))


def gather_and_encode(place, images, encoder_block, decoder_block, counts, amounts):
    rows = images.shape[0]
    tables = rows // IMG
    count = place.count
    layouts = (encoder_layout(), decoder_layout())
    shapes = [weight_shapes(layout) for layout in layouts]
    small, large = encoder_block.shape[0], decoder_block.shape[0]
    near, cut = small // 32 * 16, large // 32 * 16
    flat_counts = [flat_rows(amount, count) for amount in amounts]
    first, second = len(shapes[0]), len(shapes[1])
    matrices = [name for name in shapes[0] if name != "norms"]

    def kernel(x_ref, encoder_ref, decoder_ref, counts_ref, *refs):
        encoder_out = dict(zip(shapes[0], refs[:first]))
        decoder_out = dict(zip(shapes[1], refs[first : first + second]))
        count_ref, qkv_out, o_ref, lse_ref, x1_ref, mem_ref = refs[first + second : first + second + 6]
        rest = refs[first + second + 6 :]
        encoder_all, decoder_all, flat_ref, qkv_ref, h_ref, g_ref = rest[:6]
        local = dict(zip(matrices, rest[6 : 6 + len(matrices)]))
        local["norms"] = encoder_out["norms"]
        out_sem = rest[6 + len(matrices)]
        signals = rest[7 + len(matrices) :]
        views = (
            lambda block: encoder_all.at[block, :near],
            lambda block: encoder_all.at[block, near:],
            lambda block: decoder_all.at[block, :cut],
            lambda block: decoder_all.at[block, cut:],
        )
        place.locate()
        me = place.index(place.here)

        def go(*tasks):
            for core in range(2):

                @pl.when(place.here["c"] == core)
                def _():
                    for group, stage in tasks:
                        work = Spread(place, core, views[group], *signals[2 * group : 2 * group + 2])
                        getattr(work, stage)()

        own = shifted(encoder_ref[...], lax.rem(me * amounts[0], 128))
        row = lax.broadcasted_iota(jnp.int32, own.shape, 0)
        encoder_all[me] = jnp.where(row == small - 1, counts_ref[...], own).astype(bf16)
        place.greet()
        go((0, "one"), (1, "one"))
        decoder_all[me] = shifted(decoder_ref[...], lax.rem(me * amounts[1], 128)).astype(bf16)
        go(
            (0, "two"), (1, "two"), (0, "three"), (2, "one"), (1, "three"), (3, "one"), (0, "four"), (1, "four"), (0, "five"), (1, "five"),
        )
        total = jnp.zeros((1, 128), f32)
        for device in range(count):
            total = total + encoder_all[device, small - 16 :, :].astype(f32)[15:16]
        count_ref[...] = jnp.broadcast_to(jnp.sum(total, 1, keepdims=True), count_ref.shape)
        place_blocks(encoder_all, flat_ref, amounts[0])
        take_matrices(flat_ref, layouts[0], local)
        outs = [
            pltpu.make_async_copy(local[name], encoder_out[name], out_sem.at[k])
            for k, name in enumerate(matrices)
        ]
        outs.append(pltpu.make_async_copy(qkv_ref, qkv_out, out_sem.at[len(matrices)]))
        for out in outs[:-1]:
            out.start()
        go((2, "two"), (3, "two"))
        norms = local["norms"]
        norm_all(x_ref, norms, 0, h_ref, rows, IMG_CHUNK)
        project(h_ref, local["qkv"], qkv_ref, 3 * D, 0.125)
        outs[-1].start()

        def between(step):
            for number, task in ((0, (2, "three")), (1, (3, "three")), (4, (2, "four")), (7, (3, "four"))):

                @pl.when(step == number)
                def _():
                    go(task)

        attend_with(
            tables, qkv_ref, qkv_ref, D, qkv_ref, 2 * D, o_ref, lse_ref, IMG, IMG, False, True, between
        )
        add_project(x_ref, o_ref, local["out"], x1_ref)
        norm_all(x1_ref, norms, 2, h_ref, rows, IMG_CHUNK)

        @pl.loop(0, tables)
        def _(table):
            part = pl.ds(pl.multiple_of(table * IMG, 16), IMG)
            for start in range(0, FF, 256):
                lanes = slice(start, start + 256)
                g_ref[:, lanes] = gelu(dot(h_ref[part, :], local["ffn_in"][:, lanes])).astype(bf16)
            for start in range(0, D, 256):
                lanes = slice(start, start + 256)
                value = x1_ref[part, lanes] + dot(g_ref[...], local["ffn_out"][:, lanes])
                mem_ref[part, lanes] = value.astype(bf16)

        go((2, "five"), (3, "five"))
        place_blocks(decoder_all, flat_ref, amounts[1])
        take_matrices(flat_ref, layouts[1], decoder_out)
        go((0, "close"), (1, "close"), (2, "close"), (3, "close"))
        for out in outs:
            out.wait()

    vmem, hbm = pl.BlockSpec(memory_space=pltpu.VMEM), pl.BlockSpec(memory_space=pl.ANY)
    outs = pl.pallas_call(
        kernel,
        out_shape=(
            *shapes[0].values(),
            *shapes[1].values(),
            jax.ShapeDtypeStruct((8, 128), f32),
            jax.ShapeDtypeStruct((rows, 3 * D), bf16),
            jax.ShapeDtypeStruct((rows, D), bf16),
            jax.ShapeDtypeStruct((tables * HEADS, IMG), f32),
            jax.ShapeDtypeStruct((rows, D), f32),
            jax.ShapeDtypeStruct((rows, D), bf16),
        ),
        in_specs=[vmem] * 4,
        out_specs=(
            *[vmem if name == "norms" else hbm for name in shapes[0]],
            *[vmem] * second,
            vmem, hbm, vmem, vmem, vmem, vmem,
        ),
        scratch_shapes=[
            pltpu.VMEM((count, small, 128), bf16),
            pltpu.VMEM((count, large, 128), bf16),
            pltpu.VMEM((max(flat_counts), 128), f32),
            pltpu.VMEM((rows, 3 * D), bf16),
            pltpu.VMEM((rows, D), bf16),
            pltpu.VMEM((IMG, FF), bf16),
            *[pltpu.VMEM(shapes[0][name].shape, bf16) for name in matrices],
            pltpu.SemaphoreType.DMA((len(matrices) + 1,)),
            *[pltpu.SemaphoreType.DMA((n,)) for n in (count - 1, count) * 4],
        ],
        compiler_params=pltpu.CompilerParams(
            collective_id=1, has_side_effects=True, vmem_limit_bytes=VMEM_LIMIT
        ),
        name="gather_and_encode",
    )(images, encoder_block, decoder_block, counts)
    encoder_weights = dict(zip(shapes[0], outs[:first]))
    decoder_weights = dict(zip(shapes[1], outs[first : first + second]))
    number, *stored, memory = outs[first + second :]
    return encoder_weights, decoder_weights, number[0, 0], stored, memory


def adam_update(gradient, master, first_state, second_state, average):
    first_new = BETA_ONE * first_state + (1.0 - BETA_ONE) * gradient
    second_new = BETA_TWO * second_state + (1.0 - BETA_TWO) * gradient * gradient
    first_hat = first_new / (1.0 - BETA_ONE**STEP)
    second_hat = second_new / (1.0 - BETA_TWO**STEP)
    master_new = master - LEARN_RATE * (
        first_hat / (jnp.sqrt(second_hat) + EPSILON) + WEIGHT_DECAY * master
    )
    average_new = SMOOTH * average + (1.0 - SMOOTH) * master_new
    return (first_new, second_new, master_new, average_new)


def shard_block(shard):
    rows = block_rows(shard.shape[0])
    return jnp.pad(shard, (0, rows * 128 - shard.shape[0])).reshape(rows, 128)


def on_device(place, *arguments):
    (
        images, tag_ids, tag_lengths, cell_mask, cell_index, box_targets,
        encoder_params, encoder_first, encoder_second, encoder_average,
        decoder_params, decoder_first, decoder_second, decoder_average,
    ) = arguments
    encoder_amount, decoder_amount = encoder_params.shape[0], decoder_params.shape[0]
    cell_slots = jnp.arange(CELLS)
    alive = ((cell_mask > 0) & (cell_slots[None, :] < (tag_lengths // 4)[:, None])).astype(f32)
    cells = cell_index % tag_lengths[:, None]
    counted = (jnp.arange(TAGS)[None, :] < (tag_lengths - 1)[:, None]).astype(f32)
    upcoming = jnp.roll(tag_ids, -1, 1)
    prepared = (
        tag_ids[:, None, :], upcoming[:, None, :], counted[:, None, :], cells[:, None, :], alive[:, None, :], box_targets,
    )

    counts = jnp.sum(alive, 1)
    counts = jnp.pad(counts, (0, 128 - counts.shape[0])).reshape(1, 128)
    amounts = (encoder_amount, decoder_amount)
    encoder_weights, decoder_weights, cell_total, stored, memory = gather_and_encode(
        place, images, shard_block(encoder_params), shard_block(decoder_params), counts, amounts
    )
    scale = (1.0 / cell_total).reshape(1, 1)
    loss_block, dmemory, decoder_grads = decoder_step(prepared, scale, memory, decoder_weights)
    decoder_packed = pack_grads(
        decoder_grads, decoder_layout(), decoder_amount, place.count, "pack_decoder"
    )
    encoder_sum, decoder_sum, stats = encoder_backward(
        place, images, stored, dmemory, encoder_weights, decoder_packed, amounts, loss_block
    )
    grad_norm = jnp.sqrt(stats[0, 0])
    factor = CLIP_NORM / jnp.maximum(grad_norm, CLIP_NORM)
    encoder_grad = encoder_sum.reshape(-1)[:encoder_amount]
    decoder_grad = decoder_sum.reshape(-1)[:decoder_amount]
    encoder_new = adam_update(
        encoder_grad * factor, encoder_params, encoder_first, encoder_second, encoder_average
    )
    decoder_new = adam_update(
        decoder_grad * factor, decoder_params, decoder_first, decoder_second, decoder_average
    )
    return (stats[1, 0], cell_total, grad_norm, *encoder_new, *decoder_new)


def solution(mesh):
    rows, flat = P(AXES, None), P(AXES)
    return jax.shard_map(
        functools.partial(on_device, Place(mesh.shape["wide"], mesh.shape["narrow"])),
        mesh=mesh,
        in_specs=(rows, rows, flat, rows, rows, P(AXES, None, None)) + (flat,) * 8,
        out_specs=(P(), P(), P()) + (flat,) * 8,
        check_vma=False,
    )
```

```python
import functools

import jax
import jax.numpy as jnp
from jax import lax
from jax.experimental import pallas as pl
from jax.experimental.pallas import tpu as pltpu
from jax.sharding import PartitionSpec as P

D = 512
HEADS = 8
HEAD = D // HEADS
PAIRS = HEADS // 2
FF = 1024
V = 32
IMG = 784
TAGS = 512
STEP = 5
CELLS = 128
IMG_CHUNK = 784
TAG_CHUNK = 512
SAFE_SCORE = 50.0

BETA_ONE = 0.5
BETA_TWO = 0.5
CLIP_NORM = 0.01
LEARN_RATE = 0.05
WEIGHT_DECAY = 0.01
EPSILON = 1e-08
SMOOTH = 0.9

VMEM_LIMIT = 62 * 2**20
bf16 = jnp.bfloat16
f32 = jnp.float32


def encoder_layout():
    return [
        ("qkv", (D, 3 * D)),
        ("out", (D, D)),
        ("ffn_in", (D, FF)),
        ("ffn_out", (FF, D)),
        ("norms", (4, D)),
    ]


def decoder_layout():
    return [
        ("qkv", (D, 3 * D)),
        ("out", (D, D)),
        ("cross_q", (D, D)),
        ("cross_kv", (D, 2 * D)),
        ("cross_out", (D, D)),
        ("ffn_in", (D, FF)),
        ("ffn_out", (FF, D)),
        ("embed", (V, D)),
        ("head", (D, V)),
        ("box_in", (D, D)),
        ("norms", (8, D)),
        ("box_out", (D, 4)),
    ]


def dot(left, right, over_left=1, over_right=0):
    return lax.dot_general(
        left, right, (((over_left,), (over_right,)), ((), ())), preferred_element_type=f32
    )


def each_rows(total, step, body, first=0):
    @pl.loop(first // step, total // step)
    def _(index):
        body(pl.ds(pl.multiple_of(index * step, step), step))


def norm_rows(value, gain, shift):
    centred = value - jnp.mean(value, -1, keepdims=True)
    variance = jnp.mean(centred * centred, -1, keepdims=True)
    return centred * lax.rsqrt(variance + 1e-05) * gain + shift


def norm_rows_back(value, gain, upstream):
    centred = value - jnp.mean(value, -1, keepdims=True)
    variance = jnp.mean(centred * centred, -1, keepdims=True)
    scale = lax.rsqrt(variance + 1e-05)
    unit = centred * scale
    inner = upstream * gain
    mean_inner = jnp.mean(inner, -1, keepdims=True)
    mean_both = jnp.mean(inner * unit, -1, keepdims=True)
    down = scale * (inner - mean_inner - unit * mean_both)
    return (
        down,
        jnp.sum(upstream * unit, 0, keepdims=True),
        jnp.sum(upstream, 0, keepdims=True),
    )


GELU_A = 0.7978845608028654
GELU_B = 0.044715


def gelu(value):
    inner = jnp.tanh(GELU_A * (value + GELU_B * value * value * value))
    return 0.5 * value * (1.0 + inner)


def gelu_slope(value):
    square = value * value
    inner = jnp.tanh(GELU_A * (value + GELU_B * square * value))
    slope = GELU_A * (1.0 + 3.0 * GELU_B * square)
    return 0.5 * (1.0 + inner) + 0.5 * value * (1.0 - inner * inner) * slope


def half_masks():
    lane = lax.broadcasted_iota(jnp.int32, (1, 2 * HEAD), 1)
    first = (lane < HEAD).astype(f32)
    return (first.astype(bf16), (1.0 - first).astype(bf16))


def query_blocks(query_rows, key_rows, causal):
    if not causal:
        return [(0, query_rows, key_rows)]
    return [(start, 256, start + 256) for start in range(0, query_rows, 256)]


def key_tiles(start, depth, causal):
    if not causal or start == 0:
        return [(0, depth)]
    return [(0, start), (start, depth)]


def causal_keep(depth, width):
    key = lax.broadcasted_iota(jnp.int32, (depth, width), 0)
    query = lax.broadcasted_iota(jnp.int32, (depth, width), 1)
    return key <= query


def head_members():
    row = lax.broadcasted_iota(jnp.int32, (16, D), 0)
    lane = lax.broadcasted_iota(jnp.int32, (16, D), 1)
    return (lax.shift_right_logical(lane, 6) == row).astype(f32).astype(bf16)


def largest_norm(ref, column, rows, start):
    value = ref[start : start + rows, column : column + D]
    return jnp.max(dot(head_members(), value * value, 1, 1), 1, keepdims=True)


def attend(tables, q_ref, k_ref, k_col, v_ref, v_col, o_ref, lse_ref, query_rows, key_rows, causal):
    bound = jnp.zeros((16, 1), f32)
    for table in range(tables):
        of_queries = largest_norm(q_ref, 0, query_rows, table * query_rows)
        of_keys = largest_norm(k_ref, k_col, key_rows, table * key_rows)
        bound = jnp.maximum(bound, of_queries * of_keys)
    small = jnp.max(bound) < (0.98 * SAFE_SCORE) ** 2
    for wanted in (True, False):

        @pl.when(small == wanted)
        def _():
            attend_with(
                tables, q_ref, k_ref, k_col, v_ref, v_col, o_ref, lse_ref,
                query_rows, key_rows, causal, not wanted,
            )


def attend_with(
    tables, q_ref, k_ref, k_col, v_ref, v_col, o_ref, lse_ref, query_rows, key_rows, causal, take_peak, between=None,
):
    masks = half_masks()
    blocks = query_blocks(query_rows, key_rows, causal)

    @pl.loop(0, tables * PAIRS)
    def _(step):
        table = lax.div(step, PAIRS)
        pair = lax.rem(step, PAIRS)
        q_rows = pl.ds(pl.multiple_of(table * query_rows, 16), query_rows)
        k_rows = pl.ds(pl.multiple_of(table * key_rows, 16), key_rows)
        lanes = pl.multiple_of(pair * 128, 128)
        queries = q_ref[q_rows, pl.ds(lanes, 128)]
        keys = k_ref[k_rows, pl.ds(k_col + lanes, 128)]
        values = v_ref[k_rows, pl.ds(v_col + lanes, 128)].T
        scores = {}
        for half in range(2):
            own = queries * masks[half]
            for start, width, depth in blocks:
                for low, high in key_tiles(start, depth, causal):
                    tile = dot(keys[low:high], own[start : start + width], 1, 1)
                    if causal and low == start:
                        tile = jnp.where(causal_keep(high - low, width), tile, -1e30)
                    scores[half, start, low] = tile
        outs = []
        for half in range(2):
            own_values = values[half * HEAD : (half + 1) * HEAD, :]
            parts, sums = [], []
            for start, width, depth in blocks:
                tiles = key_tiles(start, depth, causal)
                weights = [scores[half, start, low] for low, _ in tiles]
                peak = jnp.zeros((1, width), f32)
                if take_peak:
                    peak = functools.reduce(
                        jnp.maximum, [jnp.max(tile, 0, keepdims=True) for tile in weights]
                    )
                    weights = [tile - peak for tile in weights]
                weights = [jnp.exp(tile) for tile in weights]
                total = sum(jnp.sum(tile, 0, keepdims=True) for tile in weights)
                mixed = sum(
                    dot(own_values[:, low:high], tile.astype(bf16))
                    for tile, (low, high) in zip(weights, tiles)
                )
                parts.append(mixed * (1.0 / total))
                sums.append(peak + jnp.log(total))
            outs.append(parts[0] if len(parts) == 1 else jnp.concatenate(parts, 1))
            lse_ref[pl.ds(table * HEADS + pair * 2 + half, 1), :] = (
                sums[0] if len(sums) == 1 else jnp.concatenate(sums, 1)
            )
        joined = jnp.concatenate(outs, 0).astype(bf16)
        o_ref[q_rows, pl.ds(lanes, 128)] = joined.T
        if between is not None:
            between(step)


def head_sums(tables, up_ref, o_ref, delta_ref, query_rows):
    member = head_members()
    for table in range(tables):
        rows = slice(table * query_rows, (table + 1) * query_rows)
        both = up_ref[rows, :].astype(f32) * o_ref[rows, :].astype(f32)
        high = both.astype(bf16)
        rest = (both - high.astype(f32)).astype(bf16)
        sums = dot(member, high, 1, 1) + dot(member, rest, 1, 1)
        delta_ref[table * HEADS : (table + 1) * HEADS, :] = sums[:HEADS]


def attend_back(
    span_of_tables, q_ref, k_ref, k_col, v_ref, v_col, up_ref, lse_ref, delta_ref,
    dq_ref, dk_ref, dv_ref, query_rows, key_rows, causal, between=None,
):
    masks = half_masks()

    @pl.loop(span_of_tables[0] * PAIRS, span_of_tables[1] * PAIRS)
    def _(step):
        table = lax.div(step, PAIRS)
        pair = lax.rem(step, PAIRS)
        q_rows = pl.ds(pl.multiple_of(table * query_rows, 16), query_rows)
        k_rows = pl.ds(pl.multiple_of(table * key_rows, 16), key_rows)
        lanes = pl.multiple_of(pair * 128, 128)
        queries = q_ref[q_rows, pl.ds(lanes, 128)]
        keys = k_ref[k_rows, pl.ds(k_col + lanes, 128)]
        values = v_ref[k_rows, pl.ds(v_col + lanes, 128)]
        upstream = up_ref[q_rows, pl.ds(lanes, 128)]
        keys_across = keys.T
        blocks = query_blocks(query_rows, key_rows, causal)
        grad_q = []
        grad_k = [None] * len(blocks)
        grad_v = [None] * len(blocks)
        ahead = {}
        if causal:
            for half in range(2):
                own, own_up = queries * masks[half], upstream * masks[half]
                for number, (start, width, depth) in enumerate(blocks):
                    span = slice(start, start + width)
                    ahead[half, number] = (
                        dot(keys[:depth], own[span], 1, 1),
                        dot(values[:depth], own_up[span], 1, 1),
                    )
        for half in range(2):
            index = pl.ds(table * HEADS + pair * 2 + half, 1)
            own = queries * masks[half]
            own_up = upstream * masks[half]
            logsum = lse_ref[index, :]
            delta = delta_ref[index, :]
            across = keys_across[half * HEAD : (half + 1) * HEAD, :]
            parts = []
            for number, (start, width, depth) in enumerate(blocks):
                span = slice(start, start + width)
                if causal:
                    scores, pull = ahead[half, number]
                else:
                    scores = dot(keys[:depth], own[span], 1, 1)
                    pull = dot(values[:depth], own_up[span], 1, 1)
                weight = jnp.exp(scores - logsum[:, span])
                if causal:
                    edge = jnp.where(causal_keep(width, width), weight[start:], 0.0)
                    weight = edge if start == 0 else jnp.concatenate([weight[:start], edge], 0)
                change = (weight * (pull - delta[:, span])).astype(bf16)
                add_v = dot(weight.astype(bf16), own_up[span])
                add_k = dot(change, own[span])
                grad_v[number] = add_v if half == 0 else grad_v[number] + add_v
                grad_k[number] = add_k if half == 0 else grad_k[number] + add_k
                parts.append(dot(across[:, :depth], change) * 0.125)
            grad_q.append(parts[0] if len(parts) == 1 else jnp.concatenate(parts, 1))
        dq_ref[q_rows, pl.ds(lanes, 128)] = jnp.concatenate(grad_q, 0).astype(bf16).T
        for ref, column, grads in ((dk_ref, k_col, grad_k), (dv_ref, v_col, grad_v)):
            total = grads[-1]
            if len(grads) == 2:
                low = blocks[0][2]
                total = jnp.concatenate([total[:low] + grads[0], total[low:]], 0)
            ref[k_rows, pl.ds(column + lanes, 128)] = total.astype(bf16)
        if between is not None:
            between(step)


def project(a_ref, w_ref, out_ref, width, first_scale=None):
    for start in range(0, width, 512):
        value = dot(a_ref[...], w_ref[:, start : start + 512])
        if first_scale is not None and start == 0:
            value = value * first_scale
        out_ref[:, start : start + 512] = value.astype(bf16)


def add_project(base_ref, a_ref, w_ref, out_ref):
    for start in range(0, D, 256):
        lanes = slice(start, start + 256)
        out_ref[:, lanes] = base_ref[:, lanes].astype(f32) + dot(a_ref[...], w_ref[:, lanes])


def weight_grad(a_ref, b_ref, out_ref):
    rows, columns = out_ref.shape
    for start in range(0, columns, 512):
        lanes = slice(start, start + 512)
        out_ref[:, lanes] = dot(a_ref[...], b_ref[:, lanes], 0, 0).astype(out_ref.dtype)


def ffn_forward(h_ref, w_in, u_ref, g_ref):
    for start in range(0, FF, 256):
        lanes = slice(start, start + 256)
        inner = dot(h_ref[...], w_in[:, lanes])
        if u_ref is not None:
            u_ref[:, lanes] = inner
        g_ref[:, lanes] = gelu(inner).astype(bf16)


def ffn_backward(og_ref, h_ref, u_ref, g_ref, w_in, w_out, d_in, d_out, dh_ref):
    weight_grad(g_ref, og_ref, d_out)
    for start in range(0, FF, 256):
        lanes = slice(start, start + 256)
        back = dot(og_ref[...], w_out[lanes, :], 1, 1)
        g_ref[:, lanes] = (gelu_slope(u_ref[:, lanes]) * back).astype(bf16)
    weight_grad(h_ref, g_ref, d_in)
    project_back(g_ref, w_in, dh_ref)


def project_back(g_ref, w_ref, out_ref):
    for start in range(0, D, 256):
        lanes = slice(start, start + 256)
        out_ref[:, lanes] = dot(g_ref[...], w_ref[lanes, :], 1, 1).astype(out_ref.dtype)


def norm_all(x_ref, norms_ref, row, out_ref, total, step):
    gain, shift = norms_ref[row : row + 1, :], norms_ref[row + 1 : row + 2, :]

    def body(rows):
        out_ref[rows, :] = norm_rows(x_ref[rows, :].astype(f32), gain, shift).astype(bf16)

    each_rows(total, step, body)


def norm_all_back(x_ref, norms_ref, row, upstream, dnorms_ref, total, step, keep, first=0):
    gain = norms_ref[row : row + 1, :]
    if first == 0:
        dnorms_ref[row : row + 2, :] = jnp.zeros((2, D), f32)

    def body(rows):
        arriving = upstream(rows) if callable(upstream) else upstream[rows, :]
        down, d_gain, d_shift = norm_rows_back(x_ref[rows, :].astype(f32), gain, arriving)
        dnorms_ref[row : row + 1, :] += d_gain
        dnorms_ref[row + 1 : row + 2, :] += d_shift
        if keep is not None:
            keep(rows, down)

    each_rows(total, step, body, first)


def soft_low(first_one, other_one):
    return 0.5 * (first_one + other_one - jnp.sqrt((first_one - other_one) ** 2 + 0.0001))


def soft_high(first_one, other_one):
    return 0.5 * (first_one + other_one + jnp.sqrt((first_one - other_one) ** 2 + 0.0001))


def softplus(value):
    return jnp.maximum(value, 0.0) + jnp.log1p(jnp.exp(-jnp.abs(value)))


@jax.custom_vjp
def smooth_relu(value):
    return softplus(value)


def smooth_relu_keep(value):
    return softplus(value), value


def smooth_relu_back(value, upstream):
    return (upstream * (1.0 / (1.0 + jnp.exp(-value))),)


smooth_relu.defvjp(smooth_relu_keep, smooth_relu_back)


def cell_losses(px, py, pw, ph, gx, gy, gw, gh):
    absolute = (
        jnp.sqrt((px - gx) ** 2 + 0.01)
        + jnp.sqrt((py - gy) ** 2 + 0.01)
        + jnp.sqrt((pw - gw) ** 2 + 0.01)
        + jnp.sqrt((ph - gh) ** 2 + 0.01)
    )
    left_p, right_p = px - 0.5 * pw, px + 0.5 * pw
    low_p, top_p = py - 0.5 * ph, py + 0.5 * ph
    left_g, right_g = gx - 0.5 * gw, gx + 0.5 * gw
    low_g, top_g = gy - 0.5 * gh, gy + 0.5 * gh
    across = smooth_relu(20.0 * (soft_low(right_p, right_g) - soft_high(left_p, left_g))) / 20.0
    upward = smooth_relu(20.0 * (soft_low(top_p, top_g) - soft_high(low_p, low_g))) / 20.0
    common = across * upward
    union = pw * ph + gw * gh - common
    hull = (soft_high(right_p, right_g) - soft_low(left_p, left_g)) * (
        soft_high(top_p, top_g) - soft_low(low_p, low_g)
    )
    ratio = common / union - (hull - union) / hull
    return 5.0 * absolute + 2.0 * (1.0 - ratio)


def split_sum(left, value):
    high = value.astype(bf16)
    rest = (value - high.astype(f32)).astype(bf16)
    return dot(left, high) + dot(left, rest)


def decoder_kernel(
    tags_ref, next_ref, counted_ref, place_ref, alive_ref, target_ref, scale_ref, mem_ref,
    w_qkv, w_out, w_cq, w_ckv, w_co, w_in, w_ffo, w_embed, w_head, w_box, norms, w_box_out,
    loss_ref, dmem_ref, d_qkv, d_out, d_cq, d_ckv, d_co, d_in, d_ffo, d_embed, d_head, d_box, d_norms, d_box_out,
    e_ref, h1_ref, qkv_ref, o1_ref, lse1_ref, y1_ref, h2_ref, cq_ref, ckv_ref, o2_ref, lse2_ref, y2_ref,
    h3_ref, u_ref, g_ref, y3_ref, z_ref, dy_ref, dh_ref, og_ref, up_ref, delta_ref, need, done,
):
    tables = tags_ref.shape[0]
    rows = tables * TAGS

    def tag_members(table):
        member = lax.broadcasted_iota(jnp.int32, (V, TAGS), 0) == tags_ref[table]
        return member.astype(f32).astype(bf16)

    for table in range(tables):
        e_ref[table * TAGS : (table + 1) * TAGS, :] = dot(tag_members(table), w_embed[...], 0, 0)
    norm_all(e_ref, norms, 0, h1_ref, rows, TAG_CHUNK)
    need("qkv")
    project(h1_ref, w_qkv, qkv_ref, 3 * D, 0.125)
    attend(tables, qkv_ref, qkv_ref, D, qkv_ref, 2 * D, o1_ref, lse1_ref, TAGS, TAGS, True)
    need("out")
    add_project(e_ref, o1_ref, w_out, y1_ref)
    norm_all(y1_ref, norms, 2, h2_ref, rows, TAG_CHUNK)
    need("cross_q")
    project(h2_ref, w_cq, cq_ref, D, 0.125)
    need("mem")
    need("cross_kv")
    project(mem_ref, w_ckv, ckv_ref, 2 * D)
    attend(tables, cq_ref, ckv_ref, 0, ckv_ref, D, o2_ref, lse2_ref, TAGS, IMG, False)
    need("cross_out")
    add_project(y1_ref, o2_ref, w_co, y2_ref)
    norm_all(y2_ref, norms, 4, h3_ref, rows, TAG_CHUNK)
    need("ffn_in")
    ffn_forward(h3_ref, w_in, u_ref, g_ref)
    need("ffn_out")
    add_project(y2_ref, g_ref, w_ffo, y3_ref)
    norm_all(y3_ref, norms, 6, z_ref, rows, TAG_CHUNK)

    need("box_in")
    scale = scale_ref[0, 0]
    loss = jnp.zeros((1, 1), f32)
    picked, inners, box_ups = [], [], []
    head_sum = jnp.zeros((V, D), f32)
    box_in_sum = jnp.zeros((D, D), f32)
    box_out_sum = jnp.zeros((16, D), f32)
    for table in range(tables):
        own = slice(table * TAGS, (table + 1) * TAGS)
        final = z_ref[own, :]
        logits = dot(w_head[...], final, 1, 1)
        peak = jnp.max(logits, 0, keepdims=True)
        weight = jnp.exp(logits - peak)
        total = jnp.sum(weight, 0, keepdims=True)
        counted = counted_ref[table]
        wanted = lax.broadcasted_iota(jnp.int32, (V, TAGS), 0) == next_ref[table]
        chosen = jnp.sum(jnp.where(wanted, logits - peak - jnp.log(total), 0.0), 0, keepdims=True)
        loss = loss - jnp.sum(counted * chosen, 1, keepdims=True)
        dlogits = (weight / total - wanted.astype(f32)) * counted * scale
        tag_up = dlogits.astype(bf16)
        head_sum = head_sum + dot(tag_up, final)
        dfinal = dot(tag_up, w_head[...], 0, 0)
        select = (
            (lax.broadcasted_iota(jnp.int32, (TAGS, CELLS), 0) == place_ref[table])
            .astype(f32)
            .astype(bf16)
        )
        cells = dot(select, final, 0, 0).astype(bf16)
        inner = dot(cells, w_box[...])
        active = gelu(inner).astype(bf16)
        raw = dot(w_box_out[...], active, 1, 1)
        soft = 1.0 / (1.0 + jnp.exp(-raw))
        ratios = tuple(soft[k : k + 1, :] for k in range(4))
        wished = tuple(target_ref[table, k : k + 1, :] for k in range(4))
        alive = alive_ref[table]
        cell, pull = jax.vjp(lambda *parts: cell_losses(*parts, *wished), *ratios)
        loss = loss + jnp.sum(alive * cell, 1, keepdims=True)
        downs = pull(alive * scale)
        fill = jnp.zeros((16, CELLS), f32)
        index = lax.broadcasted_iota(jnp.int32, (16, CELLS), 0)
        for k in range(4):
            value = downs[k] * ratios[k] * (1.0 - ratios[k])
            fill = jnp.where(index == k, value, fill)
        box_up = fill.astype(bf16)
        box_out_sum = box_out_sum + dot(box_up, active)
        dinner = (gelu_slope(inner) * dot(box_up, w_box_out[...], 0, 0)).astype(bf16)
        box_in_sum = box_in_sum + dot(cells, dinner, 0, 0)
        dh_ref[own, :] = dfinal + split_sum(select, dot(dinner, w_box[...], 1, 1))
    loss_ref[...] = jnp.broadcast_to(loss, loss_ref.shape)
    d_head[...] = head_sum.astype(bf16)
    d_box[...] = box_in_sum.astype(bf16)
    done("box_in")
    d_box_out[...] = box_out_sum.astype(bf16)

    def start_sum(block, down):
        dy_ref[block, :] = down
        og_ref[block, :] = down.astype(bf16)

    def add_sum(block, down):
        total = down + dy_ref[block, :]
        dy_ref[block, :] = total
        og_ref[block, :] = total.astype(bf16)

    norm_all_back(y3_ref, norms, 6, dh_ref, d_norms, rows, TAG_CHUNK, start_sum)
    ffn_backward(og_ref, h3_ref, u_ref, g_ref, w_in, w_ffo, d_in, d_ffo, dh_ref)
    done("ffn_in")
    done("ffn_out")
    norm_all_back(y2_ref, norms, 4, dh_ref, d_norms, rows, TAG_CHUNK, add_sum)

    weight_grad(o2_ref, og_ref, d_co)
    done("cross_out")
    project_back(og_ref, w_co, up_ref)
    head_sums(tables, up_ref, o2_ref, delta_ref, TAGS)
    attend_back(
        (0, tables), cq_ref, ckv_ref, 0, ckv_ref, D, up_ref, lse2_ref, delta_ref,
        cq_ref, ckv_ref, ckv_ref, TAGS, IMG, False,
    )
    weight_grad(h2_ref, cq_ref, d_cq)
    done("cross_q")
    weight_grad(mem_ref, ckv_ref, d_ckv)
    done("cross_kv")
    project_back(ckv_ref, w_ckv, dmem_ref)
    done("mem")
    project_back(cq_ref, w_cq, dh_ref)
    norm_all_back(y1_ref, norms, 2, dh_ref, d_norms, rows, TAG_CHUNK, add_sum)

    weight_grad(o1_ref, og_ref, d_out)
    done("out")
    project_back(og_ref, w_out, up_ref)
    head_sums(tables, up_ref, o1_ref, delta_ref, TAGS)
    attend_back(
        (0, tables), qkv_ref, qkv_ref, D, qkv_ref, 2 * D, up_ref, lse1_ref, delta_ref,
        qkv_ref, qkv_ref, qkv_ref, TAGS, TAGS, True,
    )
    weight_grad(h1_ref, qkv_ref, d_qkv)
    done("qkv")
    project_back(qkv_ref, w_qkv, dh_ref)
    norm_all_back(e_ref, norms, 0, dh_ref, d_norms, rows, TAG_CHUNK, add_sum)
    embed_sum = jnp.zeros((V, D), f32)
    for table in range(tables):
        embed_sum = embed_sum + split_sum(
            tag_members(table), dy_ref[table * TAGS : (table + 1) * TAGS, :]
        )
    d_embed[...] = embed_sum.astype(bf16)


DECODER_NAMES = (
    "qkv", "out", "cross_q", "cross_kv", "cross_out", "ffn_in", "ffn_out", "embed", "head", "box_in", "norms", "box_out",
)


DECODER_MOVED = ("qkv", "out", "cross_q", "mem", "cross_kv", "cross_out", "ffn_in", "ffn_out", "box_in")


def decoder_step(prepared, scale, memory, weights):
    tables = prepared[0].shape[0]
    rows = tables * TAGS
    image_rows = memory.shape[0]
    arrays = {"mem": memory, **{name: weights[name] for name in DECODER_NAMES}}
    grads = {
        name: jax.ShapeDtypeStruct(array.shape, f32 if name in ("norms", "mem") else bf16)
        for name, array in arrays.items()
    }
    vmem, hbm = pl.BlockSpec(memory_space=pltpu.VMEM), pl.BlockSpec(memory_space=pl.ANY)
    low = lambda width, height=rows: pltpu.VMEM((height, width), bf16)
    full = lambda width, height=rows: pltpu.VMEM((height, width), f32)
    stats = pltpu.VMEM((tables * HEADS, TAGS), f32)
    places = [hbm if name in DECODER_MOVED else vmem for name in arrays]
    moved, total = len(DECODER_MOVED), len(arrays)

    def kernel(*refs):
        ready, refs = refs[:7], refs[7:]
        sources, refs = dict(zip(arrays, refs[:total])), refs[total:]
        loss_ref, targets, refs = refs[0], dict(zip(arrays, refs[1 : total + 1])), refs[total + 1 :]
        inside = dict(zip(DECODER_MOVED, refs[:moved]))
        outside = dict(zip(DECODER_MOVED, refs[moved : 2 * moved]))
        in_sem, out_sem = refs[2 * moved : 2 * moved + 2]
        fetch = {
            name: pltpu.make_async_copy(sources[name], inside[name], in_sem.at[k])
            for k, name in enumerate(DECODER_MOVED)
        }
        give = {
            name: pltpu.make_async_copy(outside[name], targets[name], out_sem.at[k])
            for k, name in enumerate(DECODER_MOVED)
        }
        for name in DECODER_MOVED:
            fetch[name].start()
        given = {**sources, **inside}
        taken = {**targets, **outside}
        decoder_kernel(
            *ready, given["mem"], *[given[name] for name in DECODER_NAMES],
            loss_ref, taken["mem"], *[taken[name] for name in DECODER_NAMES],
            *refs[2 * moved + 2 :], lambda name: fetch[name].wait(), lambda name: give[name].start(),
        )
        for name in DECODER_MOVED:
            give[name].wait()

    outs = pl.pallas_call(
        kernel,
        out_shape=(jax.ShapeDtypeStruct((8, 128), f32), *grads.values()),
        in_specs=[vmem] * 6 + [pl.BlockSpec(memory_space=pltpu.SMEM)] + places,
        out_specs=(vmem, *places),
        scratch_shapes=[
            *[pltpu.VMEM(arrays[name].shape, arrays[name].dtype) for name in DECODER_MOVED],
            *[pltpu.VMEM(grads[name].shape, grads[name].dtype) for name in DECODER_MOVED],
            pltpu.SemaphoreType.DMA((moved,)), pltpu.SemaphoreType.DMA((moved,)),
            full(D), low(D), low(3 * D), low(D), stats, full(D), low(D), low(D), low(2 * D, image_rows), low(D), stats,
            full(D), low(D), full(FF), low(FF), full(D), low(D), full(D), full(D), low(D), low(D), stats,
        ],
        compiler_params=pltpu.CompilerParams(vmem_limit_bytes=VMEM_LIMIT),
        name="decoder_step",
    )(*prepared, scale, *arrays.values())
    return outs[0], outs[1], dict(zip(DECODER_NAMES, outs[2:]))


AXES = ("wide", "narrow")
MESH = pl.DeviceIdType.MESH
ORDERS = (("a", "y", "b"), ("a", "b", "y"))


class Place:
    def __init__(self, wide, narrow):
        inner = 2 if wide % 2 == 0 else 1
        self.sizes = {"a": wide // inner, "b": inner, "y": narrow // 2, "c": 2}
        self.narrow = narrow
        self.count = wide * narrow

    def locate(self):
        wide, narrow = lax.axis_index("wide"), lax.axis_index("narrow")
        inner = self.sizes["b"]
        self.here = {
            "a": lax.div(wide, inner),
            "b": lax.rem(wide, inner),
            "y": lax.div(narrow, 2),
            "c": lax.rem(narrow, 2),
        }
        return self

    def moved(self, steps):
        there = dict(self.here)
        for part, step in steps.items():
            there[part] = lax.rem(there[part] + step, self.sizes[part])
        return there

    def device(self, there):
        return (there["a"] * self.sizes["b"] + there["b"], there["y"] * 2 + there["c"])

    def index(self, there):
        wide, narrow = self.device(there)
        return wide * self.narrow + narrow

    def peers(self):
        return [(part, step) for part, size in self.sizes.items() for step in range(1, size)]

    def in_plane(self, step):
        size, wide = self.sizes["b"], self.sizes["y"]
        here = (self.here["b"] * wide + self.here["y"]) * 2 + self.here["c"]
        there = lax.rem(here + step, size * wide * 2)
        return there, {
            **self.here,
            "b": lax.div(there, wide * 2),
            "y": lax.rem(lax.div(there, 2), wide),
            "c": lax.rem(there, 2),
        }

    def plane(self):
        return self.sizes["b"] * self.sizes["y"] * 2

    def greet(self, whole_plane=False):
        barrier = pltpu.get_barrier_semaphore()
        peers = [self.moved({part: step}) for part, step in self.peers()]
        if whole_plane:
            peers = [self.in_plane(step)[1] for step in range(1, self.plane())] + [
                self.moved({"a": step}) for step in range(1, self.sizes["a"])
            ]
        for there in peers:
            pl.semaphore_signal(
                barrier, inc=1, device_id=self.device(there), device_id_type=MESH
            )
        pl.semaphore_wait(barrier, len(peers))


def block_rows(amount):
    return -(-(amount // 128 + 3) // 16) * 16


def flat_rows(amount, count):
    return -(-((count - 1) * amount // 128 + block_rows(amount)) // 8) * 8


def layout_bases(layout):
    offset = 0
    for name, (height, breadth) in layout:
        yield name, height, breadth, offset // 128
        offset += height * breadth


def place_blocks(all_ref, flat_ref, amount):
    count, rows, _ = all_ref.shape
    used = amount // 128 + 2
    flat_ref[0:8, :] = jnp.zeros((8, 128), f32)

    @pl.loop(0, count)
    def _(device):
        start = lax.div(device * amount, 128)
        before = flat_ref[pl.ds(start, 1), :]
        flat_ref[pl.ds(start, used), :] = all_ref[device, :used, :].astype(f32)
        flat_ref[pl.ds(start, 1), :] = before + all_ref[device, 0:16, :].astype(f32)[0:1]


def one_hot(shape, match):
    first = lax.broadcasted_iota(jnp.int32, shape, 0)
    second = lax.broadcasted_iota(jnp.int32, shape, 1)
    return match(first, second).astype(f32).astype(bf16)


def take_matrices(flat_ref, layout, out_refs, done=lambda name: None):
    for name, height, breadth, base in layout_bases(layout):
        out_ref = out_refs[name]
        if name == "head":
            turned = flat_ref[base : base + 128, :].T.astype(bf16)
            total = jnp.zeros((V, D), f32)
            for part in range(4):
                spread = one_hot((128, D), lambda row, column: column == 4 * row + part)
                total = total + dot(turned[part * V : (part + 1) * V, :], spread)
            out_ref[...] = total.astype(bf16)
        elif name == "box_out":
            block = flat_ref[base : base + 16, :].astype(bf16)
            own = one_hot((16, D), lambda row, column: lax.div(column, 32) == row).astype(f32)
            index = lax.broadcasted_iota(jnp.int32, (16, D), 0)
            total = jnp.zeros((16, D), f32)
            for k in range(4):
                pick = one_hot((128, D), lambda lane, column: lane == 4 * lax.rem(column, 32) + k)
                line = jnp.sum(dot(block, pick) * own, 0, keepdims=True)
                total = jnp.where(index == k, line, total)
            out_ref[...] = total.astype(bf16)
        else:
            wide = breadth // 128
            for column in range(wide):
                out_ref[:, column * 128 : (column + 1) * 128] = flat_ref[
                    pl.ds(base + column, height, stride=wide), :
                ].astype(out_ref.dtype)
        done(name)


def put_matrices(flat_ref, layout, refs, need):
    for name, height, breadth, base in layout_bases(layout):
        ref = refs[name]
        need(name)
        if name == "head":
            total = jnp.zeros((128, 128), f32)
            for part in range(4):
                pick = one_hot((128, D), lambda row, column: column == 4 * row + part)
                shift = one_hot((V, 128), lambda row, lane: lane == V * part + row)
                total = total + dot(dot(pick, ref[...], 1, 1).astype(bf16), shift)
            flat_ref[base : base + 128, :] = total
        elif name == "box_out":
            own = one_hot((16, D), lambda row, column: lax.div(column, 32) == row).astype(f32)
            total = jnp.zeros((16, 128), f32)
            for k in range(4):
                line = ref[...].astype(f32)[k : k + 1, :]
                spread = one_hot((D, 128), lambda column, lane: lane == 4 * lax.rem(column, 32) + k)
                total = total + dot((own * line).astype(bf16), spread)
            flat_ref[base : base + 16, :] = total
        else:
            wide = breadth // 128
            for column in range(wide):
                flat_ref[pl.ds(base + column, height, stride=wide), :] = ref[
                    :, column * 128 : (column + 1) * 128
                ].astype(f32)


def weight_shapes(layout):
    shapes = {name: extent for name, extent in layout}
    if "head" in shapes:
        shapes["head"], shapes["box_out"] = (V, D), (16, D)
    return {
        name: jax.ShapeDtypeStruct(extent, f32 if name == "norms" else bf16)
        for name, extent in shapes.items()
    }


def pack_grads(grads, layout, amount, count, name):
    names = [piece for piece, _ in layout]
    pieces = len(names)
    rows = block_rows(amount)

    def kernel(*refs):
        sources, block_hbm, refs = refs[:pieces], refs[pieces], refs[pieces + 1 :]
        local, (flat_ref, block_ref, in_sem, out_sem) = refs[:pieces], refs[pieces:]
        fetch = {
            piece: pltpu.make_async_copy(source, target, in_sem.at[k])
            for k, (piece, source, target) in enumerate(zip(names, sources, local))
        }
        for one in fetch.values():
            one.start()
        tail = sum(extent[0] * extent[1] for _, extent in layout) // 128
        flat_ref[tail:, :] = jnp.zeros((flat_ref.shape[0] - tail, 128), f32)
        put_matrices(flat_ref, layout, dict(zip(names, local)), lambda piece: fetch[piece].wait())

        def give(owner):
            return pltpu.make_async_copy(block_ref.at[owner], block_hbm.at[owner], out_sem.at[owner])

        @pl.loop(0, count)
        def _(owner):
            start = lax.div(owner * amount, 128)
            block_ref[owner, :, :] = flat_ref[pl.ds(start, rows), :].astype(bf16)
            give(owner).start()

        @pl.loop(0, count)
        def _(owner):
            give(owner).wait()

    hbm = pl.BlockSpec(memory_space=pl.ANY)
    return pl.pallas_call(
        kernel,
        out_shape=jax.ShapeDtypeStruct((count, rows, 128), bf16),
        in_specs=[hbm] * pieces,
        out_specs=hbm,
        scratch_shapes=[
            *[pltpu.VMEM(grads[piece].shape, grads[piece].dtype) for piece in names],
            pltpu.VMEM((flat_rows(amount, count), 128), f32),
            pltpu.VMEM((count, rows, 128), bf16),
            pltpu.SemaphoreType.DMA((pieces,)),
            pltpu.SemaphoreType.DMA((count,)),
        ],
        compiler_params=pltpu.CompilerParams(vmem_limit_bytes=VMEM_LIMIT),
        name=name,
    )(*[grads[piece] for piece in names])


class Reduction:
    def __init__(self, place, core, pick, own_ref, mine_ref, got_ref, load_sem, send_sem, recv_sem):
        self.place, self.pick = place, pick
        self.own, self.mine, self.got = own_ref, mine_ref, got_ref
        self.load_sem, self.send_sem, self.recv_sem = load_sem, send_sem, recv_sem
        self.order, self.other = ORDERS[core], ORDERS[1 - core]
        self.s1, self.s2, self.s3 = (place.sizes[part] for part in self.order)
        self.half = place.count // 2
        self.base3 = self.half
        self.base2 = self.base3 + (self.s3 - 1) * self.s1 * self.s2
        self.base1 = self.base2 + (self.s2 - 1) * self.s1

    def slot(self, steps):
        sizes = self.place.sizes
        return (steps["a"] * sizes["b"] + steps["b"]) * sizes["y"] + steps["y"]

    def owner(self, steps):
        return self.place.index(self.place.moved(steps))

    def only(self, steps, body):
        if self.pick is None:
            body()
        else:
            pl.when(self.pick(self.owner(steps)))(body)

    def copy(self, source, slot, part, step):
        return pltpu.make_async_remote_copy(
            src_ref=source,
            dst_ref=self.got.at[slot],
            send_sem=self.send_sem.at[slot],
            recv_sem=self.recv_sem.at[slot],
            device_id=self.place.device(self.place.moved({part: step})),
            device_id_type=MESH,
        )

    def load(self, steps):
        slot = self.slot(steps)
        return pltpu.make_async_copy(
            self.own.at[self.owner(steps)], self.mine.at[slot], self.load_sem.at[slot]
        )

    def took(self, slot):
        self.copy(self.mine.at[0], slot, "c", 1).wait_recv()

    def value(self, slot):
        return self.got[slot].astype(f32)

    def levels(self, order):
        s1, s2, s3 = (self.place.sizes[part] for part in order)
        return (
            (s1 * s2 * (s3 - 1), lambda n: (s1 - 1 - lax.rem(n, s1), s2 - 1 - lax.rem(lax.div(n, s1), s2), lax.div(n, s1 * s2) + 1)),
            (s1 * (s2 - 1), lambda n: (s1 - 1 - lax.rem(n, s1), lax.div(n, s1) + 1, 0)),
            (s1, lambda n: (s1 - 1 - n, 0, 0)),
        )

    def to_sibling(self):
        if self.load_sem is not None:
            for amount, where in self.levels(self.order):

                @pl.loop(0, amount)
                def _(number):
                    self.load(dict(zip(self.order, where(number)))).start()

        for amount, where in self.levels(self.other):

            @pl.loop(0, amount)
            def _(number):
                steps = dict(zip(self.other, where(number)))
                slot = self.slot(steps)

                def send():
                    block = slot if self.load_sem is None else self.owner({**steps, "c": 1})
                    self.copy(self.own.at[block], slot, "c", 1).start()

                self.only({**steps, "c": 1}, send)

    def partial(self, p, q, r):
        steps = dict(zip(self.order, (p, q, r)))
        slot = self.slot(steps)
        if self.load_sem is not None:
            self.load(steps).wait()
        self.took(slot)
        return slot, self.mine[slot].astype(f32) + self.value(slot)

    def add_third(self, total, p, q):
        for step in range(1, self.s3):
            slot = self.base3 + ((step - 1) * self.s1 + p) * self.s2 + q
            self.took(slot)
            total = total + self.value(slot)
        return total

    def add_second(self, total, p):
        for step in range(1, self.s2):
            slot = self.base2 + (step - 1) * self.s1 + p
            self.took(slot)
            total = total + self.value(slot)
        return total

    def send(self, own_slot, total, slot, part, step):
        self.mine[own_slot] = total.astype(bf16)
        self.copy(self.mine.at[own_slot], slot, part, step).start()

    def third(self):
        amount, where = self.levels(self.order)[0]

        @pl.loop(0, amount)
        def _(number):
            p, q, r = where(number)

            def body():
                own_slot, total = self.partial(p, q, r)
                slot = self.base3 + ((r - 1) * self.s1 + p) * self.s2 + q
                self.send(own_slot, total, slot, self.order[2], r)

            self.only(dict(zip(self.order, (p, q, r))), body)

    def second(self):
        amount, where = self.levels(self.order)[1]

        @pl.loop(0, amount)
        def _(number):
            p, q, _ = where(number)

            def body():
                own_slot, total = self.partial(p, q, 0)
                total = self.add_third(total, p, q)
                self.send(own_slot, total, self.base2 + (q - 1) * self.s1 + p, self.order[1], q)

            self.only(dict(zip(self.order, (p, q, 0))), body)

    def first(self):
        @pl.loop(1, self.s1)
        def _(p):
            def body():
                own_slot, total = self.partial(p, 0, 0)
                total = self.add_second(self.add_third(total, p, 0), p)
                self.send(own_slot, total, self.base1 + p - 1, self.order[0], p)

            self.only({self.order[0]: p}, body)

    def last(self, out_ref):
        def body():
            _, total = self.partial(0, 0, 0)
            out_ref[...] = self.add_second(self.add_third(total, 0, 0), 0)

            @pl.loop(1, self.s1)
            def _(p):
                slot = self.base1 + p - 1
                self.took(slot)
                out_ref[...] += self.value(slot)

        self.only({}, body)

    def close(self):
        @pl.loop(0, self.place.count - 1)
        def _(slot):
            self.copy(self.mine.at[0], slot, "c", 1).wait_send()


def reduction_memory(count, rows):
    half = count // 2
    return [pltpu.VMEM((half, rows, 128), bf16), pltpu.VMEM((count - 1, rows, 128), bf16)]


def reduction_signals(count, loads):
    return [pltpu.SemaphoreType.DMA((n,)) for n in ([count // 2] if loads else []) + [count - 1] * 2]


def reduce_stage(place, stage, pick, *members):
    for core in range(2):

        @pl.when(place.here["c"] == core)
        def _():
            stage(Reduction(place, core, pick, *members))


def cut_for_reduction(place, pick, flat_ref, amount, mine_ref, other_ref):
    rows = mine_ref.shape[1]
    sizes = place.sizes

    @pl.loop(0, place.count // 2)
    def _(slot):
        steps = {
            "a": lax.div(slot, sizes["b"] * sizes["y"]),
            "b": lax.rem(lax.div(slot, sizes["y"]), sizes["b"]),
            "y": lax.rem(slot, sizes["y"]),
        }
        for core, ref in ((0, mine_ref), (1, other_ref)):
            owner = place.index(place.moved({**steps, "c": core}))

            @pl.when(pick(owner))
            def _():
                ref[slot] = flat_ref[pl.ds(lax.div(owner * amount, 128), rows), :].astype(bf16)


def sum_everywhere(place, value, box_ref, send_sem, recv_sem):
    base = 0
    plane = [place.in_plane(step) for step in range(place.plane())]
    line = [place.moved({"a": step}) for step in range(place.sizes["a"])]
    for members in (plane, [(there["a"], there) for there in line]):

        def copy(step, number, base=base, members=members):
            return pltpu.make_async_remote_copy(
                src_ref=box_ref.at[base + number],
                dst_ref=box_ref.at[base + number],
                send_sem=send_sem.at[base + step],
                recv_sem=recv_sem.at[base + number],
                device_id=place.device(members[step][1]),
                device_id_type=MESH,
            )

        size = len(members)
        mine = members[0][0]
        box_ref[base + mine] = value
        for step in range(1, size):
            copy(step, mine).start()
        for step in range(1, size):
            copy(step, members[step][0]).wait_recv()
        for step in range(1, size):
            copy(step, mine).wait_send()
        value = box_ref[base]
        for other in range(1, size):
            value = value + box_ref[base + other]
        base += size
    return value


def own_squares(place, out_ref, amount):
    rows = out_ref.shape[0]
    offset = lax.rem(place.index(place.here) * amount, 128)
    position = (
        lax.broadcasted_iota(jnp.int32, (rows, 128), 0) * 128
        + lax.broadcasted_iota(jnp.int32, (rows, 128), 1)
        - offset
    )
    value = jnp.where((position >= 0) & (position < amount), out_ref[...], 0.0)
    return jnp.sum(jnp.sum(value * value, 0, keepdims=True), 1, keepdims=True)


def weight_grad_flat(a_ref, b_ref, flat_ref, base, breadth):
    wide = breadth // 128
    for start in range(0, breadth, 512):
        value = dot(a_ref[...], b_ref[:, start : start + 512], 0, 0)
        store_flat(value, flat_ref, base + start // 128, wide)


def store_flat(value, flat_ref, base, wide):
    rows, columns = value.shape
    for part in range(columns // 128):
        flat_ref[pl.ds(base + part, rows, stride=wide), :] = value[:, part * 128 : (part + 1) * 128]


def encoder_backward(place, images, stored, dmem, weights, decoder_blocks, amounts, loss_block):
    rows = images.shape[0]
    tables = rows // IMG
    qkv, mixed, lse, middle = stored
    bases = {name: base for name, _, _, base in layout_bases(encoder_layout())}
    block, small = decoder_blocks.shape[1], block_rows(amounts[0])
    flat_count = flat_rows(amounts[0], place.count)
    first_early = -(-bases["out"] * 128 // amounts[0])
    end_early = max((bases["norms"] - amounts[0] // 128 - 2) * 128 // amounts[0], first_early)
    steps = place.plane() + place.sizes["a"]
    early = lambda owner: (owner >= first_early) & (owner < end_early)
    late = lambda owner: owner < first_early
    latest = lambda owner: owner >= end_early

    def kernel(
        x_hbm, qkv_hbm, o_hbm, lse_ref, x1_hbm, dmem_hbm, w_qkv_hbm, w_out_hbm, w_in_hbm, w_ffo_hbm, norms, own_ref, loss_ref,
        encoder_ref, decoder_ref, stat_ref,
        w_qkv, h_ref, g_ref, og_ref, qkv_ref, delta_ref, d_norms, flat_ref, fetch_sem, o_ref, x1_ref, dmem_ref, w_out, w_in, w_ffo,
        theirs_ref, mine_ref, got_ref, far_mine_ref, far_got_ref, *signals,
    ):
        far = (None, own_ref, far_mine_ref, far_got_ref, *signals[:3])
        near = (theirs_ref, mine_ref, got_ref, None, *signals[3:5])
        box_ref, box_send, box_recv = signals[5:]
        work = functools.partial(reduce_stage, place)
        place.locate()
        fetches = [
            pltpu.make_async_copy(source, target, fetch_sem.at[k])
            for k, (source, target) in enumerate(
                (
                    (qkv_hbm, qkv_ref), (w_qkv_hbm, w_qkv), (x_hbm, g_ref.at[:, :D]), (x1_hbm, x1_ref), (dmem_hbm, dmem_ref),
                    (w_in_hbm, w_in), (w_ffo_hbm, w_ffo), (o_hbm, o_ref), (w_out_hbm, w_out),
                )
            )
        ]
        x_ref = g_ref.at[:, :D]
        for number in (3, 4, 5, 6, 7, 8, 0, 1):
            fetches[number].start()
        place.greet(True)
        work(lambda one: one.to_sibling(), *far)
        tail = bases["norms"] + 4 * D // 128
        flat_ref[tail:, :] = jnp.zeros((flat_count - tail, 128), f32)
        fetches[3].wait()
        norm_all(x1_ref, norms, 2, h_ref, rows, IMG_CHUNK)
        for number in (4, 5, 6, 7, 8):
            fetches[number].wait()
        og_ref[...] = dmem_ref[...].astype(bf16)
        for start in range(0, FF, 256):
            lanes = slice(start, start + 256)
            inner = dot(h_ref[...], w_in[:, lanes])
            back = dot(og_ref[...], w_ffo[lanes, :], 1, 1)
            part = dot(gelu(inner).astype(bf16), og_ref[...], 0, 0)
            store_flat(part, flat_ref, bases["ffn_out"] + start * 4, 4)
            g_ref[:, lanes] = (gelu_slope(inner) * back).astype(bf16)
        work(lambda one: one.third(), *far)
        weight_grad_flat(h_ref, g_ref, flat_ref, bases["ffn_in"], FF)

        def keep(part, down):
            og_ref[part, :] = (down + dmem_ref[part, :]).astype(bf16)

        norm_all_back(
            x1_ref, norms, 2, lambda part: dot(g_ref[part, :], w_in[...], 1, 1), d_norms, rows, IMG_CHUNK, keep
        )
        fetches[2].start()
        weight_grad_flat(o_ref, og_ref, flat_ref, bases["out"], D)
        cut_for_reduction(place, early, flat_ref, amounts[0], mine_ref, theirs_ref)
        work(lambda one: one.to_sibling(), early, *near)

        def project_rows(part):
            og_ref[part, :] = dot(og_ref[part, :], w_out[...], 1, 1).astype(bf16)

        each_rows(rows, IMG_CHUNK, project_rows)
        head_sums(tables, og_ref, o_ref, delta_ref, IMG)
        work(lambda one: one.second(), *far)
        fetches[0].wait()

        def between(step):
            @pl.when(step == 1)
            def _():
                work(lambda one: one.third(), early, *near)

            @pl.when(step == 2)
            def _():
                work(lambda one: one.first(), *far)

            @pl.when(step == 4)
            def _():
                work(lambda one: one.second(), early, *near)

            @pl.when(step == 5)
            def _():
                work(lambda one: one.last(decoder_ref), *far)

            @pl.when(step == 6)
            def _():
                work(lambda one: one.first(), early, *near)

        attend_back(
            (0, tables), qkv_ref, qkv_ref, D, qkv_ref, 2 * D, og_ref, lse_ref, delta_ref,
            qkv_ref, qkv_ref, qkv_ref, IMG, IMG, False, between,
        )
        work(lambda one: one.last(encoder_ref), early, *near)
        fetches[1].wait()
        fetches[2].wait()
        norm_all(x_ref, norms, 0, h_ref, rows, IMG_CHUNK)
        weight_grad_flat(h_ref, qkv_ref, flat_ref, bases["qkv"], 3 * D)
        cut_for_reduction(place, late, flat_ref, amounts[0], mine_ref, theirs_ref)
        work(lambda one: one.to_sibling(), late, *near)
        for table in range(tables):
            norm_all_back(
                x_ref, norms, 0, lambda part: dot(qkv_ref[part, :], w_qkv[...], 1, 1), d_norms,
                (table + 1) * IMG, IMG, None, table * IMG,
            )
            if table == 0:
                work(lambda one: one.third(), late, *near)
        store_flat(d_norms[...], flat_ref, bases["norms"], 4)
        cut_for_reduction(place, latest, flat_ref, amounts[0], mine_ref, theirs_ref)
        work(lambda one: one.to_sibling(), latest, *near)
        work(lambda one: one.second(), late, *near)
        work(lambda one: one.third(), latest, *near)
        work(lambda one: one.first(), late, *near)
        work(lambda one: one.second(), latest, *near)
        work(lambda one: one.first(), latest, *near)
        work(lambda one: one.last(encoder_ref), late, *near)
        work(lambda one: one.last(encoder_ref), latest, *near)
        squares = own_squares(place, encoder_ref, amounts[0]) + own_squares(
            place, decoder_ref, amounts[1]
        )
        me = place.index(place.here)
        for ref, amount in ((encoder_ref, amounts[0]), (decoder_ref, amounts[1])):
            ref[...] = shifted_back(ref[...], lax.rem(me * amount, 128))
        index = lax.broadcasted_iota(jnp.int32, (8, 128), 0)
        value = jnp.where(index == 0, squares, jnp.where(index == 1, loss_ref[...], 0.0))
        stat_ref[...] = sum_everywhere(place, value, box_ref, box_send, box_recv)
        work(lambda one: one.close(), *far)
        work(lambda one: one.close(), early, *near)

    vmem, hbm = pl.BlockSpec(memory_space=pltpu.VMEM), pl.BlockSpec(memory_space=pl.ANY)
    count = place.count
    return pl.pallas_call(
        kernel,
        out_shape=(
            jax.ShapeDtypeStruct((small, 128), f32),
            jax.ShapeDtypeStruct((block, 128), f32),
            jax.ShapeDtypeStruct((8, 128), f32),
        ),
        in_specs=[hbm, hbm, hbm, vmem, hbm, hbm, hbm, hbm, hbm, hbm, vmem, hbm, vmem],
        scratch_shapes=[
            pltpu.VMEM((D, 3 * D), bf16),
            pltpu.VMEM((rows, D), bf16),
            pltpu.VMEM((rows, FF), bf16),
            pltpu.VMEM((rows, D), bf16),
            pltpu.VMEM((rows, 3 * D), bf16),
            pltpu.VMEM((tables * HEADS, IMG), f32),
            pltpu.VMEM((4, D), f32),
            pltpu.VMEM((flat_count, 128), f32),
            pltpu.SemaphoreType.DMA((9,)),
            pltpu.VMEM((rows, D), bf16),
            pltpu.VMEM((rows, D), f32),
            pltpu.VMEM((rows, D), f32),
            pltpu.VMEM((D, D), bf16),
            pltpu.VMEM((D, FF), bf16),
            pltpu.VMEM((FF, D), bf16),
            pltpu.VMEM((count // 2, small, 128), bf16),
            *reduction_memory(count, small),
            *reduction_memory(count, block),
            *reduction_signals(count, True),
            *reduction_signals(count, False),
            pltpu.VMEM((steps, 8, 128), f32),
            pltpu.SemaphoreType.DMA((steps,)),
            pltpu.SemaphoreType.DMA((steps,)),
        ],
        compiler_params=pltpu.CompilerParams(
            collective_id=2, has_side_effects=True, vmem_limit_bytes=VMEM_LIMIT
        ),
        name="encoder_backward",
    )(
        images, qkv, mixed, lse, middle, dmem, weights["qkv"], weights["out"], weights["ffn_in"], weights["ffn_out"],
        weights["norms"], decoder_blocks, loss_block,
    )


class Spread:
    def __init__(self, place, core, view, send_sem, recv_sem):
        self.place, self.view, self.send_sem, self.recv_sem = place, view, send_sem, recv_sem
        self.order = ORDERS[core]
        self.s1, self.s2, self.s3 = (place.sizes[part] for part in self.order)
        self.base2 = self.s1 - 1
        self.base3 = self.base2 + self.s1 * (self.s2 - 1)
        self.base4 = self.base3 + self.s1 * self.s2 * (self.s3 - 1)

    def copy(self, p, q, r, core, part, step, number):
        one, two, three = self.order
        block = self.place.index(self.place.moved({one: p, two: q, three: r, "c": core}))
        return pltpu.make_async_remote_copy(
            src_ref=self.view(block),
            dst_ref=self.view(block),
            send_sem=self.send_sem.at[number],
            recv_sem=self.recv_sem.at[block],
            device_id=self.place.device(self.place.moved({part: step})),
            device_id_type=MESH,
        )

    def arrived(self, p, q, r, core=0):
        self.copy(p, q, r, core, "c", 1, 0).wait_recv()

    def to_sibling(self, p, q, r):
        number = self.base4 + (p * self.s2 + q) * self.s3 + r
        self.copy(p, q, r, 0, "c", 1, number).start()

    def to_third(self, p, q):
        for step in range(1, self.s3):
            number = self.base3 + (p * self.s2 + q) * (self.s3 - 1) + step - 1
            self.copy(p, q, 0, 0, self.order[2], step, number).start()

    def to_second(self, p):
        for step in range(1, self.s2):
            number = self.base2 + p * (self.s2 - 1) + step - 1
            self.copy(p, 0, 0, 0, self.order[1], step, number).start()

    def one(self):
        @pl.loop(1, self.s1)
        def _(step):
            self.copy(0, 0, 0, 0, self.order[0], step, step - 1).start()

        self.to_second(0)
        self.to_third(0, 0)
        self.to_sibling(0, 0, 0)

    def two(self):
        @pl.loop(1, self.s1)
        def _(p):
            self.arrived(p, 0, 0)
            self.to_second(p)
            self.to_third(p, 0)
            self.to_sibling(p, 0, 0)

    def three(self):
        @pl.loop(0, self.s1 * (self.s2 - 1))
        def _(number):
            p, q = lax.rem(number, self.s1), lax.div(number, self.s1) + 1
            self.arrived(p, q, 0)
            self.to_third(p, q)
            self.to_sibling(p, q, 0)

    def four(self):
        @pl.loop(0, self.s1 * self.s2 * (self.s3 - 1))
        def _(number):
            p, q = lax.rem(number, self.s1), lax.rem(lax.div(number, self.s1), self.s2)
            r = lax.div(number, self.s1 * self.s2) + 1
            self.arrived(p, q, r)
            self.to_sibling(p, q, r)

    def five(self):
        @pl.loop(0, self.s1 * self.s2 * self.s3)
        def _(number):
            p, q = lax.rem(number, self.s1), lax.rem(lax.div(number, self.s1), self.s2)
            self.arrived(p, q, lax.div(number, self.s1 * self.s2), 1)

    def close(self):
        @pl.loop(0, self.place.count - 1)
        def _(number):
            self.copy(0, 0, 0, 0, "c", 1, number).wait_send()


def shifted(value, offset):
    lane = lax.broadcasted_iota(jnp.int32, value.shape, 1)
    turned = pltpu.roll(value, offset, 1)
    return jnp.where(lane < offset, pltpu.roll(turned, 1, 0), turned)


def shifted_back(value, offset):
    lane = lax.broadcasted_iota(jnp.int32, value.shape, 1)
    turned = pltpu.roll(value, lax.rem(128 - offset, 128), 1)
    return jnp.where(lane < 128 - offset, turned, pltpu.roll(turned, value.shape[0] - 1, 0))


def gather_and_encode(place, images, encoder_block, decoder_block, counts, amounts):
    rows = images.shape[0]
    tables = rows // IMG
    count = place.count
    layouts = (encoder_layout(), decoder_layout())
    shapes = [weight_shapes(layout) for layout in layouts]
    small, large = encoder_block.shape[0], decoder_block.shape[0]
    near, cut = small // 32 * 16, large // 32 * 16
    flat_counts = [flat_rows(amount, count) for amount in amounts]
    first, second = len(shapes[0]), len(shapes[1])
    matrices = [name for name in shapes[0] if name != "norms"]
    moved = [name for name in DECODER_MOVED if name != "mem"]

    def kernel(x_ref, encoder_ref, decoder_ref, counts_ref, *refs):
        encoder_out = dict(zip(shapes[0], refs[:first]))
        decoder_out = dict(zip(shapes[1], refs[first : first + second]))
        count_ref, qkv_out, o_out, lse_ref, x1_out, mem_out = refs[first + second : first + second + 6]
        rest = refs[first + second + 6 :]
        encoder_all, decoder_all, flat_ref, qkv_ref, h_ref, g_ref = rest[:6]
        local = dict(zip(matrices, rest[6 : 6 + len(matrices)]))
        local["norms"] = encoder_out["norms"]
        o_ref, x1_ref, mem_ref, out_sem, far_sem = rest[6 + len(matrices) : 11 + len(matrices)]
        far = dict(zip(moved, rest[11 + len(matrices) : 11 + len(matrices) + len(moved)]))
        signals = rest[11 + len(matrices) + len(moved) :]
        views = (
            lambda block: encoder_all.at[block, :near],
            lambda block: encoder_all.at[block, near:],
            lambda block: decoder_all.at[block, :cut],
            lambda block: decoder_all.at[block, cut:],
        )
        place.locate()
        me = place.index(place.here)

        def go(*tasks):
            for core in range(2):

                @pl.when(place.here["c"] == core)
                def _():
                    for group, stage in tasks:
                        work = Spread(place, core, views[group], *signals[2 * group : 2 * group + 2])
                        getattr(work, stage)()

        own = shifted(encoder_ref[...], lax.rem(me * amounts[0], 128))
        row = lax.broadcasted_iota(jnp.int32, own.shape, 0)
        encoder_all[me] = jnp.where(row == small - 1, counts_ref[...], own).astype(bf16)
        place.greet()
        go((0, "one"), (1, "one"))
        decoder_all[me] = shifted(decoder_ref[...], lax.rem(me * amounts[1], 128)).astype(bf16)
        go(
            (0, "two"), (1, "two"), (0, "three"), (2, "one"), (1, "three"), (3, "one"), (0, "four"), (1, "four"), (0, "five"), (1, "five"),
        )
        total = jnp.zeros((1, 128), f32)
        for device in range(count):
            total = total + encoder_all[device, small - 16 :, :].astype(f32)[15:16]
        count_ref[...] = jnp.broadcast_to(jnp.sum(total, 1, keepdims=True), count_ref.shape)
        place_blocks(encoder_all, flat_ref, amounts[0])
        take_matrices(flat_ref, layouts[0], local)
        outs = [
            pltpu.make_async_copy(local[name], encoder_out[name], out_sem.at[k])
            for k, name in enumerate(matrices)
        ]
        for out in outs:
            out.start()
        stored = ((qkv_ref, qkv_out), (o_ref, o_out), (x1_ref, x1_out), (mem_ref, mem_out))
        for k, (source, target) in enumerate(stored):
            outs.append(pltpu.make_async_copy(source, target, out_sem.at[len(matrices) + k]))
        go((2, "two"), (3, "two"))
        norms = local["norms"]
        norm_all(x_ref, norms, 0, h_ref, rows, IMG_CHUNK)
        project(h_ref, local["qkv"], qkv_ref, 3 * D, 0.125)
        outs[-4].start()

        def between(step):
            for number, task in ((0, (2, "three")), (1, (3, "three")), (4, (2, "four")), (7, (3, "four"))):

                @pl.when(step == number)
                def _():
                    go(task)

        attend_with(
            tables, qkv_ref, qkv_ref, D, qkv_ref, 2 * D, o_ref, lse_ref, IMG, IMG, False, True, between
        )
        outs[-3].start()
        add_project(x_ref, o_ref, local["out"], x1_ref)
        outs[-2].start()
        norm_all(x1_ref, norms, 2, h_ref, rows, IMG_CHUNK)

        @pl.loop(0, tables)
        def _(table):
            part = pl.ds(pl.multiple_of(table * IMG, 16), IMG)
            for start in range(0, FF, 256):
                lanes = slice(start, start + 256)
                g_ref[:, lanes] = gelu(dot(h_ref[part, :], local["ffn_in"][:, lanes])).astype(bf16)
            for start in range(0, D, 256):
                lanes = slice(start, start + 256)
                value = x1_ref[part, lanes] + dot(g_ref[...], local["ffn_out"][:, lanes])
                mem_ref[part, lanes] = value.astype(bf16)

        outs[-1].start()
        go((2, "five"), (3, "five"))
        place_blocks(decoder_all, flat_ref, amounts[1])
        give = {
            name: pltpu.make_async_copy(far[name], decoder_out[name], far_sem.at[k])
            for k, name in enumerate(moved)
        }
        take_matrices(
            flat_ref, layouts[1], {**decoder_out, **far}, lambda name: name in give and give[name].start()
        )
        outs.extend(give.values())
        go((0, "close"), (1, "close"), (2, "close"), (3, "close"))
        for out in outs:
            out.wait()

    vmem, hbm = pl.BlockSpec(memory_space=pltpu.VMEM), pl.BlockSpec(memory_space=pl.ANY)
    outs = pl.pallas_call(
        kernel,
        out_shape=(
            *shapes[0].values(),
            *shapes[1].values(),
            jax.ShapeDtypeStruct((8, 128), f32),
            jax.ShapeDtypeStruct((rows, 3 * D), bf16),
            jax.ShapeDtypeStruct((rows, D), bf16),
            jax.ShapeDtypeStruct((tables * HEADS, IMG), f32),
            jax.ShapeDtypeStruct((rows, D), f32),
            jax.ShapeDtypeStruct((rows, D), bf16),
        ),
        in_specs=[vmem] * 4,
        out_specs=(
            *[vmem if name == "norms" else hbm for name in shapes[0]],
            *[hbm if name in moved else vmem for name in shapes[1]],
            vmem, hbm, hbm, vmem, hbm, hbm,
        ),
        scratch_shapes=[
            pltpu.VMEM((count, small, 128), bf16),
            pltpu.VMEM((count, large, 128), bf16),
            pltpu.VMEM((max(flat_counts), 128), f32),
            pltpu.VMEM((rows, 3 * D), bf16),
            pltpu.VMEM((rows, D), bf16),
            pltpu.VMEM((IMG, FF), bf16),
            *[pltpu.VMEM(shapes[0][name].shape, bf16) for name in matrices],
            pltpu.VMEM((rows, D), bf16),
            pltpu.VMEM((rows, D), f32),
            pltpu.VMEM((rows, D), bf16),
            pltpu.SemaphoreType.DMA((len(matrices) + 4,)),
            pltpu.SemaphoreType.DMA((len(moved),)),
            *[pltpu.VMEM(shapes[1][name].shape, bf16) for name in moved],
            *[pltpu.SemaphoreType.DMA((n,)) for n in (count - 1, count) * 4],
        ],
        compiler_params=pltpu.CompilerParams(
            collective_id=1, has_side_effects=True, vmem_limit_bytes=VMEM_LIMIT
        ),
        name="gather_and_encode",
    )(images, encoder_block, decoder_block, counts)
    encoder_weights = dict(zip(shapes[0], outs[:first]))
    decoder_weights = dict(zip(shapes[1], outs[first : first + second]))
    number, *stored, memory = outs[first + second :]
    return encoder_weights, decoder_weights, number[0, 0], stored, memory


def adam_update(gradient, master, first_state, second_state, average):
    first_new = BETA_ONE * first_state + (1.0 - BETA_ONE) * gradient
    second_new = BETA_TWO * second_state + (1.0 - BETA_TWO) * gradient * gradient
    first_hat = first_new / (1.0 - BETA_ONE**STEP)
    second_hat = second_new / (1.0 - BETA_TWO**STEP)
    master_new = master - LEARN_RATE * (
        first_hat / (jnp.sqrt(second_hat) + EPSILON) + WEIGHT_DECAY * master
    )
    average_new = SMOOTH * average + (1.0 - SMOOTH) * master_new
    return (first_new, second_new, master_new, average_new)


def shard_block(shard):
    rows = block_rows(shard.shape[0])
    return jnp.pad(shard, (0, rows * 128 - shard.shape[0])).reshape(rows, 128)


def on_device(place, *arguments):
    (
        images, tag_ids, tag_lengths, cell_mask, cell_index, box_targets,
        encoder_params, encoder_first, encoder_second, encoder_average,
        decoder_params, decoder_first, decoder_second, decoder_average,
    ) = arguments
    encoder_amount, decoder_amount = encoder_params.shape[0], decoder_params.shape[0]
    cell_slots = jnp.arange(CELLS)
    alive = ((cell_mask > 0) & (cell_slots[None, :] < (tag_lengths // 4)[:, None])).astype(f32)
    cells = cell_index % tag_lengths[:, None]
    counted = (jnp.arange(TAGS)[None, :] < (tag_lengths - 1)[:, None]).astype(f32)
    upcoming = jnp.roll(tag_ids, -1, 1)
    prepared = (
        tag_ids[:, None, :], upcoming[:, None, :], counted[:, None, :], cells[:, None, :], alive[:, None, :], box_targets,
    )

    counts = jnp.sum(alive, 1)
    counts = jnp.pad(counts, (0, 128 - counts.shape[0])).reshape(1, 128)
    amounts = (encoder_amount, decoder_amount)
    encoder_weights, decoder_weights, cell_total, stored, memory = gather_and_encode(
        place, images, shard_block(encoder_params), shard_block(decoder_params), counts, amounts
    )
    scale = (1.0 / cell_total).reshape(1, 1)
    loss_block, dmemory, decoder_grads = decoder_step(prepared, scale, memory, decoder_weights)
    decoder_packed = pack_grads(
        decoder_grads, decoder_layout(), decoder_amount, place.count, "pack_decoder"
    )
    encoder_sum, decoder_sum, stats = encoder_backward(
        place, images, stored, dmemory, encoder_weights, decoder_packed, amounts, loss_block
    )
    grad_norm = jnp.sqrt(stats[0, 0])
    factor = CLIP_NORM / jnp.maximum(grad_norm, CLIP_NORM)
    encoder_grad = encoder_sum.reshape(-1)[:encoder_amount]
    decoder_grad = decoder_sum.reshape(-1)[:decoder_amount]
    encoder_new = adam_update(
        encoder_grad * factor, encoder_params, encoder_first, encoder_second, encoder_average
    )
    decoder_new = adam_update(
        decoder_grad * factor, decoder_params, decoder_first, decoder_second, decoder_average
    )
    return (stats[1, 0], cell_total, grad_norm, *encoder_new, *decoder_new)


def solution(mesh):
    rows, flat = P(AXES, None), P(AXES)
    return jax.shard_map(
        functools.partial(on_device, Place(mesh.shape["wide"], mesh.shape["narrow"])),
        mesh=mesh,
        in_specs=(rows, rows, flat, rows, rows, P(AXES, None, None)) + (flat,) * 8,
        out_specs=(P(), P(), P()) + (flat,) * 8,
        check_vma=False,
    )
```

```python
import functools

import jax
import jax.numpy as jnp
from jax import lax
from jax.experimental import pallas as pl
from jax.experimental.pallas import tpu as pltpu
from jax.sharding import PartitionSpec as P

D = 512
HEADS = 8
HEAD = D // HEADS
PAIRS = HEADS // 2
FF = 1024
V = 32
IMG = 784
TAGS = 512
STEP = 5
CELLS = 128
IMG_CHUNK = 784
TAG_CHUNK = 512
SAFE_SCORE = 50.0

BETA_ONE = 0.5
BETA_TWO = 0.5
CLIP_NORM = 0.01
LEARN_RATE = 0.05
WEIGHT_DECAY = 0.01
EPSILON = 1e-08
SMOOTH = 0.9

VMEM_LIMIT = 62 * 2**20
bf16 = jnp.bfloat16
f32 = jnp.float32


def encoder_layout():
    return [
        ("qkv", (D, 3 * D)),
        ("out", (D, D)),
        ("ffn_in", (D, FF)),
        ("ffn_out", (FF, D)),
        ("norms", (4, D)),
    ]


def decoder_layout():
    return [
        ("qkv", (D, 3 * D)),
        ("out", (D, D)),
        ("cross_q", (D, D)),
        ("cross_kv", (D, 2 * D)),
        ("cross_out", (D, D)),
        ("ffn_in", (D, FF)),
        ("ffn_out", (FF, D)),
        ("embed", (V, D)),
        ("head", (D, V)),
        ("box_in", (D, D)),
        ("norms", (8, D)),
        ("box_out", (D, 4)),
    ]


def dot(left, right, over_left=1, over_right=0):
    return lax.dot_general(
        left, right, (((over_left,), (over_right,)), ((), ())), preferred_element_type=f32
    )


def each_rows(total, step, body, first=0):
    @pl.loop(first // step, total // step)
    def _(index):
        body(pl.ds(pl.multiple_of(index * step, step), step))


def norm_rows(value, gain, shift):
    centred = value - jnp.mean(value, -1, keepdims=True)
    variance = jnp.mean(centred * centred, -1, keepdims=True)
    return centred * lax.rsqrt(variance + 1e-05) * gain + shift


def norm_rows_back(value, gain, upstream):
    centred = value - jnp.mean(value, -1, keepdims=True)
    variance = jnp.mean(centred * centred, -1, keepdims=True)
    scale = lax.rsqrt(variance + 1e-05)
    unit = centred * scale
    inner = upstream * gain
    mean_inner = jnp.mean(inner, -1, keepdims=True)
    mean_both = jnp.mean(inner * unit, -1, keepdims=True)
    down = scale * (inner - mean_inner - unit * mean_both)
    return (
        down,
        jnp.sum(upstream * unit, 0, keepdims=True),
        jnp.sum(upstream, 0, keepdims=True),
    )


GELU_A = 0.7978845608028654
GELU_B = 0.044715


def gelu(value):
    inner = jnp.tanh(GELU_A * (value + GELU_B * value * value * value))
    return 0.5 * value * (1.0 + inner)


def gelu_slope(value):
    square = value * value
    inner = jnp.tanh(GELU_A * (value + GELU_B * square * value))
    slope = GELU_A * (1.0 + 3.0 * GELU_B * square)
    return 0.5 * (1.0 + inner) + 0.5 * value * (1.0 - inner * inner) * slope


def half_masks():
    lane = lax.broadcasted_iota(jnp.int32, (1, 2 * HEAD), 1)
    first = (lane < HEAD).astype(f32)
    return (first.astype(bf16), (1.0 - first).astype(bf16))


def query_blocks(query_rows, key_rows, causal):
    if not causal:
        return [(0, query_rows, key_rows)]
    return [(start, 256, start + 256) for start in range(0, query_rows, 256)]


def key_tiles(start, depth, causal):
    if not causal or start == 0:
        return [(0, depth)]
    return [(0, start), (start, depth)]


def causal_keep(depth, width):
    key = lax.broadcasted_iota(jnp.int32, (depth, width), 0)
    query = lax.broadcasted_iota(jnp.int32, (depth, width), 1)
    return key <= query


def head_members():
    row = lax.broadcasted_iota(jnp.int32, (16, D), 0)
    lane = lax.broadcasted_iota(jnp.int32, (16, D), 1)
    return (lax.shift_right_logical(lane, 6) == row).astype(f32).astype(bf16)


def largest_norm(ref, column, rows, start):
    value = ref[start : start + rows, column : column + D]
    return jnp.max(dot(head_members(), value * value, 1, 1), 1, keepdims=True)


def attend(tables, q_ref, k_ref, k_col, v_ref, v_col, o_ref, lse_ref, query_rows, key_rows, causal):
    bound = jnp.zeros((16, 1), f32)
    for table in range(tables):
        of_queries = largest_norm(q_ref, 0, query_rows, table * query_rows)
        of_keys = largest_norm(k_ref, k_col, key_rows, table * key_rows)
        bound = jnp.maximum(bound, of_queries * of_keys)
    small = jnp.max(bound) < (0.98 * SAFE_SCORE) ** 2
    for wanted in (True, False):

        @pl.when(small == wanted)
        def _():
            attend_with(
                tables, q_ref, k_ref, k_col, v_ref, v_col, o_ref, lse_ref,
                query_rows, key_rows, causal, not wanted,
            )


def attend_with(
    tables, q_ref, k_ref, k_col, v_ref, v_col, o_ref, lse_ref, query_rows, key_rows, causal, take_peak, between=None,
):
    masks = half_masks()
    blocks = query_blocks(query_rows, key_rows, causal)

    @pl.loop(0, tables * PAIRS)
    def _(step):
        table = lax.div(step, PAIRS)
        pair = lax.rem(step, PAIRS)
        q_rows = pl.ds(pl.multiple_of(table * query_rows, 16), query_rows)
        k_rows = pl.ds(pl.multiple_of(table * key_rows, 16), key_rows)
        lanes = pl.multiple_of(pair * 128, 128)
        queries = q_ref[q_rows, pl.ds(lanes, 128)]
        keys = k_ref[k_rows, pl.ds(k_col + lanes, 128)]
        values = v_ref[k_rows, pl.ds(v_col + lanes, 128)].T
        scores = {}
        for half in range(2):
            own = queries * masks[half]
            for start, width, depth in blocks:
                for low, high in key_tiles(start, depth, causal):
                    tile = dot(keys[low:high], own[start : start + width], 1, 1)
                    if causal and low == start:
                        tile = jnp.where(causal_keep(high - low, width), tile, -1e30)
                    scores[half, start, low] = tile
        outs = []
        for half in range(2):
            own_values = values[half * HEAD : (half + 1) * HEAD, :]
            parts, sums = [], []
            for start, width, depth in blocks:
                tiles = key_tiles(start, depth, causal)
                weights = [scores[half, start, low] for low, _ in tiles]
                peak = jnp.zeros((1, width), f32)
                if take_peak:
                    peak = functools.reduce(
                        jnp.maximum, [jnp.max(tile, 0, keepdims=True) for tile in weights]
                    )
                    weights = [tile - peak for tile in weights]
                weights = [jnp.exp(tile) for tile in weights]
                total = sum(jnp.sum(tile, 0, keepdims=True) for tile in weights)
                mixed = sum(
                    dot(own_values[:, low:high], tile.astype(bf16))
                    for tile, (low, high) in zip(weights, tiles)
                )
                parts.append(mixed * (1.0 / total))
                sums.append(peak + jnp.log(total))
            outs.append(parts[0] if len(parts) == 1 else jnp.concatenate(parts, 1))
            lse_ref[pl.ds(table * HEADS + pair * 2 + half, 1), :] = (
                sums[0] if len(sums) == 1 else jnp.concatenate(sums, 1)
            )
        joined = jnp.concatenate(outs, 0).astype(bf16)
        o_ref[q_rows, pl.ds(lanes, 128)] = joined.T
        if between is not None:
            between(step)


def head_sums(tables, up_ref, o_ref, delta_ref, query_rows):
    member = head_members()
    for table in range(tables):
        rows = slice(table * query_rows, (table + 1) * query_rows)
        both = up_ref[rows, :].astype(f32) * o_ref[rows, :].astype(f32)
        high = both.astype(bf16)
        rest = (both - high.astype(f32)).astype(bf16)
        sums = dot(member, high, 1, 1) + dot(member, rest, 1, 1)
        delta_ref[table * HEADS : (table + 1) * HEADS, :] = sums[:HEADS]


def attend_back(
    span_of_tables, q_ref, k_ref, k_col, v_ref, v_col, up_ref, lse_ref, delta_ref,
    dq_ref, dk_ref, dv_ref, query_rows, key_rows, causal, between=None,
):
    masks = half_masks()

    @pl.loop(span_of_tables[0] * PAIRS, span_of_tables[1] * PAIRS)
    def _(step):
        table = lax.div(step, PAIRS)
        pair = lax.rem(step, PAIRS)
        q_rows = pl.ds(pl.multiple_of(table * query_rows, 16), query_rows)
        k_rows = pl.ds(pl.multiple_of(table * key_rows, 16), key_rows)
        lanes = pl.multiple_of(pair * 128, 128)
        queries = q_ref[q_rows, pl.ds(lanes, 128)]
        keys = k_ref[k_rows, pl.ds(k_col + lanes, 128)]
        values = v_ref[k_rows, pl.ds(v_col + lanes, 128)]
        upstream = up_ref[q_rows, pl.ds(lanes, 128)]
        keys_across = keys.T
        blocks = query_blocks(query_rows, key_rows, causal)
        grad_q = []
        grad_k = [None] * len(blocks)
        grad_v = [None] * len(blocks)
        ahead = {}
        if causal:
            for half in range(2):
                own, own_up = queries * masks[half], upstream * masks[half]
                for number, (start, width, depth) in enumerate(blocks):
                    span = slice(start, start + width)
                    ahead[half, number] = (
                        dot(keys[:depth], own[span], 1, 1),
                        dot(values[:depth], own_up[span], 1, 1),
                    )
        for half in range(2):
            index = pl.ds(table * HEADS + pair * 2 + half, 1)
            own = queries * masks[half]
            own_up = upstream * masks[half]
            logsum = lse_ref[index, :]
            delta = delta_ref[index, :]
            across = keys_across[half * HEAD : (half + 1) * HEAD, :]
            parts = []
            for number, (start, width, depth) in enumerate(blocks):
                span = slice(start, start + width)
                if causal:
                    scores, pull = ahead[half, number]
                else:
                    scores = dot(keys[:depth], own[span], 1, 1)
                    pull = dot(values[:depth], own_up[span], 1, 1)
                weight = jnp.exp(scores - logsum[:, span])
                if causal:
                    edge = jnp.where(causal_keep(width, width), weight[start:], 0.0)
                    weight = edge if start == 0 else jnp.concatenate([weight[:start], edge], 0)
                change = (weight * (pull - delta[:, span])).astype(bf16)
                add_v = dot(weight.astype(bf16), own_up[span])
                add_k = dot(change, own[span])
                grad_v[number] = add_v if half == 0 else grad_v[number] + add_v
                grad_k[number] = add_k if half == 0 else grad_k[number] + add_k
                parts.append(dot(across[:, :depth], change) * 0.125)
            grad_q.append(parts[0] if len(parts) == 1 else jnp.concatenate(parts, 1))
        dq_ref[q_rows, pl.ds(lanes, 128)] = jnp.concatenate(grad_q, 0).astype(bf16).T
        for ref, column, grads in ((dk_ref, k_col, grad_k), (dv_ref, v_col, grad_v)):
            total = grads[-1]
            if len(grads) == 2:
                low = blocks[0][2]
                total = jnp.concatenate([total[:low] + grads[0], total[low:]], 0)
            ref[k_rows, pl.ds(column + lanes, 128)] = total.astype(bf16)
        if between is not None:
            between(step)


def project(a_ref, w_ref, out_ref, width, first_scale=None):
    for start in range(0, width, 512):
        value = dot(a_ref[...], w_ref[:, start : start + 512])
        if first_scale is not None and start == 0:
            value = value * first_scale
        out_ref[:, start : start + 512] = value.astype(bf16)


def add_project(base_ref, a_ref, w_ref, out_ref):
    for start in range(0, D, 256):
        lanes = slice(start, start + 256)
        out_ref[:, lanes] = base_ref[:, lanes].astype(f32) + dot(a_ref[...], w_ref[:, lanes])


def weight_grad(a_ref, b_ref, out_ref):
    rows, columns = out_ref.shape
    for start in range(0, columns, 512):
        lanes = slice(start, start + 512)
        out_ref[:, lanes] = dot(a_ref[...], b_ref[:, lanes], 0, 0).astype(out_ref.dtype)


def ffn_forward(h_ref, w_in, u_ref, g_ref):
    for start in range(0, FF, 256):
        lanes = slice(start, start + 256)
        inner = dot(h_ref[...], w_in[:, lanes])
        if u_ref is not None:
            u_ref[:, lanes] = inner
        g_ref[:, lanes] = gelu(inner).astype(bf16)


def ffn_backward(og_ref, h_ref, u_ref, g_ref, w_in, w_out, d_in, d_out, dh_ref):
    weight_grad(g_ref, og_ref, d_out)
    for start in range(0, FF, 256):
        lanes = slice(start, start + 256)
        back = dot(og_ref[...], w_out[lanes, :], 1, 1)
        g_ref[:, lanes] = (gelu_slope(u_ref[:, lanes]) * back).astype(bf16)
    weight_grad(h_ref, g_ref, d_in)
    project_back(g_ref, w_in, dh_ref)


def project_back(g_ref, w_ref, out_ref):
    for start in range(0, D, 256):
        lanes = slice(start, start + 256)
        out_ref[:, lanes] = dot(g_ref[...], w_ref[lanes, :], 1, 1).astype(out_ref.dtype)


def norm_all(x_ref, norms_ref, row, out_ref, total, step):
    gain, shift = norms_ref[row : row + 1, :], norms_ref[row + 1 : row + 2, :]

    def body(rows):
        out_ref[rows, :] = norm_rows(x_ref[rows, :].astype(f32), gain, shift).astype(bf16)

    each_rows(total, step, body)


def norm_all_back(x_ref, norms_ref, row, upstream, dnorms_ref, total, step, keep, first=0):
    gain = norms_ref[row : row + 1, :]
    if first == 0:
        dnorms_ref[row : row + 2, :] = jnp.zeros((2, D), f32)

    def body(rows):
        arriving = upstream(rows) if callable(upstream) else upstream[rows, :]
        down, d_gain, d_shift = norm_rows_back(x_ref[rows, :].astype(f32), gain, arriving)
        dnorms_ref[row : row + 1, :] += d_gain
        dnorms_ref[row + 1 : row + 2, :] += d_shift
        if keep is not None:
            keep(rows, down)

    each_rows(total, step, body, first)


def soft_low(first_one, other_one):
    return 0.5 * (first_one + other_one - jnp.sqrt((first_one - other_one) ** 2 + 0.0001))


def soft_high(first_one, other_one):
    return 0.5 * (first_one + other_one + jnp.sqrt((first_one - other_one) ** 2 + 0.0001))


def softplus(value):
    return jnp.maximum(value, 0.0) + jnp.log1p(jnp.exp(-jnp.abs(value)))


@jax.custom_vjp
def smooth_relu(value):
    return softplus(value)


def smooth_relu_keep(value):
    return softplus(value), value


def smooth_relu_back(value, upstream):
    return (upstream * (1.0 / (1.0 + jnp.exp(-value))),)


smooth_relu.defvjp(smooth_relu_keep, smooth_relu_back)


def cell_losses(px, py, pw, ph, gx, gy, gw, gh):
    absolute = (
        jnp.sqrt((px - gx) ** 2 + 0.01)
        + jnp.sqrt((py - gy) ** 2 + 0.01)
        + jnp.sqrt((pw - gw) ** 2 + 0.01)
        + jnp.sqrt((ph - gh) ** 2 + 0.01)
    )
    left_p, right_p = px - 0.5 * pw, px + 0.5 * pw
    low_p, top_p = py - 0.5 * ph, py + 0.5 * ph
    left_g, right_g = gx - 0.5 * gw, gx + 0.5 * gw
    low_g, top_g = gy - 0.5 * gh, gy + 0.5 * gh
    across = smooth_relu(20.0 * (soft_low(right_p, right_g) - soft_high(left_p, left_g))) / 20.0
    upward = smooth_relu(20.0 * (soft_low(top_p, top_g) - soft_high(low_p, low_g))) / 20.0
    common = across * upward
    union = pw * ph + gw * gh - common
    hull = (soft_high(right_p, right_g) - soft_low(left_p, left_g)) * (
        soft_high(top_p, top_g) - soft_low(low_p, low_g)
    )
    ratio = common / union - (hull - union) / hull
    return 5.0 * absolute + 2.0 * (1.0 - ratio)


def split_sum(left, value):
    high = value.astype(bf16)
    rest = (value - high.astype(f32)).astype(bf16)
    return dot(left, high) + dot(left, rest)


def alive_cells(mask, length):
    slot = lax.broadcasted_iota(jnp.int32, (1, CELLS), 1)
    return ((mask > 0) & (slot < lax.div(length, 4))).astype(f32)


def cell_rows(index, length):
    whole = jnp.floor((index.astype(f32) + 0.5) / length.astype(f32))
    return index - whole.astype(jnp.int32) * length


def decoder_kernel(
    tags_ref, lengths_ref, mask_ref, index_ref, target_ref, scale_ref, mem_ref,
    w_qkv, w_out, w_cq, w_ckv, w_co, w_in, w_ffo, w_embed, w_head, w_box, norms, w_box_out,
    loss_ref, dmem_ref, d_qkv, d_out, d_cq, d_ckv, d_co, d_in, d_ffo, d_embed, d_head, d_box, d_norms, d_box_out,
    e_ref, h1_ref, qkv_ref, o1_ref, lse1_ref, y1_ref, h2_ref, cq_ref, ckv_ref, o2_ref, lse2_ref, y2_ref,
    h3_ref, u_ref, g_ref, y3_ref, z_ref, dy_ref, dh_ref, og_ref, up_ref, delta_ref, need, done,
):
    tables = tags_ref.shape[0]
    rows = tables * TAGS

    def tag_members(table):
        member = lax.broadcasted_iota(jnp.int32, (V, TAGS), 0) == tags_ref[table : table + 1, :]
        return member.astype(f32).astype(bf16)

    for table in range(tables):
        e_ref[table * TAGS : (table + 1) * TAGS, :] = dot(tag_members(table), w_embed[...], 0, 0)
    norm_all(e_ref, norms, 0, h1_ref, rows, TAG_CHUNK)
    need("qkv")
    project(h1_ref, w_qkv, qkv_ref, 3 * D, 0.125)
    attend(tables, qkv_ref, qkv_ref, D, qkv_ref, 2 * D, o1_ref, lse1_ref, TAGS, TAGS, True)
    need("out")
    add_project(e_ref, o1_ref, w_out, y1_ref)
    norm_all(y1_ref, norms, 2, h2_ref, rows, TAG_CHUNK)
    need("cross_q")
    project(h2_ref, w_cq, cq_ref, D, 0.125)
    need("mem")
    need("cross_kv")
    project(mem_ref, w_ckv, ckv_ref, 2 * D)
    attend(tables, cq_ref, ckv_ref, 0, ckv_ref, D, o2_ref, lse2_ref, TAGS, IMG, False)
    need("cross_out")
    add_project(y1_ref, o2_ref, w_co, y2_ref)
    norm_all(y2_ref, norms, 4, h3_ref, rows, TAG_CHUNK)
    need("ffn_in")
    ffn_forward(h3_ref, w_in, u_ref, g_ref)
    need("ffn_out")
    add_project(y2_ref, g_ref, w_ffo, y3_ref)
    norm_all(y3_ref, norms, 6, z_ref, rows, TAG_CHUNK)

    need("box_in")
    scale = scale_ref[0, 0]
    loss = jnp.zeros((1, 1), f32)
    picked, inners, box_ups = [], [], []
    head_sum = jnp.zeros((V, D), f32)
    box_in_sum = jnp.zeros((D, D), f32)
    box_out_sum = jnp.zeros((16, D), f32)
    for table in range(tables):
        own = slice(table * TAGS, (table + 1) * TAGS)
        final = z_ref[own, :]
        logits = dot(w_head[...], final, 1, 1)
        peak = jnp.max(logits, 0, keepdims=True)
        weight = jnp.exp(logits - peak)
        total = jnp.sum(weight, 0, keepdims=True)
        length = lengths_ref[table]
        slot = lax.broadcasted_iota(jnp.int32, (1, TAGS), 1)
        counted = (slot < length - 1).astype(f32)
        tags = jnp.broadcast_to(tags_ref[table : table + 1, :], (8, TAGS))
        upcoming = pltpu.roll(tags, TAGS - 1, 1)[0:1]
        wanted = lax.broadcasted_iota(jnp.int32, (V, TAGS), 0) == upcoming
        chosen = jnp.sum(jnp.where(wanted, logits - peak - jnp.log(total), 0.0), 0, keepdims=True)
        loss = loss - jnp.sum(counted * chosen, 1, keepdims=True)
        dlogits = (weight / total - wanted.astype(f32)) * counted * scale
        tag_up = dlogits.astype(bf16)
        head_sum = head_sum + dot(tag_up, final)
        dfinal = dot(tag_up, w_head[...], 0, 0)
        select = (
            (lax.broadcasted_iota(jnp.int32, (TAGS, CELLS), 0) == cell_rows(index_ref[table : table + 1, :], length))
            .astype(f32)
            .astype(bf16)
        )
        cells = dot(select, final, 0, 0).astype(bf16)
        inner = dot(cells, w_box[...])
        active = gelu(inner).astype(bf16)
        raw = dot(w_box_out[...], active, 1, 1)
        soft = 1.0 / (1.0 + jnp.exp(-raw))
        ratios = tuple(soft[k : k + 1, :] for k in range(4))
        wished = tuple(target_ref[table, k : k + 1, :] for k in range(4))
        alive = alive_cells(mask_ref[table : table + 1, :], length)
        cell, pull = jax.vjp(lambda *parts: cell_losses(*parts, *wished), *ratios)
        loss = loss + jnp.sum(alive * cell, 1, keepdims=True)
        downs = pull(alive * scale)
        fill = jnp.zeros((16, CELLS), f32)
        index = lax.broadcasted_iota(jnp.int32, (16, CELLS), 0)
        for k in range(4):
            value = downs[k] * ratios[k] * (1.0 - ratios[k])
            fill = jnp.where(index == k, value, fill)
        box_up = fill.astype(bf16)
        box_out_sum = box_out_sum + dot(box_up, active)
        dinner = (gelu_slope(inner) * dot(box_up, w_box_out[...], 0, 0)).astype(bf16)
        box_in_sum = box_in_sum + dot(cells, dinner, 0, 0)
        dh_ref[own, :] = dfinal + split_sum(select, dot(dinner, w_box[...], 1, 1))
    loss_ref[...] = jnp.broadcast_to(loss, loss_ref.shape)
    d_head[...] = head_sum.astype(bf16)
    d_box[...] = box_in_sum.astype(bf16)
    done("box_in")
    d_box_out[...] = box_out_sum.astype(bf16)

    def start_sum(block, down):
        dy_ref[block, :] = down
        og_ref[block, :] = down.astype(bf16)

    def add_sum(block, down):
        total = down + dy_ref[block, :]
        dy_ref[block, :] = total
        og_ref[block, :] = total.astype(bf16)

    norm_all_back(y3_ref, norms, 6, dh_ref, d_norms, rows, TAG_CHUNK, start_sum)
    ffn_backward(og_ref, h3_ref, u_ref, g_ref, w_in, w_ffo, d_in, d_ffo, dh_ref)
    done("ffn_in")
    done("ffn_out")
    norm_all_back(y2_ref, norms, 4, dh_ref, d_norms, rows, TAG_CHUNK, add_sum)

    weight_grad(o2_ref, og_ref, d_co)
    done("cross_out")
    project_back(og_ref, w_co, up_ref)
    head_sums(tables, up_ref, o2_ref, delta_ref, TAGS)
    attend_back(
        (0, tables), cq_ref, ckv_ref, 0, ckv_ref, D, up_ref, lse2_ref, delta_ref,
        cq_ref, ckv_ref, ckv_ref, TAGS, IMG, False,
    )
    weight_grad(h2_ref, cq_ref, d_cq)
    done("cross_q")
    weight_grad(mem_ref, ckv_ref, d_ckv)
    done("cross_kv")
    project_back(ckv_ref, w_ckv, dmem_ref)
    done("mem")
    project_back(cq_ref, w_cq, dh_ref)
    norm_all_back(y1_ref, norms, 2, dh_ref, d_norms, rows, TAG_CHUNK, add_sum)

    weight_grad(o1_ref, og_ref, d_out)
    done("out")
    project_back(og_ref, w_out, up_ref)
    head_sums(tables, up_ref, o1_ref, delta_ref, TAGS)
    attend_back(
        (0, tables), qkv_ref, qkv_ref, D, qkv_ref, 2 * D, up_ref, lse1_ref, delta_ref,
        qkv_ref, qkv_ref, qkv_ref, TAGS, TAGS, True,
    )
    weight_grad(h1_ref, qkv_ref, d_qkv)
    done("qkv")
    project_back(qkv_ref, w_qkv, dh_ref)
    norm_all_back(e_ref, norms, 0, dh_ref, d_norms, rows, TAG_CHUNK, add_sum)
    embed_sum = jnp.zeros((V, D), f32)
    for table in range(tables):
        embed_sum = embed_sum + split_sum(
            tag_members(table), dy_ref[table * TAGS : (table + 1) * TAGS, :]
        )
    d_embed[...] = embed_sum.astype(bf16)


DECODER_NAMES = (
    "qkv", "out", "cross_q", "cross_kv", "cross_out", "ffn_in", "ffn_out", "embed", "head", "box_in", "norms", "box_out",
)


DECODER_MOVED = ("qkv", "out", "cross_q", "mem", "cross_kv", "cross_out", "ffn_in", "ffn_out", "box_in")


def decoder_step(prepared, scale, memory, weights):
    tables = prepared[0].shape[0]
    rows = tables * TAGS
    image_rows = memory.shape[0]
    arrays = {"mem": memory, **{name: weights[name] for name in DECODER_NAMES}}
    grads = {
        name: jax.ShapeDtypeStruct(array.shape, f32 if name in ("norms", "mem") else bf16)
        for name, array in arrays.items()
    }
    vmem, hbm = pl.BlockSpec(memory_space=pltpu.VMEM), pl.BlockSpec(memory_space=pl.ANY)
    smem = pl.BlockSpec(memory_space=pltpu.SMEM)
    low = lambda width, height=rows: pltpu.VMEM((height, width), bf16)
    full = lambda width, height=rows: pltpu.VMEM((height, width), f32)
    stats = pltpu.VMEM((tables * HEADS, TAGS), f32)
    places = [hbm if name in DECODER_MOVED else vmem for name in arrays]
    moved, total = len(DECODER_MOVED), len(arrays)

    def kernel(*refs):
        ready, refs = refs[:6], refs[6:]
        sources, refs = dict(zip(arrays, refs[:total])), refs[total:]
        loss_ref, targets, refs = refs[0], dict(zip(arrays, refs[1 : total + 1])), refs[total + 1 :]
        inside = dict(zip(DECODER_MOVED, refs[:moved]))
        outside = dict(zip(DECODER_MOVED, refs[moved : 2 * moved]))
        in_sem, out_sem = refs[2 * moved : 2 * moved + 2]
        fetch = {
            name: pltpu.make_async_copy(sources[name], inside[name], in_sem.at[k])
            for k, name in enumerate(DECODER_MOVED)
        }
        give = {
            name: pltpu.make_async_copy(outside[name], targets[name], out_sem.at[k])
            for k, name in enumerate(DECODER_MOVED)
        }
        for name in DECODER_MOVED:
            fetch[name].start()
        given = {**sources, **inside}
        taken = {**targets, **outside}
        decoder_kernel(
            *ready, given["mem"], *[given[name] for name in DECODER_NAMES],
            loss_ref, taken["mem"], *[taken[name] for name in DECODER_NAMES],
            *refs[2 * moved + 2 :], lambda name: fetch[name].wait(), lambda name: give[name].start(),
        )
        for name in DECODER_MOVED:
            give[name].wait()

    outs = pl.pallas_call(
        kernel,
        out_shape=(jax.ShapeDtypeStruct((8, 128), f32), *grads.values()),
        in_specs=[vmem, smem, vmem, vmem, vmem, smem] + places,
        out_specs=(vmem, *places),
        scratch_shapes=[
            *[pltpu.VMEM(arrays[name].shape, arrays[name].dtype) for name in DECODER_MOVED],
            *[pltpu.VMEM(grads[name].shape, grads[name].dtype) for name in DECODER_MOVED],
            pltpu.SemaphoreType.DMA((moved,)), pltpu.SemaphoreType.DMA((moved,)),
            full(D), low(D), low(3 * D), low(D), stats, full(D), low(D), low(D), low(2 * D, image_rows), low(D), stats,
            full(D), low(D), full(FF), low(FF), full(D), low(D), full(D), full(D), low(D), low(D), stats,
        ],
        compiler_params=pltpu.CompilerParams(vmem_limit_bytes=VMEM_LIMIT),
        name="decoder_step",
    )(*prepared, scale, *arrays.values())
    return outs[0], outs[1], dict(zip(DECODER_NAMES, outs[2:]))


AXES = ("wide", "narrow")
MESH = pl.DeviceIdType.MESH
ORDERS = (("a", "y", "b"), ("a", "b", "y"))


class Place:
    def __init__(self, wide, narrow):
        inner = 2 if wide % 2 == 0 else 1
        self.sizes = {"a": wide // inner, "b": inner, "y": narrow // 2, "c": 2}
        self.narrow = narrow
        self.count = wide * narrow

    def locate(self):
        wide, narrow = lax.axis_index("wide"), lax.axis_index("narrow")
        inner = self.sizes["b"]
        self.here = {
            "a": lax.div(wide, inner),
            "b": lax.rem(wide, inner),
            "y": lax.div(narrow, 2),
            "c": lax.rem(narrow, 2),
        }
        return self

    def moved(self, steps):
        there = dict(self.here)
        for part, step in steps.items():
            there[part] = lax.rem(there[part] + step, self.sizes[part])
        return there

    def device(self, there):
        return (there["a"] * self.sizes["b"] + there["b"], there["y"] * 2 + there["c"])

    def index(self, there):
        wide, narrow = self.device(there)
        return wide * self.narrow + narrow

    def peers(self):
        return [(part, step) for part, size in self.sizes.items() for step in range(1, size)]

    def in_plane(self, step):
        size, wide = self.sizes["b"], self.sizes["y"]
        here = (self.here["b"] * wide + self.here["y"]) * 2 + self.here["c"]
        there = lax.rem(here + step, size * wide * 2)
        return there, {
            **self.here,
            "b": lax.div(there, wide * 2),
            "y": lax.rem(lax.div(there, 2), wide),
            "c": lax.rem(there, 2),
        }

    def plane(self):
        return self.sizes["b"] * self.sizes["y"] * 2

    def greet(self, whole_plane=False):
        barrier = pltpu.get_barrier_semaphore()
        peers = [self.moved({part: step}) for part, step in self.peers()]
        if whole_plane:
            peers = [self.in_plane(step)[1] for step in range(1, self.plane())] + [
                self.moved({"a": step}) for step in range(1, self.sizes["a"])
            ]
        for there in peers:
            pl.semaphore_signal(
                barrier, inc=1, device_id=self.device(there), device_id_type=MESH
            )
        pl.semaphore_wait(barrier, len(peers))


def block_rows(amount):
    return -(-(amount // 128 + 3) // 16) * 16


def flat_rows(amount, count):
    return -(-((count - 1) * amount // 128 + block_rows(amount)) // 8) * 8


def layout_bases(layout):
    offset = 0
    for name, (height, breadth) in layout:
        yield name, height, breadth, offset // 128
        offset += height * breadth


def place_blocks(all_ref, flat_ref, amount):
    count, rows, _ = all_ref.shape
    used = amount // 128 + 2
    flat_ref[0:8, :] = jnp.zeros((8, 128), f32)

    @pl.loop(0, count)
    def _(device):
        start = lax.div(device * amount, 128)
        before = flat_ref[pl.ds(start, 1), :]
        flat_ref[pl.ds(start, used), :] = all_ref[device, :used, :].astype(f32)
        flat_ref[pl.ds(start, 1), :] = before + all_ref[device, 0:16, :].astype(f32)[0:1]


def one_hot(shape, match):
    first = lax.broadcasted_iota(jnp.int32, shape, 0)
    second = lax.broadcasted_iota(jnp.int32, shape, 1)
    return match(first, second).astype(f32).astype(bf16)


def take_matrices(flat_ref, layout, out_refs, done=lambda name: None):
    for name, height, breadth, base in layout_bases(layout):
        out_ref = out_refs[name]
        if name == "head":
            turned = flat_ref[base : base + 128, :].T.astype(bf16)
            total = jnp.zeros((V, D), f32)
            for part in range(4):
                spread = one_hot((128, D), lambda row, column: column == 4 * row + part)
                total = total + dot(turned[part * V : (part + 1) * V, :], spread)
            out_ref[...] = total.astype(bf16)
        elif name == "box_out":
            block = flat_ref[base : base + 16, :].astype(bf16)
            own = one_hot((16, D), lambda row, column: lax.div(column, 32) == row).astype(f32)
            index = lax.broadcasted_iota(jnp.int32, (16, D), 0)
            total = jnp.zeros((16, D), f32)
            for k in range(4):
                pick = one_hot((128, D), lambda lane, column: lane == 4 * lax.rem(column, 32) + k)
                line = jnp.sum(dot(block, pick) * own, 0, keepdims=True)
                total = jnp.where(index == k, line, total)
            out_ref[...] = total.astype(bf16)
        else:
            wide = breadth // 128
            for column in range(wide):
                out_ref[:, column * 128 : (column + 1) * 128] = flat_ref[
                    pl.ds(base + column, height, stride=wide), :
                ].astype(out_ref.dtype)
        done(name)


def put_matrices(flat_ref, layout, refs, need):
    for name, height, breadth, base in layout_bases(layout):
        ref = refs[name]
        need(name)
        if name == "head":
            total = jnp.zeros((128, 128), f32)
            for part in range(4):
                pick = one_hot((128, D), lambda row, column: column == 4 * row + part)
                shift = one_hot((V, 128), lambda row, lane: lane == V * part + row)
                total = total + dot(dot(pick, ref[...], 1, 1).astype(bf16), shift)
            flat_ref[base : base + 128, :] = total
        elif name == "box_out":
            own = one_hot((16, D), lambda row, column: lax.div(column, 32) == row).astype(f32)
            total = jnp.zeros((16, 128), f32)
            for k in range(4):
                line = ref[...].astype(f32)[k : k + 1, :]
                spread = one_hot((D, 128), lambda column, lane: lane == 4 * lax.rem(column, 32) + k)
                total = total + dot((own * line).astype(bf16), spread)
            flat_ref[base : base + 16, :] = total
        else:
            wide = breadth // 128
            for column in range(wide):
                flat_ref[pl.ds(base + column, height, stride=wide), :] = ref[
                    :, column * 128 : (column + 1) * 128
                ].astype(f32)


def weight_shapes(layout):
    shapes = {name: extent for name, extent in layout}
    if "head" in shapes:
        shapes["head"], shapes["box_out"] = (V, D), (16, D)
    return {
        name: jax.ShapeDtypeStruct(extent, f32 if name == "norms" else bf16)
        for name, extent in shapes.items()
    }


def pack_grads(grads, layout, amount, count, name):
    names = [piece for piece, _ in layout]
    pieces = len(names)
    rows = block_rows(amount)

    def kernel(*refs):
        sources, block_hbm, refs = refs[:pieces], refs[pieces], refs[pieces + 1 :]
        local, (flat_ref, block_ref, in_sem, out_sem) = refs[:pieces], refs[pieces:]
        fetch = {
            piece: pltpu.make_async_copy(source, target, in_sem.at[k])
            for k, (piece, source, target) in enumerate(zip(names, sources, local))
        }
        for one in fetch.values():
            one.start()
        tail = sum(extent[0] * extent[1] for _, extent in layout) // 128
        flat_ref[tail:, :] = jnp.zeros((flat_ref.shape[0] - tail, 128), f32)
        put_matrices(flat_ref, layout, dict(zip(names, local)), lambda piece: fetch[piece].wait())

        def give(owner):
            return pltpu.make_async_copy(block_ref.at[owner], block_hbm.at[owner], out_sem.at[owner])

        @pl.loop(0, count)
        def _(owner):
            start = lax.div(owner * amount, 128)
            block_ref[owner, :, :] = flat_ref[pl.ds(start, rows), :].astype(bf16)
            give(owner).start()

        @pl.loop(0, count)
        def _(owner):
            give(owner).wait()

    hbm = pl.BlockSpec(memory_space=pl.ANY)
    return pl.pallas_call(
        kernel,
        out_shape=jax.ShapeDtypeStruct((count, rows, 128), bf16),
        in_specs=[hbm] * pieces,
        out_specs=hbm,
        scratch_shapes=[
            *[pltpu.VMEM(grads[piece].shape, grads[piece].dtype) for piece in names],
            pltpu.VMEM((flat_rows(amount, count), 128), f32),
            pltpu.VMEM((count, rows, 128), bf16),
            pltpu.SemaphoreType.DMA((pieces,)),
            pltpu.SemaphoreType.DMA((count,)),
        ],
        compiler_params=pltpu.CompilerParams(vmem_limit_bytes=VMEM_LIMIT),
        name=name,
    )(*[grads[piece] for piece in names])


class Reduction:
    def __init__(self, place, core, pick, own_ref, mine_ref, got_ref, load_sem, send_sem, recv_sem):
        self.place, self.pick = place, pick
        self.own, self.mine, self.got = own_ref, mine_ref, got_ref
        self.load_sem, self.send_sem, self.recv_sem = load_sem, send_sem, recv_sem
        self.order, self.other = ORDERS[core], ORDERS[1 - core]
        self.s1, self.s2, self.s3 = (place.sizes[part] for part in self.order)
        self.half = place.count // 2
        self.base3 = self.half
        self.base2 = self.base3 + (self.s3 - 1) * self.s1 * self.s2
        self.base1 = self.base2 + (self.s2 - 1) * self.s1

    def slot(self, steps):
        sizes = self.place.sizes
        return (steps["a"] * sizes["b"] + steps["b"]) * sizes["y"] + steps["y"]

    def owner(self, steps):
        return self.place.index(self.place.moved(steps))

    def only(self, steps, body):
        if self.pick is None:
            body()
        else:
            pl.when(self.pick(self.owner(steps)))(body)

    def copy(self, source, slot, part, step):
        return pltpu.make_async_remote_copy(
            src_ref=source,
            dst_ref=self.got.at[slot],
            send_sem=self.send_sem.at[slot],
            recv_sem=self.recv_sem.at[slot],
            device_id=self.place.device(self.place.moved({part: step})),
            device_id_type=MESH,
        )

    def load(self, steps):
        slot = self.slot(steps)
        return pltpu.make_async_copy(
            self.own.at[self.owner(steps)], self.mine.at[slot], self.load_sem.at[slot]
        )

    def took(self, slot):
        self.copy(self.mine.at[0], slot, "c", 1).wait_recv()

    def value(self, slot):
        return self.got[slot].astype(f32)

    def levels(self, order):
        s1, s2, s3 = (self.place.sizes[part] for part in order)
        return (
            (s1 * s2 * (s3 - 1), lambda n: (s1 - 1 - lax.rem(n, s1), s2 - 1 - lax.rem(lax.div(n, s1), s2), lax.div(n, s1 * s2) + 1)),
            (s1 * (s2 - 1), lambda n: (s1 - 1 - lax.rem(n, s1), lax.div(n, s1) + 1, 0)),
            (s1, lambda n: (s1 - 1 - n, 0, 0)),
        )

    def to_sibling(self):
        if self.load_sem is not None:
            for amount, where in self.levels(self.order):

                @pl.loop(0, amount)
                def _(number):
                    self.load(dict(zip(self.order, where(number)))).start()

        for amount, where in self.levels(self.other):

            @pl.loop(0, amount)
            def _(number):
                steps = dict(zip(self.other, where(number)))
                slot = self.slot(steps)

                def send():
                    block = slot if self.load_sem is None else self.owner({**steps, "c": 1})
                    self.copy(self.own.at[block], slot, "c", 1).start()

                self.only({**steps, "c": 1}, send)

    def partial(self, p, q, r):
        steps = dict(zip(self.order, (p, q, r)))
        slot = self.slot(steps)
        if self.load_sem is not None:
            self.load(steps).wait()
        self.took(slot)
        return slot, self.mine[slot].astype(f32) + self.value(slot)

    def add_third(self, total, p, q):
        for step in range(1, self.s3):
            slot = self.base3 + ((step - 1) * self.s1 + p) * self.s2 + q
            self.took(slot)
            total = total + self.value(slot)
        return total

    def add_second(self, total, p):
        for step in range(1, self.s2):
            slot = self.base2 + (step - 1) * self.s1 + p
            self.took(slot)
            total = total + self.value(slot)
        return total

    def send(self, own_slot, total, slot, part, step):
        self.mine[own_slot] = total.astype(bf16)
        self.copy(self.mine.at[own_slot], slot, part, step).start()

    def third(self):
        amount, where = self.levels(self.order)[0]

        @pl.loop(0, amount)
        def _(number):
            p, q, r = where(number)

            def body():
                own_slot, total = self.partial(p, q, r)
                slot = self.base3 + ((r - 1) * self.s1 + p) * self.s2 + q
                self.send(own_slot, total, slot, self.order[2], r)

            self.only(dict(zip(self.order, (p, q, r))), body)

    def second(self):
        amount, where = self.levels(self.order)[1]

        @pl.loop(0, amount)
        def _(number):
            p, q, _ = where(number)

            def body():
                own_slot, total = self.partial(p, q, 0)
                total = self.add_third(total, p, q)
                self.send(own_slot, total, self.base2 + (q - 1) * self.s1 + p, self.order[1], q)

            self.only(dict(zip(self.order, (p, q, 0))), body)

    def first(self):
        @pl.loop(1, self.s1)
        def _(p):
            def body():
                own_slot, total = self.partial(p, 0, 0)
                total = self.add_second(self.add_third(total, p, 0), p)
                self.send(own_slot, total, self.base1 + p - 1, self.order[0], p)

            self.only({self.order[0]: p}, body)

    def last(self, out_ref):
        def body():
            _, total = self.partial(0, 0, 0)
            out_ref[...] = self.add_second(self.add_third(total, 0, 0), 0)

            @pl.loop(1, self.s1)
            def _(p):
                slot = self.base1 + p - 1
                self.took(slot)
                out_ref[...] += self.value(slot)

        self.only({}, body)

    def close(self):
        @pl.loop(0, self.place.count - 1)
        def _(slot):
            self.copy(self.mine.at[0], slot, "c", 1).wait_send()


def reduction_memory(count, rows):
    half = count // 2
    return [pltpu.VMEM((half, rows, 128), bf16), pltpu.VMEM((count - 1, rows, 128), bf16)]


def reduction_signals(count, loads):
    return [pltpu.SemaphoreType.DMA((n,)) for n in ([count // 2] if loads else []) + [count - 1] * 2]


def reduce_stage(place, stage, pick, *members):
    for core in range(2):

        @pl.when(place.here["c"] == core)
        def _():
            stage(Reduction(place, core, pick, *members))


def cut_for_reduction(place, pick, flat_ref, amount, mine_ref, other_ref):
    rows = mine_ref.shape[1]
    sizes = place.sizes

    @pl.loop(0, place.count // 2)
    def _(slot):
        steps = {
            "a": lax.div(slot, sizes["b"] * sizes["y"]),
            "b": lax.rem(lax.div(slot, sizes["y"]), sizes["b"]),
            "y": lax.rem(slot, sizes["y"]),
        }
        for core, ref in ((0, mine_ref), (1, other_ref)):
            owner = place.index(place.moved({**steps, "c": core}))

            @pl.when(pick(owner))
            def _():
                ref[slot] = flat_ref[pl.ds(lax.div(owner * amount, 128), rows), :].astype(bf16)


def sum_everywhere(place, value, box_ref, send_sem, recv_sem):
    base = 0
    plane = [place.in_plane(step) for step in range(place.plane())]
    line = [place.moved({"a": step}) for step in range(place.sizes["a"])]
    for members in (plane, [(there["a"], there) for there in line]):

        def copy(step, number, base=base, members=members):
            return pltpu.make_async_remote_copy(
                src_ref=box_ref.at[base + number],
                dst_ref=box_ref.at[base + number],
                send_sem=send_sem.at[base + step],
                recv_sem=recv_sem.at[base + number],
                device_id=place.device(members[step][1]),
                device_id_type=MESH,
            )

        size = len(members)
        mine = members[0][0]
        box_ref[base + mine] = value
        for step in range(1, size):
            copy(step, mine).start()
        for step in range(1, size):
            copy(step, members[step][0]).wait_recv()
        for step in range(1, size):
            copy(step, mine).wait_send()
        value = box_ref[base]
        for other in range(1, size):
            value = value + box_ref[base + other]
        base += size
    return value


def own_squares(place, out_ref, amount):
    rows = out_ref.shape[0]
    offset = lax.rem(place.index(place.here) * amount, 128)
    position = (
        lax.broadcasted_iota(jnp.int32, (rows, 128), 0) * 128
        + lax.broadcasted_iota(jnp.int32, (rows, 128), 1)
        - offset
    )
    value = jnp.where((position >= 0) & (position < amount), out_ref[...], 0.0)
    return jnp.sum(jnp.sum(value * value, 0, keepdims=True), 1, keepdims=True)


def weight_grad_flat(a_ref, b_ref, flat_ref, base, breadth):
    wide = breadth // 128
    for start in range(0, breadth, 512):
        value = dot(a_ref[...], b_ref[:, start : start + 512], 0, 0)
        store_flat(value, flat_ref, base + start // 128, wide)


def store_flat(value, flat_ref, base, wide):
    rows, columns = value.shape
    for part in range(columns // 128):
        flat_ref[pl.ds(base + part, rows, stride=wide), :] = value[:, part * 128 : (part + 1) * 128]


def encoder_backward(place, images, stored, dmem, weights, decoder_blocks, amounts, loss_block):
    rows = images.shape[0]
    tables = rows // IMG
    qkv, mixed, lse, middle = stored
    bases = {name: base for name, _, _, base in layout_bases(encoder_layout())}
    block, small = decoder_blocks.shape[1], block_rows(amounts[0])
    flat_count = flat_rows(amounts[0], place.count)
    first_early = -(-bases["out"] * 128 // amounts[0])
    end_early = max((bases["norms"] - amounts[0] // 128 - 2) * 128 // amounts[0], first_early)
    steps = place.plane() + place.sizes["a"]
    early = lambda owner: (owner >= first_early) & (owner < end_early)
    late = lambda owner: owner < first_early
    latest = lambda owner: owner >= end_early

    def kernel(
        x_hbm, qkv_hbm, o_hbm, lse_ref, x1_hbm, dmem_hbm, w_qkv_hbm, w_out_hbm, w_in_hbm, w_ffo_hbm, norms, own_ref, loss_ref,
        encoder_ref, decoder_ref, stat_ref,
        w_qkv, h_ref, g_ref, og_ref, qkv_ref, delta_ref, d_norms, flat_ref, fetch_sem, o_ref, x1_ref, dmem_ref, w_out, w_in, w_ffo,
        theirs_ref, mine_ref, got_ref, far_mine_ref, far_got_ref, *signals,
    ):
        far = (None, own_ref, far_mine_ref, far_got_ref, *signals[:3])
        near = (theirs_ref, mine_ref, got_ref, None, *signals[3:5])
        box_ref, box_send, box_recv = signals[5:]
        work = functools.partial(reduce_stage, place)
        place.locate()
        fetches = [
            pltpu.make_async_copy(source, target, fetch_sem.at[k])
            for k, (source, target) in enumerate(
                (
                    (qkv_hbm, qkv_ref), (w_qkv_hbm, w_qkv), (x_hbm, g_ref.at[:, :D]), (x1_hbm, x1_ref), (dmem_hbm, dmem_ref),
                    (w_in_hbm, w_in), (w_ffo_hbm, w_ffo), (o_hbm, o_ref), (w_out_hbm, w_out),
                )
            )
        ]
        x_ref = g_ref.at[:, :D]
        for number in (3, 4, 5, 6, 7, 8, 0, 1):
            fetches[number].start()
        place.greet(True)
        work(lambda one: one.to_sibling(), *far)
        tail = bases["norms"] + 4 * D // 128
        flat_ref[tail:, :] = jnp.zeros((flat_count - tail, 128), f32)
        fetches[3].wait()
        norm_all(x1_ref, norms, 2, h_ref, rows, IMG_CHUNK)
        for number in (4, 5, 6, 7, 8):
            fetches[number].wait()
        og_ref[...] = dmem_ref[...].astype(bf16)
        for start in range(0, FF, 256):
            lanes = slice(start, start + 256)
            inner = dot(h_ref[...], w_in[:, lanes])
            back = dot(og_ref[...], w_ffo[lanes, :], 1, 1)
            part = dot(gelu(inner).astype(bf16), og_ref[...], 0, 0)
            store_flat(part, flat_ref, bases["ffn_out"] + start * 4, 4)
            g_ref[:, lanes] = (gelu_slope(inner) * back).astype(bf16)
        work(lambda one: one.third(), *far)
        weight_grad_flat(h_ref, g_ref, flat_ref, bases["ffn_in"], FF)

        def keep(part, down):
            og_ref[part, :] = (down + dmem_ref[part, :]).astype(bf16)

        norm_all_back(
            x1_ref, norms, 2, lambda part: dot(g_ref[part, :], w_in[...], 1, 1), d_norms, rows, IMG_CHUNK, keep
        )
        fetches[2].start()
        weight_grad_flat(o_ref, og_ref, flat_ref, bases["out"], D)
        cut_for_reduction(place, early, flat_ref, amounts[0], mine_ref, theirs_ref)
        work(lambda one: one.to_sibling(), early, *near)

        def project_rows(part):
            og_ref[part, :] = dot(og_ref[part, :], w_out[...], 1, 1).astype(bf16)

        each_rows(rows, IMG_CHUNK, project_rows)
        head_sums(tables, og_ref, o_ref, delta_ref, IMG)
        work(lambda one: one.second(), *far)
        fetches[0].wait()

        def between(step):
            @pl.when(step == 1)
            def _():
                work(lambda one: one.third(), early, *near)

            @pl.when(step == 2)
            def _():
                work(lambda one: one.first(), *far)

            @pl.when(step == 4)
            def _():
                work(lambda one: one.second(), early, *near)

            @pl.when(step == 5)
            def _():
                work(lambda one: one.last(decoder_ref), *far)

            @pl.when(step == 6)
            def _():
                work(lambda one: one.first(), early, *near)

        attend_back(
            (0, tables), qkv_ref, qkv_ref, D, qkv_ref, 2 * D, og_ref, lse_ref, delta_ref,
            qkv_ref, qkv_ref, qkv_ref, IMG, IMG, False, between,
        )
        work(lambda one: one.last(encoder_ref), early, *near)
        fetches[1].wait()
        fetches[2].wait()
        norm_all(x_ref, norms, 0, h_ref, rows, IMG_CHUNK)
        weight_grad_flat(h_ref, qkv_ref, flat_ref, bases["qkv"], 3 * D)
        cut_for_reduction(place, late, flat_ref, amounts[0], mine_ref, theirs_ref)
        work(lambda one: one.to_sibling(), late, *near)
        for table in range(tables):
            norm_all_back(
                x_ref, norms, 0, lambda part: dot(qkv_ref[part, :], w_qkv[...], 1, 1), d_norms,
                (table + 1) * IMG, IMG, None, table * IMG,
            )
            if table == 0:
                work(lambda one: one.third(), late, *near)
        store_flat(d_norms[...], flat_ref, bases["norms"], 4)
        cut_for_reduction(place, latest, flat_ref, amounts[0], mine_ref, theirs_ref)
        work(lambda one: one.to_sibling(), latest, *near)
        work(lambda one: one.second(), late, *near)
        work(lambda one: one.third(), latest, *near)
        work(lambda one: one.first(), late, *near)
        work(lambda one: one.second(), latest, *near)
        work(lambda one: one.first(), latest, *near)
        work(lambda one: one.last(encoder_ref), late, *near)
        work(lambda one: one.last(encoder_ref), latest, *near)
        squares = own_squares(place, encoder_ref, amounts[0]) + own_squares(
            place, decoder_ref, amounts[1]
        )
        me = place.index(place.here)
        for ref, amount in ((encoder_ref, amounts[0]), (decoder_ref, amounts[1])):
            ref[...] = shifted_back(ref[...], lax.rem(me * amount, 128))
        index = lax.broadcasted_iota(jnp.int32, (8, 128), 0)
        value = jnp.where(index == 0, squares, jnp.where(index == 1, loss_ref[...], 0.0))
        stat_ref[...] = sum_everywhere(place, value, box_ref, box_send, box_recv)
        work(lambda one: one.close(), *far)
        work(lambda one: one.close(), early, *near)

    vmem, hbm = pl.BlockSpec(memory_space=pltpu.VMEM), pl.BlockSpec(memory_space=pl.ANY)
    count = place.count
    return pl.pallas_call(
        kernel,
        out_shape=(
            jax.ShapeDtypeStruct((small, 128), f32),
            jax.ShapeDtypeStruct((block, 128), f32),
            jax.ShapeDtypeStruct((8, 128), f32),
        ),
        in_specs=[hbm, hbm, hbm, vmem, hbm, hbm, hbm, hbm, hbm, hbm, vmem, hbm, vmem],
        scratch_shapes=[
            pltpu.VMEM((D, 3 * D), bf16),
            pltpu.VMEM((rows, D), bf16),
            pltpu.VMEM((rows, FF), bf16),
            pltpu.VMEM((rows, D), bf16),
            pltpu.VMEM((rows, 3 * D), bf16),
            pltpu.VMEM((tables * HEADS, IMG), f32),
            pltpu.VMEM((4, D), f32),
            pltpu.VMEM((flat_count, 128), f32),
            pltpu.SemaphoreType.DMA((9,)),
            pltpu.VMEM((rows, D), bf16),
            pltpu.VMEM((rows, D), f32),
            pltpu.VMEM((rows, D), f32),
            pltpu.VMEM((D, D), bf16),
            pltpu.VMEM((D, FF), bf16),
            pltpu.VMEM((FF, D), bf16),
            pltpu.VMEM((count // 2, small, 128), bf16),
            *reduction_memory(count, small),
            *reduction_memory(count, block),
            *reduction_signals(count, True),
            *reduction_signals(count, False),
            pltpu.VMEM((steps, 8, 128), f32),
            pltpu.SemaphoreType.DMA((steps,)),
            pltpu.SemaphoreType.DMA((steps,)),
        ],
        compiler_params=pltpu.CompilerParams(
            collective_id=2, has_side_effects=True, vmem_limit_bytes=VMEM_LIMIT
        ),
        name="encoder_backward",
    )(
        images, qkv, mixed, lse, middle, dmem, weights["qkv"], weights["out"], weights["ffn_in"], weights["ffn_out"],
        weights["norms"], decoder_blocks, loss_block,
    )


class Spread:
    def __init__(self, place, core, view, send_sem, recv_sem):
        self.place, self.view, self.send_sem, self.recv_sem = place, view, send_sem, recv_sem
        self.order = ORDERS[core]
        self.s1, self.s2, self.s3 = (place.sizes[part] for part in self.order)
        self.base2 = self.s1 - 1
        self.base3 = self.base2 + self.s1 * (self.s2 - 1)
        self.base4 = self.base3 + self.s1 * self.s2 * (self.s3 - 1)

    def copy(self, p, q, r, core, part, step, number):
        one, two, three = self.order
        block = self.place.index(self.place.moved({one: p, two: q, three: r, "c": core}))
        return pltpu.make_async_remote_copy(
            src_ref=self.view(block),
            dst_ref=self.view(block),
            send_sem=self.send_sem.at[number],
            recv_sem=self.recv_sem.at[block],
            device_id=self.place.device(self.place.moved({part: step})),
            device_id_type=MESH,
        )

    def arrived(self, p, q, r, core=0):
        self.copy(p, q, r, core, "c", 1, 0).wait_recv()

    def to_sibling(self, p, q, r):
        number = self.base4 + (p * self.s2 + q) * self.s3 + r
        self.copy(p, q, r, 0, "c", 1, number).start()

    def to_third(self, p, q):
        for step in range(1, self.s3):
            number = self.base3 + (p * self.s2 + q) * (self.s3 - 1) + step - 1
            self.copy(p, q, 0, 0, self.order[2], step, number).start()

    def to_second(self, p):
        for step in range(1, self.s2):
            number = self.base2 + p * (self.s2 - 1) + step - 1
            self.copy(p, 0, 0, 0, self.order[1], step, number).start()

    def one(self):
        @pl.loop(1, self.s1)
        def _(step):
            self.copy(0, 0, 0, 0, self.order[0], step, step - 1).start()

        self.to_second(0)
        self.to_third(0, 0)
        self.to_sibling(0, 0, 0)

    def two(self):
        @pl.loop(1, self.s1)
        def _(p):
            self.arrived(p, 0, 0)
            self.to_second(p)
            self.to_third(p, 0)
            self.to_sibling(p, 0, 0)

    def three(self):
        @pl.loop(0, self.s1 * (self.s2 - 1))
        def _(number):
            p, q = lax.rem(number, self.s1), lax.div(number, self.s1) + 1
            self.arrived(p, q, 0)
            self.to_third(p, q)
            self.to_sibling(p, q, 0)

    def four(self):
        @pl.loop(0, self.s1 * self.s2 * (self.s3 - 1))
        def _(number):
            p, q = lax.rem(number, self.s1), lax.rem(lax.div(number, self.s1), self.s2)
            r = lax.div(number, self.s1 * self.s2) + 1
            self.arrived(p, q, r)
            self.to_sibling(p, q, r)

    def five(self):
        @pl.loop(0, self.s1 * self.s2 * self.s3)
        def _(number):
            p, q = lax.rem(number, self.s1), lax.rem(lax.div(number, self.s1), self.s2)
            self.arrived(p, q, lax.div(number, self.s1 * self.s2), 1)

    def close(self):
        @pl.loop(0, self.place.count - 1)
        def _(number):
            self.copy(0, 0, 0, 0, "c", 1, number).wait_send()


def shifted(value, offset):
    lane = lax.broadcasted_iota(jnp.int32, value.shape, 1)
    turned = pltpu.roll(value, offset, 1)
    return jnp.where(lane < offset, pltpu.roll(turned, 1, 0), turned)


def shifted_back(value, offset):
    lane = lax.broadcasted_iota(jnp.int32, value.shape, 1)
    turned = pltpu.roll(value, lax.rem(128 - offset, 128), 1)
    return jnp.where(lane < 128 - offset, turned, pltpu.roll(turned, value.shape[0] - 1, 0))


def gather_and_encode(place, images, encoder_block, decoder_block, cell_mask, lengths, amounts):
    rows = images.shape[0]
    tables = rows // IMG
    count = place.count
    layouts = (encoder_layout(), decoder_layout())
    shapes = [weight_shapes(layout) for layout in layouts]
    small, large = encoder_block.shape[0], decoder_block.shape[0]
    near, cut = small // 32 * 16, large // 32 * 16
    flat_counts = [flat_rows(amount, count) for amount in amounts]
    first, second = len(shapes[0]), len(shapes[1])
    matrices = [name for name in shapes[0] if name != "norms"]
    moved = [name for name in DECODER_MOVED if name != "mem"]

    def kernel(x_ref, encoder_ref, decoder_ref, mask_ref, lengths_ref, *refs):
        encoder_out = dict(zip(shapes[0], refs[:first]))
        decoder_out = dict(zip(shapes[1], refs[first : first + second]))
        count_ref, qkv_out, o_out, lse_ref, x1_out, mem_out = refs[first + second : first + second + 6]
        rest = refs[first + second + 6 :]
        encoder_all, decoder_all, flat_ref, qkv_ref, h_ref, g_ref = rest[:6]
        local = dict(zip(matrices, rest[6 : 6 + len(matrices)]))
        local["norms"] = encoder_out["norms"]
        o_ref, x1_ref, mem_ref, out_sem, far_sem = rest[6 + len(matrices) : 11 + len(matrices)]
        far = dict(zip(moved, rest[11 + len(matrices) : 11 + len(matrices) + len(moved)]))
        signals = rest[11 + len(matrices) + len(moved) :]
        views = (
            lambda block: encoder_all.at[block, :near],
            lambda block: encoder_all.at[block, near:],
            lambda block: decoder_all.at[block, :cut],
            lambda block: decoder_all.at[block, cut:],
        )
        place.locate()
        me = place.index(place.here)

        def go(*tasks):
            for core in range(2):

                @pl.when(place.here["c"] == core)
                def _():
                    for group, stage in tasks:
                        work = Spread(place, core, views[group], *signals[2 * group : 2 * group + 2])
                        getattr(work, stage)()

        own = shifted(encoder_ref[...], lax.rem(me * amounts[0], 128))
        row = lax.broadcasted_iota(jnp.int32, own.shape, 0)
        lane = lax.broadcasted_iota(jnp.int32, (1, 128), 1)
        counts = jnp.zeros((1, 128), f32)
        for table in range(tables):
            alive = alive_cells(mask_ref[table : table + 1, :], lengths_ref[table])
            counts = jnp.where(lane == table, jnp.sum(alive, 1, keepdims=True), counts)
        encoder_all[me] = jnp.where(row == small - 1, counts, own).astype(bf16)
        place.greet()
        go((0, "one"), (1, "one"))
        decoder_all[me] = shifted(decoder_ref[...], lax.rem(me * amounts[1], 128)).astype(bf16)
        go(
            (0, "two"), (1, "two"), (0, "three"), (2, "one"), (1, "three"), (3, "one"), (0, "four"), (1, "four"), (0, "five"), (1, "five"),
        )
        total = jnp.zeros((1, 128), f32)
        for device in range(count):
            total = total + encoder_all[device, small - 16 :, :].astype(f32)[15:16]
        count_ref[...] = jnp.broadcast_to(jnp.sum(total, 1, keepdims=True), count_ref.shape)
        place_blocks(encoder_all, flat_ref, amounts[0])
        take_matrices(flat_ref, layouts[0], local)
        outs = [
            pltpu.make_async_copy(local[name], encoder_out[name], out_sem.at[k])
            for k, name in enumerate(matrices)
        ]
        for out in outs:
            out.start()
        stored = ((qkv_ref, qkv_out), (o_ref, o_out), (x1_ref, x1_out), (mem_ref, mem_out))
        for k, (source, target) in enumerate(stored):
            outs.append(pltpu.make_async_copy(source, target, out_sem.at[len(matrices) + k]))
        go((2, "two"), (3, "two"))
        norms = local["norms"]
        norm_all(x_ref, norms, 0, h_ref, rows, IMG_CHUNK)
        project(h_ref, local["qkv"], qkv_ref, 3 * D, 0.125)
        outs[-4].start()

        def between(step):
            for number, task in ((0, (2, "three")), (1, (3, "three")), (4, (2, "four")), (7, (3, "four"))):

                @pl.when(step == number)
                def _():
                    go(task)

        attend_with(
            tables, qkv_ref, qkv_ref, D, qkv_ref, 2 * D, o_ref, lse_ref, IMG, IMG, False, True, between
        )
        outs[-3].start()
        add_project(x_ref, o_ref, local["out"], x1_ref)
        outs[-2].start()
        norm_all(x1_ref, norms, 2, h_ref, rows, IMG_CHUNK)

        @pl.loop(0, tables)
        def _(table):
            part = pl.ds(pl.multiple_of(table * IMG, 16), IMG)
            for start in range(0, FF, 256):
                lanes = slice(start, start + 256)
                g_ref[:, lanes] = gelu(dot(h_ref[part, :], local["ffn_in"][:, lanes])).astype(bf16)
            for start in range(0, D, 256):
                lanes = slice(start, start + 256)
                value = x1_ref[part, lanes] + dot(g_ref[...], local["ffn_out"][:, lanes])
                mem_ref[part, lanes] = value.astype(bf16)

        outs[-1].start()
        go((2, "five"), (3, "five"))
        place_blocks(decoder_all, flat_ref, amounts[1])
        give = {
            name: pltpu.make_async_copy(far[name], decoder_out[name], far_sem.at[k])
            for k, name in enumerate(moved)
        }
        take_matrices(
            flat_ref, layouts[1], {**decoder_out, **far}, lambda name: name in give and give[name].start()
        )
        outs.extend(give.values())
        go((0, "close"), (1, "close"), (2, "close"), (3, "close"))
        for out in outs:
            out.wait()

    vmem, hbm = pl.BlockSpec(memory_space=pltpu.VMEM), pl.BlockSpec(memory_space=pl.ANY)
    outs = pl.pallas_call(
        kernel,
        out_shape=(
            *shapes[0].values(),
            *shapes[1].values(),
            jax.ShapeDtypeStruct((8, 128), f32),
            jax.ShapeDtypeStruct((rows, 3 * D), bf16),
            jax.ShapeDtypeStruct((rows, D), bf16),
            jax.ShapeDtypeStruct((tables * HEADS, IMG), f32),
            jax.ShapeDtypeStruct((rows, D), f32),
            jax.ShapeDtypeStruct((rows, D), bf16),
        ),
        in_specs=[vmem] * 4 + [pl.BlockSpec(memory_space=pltpu.SMEM)],
        out_specs=(
            *[vmem if name == "norms" else hbm for name in shapes[0]],
            *[hbm if name in moved else vmem for name in shapes[1]],
            vmem, hbm, hbm, vmem, hbm, hbm,
        ),
        scratch_shapes=[
            pltpu.VMEM((count, small, 128), bf16),
            pltpu.VMEM((count, large, 128), bf16),
            pltpu.VMEM((max(flat_counts), 128), f32),
            pltpu.VMEM((rows, 3 * D), bf16),
            pltpu.VMEM((rows, D), bf16),
            pltpu.VMEM((IMG, FF), bf16),
            *[pltpu.VMEM(shapes[0][name].shape, bf16) for name in matrices],
            pltpu.VMEM((rows, D), bf16),
            pltpu.VMEM((rows, D), f32),
            pltpu.VMEM((rows, D), bf16),
            pltpu.SemaphoreType.DMA((len(matrices) + 4,)),
            pltpu.SemaphoreType.DMA((len(moved),)),
            *[pltpu.VMEM(shapes[1][name].shape, bf16) for name in moved],
            *[pltpu.SemaphoreType.DMA((n,)) for n in (count - 1, count) * 4],
        ],
        compiler_params=pltpu.CompilerParams(
            collective_id=1, has_side_effects=True, vmem_limit_bytes=VMEM_LIMIT
        ),
        name="gather_and_encode",
    )(images, encoder_block, decoder_block, cell_mask, lengths)
    encoder_weights = dict(zip(shapes[0], outs[:first]))
    decoder_weights = dict(zip(shapes[1], outs[first : first + second]))
    number, *stored, memory = outs[first + second :]
    return encoder_weights, decoder_weights, number[0, 0], stored, memory


def adam_update(gradient, master, first_state, second_state, average):
    first_new = BETA_ONE * first_state + (1.0 - BETA_ONE) * gradient
    second_new = BETA_TWO * second_state + (1.0 - BETA_TWO) * gradient * gradient
    first_hat = first_new / (1.0 - BETA_ONE**STEP)
    second_hat = second_new / (1.0 - BETA_TWO**STEP)
    master_new = master - LEARN_RATE * (
        first_hat / (jnp.sqrt(second_hat) + EPSILON) + WEIGHT_DECAY * master
    )
    average_new = SMOOTH * average + (1.0 - SMOOTH) * master_new
    return (first_new, second_new, master_new, average_new)


def shard_block(shard):
    rows = block_rows(shard.shape[0])
    return jnp.pad(shard, (0, rows * 128 - shard.shape[0])).reshape(rows, 128)


def on_device(place, *arguments):
    (
        images, tag_ids, tag_lengths, cell_mask, cell_index, box_targets,
        encoder_params, encoder_first, encoder_second, encoder_average,
        decoder_params, decoder_first, decoder_second, decoder_average,
    ) = arguments
    encoder_amount, decoder_amount = encoder_params.shape[0], decoder_params.shape[0]
    amounts = (encoder_amount, decoder_amount)
    encoder_weights, decoder_weights, cell_total, stored, memory = gather_and_encode(
        place, images, shard_block(encoder_params), shard_block(decoder_params), cell_mask, tag_lengths, amounts
    )
    prepared = (tag_ids, tag_lengths, cell_mask, cell_index, box_targets)
    scale = (1.0 / cell_total).reshape(1, 1)
    loss_block, dmemory, decoder_grads = decoder_step(prepared, scale, memory, decoder_weights)
    decoder_packed = pack_grads(
        decoder_grads, decoder_layout(), decoder_amount, place.count, "pack_decoder"
    )
    encoder_sum, decoder_sum, stats = encoder_backward(
        place, images, stored, dmemory, encoder_weights, decoder_packed, amounts, loss_block
    )
    grad_norm = jnp.sqrt(stats[0, 0])
    factor = CLIP_NORM / jnp.maximum(grad_norm, CLIP_NORM)
    encoder_grad = encoder_sum.reshape(-1)[:encoder_amount]
    decoder_grad = decoder_sum.reshape(-1)[:decoder_amount]
    encoder_new = adam_update(
        encoder_grad * factor, encoder_params, encoder_first, encoder_second, encoder_average
    )
    decoder_new = adam_update(
        decoder_grad * factor, decoder_params, decoder_first, decoder_second, decoder_average
    )
    return (stats[1, 0], cell_total, grad_norm, *encoder_new, *decoder_new)


def solution(mesh):
    rows, flat = P(AXES, None), P(AXES)
    return jax.shard_map(
        functools.partial(on_device, Place(mesh.shape["wide"], mesh.shape["narrow"])),
        mesh=mesh,
        in_specs=(rows, rows, flat, rows, rows, P(AXES, None, None)) + (flat,) * 8,
        out_specs=(P(), P(), P()) + (flat,) * 8,
        check_vma=False,
    )
```
